32 devices in a mesh: hist: 16 (over z, y, x), dom: 2 (over core).
Axes of the slice: x: 2, y: 2, z: 4, core: 2. Of those that a mesh axis runs over, the one named last changes fastest.
Arguments:
- coords: float32 [6, 65536], P(None, ('dom', 'hist')), may hold values from -3 to 3
- charge: float32 [65536], P(('dom', 'hist')), may hold values from 0.02 to 0.2
- row_index: int32 [65536], P(('dom', 'hist')), may hold values from 0 to 511, as said below
- block_col: int32 [512], P(('dom', 'hist')), may hold values from 0 to 496
- col_offset: int32 [65536], P(('dom', 'hist')), may hold values from 0 to 15
- transfer_map: float32 [6, 84], replicated
- history: bfloat16 [128, 2, 512, 512], P('hist', None, 'dom'), may hold values from -6 to 6
- retard_index: int32 [128], P('hist'), may hold values from 0 to 16
- retard_frac: float32 [128], P('hist'), may hold values from 0 to 1
- retard_weight: float32 [128], P('hist'), may hold values from 0.005 to 0.05
- z_kernel: float32 [512, 512], P(None, 'dom')
- x_kernel: float32 [512, 512], replicated
Outputs:
- kicked: float32 [6, 65536], P(None, ('dom', 'hist'))
- field: float32 [2, 512, 512], P(None, 'dom', 'hist')
- deposit: float32 [2, 512, 512], P(None, 'dom', 'hist')
The draws below stay inside these ranges and needn't reach their ends.
Inputs may be any that keep to these rules, and one draw needn't show every extreme that they name: `row_index`: particle i lies in grid slab i // (65536 // 2): its row is that slab's number times 256 plus 0 to 255.
All inputs are finite; a program needn't handle non-finite values.
Results may differ from the reference program's by a relative error of at most 0.0019.
Values may be sent and summed in bfloat16 or wider, within the bound.
No kernel may reach another device: no remote copies, remote signals or barrier semaphores. Data moves between devices by JAX's collectives and lax.ppermute only.
A program may use at most 64 MiB of HBM per device.

```python
import math
import jax
import jax.numpy as jnp
from jax import lax

NR = 512
NC = 512
P_DEV = 2048
BLOCK = 128
COLW = 16
KMAX = 16
SLAB = 256
NT = 128
PARTICLES = 65536
NBLOCKS = 512
N_DOM = 2


def draw_row_index(key, part):
    index = jnp.arange(PARTICLES, dtype=jnp.int32)
    slab_number = index // (PARTICLES // N_DOM)
    within = jax.random.randint(key, (PARTICLES,), 0, SLAB, dtype=jnp.int32)
    return (slab_number * SLAB + within).astype(jnp.int32)


def kernel_draw(key, order):
    noise = jax.random.normal(key, (order, order), jnp.float32)
    identity = (jnp.arange(order)[:, None] == jnp.arange(order)[None, :]).astype(jnp.float32)
    return identity + 0.5 * noise / jnp.sqrt(jnp.float32(order))


def draw_z_kernel(key, part):
    return kernel_draw(jax.random.fold_in(key, 11), NR)


def draw_x_kernel(key, part):
    return kernel_draw(jax.random.fold_in(key, 23), NC)


def draw_transfer_map(key, part):
    noise = 0.05 * jax.random.normal(key, (6, 84), jnp.float32)
    linear = (jnp.arange(84)[None, :] == jnp.arange(6)[:, None] + 1).astype(jnp.float32)
    return linear + noise


def set_ends(drawn, own_key, low, top_value):
    longest = drawn.shape.index(max(drawn.shape))
    spots = []
    for shift in (0, 1):
        where = [jax.random.randint(jax.random.fold_in(own_key, axis), (), 0, length) for axis, length in enumerate(drawn.shape)]
        where[longest] = (where[longest] + shift) % drawn.shape[longest]
        spots.append(tuple(where))
    return drawn.at[spots[0]].set(low).at[spots[1]].set(top_value)


def spiked(values, own_key, source, target, blocks, factor):
    owner, partner = [(jnp.arange(values.shape[dim]) // (values.shape[dim] // blocks)).reshape([-1 if axis == dim else 1 for axis in range(values.ndim)]) for dim in (source, target)]
    chosen = jax.random.permutation(own_key, blocks)[partner]
    strong = (owner == chosen) | (owner == (partner + blocks // 2) % blocks)
    return jnp.where(strong, factor * values, values)


def shard_levels(stream_key, shape, pieces, low, top_value):
    gain = 1.0
    for axis_at, blocks in pieces:
        heights = jax.random.uniform(jax.random.fold_in(jax.random.fold_in(stream_key, 6), axis_at), (blocks,), jnp.float32, low / len(pieces), top_value / len(pieces))
        gain = gain * jnp.repeat(jnp.exp(heights), shape[axis_at] // blocks).reshape((-1,) + (1,) * (len(shape) - 1 - axis_at))
    return gain


def normal_values(rng, extent, deviation, limit, pieces=(), kind=jnp.bfloat16):
    drawn = deviation * jax.random.normal(rng, extent, jnp.float32)
    if pieces:
        drawn = drawn * shard_levels(rng, extent, pieces, -0.22, 0.18)
    return jnp.clip(drawn, -limit, limit).astype(kind)


def gaussian_with(rng, dims, spread, bound, shards, heavy, kind=jnp.bfloat16):
    drawn = spread * jax.random.normal(rng, dims, jnp.float32)
    if shards:
        drawn = drawn * shard_levels(rng, dims, shards, -0.22, 0.18)
    return jnp.clip(spiked(drawn, jax.random.fold_in(rng, 3), *heavy), -bound, bound).astype(kind)


def setup_inputs(seed: int = 0) -> dict:
    splits = jax.random.split(jax.random.key(seed), 13)
    return {
        "coords": normal_values(splits[0], (6, PARTICLES), 1.0, 3.0, ((1, 32),), jnp.float32),
        "charge": jnp.clip(jnp.exp(math.log(0.2) - 2.3025851 * jax.random.uniform(splits[1], (PARTICLES,), jnp.float32) ** shard_levels(splits[1], (PARTICLES,), ((0, 32),), -0.2, 0.2)), 0.02, 0.2),
        "row_index": draw_row_index(jax.random.fold_in(splits[12], 71), 0),
        "block_col": set_ends(jax.random.randint(splits[3], (NBLOCKS,), 0, NC - COLW + 1), jax.random.fold_in(splits[3], 1), 0, NC - COLW).astype(jnp.int32),
        "col_offset": set_ends(jax.random.randint(splits[4], (PARTICLES,), 0, COLW), jax.random.fold_in(splits[4], 1), 0, COLW - 1).astype(jnp.int32),
        "transfer_map": draw_transfer_map(jax.random.fold_in(splits[12], 71), 0),
        "history": gaussian_with(splits[6], (NT, 2, NR, NC), 1.0, 6.0, ((0, 16), (2, 2)), (0, 3, 16, 2.0)),
        "retard_index": set_ends(jax.random.randint(splits[7], (NT,), 0, KMAX + 1), jax.random.fold_in(splits[7], 1), 0, KMAX).astype(jnp.int32),
        "retard_frac": jnp.clip(1.0 * jax.random.uniform(splits[8], (NT,), jnp.float32) ** shard_levels(splits[8], (NT,), ((0, 16),), -0.2, 0.2), 0.0, 1.0),
        "retard_weight": jnp.clip(jnp.exp(math.log(0.05) - 2.3025851 * jax.random.uniform(splits[9], (NT,), jnp.float32) ** shard_levels(splits[9], (NT,), ((0, 16),), -0.2, 0.2)), 0.005, 0.05),
        "z_kernel": draw_z_kernel(jax.random.fold_in(splits[12], 71), 0),
        "x_kernel": draw_x_kernel(jax.random.fold_in(splits[12], 71), 0),
    }


def monomials(coords):
    products = [jnp.ones_like(coords[0])]
    for first in range(6):
        products.append(coords[first])
    for first in range(6):
        for second in range(first, 6):
            products.append(coords[first] * coords[second])
    for first in range(6):
        for second in range(first, 6):
            for third in range(second, 6):
                products.append(coords[first] * coords[second] * coords[third])
    return jnp.stack(products)


def retarded_source(history, retard_index, retard_frac, retard_weight):
    count_steps, comps, rows_here, width = history.shape

    def add_step(position, total):
        frame = lax.dynamic_index_in_dim(history, position, 0, keepdims=False).astype(jnp.float32)
        padded = jnp.pad(frame, ((0, 0), (0, 0), (width + 1, 0)))
        lag = retard_index[position].astype(jnp.int32)
        near = lax.dynamic_slice_in_dim(padded, (width + 1 - lag).astype(jnp.int32), width, 2)
        far = lax.dynamic_slice_in_dim(padded, (width - lag).astype(jnp.int32), width, 2)
        fraction = retard_frac[position]
        return total + retard_weight[position] * ((1.0 - fraction) * near + fraction * far)

    start = jnp.zeros((comps, rows_here, width), jnp.float32)
    return lax.fori_loop(0, count_steps, add_step, start)


def reference(coords, charge, row_index, block_col, col_offset, transfer_map, history, retard_index, retard_frac, retard_weight, z_kernel, x_kernel):
    highest = lax.Precision.HIGHEST
    grouped = coords.reshape(6, -1, P_DEV).transpose(1, 0, 2)

    def push_group(group_coords):
        return jnp.dot(transfer_map, monomials(group_coords), precision=highest)

    pushed = lax.map(push_group, grouped).transpose(1, 0, 2).reshape(6, -1)
    column = (jnp.repeat(block_col, BLOCK) + col_offset).astype(jnp.int32)
    weights = jnp.stack([charge, charge * pushed[1]]).astype(jnp.bfloat16)
    weights = lax.optimization_barrier(weights).astype(jnp.float32)
    flat = (row_index * NC + column).astype(jnp.int32)
    deposit = jnp.zeros((2, NR * NC), jnp.float32).at[:, flat].add(weights).reshape(2, NR, NC)
    source = retarded_source(history, retard_index, retard_frac, retard_weight)
    field = jnp.einsum("rs,csx->crx", z_kernel, source, precision=highest)
    field = jnp.einsum("crx,xy->cry", field, x_kernel, precision=highest)
    rounded = lax.optimization_barrier(field.astype(jnp.bfloat16)).astype(jnp.float32)
    sampled = rounded[:, row_index, column]
    kicked = pushed.at[5].add(0.5 * sampled[0]).at[1].add(0.5 * sampled[1])
    return kicked, field, deposit
```

```python
import functools

import jax
import jax.numpy as jnp
from jax import lax
from jax.experimental import pallas as pl
from jax.experimental.pallas import tpu as pltpu
from jax.sharding import PartitionSpec as P

SPAN = 16
LANES = 128
NT_DIMS = (((1,), (1,)), ((), ()))
VMEM = pl.BlockSpec(memory_space=pltpu.VMEM)
SMEM = pl.BlockSpec(memory_space=pltpu.SMEM)
LIMIT = 48 * 1024 * 1024


def call(kernel, out_shape, in_specs, out_specs, scratch=(), flops=0, moved=0):
    return pl.pallas_call(
        kernel,
        out_shape=out_shape,
        in_specs=in_specs,
        out_specs=out_specs,
        scratch_shapes=scratch,
        compiler_params=pltpu.CompilerParams(vmem_limit_bytes=LIMIT),
        cost_estimate=pl.CostEstimate(flops=flops, bytes_accessed=moved, transcendentals=0),
    )


def split(value):
    high = value.astype(jnp.bfloat16)
    return high, (value - high.astype(jnp.float32)).astype(jnp.bfloat16)


def shift_columns(pieces, lag, lane):
    rolled = [pltpu.roll(piece, lag, 1) for piece in pieces]
    before = [jnp.zeros_like(rolled[0])] + rolled[:-1]
    wrapped = lane < lag
    return [jnp.where(wrapped, prior, here) for prior, here in zip(before, rolled)]


def source_kernel(
    strips, history, lags, fracs, weights, x_kernel, spread, x_parts, s_parts, spread_all
):
    comp, chunk = pl.program_id(0), pl.program_id(1)
    count_steps, _, chunk_rows, width = history.shape
    strip = width // strips
    lane = lax.broadcasted_iota(jnp.int32, (16, LANES), 1)

    @pl.when((comp == 0) & (chunk == 0))
    def _():
        high, low = split(x_kernel[...].T)
        x_parts[:, :width] = high
        x_parts[:, width : 2 * width] = high
        x_parts[:, 2 * width :] = low

    lag = [lags[t] for t in range(count_steps)]
    far_weight = [weights[t] * fracs[t] for t in range(count_steps)]
    near_weight = [weights[t] * (1.0 - fracs[t]) for t in range(count_steps)]
    pieces = width // LANES

    def one_group(group, carry):
        first = pl.multiple_of(group * 16, 16)
        near = [jnp.zeros((16, LANES), jnp.float32)] * pieces
        far = [jnp.zeros((16, LANES), jnp.float32)] * pieces
        for t in range(count_steps):
            frame = history[t, 0, pl.ds(first, 16), :].astype(jnp.float32)
            parts = [frame[:, LANES * q : LANES * (q + 1)] for q in range(pieces)]
            moved = shift_columns(parts, lag[t], lane)
            near = [total + near_weight[t] * part for total, part in zip(near, moved)]
            far = [total + far_weight[t] * part for total, part in zip(far, moved)]
        far = shift_columns(far, 1, lane)
        rows = pl.ds(pl.multiple_of(chunk * chunk_rows + first, 16), 16)
        for q in range(pieces):
            high, low = split(near[q] + far[q])
            s_parts[rows, LANES * q : LANES * (q + 1)] = high
            s_parts[rows, width + LANES * q : width + LANES * (q + 1)] = low
            s_parts[rows, 2 * width + LANES * q : 2 * width + LANES * (q + 1)] = high
        return carry

    lax.fori_loop(0, chunk_rows // 16, one_group, 0)

    @pl.when(chunk == pl.num_programs(1) - 1)
    def _():
        spread_all[comp] = lax.dot_general(
            x_parts[...], s_parts[...], NT_DIMS, preferred_element_type=jnp.float32
        )

    @pl.when((chunk == pl.num_programs(1) - 1) & (comp == pl.num_programs(0) - 1))
    def _():
        for place in range(strips):
            columns = slice(place * strip, (place + 1) * strip)
            both = jnp.concatenate([spread_all[0, columns], spread_all[1, columns]], axis=0)
            spread[place] = both.astype(spread.dtype)


def retarded_spread(history, retard_index, retard_frac, retard_weight, x_kernel, strips):
    count_steps, comps, rows, width = history.shape
    chunk = min(64, rows)
    return pl.pallas_call(
        functools.partial(source_kernel, strips),
        grid=(comps, rows // chunk),
        out_shape=jax.ShapeDtypeStruct((strips, comps * width // strips, rows), jnp.bfloat16),
        in_specs=[
            pl.BlockSpec((count_steps, 1, chunk, width), lambda c, j: (0, c, j, 0)),
            SMEM,
            SMEM,
            SMEM,
            pl.BlockSpec((width, width), lambda c, j: (0, 0)),
        ],
        out_specs=pl.BlockSpec((strips, comps * width // strips, rows), lambda c, j: (0, 0, 0)),
        scratch_shapes=[
            pltpu.VMEM((width, 3 * width), jnp.bfloat16),
            pltpu.VMEM((rows, 3 * width), jnp.bfloat16),
            pltpu.VMEM((comps, width, rows), jnp.float32),
        ],
        compiler_params=pltpu.CompilerParams(vmem_limit_bytes=LIMIT),
        cost_estimate=pl.CostEstimate(
            flops=6 * comps * rows * width * width,
            bytes_accessed=history.size * 2 + 2 * x_kernel.size * 4,
            transcendentals=0,
        ),
    )(history, retard_index, retard_frac, retard_weight, x_kernel)


def push_kernel(place, transfer, coords, charge, rows, offsets, block_col, pushed, record):
    blocks = charge.shape[0]
    width = place[2]
    u = [
        jnp.concatenate(
            [coords[i : i + 1, LANES * b : LANES * (b + 1)] for b in range(blocks)], axis=0
        )
        for i in range(6)
    ]
    total = [jnp.full((blocks, LANES), transfer[i, 0], jnp.float32) for i in range(6)]
    column = 1
    degree1 = u
    degree2 = {}
    for term in degree1:
        total = [total[i] + transfer[i, column] * term for i in range(6)]
        column += 1
    for first in range(6):
        for second in range(first, 6):
            term = u[first] * u[second]
            degree2[first, second] = term
            total = [total[i] + transfer[i, column] * term for i in range(6)]
            column += 1
    for first in range(6):
        for second in range(first, 6):
            for third in range(second, 6):
                term = degree2[first, second] * u[third]
                total = [total[i] + transfer[i, column] * term for i in range(6)]
                column += 1
    for i in range(6):
        pushed[i] = total[i]
    weight0 = charge[...]
    weight1 = weight0 * total[1]
    row_of = lax.broadcasted_iota(jnp.int32, (blocks, LANES), 0)
    lane = lax.broadcasted_iota(jnp.int32, (8, LANES), 1)
    base = jnp.zeros((blocks, LANES), jnp.int32)
    starts = jnp.zeros((8, LANES), jnp.int32)
    for b in range(blocks):
        base = jnp.where(row_of == b, block_col[b], base)
        starts = jnp.where(lane == b, block_col[b], starts)
    flat = (rows[...] - place[1]) * width + base + offsets[...]
    record[0:blocks] = flat.astype(jnp.float32)
    record[blocks : 2 * blocks] = weight0.astype(jnp.bfloat16).astype(jnp.float32)
    record[2 * blocks : 3 * blocks] = weight1.astype(jnp.bfloat16).astype(jnp.float32)
    record[3 * blocks : 3 * blocks + 8] = starts.astype(jnp.float32)


def deposit_kernel(width, place, starts, record, deposit, chosen, total):
    senders, _, _ = record.shape
    blocks = starts.shape[0] // senders
    slab_rows, strip = deposit.shape[1:]
    first_column = place[0] * strip

    def mark(block, count):
        chosen[1 + count] = block
        start = starts[block]
        meets = (start + (SPAN - 1) >= first_column) & (start < first_column + strip)
        return count + jnp.where(meets, 1, 0)

    count = lax.fori_loop(0, senders * blocks, mark, 0)
    chosen[0] = count
    total[...] = jnp.zeros_like(total)
    row_iota = lax.broadcasted_iota(jnp.int32, (slab_rows, LANES), 0)
    column_iota = lax.broadcasted_iota(jnp.int32, (strip, LANES), 0)

    def block_pair(index):
        block = chosen[1 + index]
        sender, own = block // blocks, lax.rem(block, blocks)
        flat = record[sender, pl.ds(own, 1), :].astype(jnp.int32)
        weight0 = record[sender, pl.ds(blocks + own, 1), :]
        weight1 = record[sender, pl.ds(2 * blocks + own, 1), :]
        row, column = flat // width, lax.rem(flat, width) - first_column
        row_hot = jnp.where(row_iota == row, 1.0, 0.0).astype(jnp.bfloat16)
        hit = column_iota == column
        weighted = jnp.concatenate(
            [jnp.where(hit, weight0, 0.0), jnp.where(hit, weight1, 0.0)], axis=0
        ).astype(jnp.bfloat16)
        return row_hot, weighted

    def one_block(index, carry):
        row_hot, weighted = block_pair(index)
        total[...] += lax.dot_general(
            row_hot, weighted, NT_DIMS, preferred_element_type=jnp.float32
        )
        return carry

    lax.fori_loop(0, count, one_block, 0)
    deposit[0] = total[:, :strip]
    deposit[1] = total[:, strip:]


def join_kernel(place, z_kernel, received, kept, *sent):
    total = received[0].astype(jnp.float32)
    for sender in range(1, received.shape[0]):
        total = total + received[sender].astype(jnp.float32)
    slab_rows = total.shape[1]
    high, low = split(total)
    left = jnp.concatenate([high, low, high], axis=1)

    def part(slab):
        start = pl.multiple_of(slab * slab_rows, slab_rows)
        z_high, z_low = split(z_kernel[pl.ds(start, slab_rows), :])
        right = jnp.concatenate([z_high, z_high, z_low], axis=1)
        return lax.dot_general(left, right, NT_DIMS, preferred_element_type=jnp.float32)

    if sent:
        sent[0][...] = part(1 - place[3])
        kept[...] = part(place[3])
    else:
        for slab in range(kept.shape[0]):
            kept[slab] = part(slab)


def sample_kernel(width, place, chosen, record, *refs):
    parts, (field, samples, scratch) = refs[:-3], refs[-3:]
    senders, _, _ = record.shape
    slab_rows, strip = field.shape[1:]
    blocks = samples.shape[1] // 2
    first_column = place[0] * strip
    total = None
    for piece in parts:
        if len(piece.shape) == 3:
            values = piece[0]
            for index in range(1, piece.shape[0]):
                values = values + piece[index]
        else:
            values = piece[...]
        total = values if total is None else total + values
    field[0] = total[:strip].T
    field[1] = total[strip:].T
    rounded = total.astype(jnp.bfloat16)
    scratch[...] = jnp.zeros_like(scratch)
    row_iota = lax.broadcasted_iota(jnp.int32, (slab_rows, LANES), 0)
    column_iota = lax.broadcasted_iota(jnp.int32, (strip, LANES), 0)

    def one_block(index, carry):
        block = chosen[1 + index]
        sender, own = block // blocks, lax.rem(block, blocks)
        flat = record[sender, pl.ds(own, 1), :].astype(jnp.int32)
        row, column = flat // width, lax.rem(flat, width) - first_column
        row_hot = jnp.where(row_iota == row, 1.0, 0.0).astype(jnp.bfloat16)
        found = jnp.dot(rounded, row_hot, preferred_element_type=jnp.float32)
        hit = column_iota == column
        for comp in range(2):
            picked = jnp.where(hit, found[comp * strip : (comp + 1) * strip], 0.0)
            scratch[sender, pl.ds(comp * blocks + own, 1), :] = jnp.sum(
                picked, axis=0, keepdims=True
            )
        return carry

    lax.fori_loop(0, chosen[0], one_block, 0)
    samples[...] = scratch[...].astype(jnp.bfloat16)


def kick_kernel(pushed, received, kicked):
    blocks = pushed.shape[1]
    total = received[0].astype(jnp.float32)
    for sender in range(1, received.shape[0]):
        total = total + received[sender].astype(jnp.float32)
    values = [pushed[i] for i in range(6)]
    values[5] = values[5] + 0.5 * total[:blocks]
    values[1] = values[1] + 0.5 * total[blocks:]
    for b in range(blocks):
        kicked[:, LANES * b : LANES * (b + 1)] = jnp.concatenate(
            [value[b : b + 1] for value in values], axis=0
        )


def local(
    coords,
    charge,
    row_index,
    block_col,
    col_offset,
    transfer_map,
    history,
    retard_index,
    retard_frac,
    retard_weight,
    z_kernel,
    x_kernel,
):
    strips = lax.axis_size("hist")
    slabs = lax.axis_size("dom")
    slab_rows, width = history.shape[2:]
    strip = width // strips
    particles = coords.shape[1]
    blocks = block_col.shape[0]
    hist, dom = lax.axis_index("hist"), lax.axis_index("dom")
    place = jnp.stack([hist, dom * slab_rows, width, dom]).astype(jnp.int32)

    spread = retarded_spread(
        history, retard_index, retard_frac, retard_weight, x_kernel, strips
    )
    spread_here = lax.all_to_all(spread, "hist", 0, 0, tiled=True)

    f32 = jnp.float32
    tile = (blocks, LANES)
    record_rows = 3 * blocks + 8
    pushed, record = call(
        push_kernel,
        (
            jax.ShapeDtypeStruct((6,) + tile, f32),
            jax.ShapeDtypeStruct((record_rows, LANES), f32),
        ),
        [SMEM, SMEM, VMEM, VMEM, VMEM, VMEM, SMEM],
        (VMEM, VMEM),
        flops=1200 * particles,
        moved=1 << 18,
    )(
        place,
        transfer_map,
        coords,
        charge.reshape(tile),
        row_index.reshape(tile),
        col_offset.reshape(tile),
        block_col,
    )
    records = lax.all_gather(record, "hist", axis=0)
    starts = records[:, 3 * blocks, :blocks].astype(jnp.int32).reshape(strips * blocks)

    deposit, chosen = call(
        functools.partial(deposit_kernel, width),
        (
            jax.ShapeDtypeStruct((2, slab_rows, strip), f32),
            jax.ShapeDtypeStruct((strips * blocks + 8,), jnp.int32),
        ),
        [SMEM, SMEM, VMEM],
        (VMEM, SMEM),
        [pltpu.VMEM((slab_rows, 2 * strip), f32)],
        flops=1 << 30,
        moved=1 << 20,
    )(place, starts, records)

    part = jax.ShapeDtypeStruct((2 * strip, slab_rows), f32)
    if slabs == 2:
        kept, sent = call(
            join_kernel, (part, part), [SMEM, VMEM, VMEM], (VMEM, VMEM), flops=1 << 27, moved=1 << 20
        )(place, z_kernel, spread_here)
        parts = (kept, lax.ppermute(sent, "dom", [(0, 1), (1, 0)]))
    else:
        terms = call(
            join_kernel,
            jax.ShapeDtypeStruct((slabs, 2 * strip, slab_rows), f32),
            [SMEM, VMEM, VMEM],
            VMEM,
            flops=1 << 27,
            moved=1 << 20,
        )(place, z_kernel, spread_here)
        parts = (lax.all_to_all(terms, "dom", 0, 0, tiled=True),)

    field, samples = call(
        functools.partial(sample_kernel, width),
        (
            jax.ShapeDtypeStruct((2, slab_rows, strip), f32),
            jax.ShapeDtypeStruct((strips, 2 * blocks, LANES), jnp.bfloat16),
        ),
        [SMEM, SMEM, VMEM] + [VMEM] * len(parts),
        (VMEM, VMEM),
        [pltpu.VMEM((strips, 2 * blocks, LANES), f32)],
        flops=1 << 29,
        moved=1 << 20,
    )(place, chosen, records, *parts)
    samples_here = lax.all_to_all(samples, "hist", 0, 0, tiled=True)
    kicked = call(
        kick_kernel,
        jax.ShapeDtypeStruct((6, particles), f32),
        [VMEM, VMEM],
        VMEM,
        flops=1 << 16,
        moved=1 << 18,
    )(pushed, samples_here)
    return kicked, field, deposit


def solution(mesh):
    return jax.shard_map(
        local,
        mesh=mesh,
        in_specs=(
            P(None, ("dom", "hist")),
            P(("dom", "hist")),
            P(("dom", "hist")),
            P(("dom", "hist")),
            P(("dom", "hist")),
            P(),
            P("hist", None, "dom", None),
            P("hist"),
            P("hist"),
            P("hist"),
            P(None, "dom"),
            P(),
        ),
        out_specs=(P(None, ("dom", "hist")), P(None, "dom", "hist"), P(None, "dom", "hist")),
        check_vma=False,
    )
```

```python
import functools

import jax
import jax.numpy as jnp
from jax import lax
from jax.experimental import pallas as pl
from jax.experimental.pallas import tpu as pltpu
from jax.sharding import PartitionSpec as P

SPAN = 16
LANES = 128
NT_DIMS = (((1,), (1,)), ((), ()))
VMEM = pl.BlockSpec(memory_space=pltpu.VMEM)
SMEM = pl.BlockSpec(memory_space=pltpu.SMEM)
HBM = pl.BlockSpec(memory_space=pltpu.HBM)
LIMIT = 60 * 1024 * 1024
SMALL = 16 * 1024 * 1024
GROUP = 4


def call(kernel, out_shape, in_specs, out_specs, scratch=(), flops=0, moved=0, limit=SMALL):
    return pl.pallas_call(
        kernel,
        out_shape=out_shape,
        in_specs=in_specs,
        out_specs=out_specs,
        scratch_shapes=scratch,
        compiler_params=pltpu.CompilerParams(vmem_limit_bytes=limit),
        cost_estimate=pl.CostEstimate(flops=flops, bytes_accessed=moved, transcendentals=0),
    )


def split(value):
    high = value.astype(jnp.bfloat16)
    return high, (value - high.astype(jnp.float32)).astype(jnp.bfloat16)


def shift_columns(pieces, lag, lane):
    rolled = [pltpu.roll(piece, lag, 1) for piece in pieces]
    before = [jnp.zeros_like(rolled[0])] + rolled[:-1]
    wrapped = lane < lag
    return [jnp.where(wrapped, prior, here) for prior, here in zip(before, rolled)]


def pairwise(strips):
    return strips <= 16 and strips & (strips - 1) == 0


def exchange(pieces, strips):
    if not pairwise(strips):
        return [lax.all_to_all(pieces[0], "hist", 0, 0, tiled=True)]
    arrived = [pieces[0]]
    for k in range(1, strips):
        pairs = [(i, i ^ k) for i in range(strips)]
        arrived.append(lax.ppermute(pieces[k], "hist", pairs))
    return arrived


def piece_shapes(strips, shape, dtype):
    if not pairwise(strips):
        return [jax.ShapeDtypeStruct((strips,) + shape, dtype)]
    return [jax.ShapeDtypeStruct(shape, dtype)] * strips


def store_pieces(refs, strips, hist, make):
    if len(refs) == 1:
        for partner in range(strips):
            refs[0][partner] = make(partner).astype(refs[0].dtype)
    else:
        for k, ref in enumerate(refs):
            ref[...] = make(hist ^ k).astype(ref.dtype)


def add_pieces(refs):
    if len(refs) == 1:
        terms = [refs[0].at[sender] for sender in range(refs[0].shape[0])]
    else:
        terms = refs
    total = terms[0][...].astype(jnp.float32)
    for term in terms[1:]:
        total = total + term[...].astype(jnp.float32)
    return total


def source_kernel(strips, place, lags, fracs, weights, history, x_kernel, after, *refs):
    pieces = refs[:-6]
    frames, x_here, x_parts, s_parts, spread_all, sems = refs[-6:]
    del after
    count_steps, comps, slab_rows, width = history.shape
    strip = width // strips
    chunk_rows = min(64, slab_rows)
    chunks = slab_rows // chunk_rows
    lane = lax.broadcasted_iota(jnp.int32, (16, LANES), 1)

    def fetch(comp, chunk):
        rows = pl.ds(chunk * chunk_rows, chunk_rows)
        return pltpu.make_async_copy(
            history.at[:, comp, rows, :], frames.at[:, comp, rows, :], sems.at[comp, chunk]
        )

    fetch_x = pltpu.make_async_copy(x_kernel, x_here, sems.at[comps, 0])
    fetch(0, 0).start()
    fetch_x.start()
    for comp in range(comps):
        for chunk in range(chunks):
            if comp + chunk > 0:
                fetch(comp, chunk).start()

    lag = [lags[t] for t in range(count_steps)]
    far_weight = [weights[t] * fracs[t] for t in range(count_steps)]
    near_weight = [weights[t] * (1.0 - fracs[t]) for t in range(count_steps)]
    columns = [slice(LANES * q, LANES * (q + 1)) for q in range(width // LANES)]

    def one_group(comp, first, row):
        near = [jnp.zeros((16, LANES), jnp.float32)] * len(columns)
        far = [jnp.zeros((16, LANES), jnp.float32)] * len(columns)
        for t in range(count_steps):
            frame = frames[t, comp, pl.ds(first, 16), :].astype(jnp.float32)
            moved = shift_columns([frame[:, column] for column in columns], lag[t], lane)
            near = [total + near_weight[t] * part for total, part in zip(near, moved)]
            far = [total + far_weight[t] * part for total, part in zip(far, moved)]
        far = shift_columns(far, 1, lane)
        for q in range(len(columns)):
            high, low = split(near[q] + far[q])
            rows = pl.ds(row, 16)
            s_parts[rows, LANES * q : LANES * (q + 1)] = high
            s_parts[rows, width + LANES * q : width + LANES * (q + 1)] = low
            s_parts[rows, 2 * width + LANES * q : 2 * width + LANES * (q + 1)] = high

    for comp in range(comps):

        def one_chunk(chunk, carry):
            start = pl.multiple_of(chunk * chunk_rows, chunk_rows)
            rows = pl.ds(start, chunk_rows)
            pltpu.make_async_copy(
                history.at[:, comp, rows, :], frames.at[:, comp, rows, :], sems.at[comp, chunk]
            ).wait()
            for group in range(chunk_rows // 16):
                first = pl.multiple_of(start + 16 * group, 16)
                one_group(comp, first, pl.multiple_of(comp * slab_rows + first, 16))
            return carry

        lax.fori_loop(0, chunks, one_chunk, 0)

    fetch_x.wait()
    high, low = split(x_here[...])
    x_parts[:width] = high
    x_parts[width : 2 * width] = high
    x_parts[2 * width :] = low
    for comp in range(comps):
        spread = jnp.dot(
            s_parts[comp * slab_rows : (comp + 1) * slab_rows],
            x_parts[...],
            preferred_element_type=jnp.float32,
        )
        spread_all[comp] = spread.T

    def strip_of(partner):
        start = partner * strip
        if not isinstance(partner, int):
            start = pl.multiple_of(start, strip)
        rows = pl.ds(start, strip)
        return jnp.concatenate([spread_all[comp, rows] for comp in range(comps)], axis=0)

    store_pieces(pieces, strips, place[0], strip_of)


def retarded_spread(
    place, history, retard_index, retard_frac, retard_weight, x_kernel, after, strips
):
    count_steps, comps, rows, width = history.shape
    chunks = rows // min(64, rows)
    shapes = piece_shapes(strips, (comps * width // strips, rows), jnp.bfloat16)
    if pairwise(strips):
        shapes[0] = jax.ShapeDtypeStruct(shapes[0].shape, jnp.float32)
    return call(
        functools.partial(source_kernel, strips),
        shapes,
        [SMEM, SMEM, SMEM, SMEM, HBM, HBM, HBM],
        [VMEM] * len(shapes),
        [
            pltpu.VMEM(history.shape, jnp.bfloat16),
            pltpu.VMEM((width, width), jnp.float32),
            pltpu.VMEM((3 * width, width), jnp.bfloat16),
            pltpu.VMEM((comps * rows, 3 * width), jnp.bfloat16),
            pltpu.VMEM((comps, width, rows), jnp.float32),
            pltpu.SemaphoreType.DMA((comps + 1, chunks)),
        ],
        flops=6 * comps * rows * width * width,
        moved=history.size * 2 + x_kernel.size * 4,
    )(place, retard_index, retard_frac, retard_weight, history, x_kernel, after)


def push_kernel(place, transfer, coords, charge, rows, offsets, block_col, pushed, record):
    blocks = charge.shape[0]
    width = place[2]
    u = [
        jnp.concatenate(
            [coords[i : i + 1, LANES * b : LANES * (b + 1)] for b in range(blocks)], axis=0
        )
        for i in range(6)
    ]
    total = [jnp.full((blocks, LANES), transfer[i, 0], jnp.float32) for i in range(6)]
    column = 1
    degree1 = u
    degree2 = {}
    for term in degree1:
        total = [total[i] + transfer[i, column] * term for i in range(6)]
        column += 1
    for first in range(6):
        for second in range(first, 6):
            term = u[first] * u[second]
            degree2[first, second] = term
            total = [total[i] + transfer[i, column] * term for i in range(6)]
            column += 1
    for first in range(6):
        for second in range(first, 6):
            for third in range(second, 6):
                term = degree2[first, second] * u[third]
                total = [total[i] + transfer[i, column] * term for i in range(6)]
                column += 1
    for i in range(6):
        pushed[i] = total[i]
    weight0 = charge[...]
    weight1 = weight0 * total[1]
    row_of = lax.broadcasted_iota(jnp.int32, (blocks, LANES), 0)
    lane = lax.broadcasted_iota(jnp.int32, (8, LANES), 1)
    base = jnp.zeros((blocks, LANES), jnp.int32)
    starts = jnp.zeros((8, LANES), jnp.int32)
    for b in range(blocks):
        base = jnp.where(row_of == b, block_col[b], base)
        starts = jnp.where(lane == b, block_col[b], starts)
    flat = (rows[...] - place[1]) * width + base + offsets[...]
    record[0:blocks] = flat.astype(jnp.float32)
    record[blocks : 2 * blocks] = weight0.astype(jnp.bfloat16).astype(jnp.float32)
    record[2 * blocks : 3 * blocks] = weight1.astype(jnp.bfloat16).astype(jnp.float32)
    record[3 * blocks : 3 * blocks + 8] = starts.astype(jnp.float32)


def gather_records(refs, records):
    if len(refs) == 1:
        partners = refs[0].shape[0]
        records[0:partners] = refs[0][...]
    else:
        partners = len(refs)
        for k, ref in enumerate(refs):
            records[k] = ref[...]
    records[partners] = jnp.full(records.shape[1:], -1.0, jnp.float32)


def read_group(width, first_column, blocks, chosen, records, group):
    where = []
    for member in range(GROUP):
        block = chosen[1 + group * GROUP + member]
        where.append((block // blocks, lax.rem(block, blocks)))
    flat = jnp.concatenate(
        [records[sender, pl.ds(own, 1), :] for sender, own in where], axis=1
    ).astype(jnp.int32)
    if width & (width - 1) == 0:
        row, column = flat >> (width.bit_length() - 1), flat & (width - 1)
    else:
        row, column = flat // width, lax.rem(flat, width)
    return where, row, column - first_column


def one_hot_rows(row, slab_rows):
    row_iota = lax.broadcasted_iota(jnp.int32, (slab_rows, row.shape[1]), 0)
    return jnp.where(row_iota == row, 1.0, 0.0).astype(jnp.bfloat16)


def deposit_kernel(width, blocks, place, *refs):
    inputs, (deposit, chosen, records, total, heads, starts, sem) = refs[:-7], refs[-7:]
    partners = records.shape[0] - 1
    strip, slab_rows = deposit.shape[1:]
    first_column = place[0] * strip
    gather_records(inputs, records)
    for k in range(partners):
        heads[k : k + 1] = records[k, 3 * blocks : 3 * blocks + 1]
    copy = pltpu.make_async_copy(heads, starts, sem)
    copy.start()
    copy.wait()
    low = (first_column - (SPAN - 1)).astype(jnp.float32)
    high = (first_column + strip).astype(jnp.float32)

    def mark(k, count):
        for own in range(blocks):
            chosen[1 + count] = k * blocks + own
            start = starts[k, own]
            count = count + jnp.where((start >= low) & (start < high), 1, 0)
        return count

    count = lax.fori_loop(0, partners, mark, 0)
    groups = (count + (GROUP - 1)) // GROUP
    chosen[0] = groups
    for member in range(GROUP):
        chosen[1 + count + member] = partners * blocks
    total[...] = jnp.zeros_like(total)

    def one_group(group, carry):
        where, row, column = read_group(
            width, first_column, blocks, chosen, records, group
        )
        hit = lax.broadcasted_iota(jnp.int32, (strip, row.shape[1]), 0) == column
        weighted = []
        for comp in range(2):
            weight = jnp.concatenate(
                [records[sender, pl.ds((comp + 1) * blocks + own, 1), :] for sender, own in where],
                axis=1,
            )
            weighted.append(jnp.where(hit, weight, 0.0))
        total[...] += lax.dot_general(
            one_hot_rows(row, slab_rows),
            jnp.concatenate(weighted, axis=0).astype(jnp.bfloat16),
            NT_DIMS,
            preferred_element_type=jnp.float32,
        )
        return carry

    lax.fori_loop(0, groups, one_group, 0)
    turned = total[...].T
    deposit[0] = turned[:strip]
    deposit[1] = turned[strip:]


def join_kernel(slabs, place, z_kernel, after, *refs):
    del after
    outs = 2 if slabs == 2 else 1
    received, (kept, *sent) = refs[:-outs], refs[-outs:]
    total = add_pieces(received)
    slab_rows = total.shape[1]
    high, low = split(total)
    left = jnp.concatenate([high, low, high], axis=1)

    def part(slab):
        start = pl.multiple_of(slab * slab_rows, slab_rows)
        z_high, z_low = split(z_kernel[pl.ds(start, slab_rows), :])
        right = jnp.concatenate([z_high, z_high, z_low], axis=1)
        return lax.dot_general(left, right, NT_DIMS, preferred_element_type=jnp.float32)

    if sent:
        sent[0][...] = part(1 - place[3])
        kept[...] = part(place[3])
    else:
        for slab in range(slabs):
            kept[slab] = part(slab)


def sample_kernel(width, blocks, count_parts, count_records, place, chosen, *refs):
    parts = refs[:count_parts]
    inputs = refs[count_parts : count_parts + count_records]
    field, *samples = refs[count_parts + count_records : -2]
    records, found_all = refs[-2:]
    partners = records.shape[0] - 1
    strip, slab_rows = field.shape[1:]
    first_column = place[0] * strip
    gather_records(inputs, records)
    total = add_pieces(parts)
    field[0] = total[:strip]
    field[1] = total[strip:]
    rounded = total.astype(jnp.bfloat16)
    found_all[...] = jnp.zeros_like(found_all)

    def one_group(group, carry):
        where, row, column = read_group(
            width, first_column, blocks, chosen, records, group
        )
        found = jnp.dot(rounded, one_hot_rows(row, slab_rows), preferred_element_type=jnp.float32)
        hit = lax.broadcasted_iota(jnp.int32, (strip, row.shape[1]), 0) == column
        for comp in range(2):
            picked = jnp.where(hit, found[comp * strip : (comp + 1) * strip], 0.0)
            values = jnp.sum(picked, axis=0, keepdims=True)
            for member, (sender, own) in enumerate(where):
                found_all[sender, pl.ds(comp * blocks + own, 1), :] = values[
                    :, LANES * member : LANES * (member + 1)
                ]
        return carry

    lax.fori_loop(0, chosen[0], one_group, 0)
    if len(samples) == 1:
        samples[0][...] = found_all[:partners].astype(samples[0].dtype)
    else:
        for k, ref in enumerate(samples):
            ref[...] = found_all[k].astype(ref.dtype)


def kick_kernel(pushed, *refs):
    received, kicked = refs[:-1], refs[-1]
    blocks = pushed.shape[1]
    total = add_pieces(received)
    values = [pushed[i] for i in range(6)]
    values[5] = values[5] + 0.5 * total[:blocks]
    values[1] = values[1] + 0.5 * total[blocks:]
    for b in range(blocks):
        kicked[:, LANES * b : LANES * (b + 1)] = jnp.concatenate(
            [value[b : b + 1] for value in values], axis=0
        )


def local(
    coords,
    charge,
    row_index,
    block_col,
    col_offset,
    transfer_map,
    history,
    retard_index,
    retard_frac,
    retard_weight,
    z_kernel,
    x_kernel,
):
    strips = lax.axis_size("hist")
    slabs = lax.axis_size("dom")
    slab_rows, width = history.shape[2:]
    strip = width // strips
    particles = coords.shape[1]
    blocks = block_col.shape[0]
    hist, dom = lax.axis_index("hist"), lax.axis_index("dom")
    place = jnp.stack([hist, dom * slab_rows, width, dom]).astype(jnp.int32)

    f32 = jnp.float32
    tile = (blocks, LANES)
    record_shape = (3 * blocks + 8, LANES)
    pushed, record = call(
        push_kernel,
        (jax.ShapeDtypeStruct((6,) + tile, f32), jax.ShapeDtypeStruct(record_shape, f32)),
        [SMEM, SMEM, VMEM, VMEM, VMEM, VMEM, SMEM],
        (VMEM, VMEM),
        flops=1200 * particles,
        moved=1 << 18,
        limit=LIMIT,
    )(
        place,
        transfer_map,
        coords,
        charge.reshape(tile),
        row_index.reshape(tile),
        col_offset.reshape(tile),
        block_col,
    )
    if pairwise(strips):
        records = exchange([record] * strips, strips)
    else:
        records = [lax.all_gather(record, "hist", axis=0)]

    spread = retarded_spread(
        place, history, retard_index, retard_frac, retard_weight, x_kernel, record, strips
    )
    spread_here = exchange(spread, strips)

    stack = pltpu.VMEM((strips + 1,) + record_shape, f32)
    deposit, chosen = call(
        functools.partial(deposit_kernel, width, blocks),
        (
            jax.ShapeDtypeStruct((2, strip, slab_rows), f32),
            jax.ShapeDtypeStruct((strips * blocks + 8,), jnp.int32),
        ),
        [SMEM] + [VMEM] * len(records),
        (VMEM, SMEM),
        [
            stack,
            pltpu.VMEM((slab_rows, 2 * strip), f32),
            pltpu.VMEM((strips, LANES), f32),
            pltpu.SMEM((strips, LANES), f32),
            pltpu.SemaphoreType.DMA,
        ],
        flops=1 << 30,
        moved=1 << 20,
    )(place, *records)

    part = jax.ShapeDtypeStruct((2 * strip, slab_rows), f32)
    parts = call(
        functools.partial(join_kernel, slabs),
        (part, part) if slabs == 2 else jax.ShapeDtypeStruct((slabs,) + part.shape, f32),
        [SMEM, VMEM, HBM] + [VMEM] * len(spread_here),
        (VMEM, VMEM) if slabs == 2 else VMEM,
        flops=1 << 27,
        moved=1 << 20,
    )(place, z_kernel, chosen, *spread_here)
    if slabs == 2:
        kept, sent = parts
        parts = [kept, lax.ppermute(sent, "dom", [(0, 1), (1, 0)])]
    else:
        parts = [lax.all_to_all(parts, "dom", 0, 0, tiled=True)]

    sample_shapes = piece_shapes(strips, (2 * blocks, LANES), jnp.bfloat16)
    field, *samples = call(
        functools.partial(sample_kernel, width, blocks, len(parts), len(records)),
        [jax.ShapeDtypeStruct((2, strip, slab_rows), f32)] + sample_shapes,
        [SMEM, SMEM] + [VMEM] * (len(parts) + len(records)),
        [VMEM] * (1 + len(sample_shapes)),
        [stack, pltpu.VMEM((strips + 1, 2 * blocks, LANES), f32)],
        flops=1 << 29,
        moved=1 << 20,
    )(place, chosen, *parts, *records)
    samples_here = exchange(samples, strips)
    kicked = call(
        kick_kernel,
        jax.ShapeDtypeStruct((6, particles), f32),
        [VMEM] * (1 + len(samples_here)),
        VMEM,
        flops=1 << 16,
        moved=1 << 18,
    )(pushed, *samples_here)
    return kicked, jnp.transpose(field, (0, 2, 1)), jnp.transpose(deposit, (0, 2, 1))


def solution(mesh):
    return jax.shard_map(
        local,
        mesh=mesh,
        in_specs=(
            P(None, ("dom", "hist")),
            P(("dom", "hist")),
            P(("dom", "hist")),
            P(("dom", "hist")),
            P(("dom", "hist")),
            P(),
            P("hist", None, "dom", None),
            P("hist"),
            P("hist"),
            P("hist"),
            P(None, "dom"),
            P(),
        ),
        out_specs=(P(None, ("dom", "hist")), P(None, "dom", "hist"), P(None, "dom", "hist")),
        check_vma=False,
    )
```

```python
import functools

import jax
import jax.numpy as jnp
from jax import lax
from jax.experimental import pallas as pl
from jax.experimental.pallas import tpu as pltpu
from jax.sharding import PartitionSpec as P

LANES = 128
GROUP = 4
FIELDS = 4
NT_DIMS = (((1,), (1,)), ((), ()))
VMEM = pl.BlockSpec(memory_space=pltpu.VMEM)
SMEM = pl.BlockSpec(memory_space=pltpu.SMEM)
HBM = pl.BlockSpec(memory_space=pltpu.HBM)
LIMIT = 60 * 1024 * 1024
SMALL = 16 * 1024 * 1024


def call(kernel, out_shape, in_specs, out_specs, scratch=(), flops=0, moved=0, limit=SMALL):
    return pl.pallas_call(
        kernel,
        out_shape=out_shape,
        in_specs=in_specs,
        out_specs=out_specs,
        scratch_shapes=scratch,
        compiler_params=pltpu.CompilerParams(vmem_limit_bytes=limit),
        cost_estimate=pl.CostEstimate(flops=flops, bytes_accessed=moved, transcendentals=0),
    )


def split(value):
    high = value.astype(jnp.bfloat16)
    return high, (value - high.astype(jnp.float32)).astype(jnp.bfloat16)


def record_place(spread_rows, blocks, row_lanes, index):
    across = row_lanes // LANES
    top = spread_rows + index // across * blocks
    left = index % across * LANES
    return slice(top, top + blocks), slice(left, left + LANES)


def shift_columns(pieces, lag, lane):
    rolled = [pltpu.roll(piece, lag, 1) for piece in pieces]
    before = [jnp.zeros_like(rolled[0])] + rolled[:-1]
    wrapped = lane < lag
    return [jnp.where(wrapped, prior, here) for prior, here in zip(before, rolled)]


def push(coords, charge, rows, offsets, block_col, transfer, pushed, slab_rows):
    blocks = charge.shape[0]
    u = [
        jnp.concatenate(
            [coords[i : i + 1, LANES * b : LANES * (b + 1)] for b in range(blocks)], axis=0
        )
        for i in range(6)
    ]
    total = [jnp.full((blocks, LANES), transfer[i, 0], jnp.float32) for i in range(6)]
    pairs = {}
    terms = list(u)
    for first in range(6):
        for second in range(first, 6):
            pairs[first, second] = u[first] * u[second]
            terms.append(pairs[first, second])
    for first in range(6):
        for second in range(first, 6):
            for third in range(second, 6):
                terms.append(pairs[first, second] * u[third])
    for column, term in enumerate(terms):
        total = [total[i] + transfer[i, 1 + column] * term for i in range(6)]
    for i in range(6):
        pushed[i] = total[i]
    weight0 = charge[...]
    weight1 = weight0 * total[1]
    row_of = lax.broadcasted_iota(jnp.int32, (blocks, LANES), 0)
    column = offsets[...]
    for b in range(blocks):
        column = column + jnp.where(row_of == b, block_col[b], 0)
    return lax.rem(rows[...], slab_rows), column, weight0, weight1


def source_kernel(
    strips,
    coords,
    charge,
    rows,
    offsets,
    block_col,
    transfer,
    lags,
    fracs,
    weights,
    history,
    x_kernel,
    pushed,
    packed,
    frames,
    x_here,
    x_parts,
    s_parts,
    spread_all,
    sems,
):
    count_steps, comps, slab_rows, width = history.shape
    strip = width // strips
    spread_rows = packed.shape[1] - FIELDS * charge.shape[0] * LANES // packed.shape[2]
    chunk_rows = min(64, slab_rows)
    chunks = slab_rows // chunk_rows
    lane = lax.broadcasted_iota(jnp.int32, (16, LANES), 1)

    def fetch(comp, chunk):
        part = pl.ds(pl.multiple_of(chunk * chunk_rows, chunk_rows), chunk_rows)
        return pltpu.make_async_copy(
            history.at[:, comp, part, :], frames.at[:, comp, part, :], sems.at[comp, chunk]
        )

    fetch_x = pltpu.make_async_copy(x_kernel, x_here, sems.at[comps, 0])
    for comp in range(comps):
        for chunk in range(chunks):
            fetch(comp, chunk).start()
        if comp == 0:
            fetch_x.start()

    row, column, weight0, weight1 = push(
        coords, charge, rows, offsets, block_col, transfer, pushed, slab_rows
    )
    same = [row.astype(jnp.bfloat16), None, weight0.astype(jnp.bfloat16), weight1.astype(jnp.bfloat16)]
    for partner in range(strips):
        here = column - partner * strip
        here = jnp.where((here >= 0) & (here < strip), here, -1)
        for index in range(FIELDS):
            value = here.astype(jnp.float32).astype(jnp.bfloat16) if index == 1 else same[index]
            place = record_place(spread_rows, charge.shape[0], packed.shape[2], index)
            packed[(partner,) + place] = value

    lag = [lags[t] for t in range(count_steps)]
    far_weight = [weights[t] * fracs[t] for t in range(count_steps)]
    near_weight = [weights[t] * (1.0 - fracs[t]) for t in range(count_steps)]
    pieces = width // LANES

    def one_group(comp, first, row):
        near = [jnp.zeros((16, LANES), jnp.float32)] * pieces
        far = [jnp.zeros((16, LANES), jnp.float32)] * pieces
        for t in range(count_steps):
            frame = frames[t, comp, pl.ds(first, 16), :].astype(jnp.float32)
            parts = [frame[:, LANES * q : LANES * (q + 1)] for q in range(pieces)]
            moved = shift_columns(parts, lag[t], lane)
            near = [total + near_weight[t] * part for total, part in zip(near, moved)]
            far = [total + far_weight[t] * part for total, part in zip(far, moved)]
        far = shift_columns(far, 1, lane)
        for q in range(pieces):
            high, low = split(near[q] + far[q])
            here = pl.ds(row, 16)
            s_parts[here, LANES * q : LANES * (q + 1)] = high
            s_parts[here, width + LANES * q : width + LANES * (q + 1)] = low
            s_parts[here, 2 * width + LANES * q : 2 * width + LANES * (q + 1)] = high

    for comp in range(comps):

        def one_chunk(chunk, carry):
            fetch(comp, chunk).wait()
            for group in range(chunk_rows // 16):
                first = pl.multiple_of(chunk * chunk_rows + 16 * group, 16)
                one_group(comp, first, pl.multiple_of(comp * slab_rows + first, 16))
            return carry

        lax.fori_loop(0, chunks, one_chunk, 0)

    fetch_x.wait()
    high, low = split(x_here[...])
    x_parts[:width] = high
    x_parts[width : 2 * width] = high
    x_parts[2 * width :] = low
    for comp in range(comps):
        spread = jnp.dot(
            s_parts[comp * slab_rows : (comp + 1) * slab_rows],
            x_parts[...],
            preferred_element_type=jnp.float32,
        )
        spread_all[comp] = spread.T
    for partner in range(strips):
        part = slice(partner * strip, (partner + 1) * strip)
        both = jnp.concatenate([spread_all[comp, part] for comp in range(comps)], axis=0)
        packed[partner, : comps * strip, :slab_rows] = both.astype(packed.dtype)


def join_kernel(slabs, spread_rows, z_kernel, arrived, kept, *sent):
    slab_rows = z_kernel.shape[0] // slabs
    total = arrived[0, :spread_rows, :slab_rows].astype(jnp.float32)
    for sender in range(1, arrived.shape[0]):
        total = total + arrived[sender, :spread_rows, :slab_rows].astype(jnp.float32)
    high, low = split(total)
    left = jnp.concatenate([high, low, high], axis=1)

    def part(slab):
        start = pl.multiple_of(slab * slab_rows, slab_rows)
        z_high, z_low = split(z_kernel[pl.ds(start, slab_rows), :])
        right = jnp.concatenate([z_high, z_high, z_low], axis=1)
        return lax.dot_general(left, right, NT_DIMS, preferred_element_type=jnp.float32)

    if sent:
        me = lax.axis_index("dom")
        sent[0][...] = part(1 - me)
        kept[...] = part(me)
    else:
        for slab in range(slabs):
            kept[slab] = part(slab)


def unpack_kernel(spread_rows, blocks, arrived, records, chosen):
    senders = arrived.shape[0]
    own = lax.broadcasted_iota(jnp.int32, (blocks, 1), 0)
    bit = jnp.left_shift(jnp.ones_like(own), own).astype(jnp.float32)
    masks = []
    for sender in range(senders):
        for index in range(FIELDS):
            place = record_place(spread_rows, blocks, arrived.shape[2], index)
            value = arrived[(sender,) + place].astype(jnp.float32)
            records[sender, index * blocks : (index + 1) * blocks] = value
            if index == 1:
                meets = jnp.max(value, axis=1, keepdims=True) >= 0.0
                masks.append(jnp.sum(jnp.where(meets, bit, 0.0)).astype(jnp.int32))
    records[senders] = jnp.full(records.shape[1:], -1.0, jnp.float32)
    count = jnp.int32(0)
    for sender in range(senders):
        for block in range(blocks):
            chosen[1 + count] = sender * blocks + block
            count = count + ((masks[sender] >> block) & 1)
    chosen[0] = (count + (GROUP - 1)) // GROUP
    for member in range(GROUP):
        chosen[1 + count + member] = senders * blocks


def read_group(blocks, chosen, records, group):
    where = []
    for member in range(GROUP):
        block = chosen[1 + group * GROUP + member]
        where.append((block // blocks, lax.rem(block, blocks)))

    def field(index):
        return jnp.concatenate(
            [records[sender, pl.ds(index * blocks + own, 1), :] for sender, own in where], axis=1
        )

    return where, field


def one_hot(index, size):
    iota = lax.broadcasted_iota(jnp.int32, (size, index.shape[1]), 0).astype(jnp.float32)
    return iota == index


def deposit_kernel(blocks, chosen, records, after, deposit, total):
    del after
    strip, slab_rows = deposit.shape[1:]
    total[...] = jnp.zeros_like(total)

    def one_group(group, carry):
        _, field = read_group(blocks, chosen, records, group)
        hit = one_hot(field(1), strip)
        weighted = [jnp.where(hit, field(2 + comp), 0.0) for comp in range(2)]
        total[...] += lax.dot_general(
            jnp.where(one_hot(field(0), slab_rows), 1.0, 0.0).astype(jnp.bfloat16),
            jnp.concatenate(weighted, axis=0).astype(jnp.bfloat16),
            NT_DIMS,
            preferred_element_type=jnp.float32,
        )
        return carry

    lax.fori_loop(0, chosen[0], one_group, 0)
    turned = total[...].T
    deposit[0] = turned[:strip]
    deposit[1] = turned[strip:]


def sample_kernel(blocks, chosen, records, *refs):
    parts, (field_out, samples, found_all) = refs[:-3], refs[-3:]
    strip, slab_rows = field_out.shape[1:]
    if len(parts) == 1:
        total = parts[0][0]
        for slab in range(1, parts[0].shape[0]):
            total = total + parts[0][slab]
    else:
        total = parts[0][...] + parts[1][...]
    field_out[0] = total[:strip]
    field_out[1] = total[strip:]
    rounded = total.astype(jnp.bfloat16)
    found_all[...] = jnp.zeros_like(found_all)

    def one_group(group, carry):
        where, field = read_group(blocks, chosen, records, group)
        row_hot = jnp.where(one_hot(field(0), slab_rows), 1.0, 0.0).astype(jnp.bfloat16)
        found = jnp.dot(rounded, row_hot, preferred_element_type=jnp.float32)
        hit = one_hot(field(1), strip)
        for comp in range(2):
            picked = jnp.where(hit, found[comp * strip : (comp + 1) * strip], 0.0)
            values = jnp.sum(picked, axis=0, keepdims=True)
            for member, (sender, own) in enumerate(where):
                found_all[sender, pl.ds(comp * blocks + own, 1), :] = values[
                    :, LANES * member : LANES * (member + 1)
                ]
        return carry

    lax.fori_loop(0, chosen[0], one_group, 0)
    samples[...] = found_all[: samples.shape[0]].astype(samples.dtype)


def kick_kernel(pushed, received, kicked):
    blocks = pushed.shape[1]
    total = received[0].astype(jnp.float32)
    for sender in range(1, received.shape[0]):
        total = total + received[sender].astype(jnp.float32)
    values = [pushed[i] for i in range(6)]
    values[5] = values[5] + 0.5 * total[:blocks]
    values[1] = values[1] + 0.5 * total[blocks:]
    for b in range(blocks):
        kicked[:, LANES * b : LANES * (b + 1)] = jnp.concatenate(
            [value[b : b + 1] for value in values], axis=0
        )


def local(
    coords,
    charge,
    row_index,
    block_col,
    col_offset,
    transfer_map,
    history,
    retard_index,
    retard_frac,
    retard_weight,
    z_kernel,
    x_kernel,
):
    strips = lax.axis_size("hist")
    slabs = lax.axis_size("dom")
    count_steps, comps, slab_rows, width = history.shape
    strip = width // strips
    particles = coords.shape[1]
    blocks = block_col.shape[0]
    tile = (blocks, LANES)
    spread_rows = comps * strip
    row_lanes = max(slab_rows, LANES)
    packed_rows = spread_rows + FIELDS * blocks * LANES // row_lanes

    f32, bf16 = jnp.float32, jnp.bfloat16
    pushed, packed = call(
        functools.partial(source_kernel, strips),
        (
            jax.ShapeDtypeStruct((6,) + tile, f32),
            jax.ShapeDtypeStruct((strips, packed_rows, row_lanes), bf16),
        ),
        [VMEM] * 4 + [SMEM] * 5 + [HBM] * 2,
        (VMEM, VMEM),
        [
            pltpu.VMEM(history.shape, bf16),
            pltpu.VMEM((width, width), f32),
            pltpu.VMEM((3 * width, width), bf16),
            pltpu.VMEM((comps * slab_rows, 3 * width), bf16),
            pltpu.VMEM((comps, width, slab_rows), f32),
            pltpu.SemaphoreType.DMA((comps + 1, max(1, slab_rows // 64))),
        ],
        flops=6 * comps * slab_rows * width * width,
        moved=history.size * 2 + x_kernel.size * 4,
        limit=LIMIT,
    )(
        coords,
        charge.reshape(tile),
        row_index.reshape(tile),
        col_offset.reshape(tile),
        block_col,
        transfer_map,
        retard_index,
        retard_frac,
        retard_weight,
        history,
        x_kernel,
    )
    arrived = lax.all_to_all(packed, "hist", 0, 0, tiled=True)

    part = jax.ShapeDtypeStruct((spread_rows, slab_rows), f32)
    parts = call(
        functools.partial(join_kernel, slabs, spread_rows),
        (part, part) if slabs == 2 else jax.ShapeDtypeStruct((slabs,) + part.shape, f32),
        [VMEM, VMEM],
        (VMEM, VMEM) if slabs == 2 else VMEM,
        flops=1 << 27,
        moved=1 << 20,
    )(z_kernel, arrived)
    if slabs == 2:
        kept, sent = parts
        parts = [kept, lax.ppermute(sent, "dom", [(0, 1), (1, 0)])]
    else:
        parts = [lax.all_to_all(parts, "dom", 0, 0, tiled=True)]

    records, chosen = call(
        functools.partial(unpack_kernel, spread_rows, blocks),
        (
            jax.ShapeDtypeStruct((strips + 1, FIELDS * blocks, LANES), f32),
            jax.ShapeDtypeStruct((strips * blocks + 8,), jnp.int32),
        ),
        [VMEM],
        (VMEM, SMEM),
        flops=1 << 20,
        moved=1 << 20,
    )(arrived)

    field, samples = call(
        functools.partial(sample_kernel, blocks),
        (
            jax.ShapeDtypeStruct((comps, strip, slab_rows), f32),
            jax.ShapeDtypeStruct((strips, comps * blocks, LANES), bf16),
        ),
        [SMEM, VMEM] + [VMEM] * len(parts),
        (VMEM, VMEM),
        [pltpu.VMEM((strips + 1, comps * blocks, LANES), f32)],
        flops=1 << 29,
        moved=1 << 20,
    )(chosen, records, *parts)
    samples_here = lax.all_to_all(samples, "hist", 0, 0, tiled=True)

    deposit = call(
        functools.partial(deposit_kernel, blocks),
        jax.ShapeDtypeStruct((comps, strip, slab_rows), f32),
        [SMEM, VMEM, HBM],
        VMEM,
        [pltpu.VMEM((slab_rows, comps * strip), f32)],
        flops=1 << 29,
        moved=1 << 20,
    )(chosen, records, samples)

    kicked = call(
        kick_kernel,
        jax.ShapeDtypeStruct((6, particles), f32),
        [VMEM, VMEM],
        VMEM,
        flops=1 << 16,
        moved=1 << 18,
    )(pushed, samples_here)
    return kicked, jnp.transpose(field, (0, 2, 1)), jnp.transpose(deposit, (0, 2, 1))


def solution(mesh):
    return jax.shard_map(
        local,
        mesh=mesh,
        in_specs=(
            P(None, ("dom", "hist")),
            P(("dom", "hist")),
            P(("dom", "hist")),
            P(("dom", "hist")),
            P(("dom", "hist")),
            P(),
            P("hist", None, "dom", None),
            P("hist"),
            P("hist"),
            P("hist"),
            P(None, "dom"),
            P(),
        ),
        out_specs=(P(None, ("dom", "hist")), P(None, "dom", "hist"), P(None, "dom", "hist")),
        check_vma=False,
    )
```

```python
import functools

import jax
import jax.numpy as jnp
from jax import lax
from jax.experimental import pallas as pl
from jax.experimental.pallas import tpu as pltpu
from jax.sharding import PartitionSpec as P

LANES = 128
GROUP = 4
FIELDS = 4
NT_DIMS = (((1,), (1,)), ((), ()))
VMEM = pl.BlockSpec(memory_space=pltpu.VMEM)
SMEM = pl.BlockSpec(memory_space=pltpu.SMEM)
HBM = pl.BlockSpec(memory_space=pltpu.HBM)
LIMIT = 60 * 1024 * 1024
SMALL = 16 * 1024 * 1024


def call(kernel, out_shape, in_specs, out_specs, scratch=(), flops=0, moved=0, limit=SMALL):
    return pl.pallas_call(
        kernel,
        out_shape=out_shape,
        in_specs=in_specs,
        out_specs=out_specs,
        scratch_shapes=scratch,
        compiler_params=pltpu.CompilerParams(vmem_limit_bytes=limit),
        cost_estimate=pl.CostEstimate(flops=flops, bytes_accessed=moved, transcendentals=0),
    )


def factors(strips):
    inner = 1
    while inner * inner < strips:
        inner *= 2
    return strips // inner, inner


def exchange_inner(value):
    outer, inner = factors(lax.axis_size("hist"))
    groups = [[o * inner + i for i in range(inner)] for o in range(outer)]
    return lax.all_to_all(value, "hist", 0, 0, axis_index_groups=groups, tiled=True)


def exchange_outer(value):
    outer, inner = factors(lax.axis_size("hist"))
    groups = [[o * inner + i for o in range(outer)] for i in range(inner)]
    return lax.all_to_all(value, "hist", 0, 0, axis_index_groups=groups, tiled=True)


def split(value):
    high = value.astype(jnp.bfloat16)
    return high, (value - high.astype(jnp.float32)).astype(jnp.bfloat16)


def record_place(spread_rows, blocks, row_lanes, index):
    across = row_lanes // LANES
    top = spread_rows + index // across * blocks
    left = index % across * LANES
    return slice(top, top + blocks), slice(left, left + LANES)


def shift_columns(pieces, lag, lane):
    rolled = [pltpu.roll(piece, lag, 1) for piece in pieces]
    before = [jnp.zeros_like(rolled[0])] + rolled[:-1]
    wrapped = lane < lag
    return [jnp.where(wrapped, prior, here) for prior, here in zip(before, rolled)]


def push(coords, charge, rows, offsets, block_col, transfer, pushed, slab_rows):
    blocks = charge.shape[0]
    u = [
        jnp.concatenate(
            [coords[i : i + 1, LANES * b : LANES * (b + 1)] for b in range(blocks)], axis=0
        )
        for i in range(6)
    ]
    total = [jnp.full((blocks, LANES), transfer[i, 0], jnp.float32) for i in range(6)]
    pairs = {}
    terms = list(u)
    for first in range(6):
        for second in range(first, 6):
            pairs[first, second] = u[first] * u[second]
            terms.append(pairs[first, second])
    for first in range(6):
        for second in range(first, 6):
            for third in range(second, 6):
                terms.append(pairs[first, second] * u[third])
    for column, term in enumerate(terms):
        total = [total[i] + transfer[i, 1 + column] * term for i in range(6)]
    for i in range(6):
        pushed[i] = total[i]
    weight0 = charge[...]
    weight1 = weight0 * total[1]
    row_of = lax.broadcasted_iota(jnp.int32, (blocks, LANES), 0)
    column = offsets[...]
    for b in range(blocks):
        column = column + jnp.where(row_of == b, block_col[b], 0)
    return lax.rem(rows[...], slab_rows), column, weight0, weight1


def source_kernel(
    strips,
    coords,
    charge,
    rows,
    offsets,
    block_col,
    transfer,
    lags,
    fracs,
    weights,
    history,
    x_kernel,
    pushed,
    packed,
    frames,
    x_here,
    x_parts,
    s_parts,
    spread_all,
    sems,
):
    count_steps, comps, slab_rows, width = history.shape
    strip = width // strips
    spread_rows = packed.shape[1] - FIELDS * charge.shape[0] * LANES // packed.shape[2]
    chunk_rows = min(64, slab_rows)
    chunks = slab_rows // chunk_rows
    lane = lax.broadcasted_iota(jnp.int32, (16, LANES), 1)

    def fetch(comp, chunk):
        part = pl.ds(pl.multiple_of(chunk * chunk_rows, chunk_rows), chunk_rows)
        return pltpu.make_async_copy(
            history.at[:, comp, part, :], frames.at[:, comp, part, :], sems.at[comp, chunk]
        )

    fetch_x = pltpu.make_async_copy(x_kernel, x_here, sems.at[comps, 0])
    for comp in range(comps):
        for chunk in range(chunks):
            fetch(comp, chunk).start()
        if comp == 0:
            fetch_x.start()

    row, column, weight0, weight1 = push(
        coords, charge, rows, offsets, block_col, transfer, pushed, slab_rows
    )
    same = [row.astype(jnp.bfloat16), None, weight0.astype(jnp.bfloat16), weight1.astype(jnp.bfloat16)]
    for partner in range(strips):
        here = column - partner * strip
        here = jnp.where((here >= 0) & (here < strip), here, -1)
        for index in range(FIELDS):
            value = here.astype(jnp.float32).astype(jnp.bfloat16) if index == 1 else same[index]
            place = record_place(spread_rows, charge.shape[0], packed.shape[2], index)
            packed[(partner,) + place] = value

    lag = [lags[t] for t in range(count_steps)]
    far_weight = [weights[t] * fracs[t] for t in range(count_steps)]
    near_weight = [weights[t] * (1.0 - fracs[t]) for t in range(count_steps)]
    pieces = width // LANES

    def one_group(comp, first, row):
        near = [jnp.zeros((16, LANES), jnp.float32)] * pieces
        far = [jnp.zeros((16, LANES), jnp.float32)] * pieces
        for t in range(count_steps):
            frame = frames[t, comp, pl.ds(first, 16), :].astype(jnp.float32)
            parts = [frame[:, LANES * q : LANES * (q + 1)] for q in range(pieces)]
            moved = shift_columns(parts, lag[t], lane)
            near = [total + near_weight[t] * part for total, part in zip(near, moved)]
            far = [total + far_weight[t] * part for total, part in zip(far, moved)]
        far = shift_columns(far, 1, lane)
        for q in range(pieces):
            high, low = split(near[q] + far[q])
            here = pl.ds(row, 16)
            s_parts[here, LANES * q : LANES * (q + 1)] = high
            s_parts[here, width + LANES * q : width + LANES * (q + 1)] = low
            s_parts[here, 2 * width + LANES * q : 2 * width + LANES * (q + 1)] = high

    for comp in range(comps):

        def one_chunk(chunk, carry):
            fetch(comp, chunk).wait()
            for group in range(chunk_rows // 16):
                first = pl.multiple_of(chunk * chunk_rows + 16 * group, 16)
                one_group(comp, first, pl.multiple_of(comp * slab_rows + first, 16))
            return carry

        lax.fori_loop(0, chunks, one_chunk, 0)

    fetch_x.wait()
    high, low = split(x_here[...])
    x_parts[:width] = high
    x_parts[width : 2 * width] = high
    x_parts[2 * width :] = low
    for comp in range(comps):
        spread = jnp.dot(
            s_parts[comp * slab_rows : (comp + 1) * slab_rows],
            x_parts[...],
            preferred_element_type=jnp.float32,
        )
        spread_all[comp] = spread.T
    for partner in range(strips):
        part = slice(partner * strip, (partner + 1) * strip)
        both = jnp.concatenate([spread_all[comp, part] for comp in range(comps)], axis=0)
        packed[partner, : comps * strip, :slab_rows] = both.astype(packed.dtype)


def join_kernel(slabs, spread_rows, z_kernel, arrived, kept, *sent):
    slab_rows = z_kernel.shape[0] // slabs
    total = arrived[0, :spread_rows, :slab_rows].astype(jnp.float32)
    for sender in range(1, arrived.shape[0]):
        total = total + arrived[sender, :spread_rows, :slab_rows].astype(jnp.float32)
    high, low = split(total)
    left = jnp.concatenate([high, low, high], axis=1)

    def part(slab):
        start = pl.multiple_of(slab * slab_rows, slab_rows)
        z_high, z_low = split(z_kernel[pl.ds(start, slab_rows), :])
        right = jnp.concatenate([z_high, z_high, z_low], axis=1)
        return lax.dot_general(left, right, NT_DIMS, preferred_element_type=jnp.float32)

    if sent:
        me = lax.axis_index("dom")
        sent[0][...] = part(1 - me)
        kept[...] = part(me)
    else:
        for slab in range(slabs):
            kept[slab] = part(slab)


def unpack_kernel(spread_rows, blocks, arrived, records, chosen):
    senders = arrived.shape[0]
    own = lax.broadcasted_iota(jnp.int32, (blocks, 1), 0)
    bit = jnp.left_shift(jnp.ones_like(own), own).astype(jnp.float32)
    masks = []
    for sender in range(senders):
        for index in range(FIELDS):
            place = record_place(spread_rows, blocks, arrived.shape[2], index)
            value = arrived[(sender,) + place].astype(jnp.float32)
            records[sender, index * blocks : (index + 1) * blocks] = value
            if index == 1:
                meets = jnp.max(value, axis=1, keepdims=True) >= 0.0
                masks.append(jnp.sum(jnp.where(meets, bit, 0.0)).astype(jnp.int32))
    records[senders] = jnp.full(records.shape[1:], -1.0, jnp.float32)
    count = jnp.int32(0)
    for sender in range(senders):
        for block in range(blocks):
            chosen[1 + count] = sender * blocks + block
            count = count + ((masks[sender] >> block) & 1)
    chosen[0] = (count + (GROUP - 1)) // GROUP
    for member in range(GROUP):
        chosen[1 + count + member] = senders * blocks


def read_group(blocks, chosen, records, group):
    where = []
    for member in range(GROUP):
        block = chosen[1 + group * GROUP + member]
        where.append((block // blocks, lax.rem(block, blocks)))

    def field(index):
        return jnp.concatenate(
            [records[sender, pl.ds(index * blocks + own, 1), :] for sender, own in where], axis=1
        )

    return where, field


def one_hot(index, size):
    iota = lax.broadcasted_iota(jnp.int32, (size, index.shape[1]), 0).astype(jnp.float32)
    return iota == index


def deposit_kernel(blocks, chosen, records, after, deposit, total):
    del after
    strip, slab_rows = deposit.shape[1:]
    total[...] = jnp.zeros_like(total)

    def one_group(group, carry):
        _, field = read_group(blocks, chosen, records, group)
        hit = one_hot(field(1), strip)
        weighted = [jnp.where(hit, field(2 + comp), 0.0) for comp in range(2)]
        total[...] += lax.dot_general(
            jnp.where(one_hot(field(0), slab_rows), 1.0, 0.0).astype(jnp.bfloat16),
            jnp.concatenate(weighted, axis=0).astype(jnp.bfloat16),
            NT_DIMS,
            preferred_element_type=jnp.float32,
        )
        return carry

    lax.fori_loop(0, chosen[0], one_group, 0)
    turned = total[...].T
    deposit[0] = turned[:strip]
    deposit[1] = turned[strip:]


def sample_kernel(blocks, chosen, records, *refs):
    parts, (field_out, samples, found_all) = refs[:-3], refs[-3:]
    strip, slab_rows = field_out.shape[1:]
    if len(parts) == 1:
        total = parts[0][0]
        for slab in range(1, parts[0].shape[0]):
            total = total + parts[0][slab]
    else:
        total = parts[0][...] + parts[1][...]
    field_out[0] = total[:strip]
    field_out[1] = total[strip:]
    rounded = total.astype(jnp.bfloat16)
    found_all[...] = jnp.zeros_like(found_all)

    def one_group(group, carry):
        where, field = read_group(blocks, chosen, records, group)
        row_hot = jnp.where(one_hot(field(0), slab_rows), 1.0, 0.0).astype(jnp.bfloat16)
        found = jnp.dot(rounded, row_hot, preferred_element_type=jnp.float32)
        hit = one_hot(field(1), strip)
        for comp in range(2):
            picked = jnp.where(hit, found[comp * strip : (comp + 1) * strip], 0.0)
            values = jnp.sum(picked, axis=0, keepdims=True)
            for member, (sender, own) in enumerate(where):
                found_all[sender, pl.ds(comp * blocks + own, 1), :] = values[
                    :, LANES * member : LANES * (member + 1)
                ]
        return carry

    lax.fori_loop(0, chosen[0], one_group, 0)
    for place in range(samples.shape[0]):
        for part in range(samples.shape[1]):
            found = found_all[part * samples.shape[0] + place]
            samples[place, part] = found.astype(samples.dtype)


def sum_kernel(received, total):
    value = received[0].astype(jnp.float32)
    for sender in range(1, received.shape[0]):
        value = value + received[sender].astype(jnp.float32)
    total[...] = value.astype(total.dtype)


def kick_kernel(pushed, received, kicked):
    blocks = pushed.shape[1]
    total = received[0].astype(jnp.float32)
    for sender in range(1, received.shape[0]):
        total = total + received[sender].astype(jnp.float32)
    values = [pushed[i] for i in range(6)]
    values[5] = values[5] + 0.5 * total[:blocks]
    values[1] = values[1] + 0.5 * total[blocks:]
    for b in range(blocks):
        kicked[:, LANES * b : LANES * (b + 1)] = jnp.concatenate(
            [value[b : b + 1] for value in values], axis=0
        )


def local(
    coords,
    charge,
    row_index,
    block_col,
    col_offset,
    transfer_map,
    history,
    retard_index,
    retard_frac,
    retard_weight,
    z_kernel,
    x_kernel,
):
    strips = lax.axis_size("hist")
    slabs = lax.axis_size("dom")
    count_steps, comps, slab_rows, width = history.shape
    strip = width // strips
    outer, inner = factors(strips)
    particles = coords.shape[1]
    blocks = block_col.shape[0]
    tile = (blocks, LANES)
    spread_rows = comps * strip
    row_lanes = max(slab_rows, LANES)
    packed_rows = spread_rows + FIELDS * blocks * LANES // row_lanes

    f32, bf16 = jnp.float32, jnp.bfloat16
    pushed, packed = call(
        functools.partial(source_kernel, strips),
        (
            jax.ShapeDtypeStruct((6,) + tile, f32),
            jax.ShapeDtypeStruct((strips, packed_rows, row_lanes), bf16),
        ),
        [VMEM] * 4 + [SMEM] * 5 + [HBM] * 2,
        (VMEM, VMEM),
        [
            pltpu.VMEM(history.shape, bf16),
            pltpu.VMEM((width, width), f32),
            pltpu.VMEM((3 * width, width), bf16),
            pltpu.VMEM((comps * slab_rows, 3 * width), bf16),
            pltpu.VMEM((comps, width, slab_rows), f32),
            pltpu.SemaphoreType.DMA((comps + 1, max(1, slab_rows // 64))),
        ],
        flops=6 * comps * slab_rows * width * width,
        moved=history.size * 2 + x_kernel.size * 4,
        limit=LIMIT,
    )(
        coords,
        charge.reshape(tile),
        row_index.reshape(tile),
        col_offset.reshape(tile),
        block_col,
        transfer_map,
        retard_index,
        retard_frac,
        retard_weight,
        history,
        x_kernel,
    )
    arrived = lax.all_to_all(packed, "hist", 0, 0, tiled=True)

    part = jax.ShapeDtypeStruct((spread_rows, slab_rows), f32)
    parts = call(
        functools.partial(join_kernel, slabs, spread_rows),
        (part, part) if slabs == 2 else jax.ShapeDtypeStruct((slabs,) + part.shape, f32),
        [VMEM, VMEM],
        (VMEM, VMEM) if slabs == 2 else VMEM,
        flops=1 << 27,
        moved=1 << 20,
    )(z_kernel, arrived)
    if slabs == 2:
        kept, sent = parts
        parts = [kept, lax.ppermute(sent, "dom", [(0, 1), (1, 0)])]
    else:
        parts = [lax.all_to_all(parts, "dom", 0, 0, tiled=True)]

    records, chosen = call(
        functools.partial(unpack_kernel, spread_rows, blocks),
        (
            jax.ShapeDtypeStruct((strips + 1, FIELDS * blocks, LANES), f32),
            jax.ShapeDtypeStruct((strips * blocks + 8,), jnp.int32),
        ),
        [VMEM],
        (VMEM, SMEM),
        flops=1 << 20,
        moved=1 << 20,
    )(arrived)

    field, samples = call(
        functools.partial(sample_kernel, blocks),
        (
            jax.ShapeDtypeStruct((comps, strip, slab_rows), f32),
            jax.ShapeDtypeStruct((inner, outer, comps * blocks, LANES), bf16),
        ),
        [SMEM, VMEM] + [VMEM] * len(parts),
        (VMEM, VMEM),
        [pltpu.VMEM((strips + 1, comps * blocks, LANES), f32)],
        flops=1 << 29,
        moved=1 << 20,
    )(chosen, records, *parts)
    samples_near = exchange_inner(samples)

    deposit = call(
        functools.partial(deposit_kernel, blocks),
        jax.ShapeDtypeStruct((comps, strip, slab_rows), f32),
        [SMEM, VMEM, HBM],
        VMEM,
        [pltpu.VMEM((slab_rows, comps * strip), f32)],
        flops=1 << 29,
        moved=1 << 20,
    )(chosen, records, samples)

    samples_sum = call(
        sum_kernel,
        jax.ShapeDtypeStruct((outer, comps * blocks, LANES), bf16),
        [VMEM],
        VMEM,
        flops=1 << 18,
        moved=1 << 18,
    )(samples_near)
    samples_here = exchange_outer(samples_sum)
    kicked = call(
        kick_kernel,
        jax.ShapeDtypeStruct((6, particles), f32),
        [VMEM, VMEM],
        VMEM,
        flops=1 << 16,
        moved=1 << 18,
    )(pushed, samples_here)
    return kicked, jnp.transpose(field, (0, 2, 1)), jnp.transpose(deposit, (0, 2, 1))


def solution(mesh):
    return jax.shard_map(
        local,
        mesh=mesh,
        in_specs=(
            P(None, ("dom", "hist")),
            P(("dom", "hist")),
            P(("dom", "hist")),
            P(("dom", "hist")),
            P(("dom", "hist")),
            P(),
            P("hist", None, "dom", None),
            P("hist"),
            P("hist"),
            P("hist"),
            P(None, "dom"),
            P(),
        ),
        out_specs=(P(None, ("dom", "hist")), P(None, "dom", "hist"), P(None, "dom", "hist")),
        check_vma=False,
    )
```

```python
import functools

import jax
import jax.numpy as jnp
from jax import lax
from jax.experimental import pallas as pl
from jax.experimental.pallas import tpu as pltpu
from jax.sharding import PartitionSpec as P

LANES = 128
GROUP = 4
FIELDS = 4
NT_DIMS = (((1,), (1,)), ((), ()))
VMEM = pl.BlockSpec(memory_space=pltpu.VMEM)
SMEM = pl.BlockSpec(memory_space=pltpu.SMEM)
HBM = pl.BlockSpec(memory_space=pltpu.HBM)
LIMIT = 59 * 1024 * 1024
SMALL = 16 * 1024 * 1024


def call(kernel, out_shape, in_specs, out_specs, scratch=(), flops=0, moved=0, limit=SMALL):
    return pl.pallas_call(
        kernel,
        out_shape=out_shape,
        in_specs=in_specs,
        out_specs=out_specs,
        scratch_shapes=scratch,
        compiler_params=pltpu.CompilerParams(vmem_limit_bytes=limit),
        cost_estimate=pl.CostEstimate(flops=flops, bytes_accessed=moved, transcendentals=0),
    )


def split(value):
    high = value.astype(jnp.bfloat16)
    return high, (value - high.astype(jnp.float32)).astype(jnp.bfloat16)


def record_place(spread_rows, blocks, row_lanes, index):
    across = row_lanes // LANES
    top = spread_rows + index // across * blocks
    left = index % across * LANES
    return slice(top, top + blocks), slice(left, left + LANES)


def shift_columns(pieces, lag, lane):
    rolled = [pltpu.roll(piece, lag, 1) for piece in pieces]
    before = [jnp.zeros_like(rolled[0])] + rolled[:-1]
    wrapped = lane < jnp.asarray(lag, jnp.int32).astype(lane.dtype)
    return [jnp.where(wrapped, prior, here) for prior, here in zip(before, rolled)]


def push(coords, charge, rows, offsets, block_col, transfer, pushed, slab_rows):
    blocks = charge.shape[0]
    u = [
        jnp.concatenate(
            [coords[i : i + 1, LANES * b : LANES * (b + 1)] for b in range(blocks)], axis=0
        )
        for i in range(6)
    ]
    total = [jnp.full((blocks, LANES), transfer[i, 0], jnp.float32) for i in range(6)]
    pairs = {}
    terms = list(u)
    for first in range(6):
        for second in range(first, 6):
            pairs[first, second] = u[first] * u[second]
            terms.append(pairs[first, second])
    for first in range(6):
        for second in range(first, 6):
            for third in range(second, 6):
                terms.append(pairs[first, second] * u[third])
    for column, term in enumerate(terms):
        total = [total[i] + transfer[i, 1 + column] * term for i in range(6)]
    for i in range(6):
        pushed[i] = total[i]
    weight0 = charge[...]
    weight1 = weight0 * total[1]
    row_of = lax.broadcasted_iota(jnp.int32, (blocks, LANES), 0)
    column = offsets[...]
    for b in range(blocks):
        column = column + jnp.where(row_of == b, block_col[b], 0)
    return lax.rem(rows[...], slab_rows), column, weight0, weight1


def source_kernel(
    strips,
    block_col,
    lags,
    fracs,
    weights,
    coords_from,
    charge_from,
    rows_from,
    offsets_from,
    transfer_from,
    history,
    x_kernel,
    pushed,
    packed,
    coords,
    charge,
    rows,
    offsets,
    transfer,
    frames,
    x_here,
    x_parts,
    s_parts,
    spread_all,
    sems,
    small_sems,
):
    count_steps, comps, slab_rows, width = history.shape
    strip = width // strips
    spread_rows = packed.shape[1] - FIELDS * charge.shape[0] * LANES // packed.shape[2]
    chunk_rows = min(64, slab_rows)
    chunks = slab_rows // chunk_rows
    lane = lax.broadcasted_iota(jnp.int32, (16, LANES), 1)
    lane16 = lane.astype(jnp.int16)

    def fetch(comp, chunk):
        part = pl.ds(pl.multiple_of(chunk * chunk_rows, chunk_rows), chunk_rows)
        return pltpu.make_async_copy(
            history.at[:, comp, part, :], frames.at[:, comp, part, :], sems.at[comp, chunk]
        )

    fetch_x = pltpu.make_async_copy(x_kernel, x_here, sems.at[comps, 0])
    small = [
        pltpu.make_async_copy(source, target, small_sems.at[index])
        for index, (source, target) in enumerate(
            [
                (coords_from, coords),
                (charge_from, charge),
                (rows_from, rows),
                (offsets_from, offsets),
                (transfer_from, transfer),
            ]
        )
    ]
    for copy in small:
        copy.start()
    for comp in range(comps):
        for chunk in range(chunks):
            fetch(comp, chunk).start()
        if comp == 0:
            fetch_x.start()

    for copy in small:
        copy.wait()
    row, column, weight0, weight1 = push(
        coords, charge, rows, offsets, block_col, transfer, pushed, slab_rows
    )
    same = [row.astype(jnp.bfloat16), None, weight0.astype(jnp.bfloat16), weight1.astype(jnp.bfloat16)]
    for partner in range(strips):
        here = column - partner * strip
        here = jnp.where((here >= 0) & (here < strip), here, -1)
        for index in range(FIELDS):
            value = here.astype(jnp.float32).astype(jnp.bfloat16) if index == 1 else same[index]
            place = record_place(spread_rows, charge.shape[0], packed.shape[2], index)
            packed[(partner,) + place] = value

    lag = [lags[t] for t in range(count_steps)]
    far_weight = [weights[t] * fracs[t] for t in range(count_steps)]
    near_weight = [weights[t] * (1.0 - fracs[t]) for t in range(count_steps)]
    pieces = width // LANES

    def one_group(comp, first, row):
        near = [jnp.zeros((16, LANES), jnp.float32)] * pieces
        far = [jnp.zeros((16, LANES), jnp.float32)] * pieces
        for t in range(count_steps):
            frame = frames[t, comp, pl.ds(first, 16), :]
            parts = [frame[:, LANES * q : LANES * (q + 1)] for q in range(pieces)]
            moved = shift_columns(parts, lag[t], lane16)
            moved = [part.astype(jnp.float32) for part in moved]
            near = [total + near_weight[t] * part for total, part in zip(near, moved)]
            far = [total + far_weight[t] * part for total, part in zip(far, moved)]
        far = shift_columns(far, 1, lane)
        for q in range(pieces):
            high, low = split(near[q] + far[q])
            here = pl.ds(row, 16)
            s_parts[here, LANES * q : LANES * (q + 1)] = high
            s_parts[here, width + LANES * q : width + LANES * (q + 1)] = low
            s_parts[here, 2 * width + LANES * q : 2 * width + LANES * (q + 1)] = high

    for comp in range(comps):

        def one_chunk(chunk, carry):
            fetch(comp, chunk).wait()
            for group in range(chunk_rows // 16):
                first = pl.multiple_of(chunk * chunk_rows + 16 * group, 16)
                one_group(comp, first, pl.multiple_of(comp * slab_rows + first, 16))
            return carry

        lax.fori_loop(0, chunks, one_chunk, 0)

    fetch_x.wait()
    high, low = split(x_here[...])
    x_parts[:width] = high
    x_parts[width : 2 * width] = high
    x_parts[2 * width :] = low
    for comp in range(comps):
        spread = jnp.dot(
            s_parts[comp * slab_rows : (comp + 1) * slab_rows],
            x_parts[...],
            preferred_element_type=jnp.float32,
        )
        if strip % 16 == 0:
            turned = spread.astype(packed.dtype).T
            for partner in range(strips):
                packed[partner, comp * strip : (comp + 1) * strip, :slab_rows] = turned[
                    partner * strip : (partner + 1) * strip
                ]
        else:
            spread_all[comp] = spread.T
    if strip % 16:
        for partner in range(strips):
            part = slice(partner * strip, (partner + 1) * strip)
            both = jnp.concatenate([spread_all[comp, part] for comp in range(comps)], axis=0)
            packed[partner, : comps * strip, :slab_rows] = both.astype(packed.dtype)


def join_kernel(slabs, spread_rows, z_kernel, arrived, kept, *sent):
    slab_rows = z_kernel.shape[0] // slabs
    total = arrived[0, :spread_rows, :slab_rows].astype(jnp.float32)
    for sender in range(1, arrived.shape[0]):
        total = total + arrived[sender, :spread_rows, :slab_rows].astype(jnp.float32)
    high, low = split(total)
    left = jnp.concatenate([high, low, high], axis=1)

    def part(slab):
        start = pl.multiple_of(slab * slab_rows, slab_rows)
        z_high, z_low = split(z_kernel[pl.ds(start, slab_rows), :])
        right = jnp.concatenate([z_high, z_high, z_low], axis=1)
        return lax.dot_general(left, right, NT_DIMS, preferred_element_type=jnp.float32)

    if sent:
        me = lax.axis_index("dom")
        sent[0][...] = part(1 - me)
        kept[...] = part(me)
    else:
        for slab in range(slabs):
            kept[slab] = part(slab)


def unpack_kernel(spread_rows, blocks, arrived, records, chosen):
    senders = arrived.shape[0]
    own = lax.broadcasted_iota(jnp.int32, (blocks, 1), 0)
    bit = jnp.left_shift(jnp.ones_like(own), own).astype(jnp.float32)
    masks = []
    for sender in range(senders):
        for index in range(FIELDS):
            place = record_place(spread_rows, blocks, arrived.shape[2], index)
            value = arrived[(sender,) + place].astype(jnp.float32)
            records[sender, index * blocks : (index + 1) * blocks] = value
            if index == 1:
                meets = jnp.max(value, axis=1, keepdims=True) >= 0.0
                masks.append(jnp.sum(jnp.where(meets, bit, 0.0)).astype(jnp.int32))
    records[senders] = jnp.full(records.shape[1:], -1.0, jnp.float32)
    count = jnp.int32(0)
    for sender in range(senders):
        for block in range(blocks):
            chosen[1 + count] = sender * blocks + block
            count = count + ((masks[sender] >> block) & 1)
    chosen[0] = (count + (GROUP - 1)) // GROUP
    for member in range(GROUP):
        chosen[1 + count + member] = senders * blocks


def read_group(blocks, chosen, records, group):
    where = []
    for member in range(GROUP):
        block = chosen[1 + group * GROUP + member]
        where.append((block // blocks, lax.rem(block, blocks)))

    def field(index):
        return jnp.concatenate(
            [records[sender, pl.ds(index * blocks + own, 1), :] for sender, own in where], axis=1
        )

    return where, field


def one_hot(index, size):
    iota = lax.broadcasted_iota(jnp.int32, (size, index.shape[1]), 0).astype(jnp.float32)
    return iota == index


def one_hot_rows(row, size):
    iota = lax.broadcasted_iota(jnp.int32, (size, row.shape[1]), 0)
    if size <= 256:
        hit = iota.astype(jnp.bfloat16) == row.astype(jnp.bfloat16)
        return jnp.where(hit, jnp.bfloat16(1.0), jnp.bfloat16(0.0))
    return jnp.where(iota.astype(jnp.float32) == row, 1.0, 0.0).astype(jnp.bfloat16)


def deposit_kernel(blocks, chosen, records, after, deposit, total):
    del after
    strip, slab_rows = deposit.shape[1:]
    total[...] = jnp.zeros_like(total)

    def one_group(group, carry):
        _, field = read_group(blocks, chosen, records, group)
        hit = one_hot(field(1), strip)
        weighted = [jnp.where(hit, field(2 + comp), 0.0) for comp in range(2)]
        total[...] += lax.dot_general(
            one_hot_rows(field(0), slab_rows),
            jnp.concatenate(weighted, axis=0).astype(jnp.bfloat16),
            NT_DIMS,
            preferred_element_type=jnp.float32,
        )
        return carry

    lax.fori_loop(0, chosen[0], one_group, 0)
    turned = total[...].T
    deposit[0] = turned[:strip]
    deposit[1] = turned[strip:]


def sample_kernel(blocks, chosen, records, *refs):
    parts, (field_out, samples, found_all) = refs[:-3], refs[-3:]
    strip, slab_rows = field_out.shape[1:]
    if len(parts) == 1:
        total = parts[0][0]
        for slab in range(1, parts[0].shape[0]):
            total = total + parts[0][slab]
    else:
        total = parts[0][...] + parts[1][...]
    field_out[0] = total[:strip]
    field_out[1] = total[strip:]
    rounded = total.astype(jnp.bfloat16)
    found_all[...] = jnp.zeros_like(found_all)

    def one_group(group, carry):
        where, field = read_group(blocks, chosen, records, group)
        row_hot = one_hot_rows(field(0), slab_rows)
        found = jnp.dot(rounded, row_hot, preferred_element_type=jnp.float32)
        hit = one_hot(field(1), strip)
        for comp in range(2):
            picked = jnp.where(hit, found[comp * strip : (comp + 1) * strip], 0.0)
            values = jnp.sum(picked, axis=0, keepdims=True)
            for member, (sender, own) in enumerate(where):
                found_all[sender, pl.ds(comp * blocks + own, 1), :] = values[
                    :, LANES * member : LANES * (member + 1)
                ]
        return carry

    lax.fori_loop(0, chosen[0], one_group, 0)
    samples[...] = found_all[: samples.shape[0]].astype(samples.dtype)


def kick_kernel(pushed, received, kicked):
    blocks = pushed.shape[1]
    total = received[0].astype(jnp.float32)
    for sender in range(1, received.shape[0]):
        total = total + received[sender].astype(jnp.float32)
    values = [pushed[i] for i in range(6)]
    values[5] = values[5] + 0.5 * total[:blocks]
    values[1] = values[1] + 0.5 * total[blocks:]
    for b in range(blocks):
        kicked[:, LANES * b : LANES * (b + 1)] = jnp.concatenate(
            [value[b : b + 1] for value in values], axis=0
        )


def local(
    coords,
    charge,
    row_index,
    block_col,
    col_offset,
    transfer_map,
    history,
    retard_index,
    retard_frac,
    retard_weight,
    z_kernel,
    x_kernel,
):
    strips = lax.axis_size("hist")
    slabs = lax.axis_size("dom")
    count_steps, comps, slab_rows, width = history.shape
    strip = width // strips
    particles = coords.shape[1]
    blocks = block_col.shape[0]
    tile = (blocks, LANES)
    spread_rows = comps * strip
    row_lanes = max(slab_rows, LANES)
    packed_rows = spread_rows + FIELDS * blocks * LANES // row_lanes

    f32, bf16 = jnp.float32, jnp.bfloat16
    pushed, packed = call(
        functools.partial(source_kernel, strips),
        (
            jax.ShapeDtypeStruct((6,) + tile, f32),
            jax.ShapeDtypeStruct((strips, packed_rows, row_lanes), bf16),
        ),
        [SMEM] * 4 + [HBM] * 7,
        (VMEM, VMEM),
        [
            pltpu.VMEM(coords.shape, f32),
            pltpu.VMEM(tile, f32),
            pltpu.VMEM(tile, jnp.int32),
            pltpu.VMEM(tile, jnp.int32),
            pltpu.SMEM(transfer_map.shape, f32),
            pltpu.VMEM(history.shape, bf16),
            pltpu.VMEM((width, width), f32),
            pltpu.VMEM((3 * width, width), bf16),
            pltpu.VMEM((comps * slab_rows, 3 * width), bf16),
            pltpu.VMEM((comps, width, slab_rows), f32),
            pltpu.SemaphoreType.DMA((comps + 1, max(1, slab_rows // 64))),
            pltpu.SemaphoreType.DMA((5,)),
        ],
        flops=6 * comps * slab_rows * width * width,
        moved=history.size * 2 + x_kernel.size * 4,
        limit=LIMIT,
    )(
        block_col,
        retard_index,
        retard_frac,
        retard_weight,
        coords,
        charge.reshape(tile),
        row_index.reshape(tile),
        col_offset.reshape(tile),
        transfer_map,
        history,
        x_kernel,
    )
    arrived = lax.all_to_all(packed, "hist", 0, 0, tiled=True)

    part = jax.ShapeDtypeStruct((spread_rows, slab_rows), f32)
    parts = call(
        functools.partial(join_kernel, slabs, spread_rows),
        (part, part) if slabs == 2 else jax.ShapeDtypeStruct((slabs,) + part.shape, f32),
        [VMEM, VMEM],
        (VMEM, VMEM) if slabs == 2 else VMEM,
        flops=1 << 27,
        moved=1 << 20,
    )(z_kernel, arrived)
    if slabs == 2:
        kept, sent = parts
        parts = [kept, lax.ppermute(sent, "dom", [(0, 1), (1, 0)])]
    else:
        parts = [lax.all_to_all(parts, "dom", 0, 0, tiled=True)]

    records, chosen = call(
        functools.partial(unpack_kernel, spread_rows, blocks),
        (
            jax.ShapeDtypeStruct((strips + 1, FIELDS * blocks, LANES), f32),
            jax.ShapeDtypeStruct((strips * blocks + 8,), jnp.int32),
        ),
        [VMEM],
        (VMEM, SMEM),
        flops=1 << 20,
        moved=1 << 20,
    )(arrived)

    field, samples = call(
        functools.partial(sample_kernel, blocks),
        (
            jax.ShapeDtypeStruct((comps, strip, slab_rows), f32),
            jax.ShapeDtypeStruct((strips, comps * blocks, LANES), bf16),
        ),
        [SMEM, VMEM] + [VMEM] * len(parts),
        (VMEM, VMEM),
        [pltpu.VMEM((strips + 1, comps * blocks, LANES), f32)],
        flops=1 << 29,
        moved=1 << 20,
    )(chosen, records, *parts)
    samples_here = lax.all_to_all(samples, "hist", 0, 0, tiled=True)

    deposit = call(
        functools.partial(deposit_kernel, blocks),
        jax.ShapeDtypeStruct((comps, strip, slab_rows), f32),
        [SMEM, VMEM, HBM],
        VMEM,
        [pltpu.VMEM((slab_rows, comps * strip), f32)],
        flops=1 << 29,
        moved=1 << 20,
    )(chosen, records, samples)

    kicked = call(
        kick_kernel,
        jax.ShapeDtypeStruct((6, particles), f32),
        [VMEM, VMEM],
        VMEM,
        flops=1 << 16,
        moved=1 << 18,
    )(pushed, samples_here)
    return kicked, jnp.transpose(field, (0, 2, 1)), jnp.transpose(deposit, (0, 2, 1))


def solution(mesh):
    return jax.shard_map(
        local,
        mesh=mesh,
        in_specs=(
            P(None, ("dom", "hist")),
            P(("dom", "hist")),
            P(("dom", "hist")),
            P(("dom", "hist")),
            P(("dom", "hist")),
            P(),
            P("hist", None, "dom", None),
            P("hist"),
            P("hist"),
            P("hist"),
            P(None, "dom"),
            P(),
        ),
        out_specs=(P(None, ("dom", "hist")), P(None, "dom", "hist"), P(None, "dom", "hist")),
        check_vma=False,
    )
```

```python
import functools

import jax
import jax.numpy as jnp
from jax import lax
from jax.experimental import pallas as pl
from jax.experimental.pallas import tpu as pltpu
from jax.sharding import PartitionSpec as P

LANES = 128
GROUP = 4
FIELDS = 4
NT_DIMS = (((1,), (1,)), ((), ()))
VMEM = pl.BlockSpec(memory_space=pltpu.VMEM)
SMEM = pl.BlockSpec(memory_space=pltpu.SMEM)
HBM = pl.BlockSpec(memory_space=pltpu.HBM)
LIMIT = 59 * 1024 * 1024
SMALL = 16 * 1024 * 1024


def call(kernel, out_shape, in_specs, out_specs, scratch=(), flops=0, moved=0, limit=SMALL):
    return pl.pallas_call(
        kernel,
        out_shape=out_shape,
        in_specs=in_specs,
        out_specs=out_specs,
        scratch_shapes=scratch,
        compiler_params=pltpu.CompilerParams(vmem_limit_bytes=limit),
        cost_estimate=pl.CostEstimate(flops=flops, bytes_accessed=moved, transcendentals=0),
    )


def split(value):
    high = value.astype(jnp.bfloat16)
    return high, (value - high.astype(jnp.float32)).astype(jnp.bfloat16)


def record_place(spread_rows, blocks, row_lanes, index):
    across = row_lanes // LANES
    top = spread_rows + index // across * blocks
    left = index % across * LANES
    return slice(top, top + blocks), slice(left, left + LANES)


def lag_band(lag, near, far):
    row = lax.broadcasted_iota(jnp.int32, (2 * LANES, LANES), 0)
    column = lax.broadcasted_iota(jnp.int32, (2 * LANES, LANES), 1)
    behind = column + LANES - row
    weight = jnp.where(behind == lag, near, jnp.where(behind == lag + 1, far, 0.0))
    return jnp.concatenate(split(weight), axis=1)


def push(coords, charge, rows, offsets, block_col, transfer, pushed, slab_rows):
    blocks = charge.shape[0]
    u = [
        jnp.concatenate(
            [coords[i : i + 1, LANES * b : LANES * (b + 1)] for b in range(blocks)], axis=0
        )
        for i in range(6)
    ]
    total = [jnp.full((blocks, LANES), transfer[i, 0], jnp.float32) for i in range(6)]
    pairs = {}
    terms = list(u)
    for first in range(6):
        for second in range(first, 6):
            pairs[first, second] = u[first] * u[second]
            terms.append(pairs[first, second])
    for first in range(6):
        for second in range(first, 6):
            for third in range(second, 6):
                terms.append(pairs[first, second] * u[third])
    for column, term in enumerate(terms):
        total = [total[i] + transfer[i, 1 + column] * term for i in range(6)]
    for i in range(6):
        pushed[i] = total[i]
    weight0 = charge[...]
    weight1 = weight0 * total[1]
    row_of = lax.broadcasted_iota(jnp.int32, (blocks, LANES), 0)
    column = offsets[...]
    for b in range(blocks):
        column = column + jnp.where(row_of == b, block_col[b], 0)
    return lax.rem(rows[...], slab_rows), column, weight0, weight1


def source_kernel(
    strips,
    block_col,
    lags,
    fracs,
    weights,
    coords_from,
    charge_from,
    rows_from,
    offsets_from,
    transfer_from,
    history,
    x_kernel,
    pushed,
    packed,
    coords,
    charge,
    rows,
    offsets,
    transfer,
    frames,
    x_here,
    x_parts,
    s_parts,
    spread_all,
    bands,
    first_bands,
    sems,
    small_sems,
):
    count_steps, comps, slab_rows, width = history.shape
    strip = width // strips
    spread_rows = packed.shape[1] - FIELDS * charge.shape[0] * LANES // packed.shape[2]
    fetch = [
        pltpu.make_async_copy(history.at[:, comp], frames.at[:, comp], sems.at[comp])
        for comp in range(comps)
    ]
    fetch_x = pltpu.make_async_copy(x_kernel, x_here, sems.at[comps])
    small = [
        pltpu.make_async_copy(source, target, small_sems.at[index])
        for index, (source, target) in enumerate(
            [
                (coords_from, coords),
                (charge_from, charge),
                (rows_from, rows),
                (offsets_from, offsets),
                (transfer_from, transfer),
            ]
        )
    ]
    fetch[0].start()
    for copy in small:
        copy.start()
    fetch_x.start()
    for copy in fetch[1:]:
        copy.start()

    for t in range(count_steps):
        far = weights[t] * fracs[t]
        near = weights[t] * (1.0 - fracs[t])
        bands[2 * LANES * t : 2 * LANES * (t + 1)] = lag_band(lags[t], near, far)
        first_bands[LANES * t : LANES * (t + 1)] = bands[
            2 * LANES * t + LANES : 2 * LANES * (t + 1)
        ]

    def source(comp):
        here = slice(comp * slab_rows, (comp + 1) * slab_rows)
        for q in range(width // LANES):
            before = slice(LANES * max(q - 1, 0), LANES * (q + 1))
            steps = [frames[t, comp, :, before] for t in range(count_steps)]
            both = jnp.dot(
                jnp.concatenate(steps, axis=1),
                bands[...] if q else first_bands[...],
                preferred_element_type=jnp.float32,
            )
            high, low = split(both[:, :LANES] + both[:, LANES:])
            s_parts[here, LANES * q : LANES * (q + 1)] = high
            s_parts[here, width + LANES * q : width + LANES * (q + 1)] = low
            s_parts[here, 2 * width + LANES * q : 2 * width + LANES * (q + 1)] = high

    for copy in small:
        copy.wait()
    fetch[0].wait()
    source(0)
    row, column, weight0, weight1 = push(
        coords, charge, rows, offsets, block_col, transfer, pushed, slab_rows
    )
    same = [row.astype(jnp.bfloat16), None, weight0.astype(jnp.bfloat16), weight1.astype(jnp.bfloat16)]
    for partner in range(strips):
        here = column - partner * strip
        here = jnp.where((here >= 0) & (here < strip), here, -1)
        for index in range(FIELDS):
            value = here.astype(jnp.float32).astype(jnp.bfloat16) if index == 1 else same[index]
            place = record_place(spread_rows, charge.shape[0], packed.shape[2], index)
            packed[(partner,) + place] = value
    fetch_x.wait()
    high, low = split(x_here[...])
    x_parts[:width] = high
    x_parts[width : 2 * width] = high
    x_parts[2 * width :] = low
    for comp in range(1, comps):
        fetch[comp].wait()
        source(comp)
    for comp in range(comps):
        spread = jnp.dot(
            s_parts[comp * slab_rows : (comp + 1) * slab_rows],
            x_parts[...],
            preferred_element_type=jnp.float32,
        )
        if strip % 16 == 0:
            turned = spread.astype(packed.dtype).T
            for partner in range(strips):
                packed[partner, comp * strip : (comp + 1) * strip, :slab_rows] = turned[
                    partner * strip : (partner + 1) * strip
                ]
        else:
            spread_all[comp] = spread.T
    if strip % 16:
        for partner in range(strips):
            part = slice(partner * strip, (partner + 1) * strip)
            both = jnp.concatenate([spread_all[comp, part] for comp in range(comps)], axis=0)
            packed[partner, : comps * strip, :slab_rows] = both.astype(packed.dtype)


def join_kernel(slabs, spread_rows, z_kernel, arrived, kept, *sent):
    slab_rows = z_kernel.shape[0] // slabs
    total = arrived[0, :spread_rows, :slab_rows].astype(jnp.float32)
    for sender in range(1, arrived.shape[0]):
        total = total + arrived[sender, :spread_rows, :slab_rows].astype(jnp.float32)
    high, low = split(total)
    left = jnp.concatenate([high, low, high], axis=1)

    def part(slab):
        start = pl.multiple_of(slab * slab_rows, slab_rows)
        z_high, z_low = split(z_kernel[pl.ds(start, slab_rows), :])
        right = jnp.concatenate([z_high, z_high, z_low], axis=1)
        return lax.dot_general(left, right, NT_DIMS, preferred_element_type=jnp.float32)

    if sent:
        me = lax.axis_index("dom")
        sent[0][...] = part(1 - me)
        kept[...] = part(me)
    else:
        for slab in range(slabs):
            kept[slab] = part(slab)


def unpack_kernel(spread_rows, blocks, arrived, records, chosen):
    senders = arrived.shape[0]
    own = lax.broadcasted_iota(jnp.int32, (blocks, 1), 0)
    bit = jnp.left_shift(jnp.ones_like(own), own).astype(jnp.float32)
    masks = []
    for sender in range(senders):
        for index in range(FIELDS):
            place = record_place(spread_rows, blocks, arrived.shape[2], index)
            value = arrived[(sender,) + place].astype(jnp.float32)
            records[sender, index * blocks : (index + 1) * blocks] = value
            if index == 1:
                meets = jnp.max(value, axis=1, keepdims=True) >= 0.0
                masks.append(jnp.sum(jnp.where(meets, bit, 0.0)).astype(jnp.int32))
    records[senders] = jnp.full(records.shape[1:], -1.0, jnp.float32)
    count = jnp.int32(0)
    for sender in range(senders):
        for block in range(blocks):
            chosen[1 + count] = sender * blocks + block
            count = count + ((masks[sender] >> block) & 1)
    chosen[0] = (count + (GROUP - 1)) // GROUP
    for member in range(GROUP):
        chosen[1 + count + member] = senders * blocks


def read_group(blocks, chosen, records, group):
    where = []
    for member in range(GROUP):
        block = chosen[1 + group * GROUP + member]
        where.append((block // blocks, lax.rem(block, blocks)))

    def field(index):
        return jnp.concatenate(
            [records[sender, pl.ds(index * blocks + own, 1), :] for sender, own in where], axis=1
        )

    return where, field


def one_hot(index, size):
    iota = lax.broadcasted_iota(jnp.int32, (size, index.shape[1]), 0).astype(jnp.float32)
    return iota == index


def one_hot_rows(row, size):
    iota = lax.broadcasted_iota(jnp.int32, (size, row.shape[1]), 0)
    if size <= 256:
        hit = iota.astype(jnp.bfloat16) == row.astype(jnp.bfloat16)
        return jnp.where(hit, jnp.bfloat16(1.0), jnp.bfloat16(0.0))
    return jnp.where(iota.astype(jnp.float32) == row, 1.0, 0.0).astype(jnp.bfloat16)


def deposit_kernel(blocks, chosen, records, after, deposit, total):
    del after
    strip, slab_rows = deposit.shape[1:]
    total[...] = jnp.zeros_like(total)

    def one_group(group, carry):
        _, field = read_group(blocks, chosen, records, group)
        hit = one_hot(field(1), strip)
        weighted = [jnp.where(hit, field(2 + comp), 0.0) for comp in range(2)]
        total[...] += lax.dot_general(
            one_hot_rows(field(0), slab_rows),
            jnp.concatenate(weighted, axis=0).astype(jnp.bfloat16),
            NT_DIMS,
            preferred_element_type=jnp.float32,
        )
        return carry

    lax.fori_loop(0, chosen[0], one_group, 0)
    turned = total[...].T
    deposit[0] = turned[:strip]
    deposit[1] = turned[strip:]


def sample_kernel(blocks, chosen, records, *refs):
    parts, (field_out, samples, found_all) = refs[:-3], refs[-3:]
    strip, slab_rows = field_out.shape[1:]
    if len(parts) == 1:
        total = parts[0][0]
        for slab in range(1, parts[0].shape[0]):
            total = total + parts[0][slab]
    else:
        total = parts[0][...] + parts[1][...]
    field_out[0] = total[:strip]
    field_out[1] = total[strip:]
    rounded = total.astype(jnp.bfloat16)
    found_all[...] = jnp.zeros_like(found_all)

    def one_group(group, carry):
        where, field = read_group(blocks, chosen, records, group)
        row_hot = one_hot_rows(field(0), slab_rows)
        found = jnp.dot(rounded, row_hot, preferred_element_type=jnp.float32)
        hit = one_hot(field(1), strip)
        for comp in range(2):
            picked = jnp.where(hit, found[comp * strip : (comp + 1) * strip], 0.0)
            values = jnp.sum(picked, axis=0, keepdims=True)
            for member, (sender, own) in enumerate(where):
                found_all[sender, pl.ds(comp * blocks + own, 1), :] = values[
                    :, LANES * member : LANES * (member + 1)
                ]
        return carry

    lax.fori_loop(0, chosen[0], one_group, 0)
    samples[...] = found_all[: samples.shape[0]].astype(samples.dtype)


def kick_kernel(pushed, received, kicked):
    blocks = pushed.shape[1]
    total = received[0].astype(jnp.float32)
    for sender in range(1, received.shape[0]):
        total = total + received[sender].astype(jnp.float32)
    values = [pushed[i] for i in range(6)]
    values[5] = values[5] + 0.5 * total[:blocks]
    values[1] = values[1] + 0.5 * total[blocks:]
    for b in range(blocks):
        kicked[:, LANES * b : LANES * (b + 1)] = jnp.concatenate(
            [value[b : b + 1] for value in values], axis=0
        )


def local(
    coords,
    charge,
    row_index,
    block_col,
    col_offset,
    transfer_map,
    history,
    retard_index,
    retard_frac,
    retard_weight,
    z_kernel,
    x_kernel,
):
    strips = lax.axis_size("hist")
    slabs = lax.axis_size("dom")
    count_steps, comps, slab_rows, width = history.shape
    strip = width // strips
    particles = coords.shape[1]
    blocks = block_col.shape[0]
    tile = (blocks, LANES)
    spread_rows = comps * strip
    row_lanes = max(slab_rows, LANES)
    packed_rows = spread_rows + FIELDS * blocks * LANES // row_lanes

    f32, bf16 = jnp.float32, jnp.bfloat16
    pushed, packed = call(
        functools.partial(source_kernel, strips),
        (
            jax.ShapeDtypeStruct((6,) + tile, f32),
            jax.ShapeDtypeStruct((strips, packed_rows, row_lanes), bf16),
        ),
        [SMEM] * 4 + [HBM] * 7,
        (VMEM, VMEM),
        [
            pltpu.VMEM(coords.shape, f32),
            pltpu.VMEM(tile, f32),
            pltpu.VMEM(tile, jnp.int32),
            pltpu.VMEM(tile, jnp.int32),
            pltpu.SMEM(transfer_map.shape, f32),
            pltpu.VMEM(history.shape, bf16),
            pltpu.VMEM((width, width), f32),
            pltpu.VMEM((3 * width, width), bf16),
            pltpu.VMEM((comps * slab_rows, 3 * width), bf16),
            pltpu.VMEM((comps, width, slab_rows), f32),
            pltpu.VMEM((2 * LANES * count_steps, 2 * LANES), bf16),
            pltpu.VMEM((LANES * count_steps, 2 * LANES), bf16),
            pltpu.SemaphoreType.DMA((comps + 1,)),
            pltpu.SemaphoreType.DMA((5,)),
        ],
        flops=6 * comps * slab_rows * width * width,
        moved=history.size * 2 + x_kernel.size * 4,
        limit=LIMIT,
    )(
        block_col,
        retard_index,
        retard_frac,
        retard_weight,
        coords,
        charge.reshape(tile),
        row_index.reshape(tile),
        col_offset.reshape(tile),
        transfer_map,
        history,
        x_kernel,
    )
    arrived = lax.all_to_all(packed, "hist", 0, 0, tiled=True)

    part = jax.ShapeDtypeStruct((spread_rows, slab_rows), f32)
    parts = call(
        functools.partial(join_kernel, slabs, spread_rows),
        (part, part) if slabs == 2 else jax.ShapeDtypeStruct((slabs,) + part.shape, f32),
        [VMEM, VMEM],
        (VMEM, VMEM) if slabs == 2 else VMEM,
        flops=1 << 27,
        moved=1 << 20,
    )(z_kernel, arrived)
    if slabs == 2:
        kept, sent = parts
        parts = [kept, lax.ppermute(sent, "dom", [(0, 1), (1, 0)])]
    else:
        parts = [lax.all_to_all(parts, "dom", 0, 0, tiled=True)]

    records, chosen = call(
        functools.partial(unpack_kernel, spread_rows, blocks),
        (
            jax.ShapeDtypeStruct((strips + 1, FIELDS * blocks, LANES), f32),
            jax.ShapeDtypeStruct((strips * blocks + 8,), jnp.int32),
        ),
        [VMEM],
        (VMEM, SMEM),
        flops=1 << 20,
        moved=1 << 20,
    )(arrived)

    field, samples = call(
        functools.partial(sample_kernel, blocks),
        (
            jax.ShapeDtypeStruct((comps, strip, slab_rows), f32),
            jax.ShapeDtypeStruct((strips, comps * blocks, LANES), bf16),
        ),
        [SMEM, VMEM] + [VMEM] * len(parts),
        (VMEM, VMEM),
        [pltpu.VMEM((strips + 1, comps * blocks, LANES), f32)],
        flops=1 << 29,
        moved=1 << 20,
    )(chosen, records, *parts)
    samples_here = lax.all_to_all(samples, "hist", 0, 0, tiled=True)

    deposit = call(
        functools.partial(deposit_kernel, blocks),
        jax.ShapeDtypeStruct((comps, strip, slab_rows), f32),
        [SMEM, VMEM, HBM],
        VMEM,
        [pltpu.VMEM((slab_rows, comps * strip), f32)],
        flops=1 << 29,
        moved=1 << 20,
    )(chosen, records, samples)

    kicked = call(
        kick_kernel,
        jax.ShapeDtypeStruct((6, particles), f32),
        [VMEM, VMEM],
        VMEM,
        flops=1 << 16,
        moved=1 << 18,
    )(pushed, samples_here)
    return kicked, jnp.transpose(field, (0, 2, 1)), jnp.transpose(deposit, (0, 2, 1))


def solution(mesh):
    return jax.shard_map(
        local,
        mesh=mesh,
        in_specs=(
            P(None, ("dom", "hist")),
            P(("dom", "hist")),
            P(("dom", "hist")),
            P(("dom", "hist")),
            P(("dom", "hist")),
            P(),
            P("hist", None, "dom", None),
            P("hist"),
            P("hist"),
            P("hist"),
            P(None, "dom"),
            P(),
        ),
        out_specs=(P(None, ("dom", "hist")), P(None, "dom", "hist"), P(None, "dom", "hist")),
        check_vma=False,
    )
```

```python
import functools

import jax
import jax.numpy as jnp
from jax import lax
from jax.experimental import pallas as pl
from jax.experimental.pallas import tpu as pltpu
from jax.sharding import PartitionSpec as P

LANES = 128
GROUP = 8
FIELDS = 4
NT_DIMS = (((1,), (1,)), ((), ()))
VMEM = pl.BlockSpec(memory_space=pltpu.VMEM)
SMEM = pl.BlockSpec(memory_space=pltpu.SMEM)
HBM = pl.BlockSpec(memory_space=pltpu.HBM)
LIMIT = 59 * 1024 * 1024
SMALL = 16 * 1024 * 1024


def call(kernel, out_shape, in_specs, out_specs, scratch=(), flops=0, moved=0, limit=SMALL):
    return pl.pallas_call(
        kernel,
        out_shape=out_shape,
        in_specs=in_specs,
        out_specs=out_specs,
        scratch_shapes=scratch,
        compiler_params=pltpu.CompilerParams(vmem_limit_bytes=limit),
        cost_estimate=pl.CostEstimate(flops=flops, bytes_accessed=moved, transcendentals=0),
    )


def split(value):
    high = value.astype(jnp.bfloat16)
    return high, (value - high.astype(jnp.float32)).astype(jnp.bfloat16)


def record_place(spread_rows, blocks, row_lanes, index):
    across = row_lanes // LANES
    top = spread_rows + index // across * blocks
    left = index % across * LANES
    return slice(top, top + blocks), slice(left, left + LANES)


def lag_band(lag, near, far):
    row = lax.broadcasted_iota(jnp.int32, (2 * LANES, LANES), 0)
    column = lax.broadcasted_iota(jnp.int32, (2 * LANES, LANES), 1)
    behind = column + LANES - row
    weight = jnp.where(behind == lag, near, jnp.where(behind == lag + 1, far, 0.0))
    return jnp.concatenate(split(weight), axis=1)


def push(coords, charge, rows, offsets, block_col, transfer, pushed, slab_rows):
    blocks = charge.shape[0]
    u = [
        jnp.concatenate(
            [coords[i : i + 1, LANES * b : LANES * (b + 1)] for b in range(blocks)], axis=0
        )
        for i in range(6)
    ]
    total = [jnp.full((blocks, LANES), transfer[i, 0], jnp.float32) for i in range(6)]
    pairs = {}
    terms = list(u)
    for first in range(6):
        for second in range(first, 6):
            pairs[first, second] = u[first] * u[second]
            terms.append(pairs[first, second])
    for first in range(6):
        for second in range(first, 6):
            for third in range(second, 6):
                terms.append(pairs[first, second] * u[third])
    for column, term in enumerate(terms):
        total = [total[i] + transfer[i, 1 + column] * term for i in range(6)]
    for i in range(6):
        pushed[i] = total[i]
    weight0 = charge[...]
    weight1 = weight0 * total[1]
    row_of = lax.broadcasted_iota(jnp.int32, (blocks, LANES), 0)
    column = offsets[...]
    for b in range(blocks):
        column = column + jnp.where(row_of == b, block_col[0, b], 0)
    return lax.rem(rows[...], slab_rows), column, weight0, weight1


def source_kernel(
    strips,
    block_col_from,
    lags_from,
    fracs_from,
    weights_from,
    coords_from,
    charge_from,
    rows_from,
    offsets_from,
    transfer_from,
    history,
    x_kernel,
    pushed_to,
    packed_to,
    block_col,
    lags,
    fracs,
    weights,
    coords,
    charge,
    rows,
    offsets,
    transfer,
    frames,
    x_here,
    x_parts,
    s_parts,
    spread_all,
    bands,
    first_bands,
    pushed,
    packed,
    sems,
):
    count_steps, comps, slab_rows, width = history.shape
    blocks = charge.shape[0]
    strip = width // strips
    spread_rows = packed.shape[1] - FIELDS * blocks * LANES // packed.shape[2]
    pairs = [
        (lags_from, lags),
        (fracs_from, fracs),
        (weights_from, weights),
        (block_col_from, block_col),
        (coords_from, coords),
        (charge_from, charge),
        (rows_from, rows),
        (offsets_from, offsets),
        (transfer_from, transfer),
        (x_kernel, x_here),
    ]
    pairs += [(history.at[:, comp], frames.at[:, comp]) for comp in range(comps)]
    fetch = [
        pltpu.make_async_copy(source, target, sems.at[index])
        for index, (source, target) in enumerate(pairs)
    ]
    for copy in fetch:
        copy.start()
    stored = []

    def store(source, target):
        copy = pltpu.make_async_copy(source, target, sems.at[len(fetch) + len(stored)])
        copy.start()
        stored.append(copy)

    for copy in fetch[:3]:
        copy.wait()
    for t in range(count_steps):
        far = weights[0, t] * fracs[0, t]
        near = weights[0, t] * (1.0 - fracs[0, t])
        bands[2 * LANES * t : 2 * LANES * (t + 1)] = lag_band(lags[0, t], near, far)
        first_bands[LANES * t : LANES * (t + 1)] = bands[
            2 * LANES * t + LANES : 2 * LANES * (t + 1)
        ]

    for copy in fetch[3:9]:
        copy.wait()
    row, column, weight0, weight1 = push(
        coords, charge, rows, offsets, block_col, transfer, pushed, slab_rows
    )
    store(pushed, pushed_to)
    same = [row.astype(jnp.bfloat16), None, weight0.astype(jnp.bfloat16), weight1.astype(jnp.bfloat16)]
    for partner in range(strips):
        here = column - partner * strip
        here = jnp.where((here >= 0) & (here < strip), here, -1)
        for index in range(FIELDS):
            value = here.astype(jnp.float32).astype(jnp.bfloat16) if index == 1 else same[index]
            place = record_place(spread_rows, blocks, packed.shape[2], index)
            packed[(partner,) + place] = value
    store(packed.at[:, spread_rows:], packed_to.at[:, spread_rows:])
    fetch[9].wait()
    high, low = split(x_here[...])
    x_parts[:width] = high
    x_parts[width : 2 * width] = high
    x_parts[2 * width :] = low

    for comp in range(comps):
        fetch[10 + comp].wait()
        here = slice(comp * slab_rows, (comp + 1) * slab_rows)
        for q in range(width // LANES):
            before = slice(LANES * max(q - 1, 0), LANES * (q + 1))
            steps = [frames[t, comp, :, before] for t in range(count_steps)]
            both = jnp.dot(
                jnp.concatenate(steps, axis=1),
                bands[...] if q else first_bands[...],
                preferred_element_type=jnp.float32,
            )
            high, low = split(both[:, :LANES] + both[:, LANES:])
            s_parts[here, LANES * q : LANES * (q + 1)] = high
            s_parts[here, width + LANES * q : width + LANES * (q + 1)] = low
            s_parts[here, 2 * width + LANES * q : 2 * width + LANES * (q + 1)] = high
        spread = jnp.dot(s_parts[here], x_parts[...], preferred_element_type=jnp.float32)
        if strip % 16 == 0:
            turned = spread.astype(packed.dtype).T
            part = slice(comp * strip, (comp + 1) * strip)
            for partner in range(strips):
                packed[partner, part, :slab_rows] = turned[
                    partner * strip : (partner + 1) * strip
                ]
            store(packed.at[:, part], packed_to.at[:, part])
        else:
            spread_all[comp] = spread.T
    if strip % 16:
        for partner in range(strips):
            part = slice(partner * strip, (partner + 1) * strip)
            both = jnp.concatenate([spread_all[comp, part] for comp in range(comps)], axis=0)
            packed[partner, :spread_rows, :slab_rows] = both.astype(packed.dtype)
        store(packed.at[:, :spread_rows], packed_to.at[:, :spread_rows])
    for copy in stored:
        copy.wait()


def join_kernel(slabs, spread_rows, z_kernel, arrived, kept, *sent):
    slab_rows = z_kernel.shape[0] // slabs
    total = arrived[0, :spread_rows, :slab_rows].astype(jnp.float32)
    for sender in range(1, arrived.shape[0]):
        total = total + arrived[sender, :spread_rows, :slab_rows].astype(jnp.float32)
    high, low = split(total)
    left = jnp.concatenate([high, low, high], axis=1)

    def part(slab):
        start = pl.multiple_of(slab * slab_rows, slab_rows)
        z_high, z_low = split(z_kernel[pl.ds(start, slab_rows), :])
        right = jnp.concatenate([z_high, z_high, z_low], axis=1)
        return lax.dot_general(left, right, NT_DIMS, preferred_element_type=jnp.float32)

    if sent:
        me = lax.axis_index("dom")
        sent[0][...] = part(1 - me)
        kept[...] = part(me)
    else:
        for slab in range(slabs):
            kept[slab] = part(slab)


def unpack_kernel(spread_rows, blocks, arrived, records, chosen):
    senders = arrived.shape[0]
    own = lax.broadcasted_iota(jnp.int32, (blocks, 1), 0)
    bit = jnp.left_shift(jnp.ones_like(own), own).astype(jnp.float32)
    masks = []
    for sender in range(senders):
        for index in range(FIELDS):
            place = record_place(spread_rows, blocks, arrived.shape[2], index)
            value = arrived[(sender,) + place].astype(jnp.float32)
            records[sender, index * blocks : (index + 1) * blocks] = value
            if index == 1:
                meets = jnp.max(value, axis=1, keepdims=True) >= 0.0
                masks.append(jnp.sum(jnp.where(meets, bit, 0.0)).astype(jnp.int32))
    records[senders] = jnp.full(records.shape[1:], -1.0, jnp.float32)
    count = jnp.int32(0)
    for sender in range(senders):
        for block in range(blocks):
            chosen[1 + count] = sender * blocks + block
            count = count + ((masks[sender] >> block) & 1)
    chosen[0] = (count + (GROUP - 1)) // GROUP
    for member in range(GROUP):
        chosen[1 + count + member] = senders * blocks


def read_group(blocks, chosen, records, group):
    where = []
    for member in range(GROUP):
        block = chosen[1 + group * GROUP + member]
        where.append((block // blocks, lax.rem(block, blocks)))

    def field(index):
        return jnp.concatenate(
            [records[sender, pl.ds(index * blocks + own, 1), :] for sender, own in where], axis=1
        )

    return where, field


def one_hot(index, size):
    iota = lax.broadcasted_iota(jnp.int32, (size, index.shape[1]), 0).astype(jnp.float32)
    return iota == index


def one_hot_rows(row, size):
    iota = lax.broadcasted_iota(jnp.int32, (size, row.shape[1]), 0)
    if size <= 256:
        hit = iota.astype(jnp.bfloat16) == row.astype(jnp.bfloat16)
        return jnp.where(hit, jnp.bfloat16(1.0), jnp.bfloat16(0.0))
    return jnp.where(iota.astype(jnp.float32) == row, 1.0, 0.0).astype(jnp.bfloat16)


def deposit_kernel(blocks, chosen, records, after, deposit, total):
    del after
    strip, slab_rows = deposit.shape[1:]
    total[...] = jnp.zeros_like(total)

    def one_group(group, carry):
        _, field = read_group(blocks, chosen, records, group)
        hit = one_hot(field(1), strip)
        weighted = [jnp.where(hit, field(2 + comp), 0.0) for comp in range(2)]
        total[...] += lax.dot_general(
            one_hot_rows(field(0), slab_rows),
            jnp.concatenate(weighted, axis=0).astype(jnp.bfloat16),
            NT_DIMS,
            preferred_element_type=jnp.float32,
        )
        return carry

    lax.fori_loop(0, chosen[0], one_group, 0)
    turned = total[...].T
    deposit[0] = turned[:strip]
    deposit[1] = turned[strip:]


def sample_kernel(blocks, chosen, records, *refs):
    parts, (field_out, samples, found_all) = refs[:-3], refs[-3:]
    strip, slab_rows = field_out.shape[1:]
    if len(parts) == 1:
        total = parts[0][0]
        for slab in range(1, parts[0].shape[0]):
            total = total + parts[0][slab]
    else:
        total = parts[0][...] + parts[1][...]
    field_out[0] = total[:strip]
    field_out[1] = total[strip:]
    rounded = total.astype(jnp.bfloat16)
    found_all[...] = jnp.zeros_like(found_all)

    def one_group(group, carry):
        where, field = read_group(blocks, chosen, records, group)
        row_hot = one_hot_rows(field(0), slab_rows)
        found = jnp.dot(rounded, row_hot, preferred_element_type=jnp.float32)
        hit = one_hot(field(1), strip)
        for comp in range(2):
            picked = jnp.where(hit, found[comp * strip : (comp + 1) * strip], 0.0)
            values = jnp.sum(picked, axis=0, keepdims=True)
            for member, (sender, own) in enumerate(where):
                found_all[sender, pl.ds(comp * blocks + own, 1), :] = values[
                    :, LANES * member : LANES * (member + 1)
                ]
        return carry

    lax.fori_loop(0, chosen[0], one_group, 0)
    samples[...] = found_all[: samples.shape[0]].astype(samples.dtype)


def kick_kernel(pushed, received, kicked):
    blocks = pushed.shape[1]
    total = received[0].astype(jnp.float32)
    for sender in range(1, received.shape[0]):
        total = total + received[sender].astype(jnp.float32)
    values = [pushed[i] for i in range(6)]
    values[5] = values[5] + 0.5 * total[:blocks]
    values[1] = values[1] + 0.5 * total[blocks:]
    for b in range(blocks):
        kicked[:, LANES * b : LANES * (b + 1)] = jnp.concatenate(
            [value[b : b + 1] for value in values], axis=0
        )


def local(
    coords,
    charge,
    row_index,
    block_col,
    col_offset,
    transfer_map,
    history,
    retard_index,
    retard_frac,
    retard_weight,
    z_kernel,
    x_kernel,
):
    strips = lax.axis_size("hist")
    slabs = lax.axis_size("dom")
    count_steps, comps, slab_rows, width = history.shape
    strip = width // strips
    particles = coords.shape[1]
    blocks = block_col.shape[0]
    tile = (blocks, LANES)
    spread_rows = comps * strip
    row_lanes = max(slab_rows, LANES)
    packed_rows = spread_rows + FIELDS * blocks * LANES // row_lanes

    f32, bf16 = jnp.float32, jnp.bfloat16
    pushed, packed = call(
        functools.partial(source_kernel, strips),
        (
            jax.ShapeDtypeStruct((6,) + tile, f32),
            jax.ShapeDtypeStruct((strips, packed_rows, row_lanes), bf16),
        ),
        [HBM] * 11,
        (HBM, HBM),
        [
            pltpu.SMEM((1, blocks), jnp.int32),
            pltpu.SMEM((1, count_steps), jnp.int32),
            pltpu.SMEM((1, count_steps), f32),
            pltpu.SMEM((1, count_steps), f32),
            pltpu.VMEM(coords.shape, f32),
            pltpu.VMEM(tile, f32),
            pltpu.VMEM(tile, jnp.int32),
            pltpu.VMEM(tile, jnp.int32),
            pltpu.SMEM(transfer_map.shape, f32),
            pltpu.VMEM(history.shape, bf16),
            pltpu.VMEM((width, width), f32),
            pltpu.VMEM((3 * width, width), bf16),
            pltpu.VMEM((comps * slab_rows, 3 * width), bf16),
            pltpu.VMEM((comps, width, slab_rows), f32),
            pltpu.VMEM((2 * LANES * count_steps, 2 * LANES), bf16),
            pltpu.VMEM((LANES * count_steps, 2 * LANES), bf16),
            pltpu.VMEM((6,) + tile, f32),
            pltpu.VMEM((strips, packed_rows, row_lanes), bf16),
            pltpu.SemaphoreType.DMA((16,)),
        ],
        flops=6 * comps * slab_rows * width * width,
        moved=history.size * 2 + x_kernel.size * 4,
        limit=LIMIT,
    )(
        block_col.reshape(1, blocks),
        retard_index.reshape(1, count_steps),
        retard_frac.reshape(1, count_steps),
        retard_weight.reshape(1, count_steps),
        coords,
        charge.reshape(tile),
        row_index.reshape(tile),
        col_offset.reshape(tile),
        transfer_map,
        history,
        x_kernel,
    )
    arrived = lax.all_to_all(packed, "hist", 0, 0, tiled=True)

    part = jax.ShapeDtypeStruct((spread_rows, slab_rows), f32)
    parts = call(
        functools.partial(join_kernel, slabs, spread_rows),
        (part, part) if slabs == 2 else jax.ShapeDtypeStruct((slabs,) + part.shape, f32),
        [VMEM, VMEM],
        (VMEM, VMEM) if slabs == 2 else VMEM,
        flops=1 << 27,
        moved=1 << 20,
    )(z_kernel, arrived)
    if slabs == 2:
        kept, sent = parts
        parts = [kept, lax.ppermute(sent, "dom", [(0, 1), (1, 0)])]
    else:
        parts = [lax.all_to_all(parts, "dom", 0, 0, tiled=True)]

    records, chosen = call(
        functools.partial(unpack_kernel, spread_rows, blocks),
        (
            jax.ShapeDtypeStruct((strips + 1, FIELDS * blocks, LANES), f32),
            jax.ShapeDtypeStruct((strips * blocks + 16,), jnp.int32),
        ),
        [VMEM],
        (VMEM, SMEM),
        flops=1 << 20,
        moved=1 << 20,
    )(arrived)

    field, samples = call(
        functools.partial(sample_kernel, blocks),
        (
            jax.ShapeDtypeStruct((comps, strip, slab_rows), f32),
            jax.ShapeDtypeStruct((strips, comps * blocks, LANES), bf16),
        ),
        [SMEM, VMEM] + [VMEM] * len(parts),
        (VMEM, VMEM),
        [pltpu.VMEM((strips + 1, comps * blocks, LANES), f32)],
        flops=1 << 29,
        moved=1 << 20,
    )(chosen, records, *parts)
    samples_here = lax.all_to_all(samples, "hist", 0, 0, tiled=True)

    deposit = call(
        functools.partial(deposit_kernel, blocks),
        jax.ShapeDtypeStruct((comps, strip, slab_rows), f32),
        [SMEM, VMEM, HBM],
        VMEM,
        [pltpu.VMEM((slab_rows, comps * strip), f32)],
        flops=1 << 29,
        moved=1 << 20,
    )(chosen, records, samples)

    kicked = call(
        kick_kernel,
        jax.ShapeDtypeStruct((6, particles), f32),
        [VMEM, VMEM],
        VMEM,
        flops=1 << 16,
        moved=1 << 18,
    )(pushed, samples_here)
    return kicked, jnp.transpose(field, (0, 2, 1)), jnp.transpose(deposit, (0, 2, 1))


def solution(mesh):
    return jax.shard_map(
        local,
        mesh=mesh,
        in_specs=(
            P(None, ("dom", "hist")),
            P(("dom", "hist")),
            P(("dom", "hist")),
            P(("dom", "hist")),
            P(("dom", "hist")),
            P(),
            P("hist", None, "dom", None),
            P("hist"),
            P("hist"),
            P("hist"),
            P(None, "dom"),
            P(),
        ),
        out_specs=(P(None, ("dom", "hist")), P(None, "dom", "hist"), P(None, "dom", "hist")),
        check_vma=False,
    )
```

```python
import functools

import jax
import jax.numpy as jnp
from jax import lax
from jax.experimental import pallas as pl
from jax.experimental.pallas import tpu as pltpu
from jax.sharding import PartitionSpec as P

LANES = 128
GROUP = 8
FIELDS = 5
NT_DIMS = (((1,), (1,)), ((), ()))
VMEM = pl.BlockSpec(memory_space=pltpu.VMEM)
SMEM = pl.BlockSpec(memory_space=pltpu.SMEM)
HBM = pl.BlockSpec(memory_space=pltpu.HBM)
LIMIT = 59 * 1024 * 1024
SMALL = 16 * 1024 * 1024


def call(kernel, out_shape, in_specs, out_specs, scratch=(), flops=0, moved=0, limit=SMALL):
    return pl.pallas_call(
        kernel,
        out_shape=out_shape,
        in_specs=in_specs,
        out_specs=out_specs,
        scratch_shapes=scratch,
        compiler_params=pltpu.CompilerParams(vmem_limit_bytes=limit),
        cost_estimate=pl.CostEstimate(flops=flops, bytes_accessed=moved, transcendentals=0),
    )


def split(value):
    high = value.astype(jnp.bfloat16)
    return high, (value - high.astype(jnp.float32)).astype(jnp.bfloat16)


def near_and_far(strips):
    if strips != 16:
        return None
    return (1, 2, 3), (4, 8, 12)


def partners_of(strips):
    near, far = near_and_far(strips)
    return [one ^ other for one in (0,) + near for other in (0,) + far]


def gather_records(record):
    strips = lax.axis_size("hist")
    if near_and_far(strips) is None:
        return [lax.all_gather(record, "hist", axis=0)]

    def meet(value, steps):
        pairs = [[(i, i ^ step) for i in range(strips)] for step in steps]
        return [value] + [lax.ppermute(value, "hist", pair) for pair in pairs]

    near, far = near_and_far(strips)
    column = jnp.concatenate(meet(record[None], far), axis=0)
    return meet(column, near)


def lag_band(lag, near, far):
    row = lax.broadcasted_iota(jnp.int32, (2 * LANES, LANES), 0)
    column = lax.broadcasted_iota(jnp.int32, (2 * LANES, LANES), 1)
    behind = column + LANES - row
    weight = jnp.where(behind == lag, near, jnp.where(behind == lag + 1, far, 0.0))
    return jnp.concatenate(split(weight), axis=1)


def push(coords, charge, rows, offsets, block_col, transfer, pushed, slab_rows):
    blocks = charge.shape[0]
    u = [
        jnp.concatenate(
            [coords[i : i + 1, LANES * b : LANES * (b + 1)] for b in range(blocks)], axis=0
        )
        for i in range(6)
    ]
    total = [jnp.full((blocks, LANES), transfer[i, 0], jnp.float32) for i in range(6)]
    pairs = {}
    terms = list(u)
    for first in range(6):
        for second in range(first, 6):
            pairs[first, second] = u[first] * u[second]
            terms.append(pairs[first, second])
    for first in range(6):
        for second in range(first, 6):
            for third in range(second, 6):
                terms.append(pairs[first, second] * u[third])
    for column, term in enumerate(terms):
        total = [total[i] + transfer[i, 1 + column] * term for i in range(6)]
    for i in range(6):
        pushed[i] = total[i]
    weight0 = charge[...]
    weight1 = weight0 * total[1]
    row_of = lax.broadcasted_iota(jnp.int32, (blocks, LANES), 0)
    column = offsets[...]
    for b in range(blocks):
        column = column + jnp.where(row_of == b, block_col[0, b], 0)
    return lax.rem(rows[...], slab_rows), column, weight0, weight1


def source_kernel(
    strips,
    block_col_from,
    lags_from,
    fracs_from,
    weights_from,
    coords_from,
    charge_from,
    rows_from,
    offsets_from,
    transfer_from,
    history,
    x_kernel,
    pushed_to,
    record_to,
    packed_to,
    block_col,
    lags,
    fracs,
    weights,
    coords,
    charge,
    rows,
    offsets,
    transfer,
    frames,
    x_here,
    x_parts,
    s_parts,
    spread_all,
    bands,
    first_bands,
    pushed,
    record,
    packed,
    sems,
):
    count_steps, comps, slab_rows, width = history.shape
    blocks = charge.shape[0]
    strip = width // strips
    pairs = [
        (lags_from, lags),
        (fracs_from, fracs),
        (weights_from, weights),
        (block_col_from, block_col),
        (coords_from, coords),
        (charge_from, charge),
        (rows_from, rows),
        (offsets_from, offsets),
        (transfer_from, transfer),
        (x_kernel, x_here),
    ]
    pairs += [(history.at[:, comp], frames.at[:, comp]) for comp in range(comps)]
    fetch = [
        pltpu.make_async_copy(source, target, sems.at[index])
        for index, (source, target) in enumerate(pairs)
    ]
    for copy in fetch:
        copy.start()
    stored = []

    def store(source, target):
        copy = pltpu.make_async_copy(source, target, sems.at[len(fetch) + len(stored)])
        copy.start()
        stored.append(copy)

    for copy in fetch[:3]:
        copy.wait()
    for t in range(count_steps):
        far = weights[0, t] * fracs[0, t]
        near = weights[0, t] * (1.0 - fracs[0, t])
        bands[2 * LANES * t : 2 * LANES * (t + 1)] = lag_band(lags[0, t], near, far)
        first_bands[LANES * t : LANES * (t + 1)] = bands[
            2 * LANES * t + LANES : 2 * LANES * (t + 1)
        ]

    for copy in fetch[3:9]:
        copy.wait()
    row, column, weight0, weight1 = push(
        coords, charge, rows, offsets, block_col, transfer, pushed, slab_rows
    )
    store(pushed, pushed_to)
    place = column // strip
    fields = [row, place, column - place * strip, weight0, weight1]
    for index, value in enumerate(fields):
        value = value.astype(jnp.float32).astype(record.dtype)
        record[index * blocks : (index + 1) * blocks] = value
    store(record, record_to)
    fetch[9].wait()
    high, low = split(x_here[...])
    x_parts[:width] = high
    x_parts[width : 2 * width] = high
    x_parts[2 * width :] = low

    for comp in range(comps):
        fetch[10 + comp].wait()
        here = slice(comp * slab_rows, (comp + 1) * slab_rows)
        for q in range(width // LANES):
            before = slice(LANES * max(q - 1, 0), LANES * (q + 1))
            steps = [frames[t, comp, :, before] for t in range(count_steps)]
            both = jnp.dot(
                jnp.concatenate(steps, axis=1),
                bands[...] if q else first_bands[...],
                preferred_element_type=jnp.float32,
            )
            high, low = split(both[:, :LANES] + both[:, LANES:])
            s_parts[here, LANES * q : LANES * (q + 1)] = high
            s_parts[here, width + LANES * q : width + LANES * (q + 1)] = low
            s_parts[here, 2 * width + LANES * q : 2 * width + LANES * (q + 1)] = high
        spread = jnp.dot(s_parts[here], x_parts[...], preferred_element_type=jnp.float32)
        if strip % 16 == 0:
            turned = spread.astype(packed.dtype).T
            part = slice(comp * strip, (comp + 1) * strip)
            for partner in range(strips):
                packed[partner, part] = turned[
                    partner * strip : (partner + 1) * strip
                ]
            store(packed.at[:, part], packed_to.at[:, part])
        else:
            spread_all[comp] = spread.T
    if strip % 16:
        for partner in range(strips):
            part = slice(partner * strip, (partner + 1) * strip)
            both = jnp.concatenate([spread_all[comp, part] for comp in range(comps)], axis=0)
            packed[partner] = both.astype(packed.dtype)
        store(packed, packed_to)
    for copy in stored:
        copy.wait()


def join_kernel(slabs, z_kernel, arrived, kept, *sent):
    slab_rows = z_kernel.shape[0] // slabs
    total = arrived[0].astype(jnp.float32)
    for sender in range(1, arrived.shape[0]):
        total = total + arrived[sender].astype(jnp.float32)
    high, low = split(total)
    left = jnp.concatenate([high, low, high], axis=1)

    def part(slab):
        start = pl.multiple_of(slab * slab_rows, slab_rows)
        z_high, z_low = split(z_kernel[pl.ds(start, slab_rows), :])
        right = jnp.concatenate([z_high, z_high, z_low], axis=1)
        return lax.dot_general(left, right, NT_DIMS, preferred_element_type=jnp.float32)

    if sent:
        me = lax.axis_index("dom")
        sent[0][...] = part(1 - me)
        kept[...] = part(me)
    else:
        for slab in range(slabs):
            kept[slab] = part(slab)


def unpack_kernel(blocks, *refs):
    gathered, (records, chosen) = refs[:-2], refs[-2:]
    senders = records.shape[0] - 1
    strip_here = lax.axis_index("hist").astype(jnp.float32)
    own = lax.broadcasted_iota(jnp.int32, (blocks, 1), 0)
    bit = jnp.left_shift(jnp.ones_like(own), own).astype(jnp.float32)
    masks = []
    sources = [ref.at[place] for ref in gathered for place in range(ref.shape[0])]
    for sender, source in enumerate(sources):
        row, place, column, weight0, weight1 = [
            source[index * blocks : (index + 1) * blocks].astype(jnp.float32)
            for index in range(FIELDS)
        ]
        column = jnp.where(place == strip_here, column, -1.0)
        for index, value in enumerate([row, column, weight0, weight1]):
            records[sender, index * blocks : (index + 1) * blocks] = value
        meets = jnp.max(column, axis=1, keepdims=True) >= 0.0
        masks.append(jnp.sum(jnp.where(meets, bit, 0.0)).astype(jnp.int32))
    records[senders] = jnp.full(records.shape[1:], -1.0, jnp.float32)
    count = jnp.int32(0)
    for sender in range(senders):
        for block in range(blocks):
            chosen[1 + count] = sender * blocks + block
            count = count + ((masks[sender] >> block) & 1)
    chosen[0] = (count + (GROUP - 1)) // GROUP
    for member in range(GROUP):
        chosen[1 + count + member] = senders * blocks


def read_group(blocks, chosen, records, group):
    where = []
    for member in range(GROUP):
        block = chosen[1 + group * GROUP + member]
        where.append((block // blocks, lax.rem(block, blocks)))

    def field(index):
        return jnp.concatenate(
            [records[sender, pl.ds(index * blocks + own, 1), :] for sender, own in where], axis=1
        )

    return where, field


def one_hot(index, size):
    iota = lax.broadcasted_iota(jnp.int32, (size, index.shape[1]), 0).astype(jnp.float32)
    return iota == index


def one_hot_rows(row, size):
    iota = lax.broadcasted_iota(jnp.int32, (size, row.shape[1]), 0)
    if size <= 256:
        hit = iota.astype(jnp.bfloat16) == row.astype(jnp.bfloat16)
        return jnp.where(hit, jnp.bfloat16(1.0), jnp.bfloat16(0.0))
    return jnp.where(iota.astype(jnp.float32) == row, 1.0, 0.0).astype(jnp.bfloat16)


def deposit_kernel(blocks, chosen, records, after, deposit, total):
    del after
    strip, slab_rows = deposit.shape[1:]
    total[...] = jnp.zeros_like(total)

    def one_group(group, carry):
        _, field = read_group(blocks, chosen, records, group)
        hit = one_hot(field(1), strip)
        weighted = [jnp.where(hit, field(2 + comp), 0.0) for comp in range(2)]
        total[...] += lax.dot_general(
            one_hot_rows(field(0), slab_rows),
            jnp.concatenate(weighted, axis=0).astype(jnp.bfloat16),
            NT_DIMS,
            preferred_element_type=jnp.float32,
        )
        return carry

    lax.fori_loop(0, chosen[0], one_group, 0)
    turned = total[...].T
    deposit[0] = turned[:strip]
    deposit[1] = turned[strip:]


def sample_kernel(blocks, chosen, records, *refs):
    parts, (field_out, samples, found_all) = refs[:-3], refs[-3:]
    strip, slab_rows = field_out.shape[1:]
    if len(parts) == 1:
        total = parts[0][0]
        for slab in range(1, parts[0].shape[0]):
            total = total + parts[0][slab]
    else:
        total = parts[0][...] + parts[1][...]
    field_out[0] = total[:strip]
    field_out[1] = total[strip:]
    rounded = total.astype(jnp.bfloat16)
    found_all[...] = jnp.zeros_like(found_all)

    def one_group(group, carry):
        where, field = read_group(blocks, chosen, records, group)
        row_hot = one_hot_rows(field(0), slab_rows)
        found = jnp.dot(rounded, row_hot, preferred_element_type=jnp.float32)
        hit = one_hot(field(1), strip)
        for comp in range(2):
            picked = jnp.where(hit, found[comp * strip : (comp + 1) * strip], 0.0)
            values = jnp.sum(picked, axis=0, keepdims=True)
            for member, (sender, own) in enumerate(where):
                found_all[sender, pl.ds(comp * blocks + own, 1), :] = values[
                    :, LANES * member : LANES * (member + 1)
                ]
        return carry

    lax.fori_loop(0, chosen[0], one_group, 0)
    strips = samples.shape[0]
    if near_and_far(strips) is None:
        samples[...] = found_all[:strips].astype(samples.dtype)
    else:
        here = lax.axis_index("hist")
        for index, step in enumerate(partners_of(strips)):
            samples[here ^ step] = found_all[index].astype(samples.dtype)


def kick_kernel(pushed, received, kicked):
    blocks = pushed.shape[1]
    total = received[0].astype(jnp.float32)
    for sender in range(1, received.shape[0]):
        total = total + received[sender].astype(jnp.float32)
    values = [pushed[i] for i in range(6)]
    values[5] = values[5] + 0.5 * total[:blocks]
    values[1] = values[1] + 0.5 * total[blocks:]
    for b in range(blocks):
        kicked[:, LANES * b : LANES * (b + 1)] = jnp.concatenate(
            [value[b : b + 1] for value in values], axis=0
        )


def local(
    coords,
    charge,
    row_index,
    block_col,
    col_offset,
    transfer_map,
    history,
    retard_index,
    retard_frac,
    retard_weight,
    z_kernel,
    x_kernel,
):
    strips = lax.axis_size("hist")
    slabs = lax.axis_size("dom")
    count_steps, comps, slab_rows, width = history.shape
    strip = width // strips
    particles = coords.shape[1]
    blocks = block_col.shape[0]
    tile = (blocks, LANES)
    spread_rows = comps * strip
    record_shape = (FIELDS * blocks, LANES)

    f32, bf16 = jnp.float32, jnp.bfloat16
    pushed, record, packed = call(
        functools.partial(source_kernel, strips),
        (
            jax.ShapeDtypeStruct((6,) + tile, f32),
            jax.ShapeDtypeStruct(record_shape, bf16),
            jax.ShapeDtypeStruct((strips, spread_rows, slab_rows), bf16),
        ),
        [HBM] * 11,
        (HBM, HBM, HBM),
        [
            pltpu.SMEM((1, blocks), jnp.int32),
            pltpu.SMEM((1, count_steps), jnp.int32),
            pltpu.SMEM((1, count_steps), f32),
            pltpu.SMEM((1, count_steps), f32),
            pltpu.VMEM(coords.shape, f32),
            pltpu.VMEM(tile, f32),
            pltpu.VMEM(tile, jnp.int32),
            pltpu.VMEM(tile, jnp.int32),
            pltpu.SMEM(transfer_map.shape, f32),
            pltpu.VMEM(history.shape, bf16),
            pltpu.VMEM((width, width), f32),
            pltpu.VMEM((3 * width, width), bf16),
            pltpu.VMEM((comps * slab_rows, 3 * width), bf16),
            pltpu.VMEM((comps, width, slab_rows), f32),
            pltpu.VMEM((2 * LANES * count_steps, 2 * LANES), bf16),
            pltpu.VMEM((LANES * count_steps, 2 * LANES), bf16),
            pltpu.VMEM((6,) + tile, f32),
            pltpu.VMEM(record_shape, bf16),
            pltpu.VMEM((strips, spread_rows, slab_rows), bf16),
            pltpu.SemaphoreType.DMA((16,)),
        ],
        flops=6 * comps * slab_rows * width * width,
        moved=history.size * 2 + x_kernel.size * 4,
        limit=LIMIT,
    )(
        block_col.reshape(1, blocks),
        retard_index.reshape(1, count_steps),
        retard_frac.reshape(1, count_steps),
        retard_weight.reshape(1, count_steps),
        coords,
        charge.reshape(tile),
        row_index.reshape(tile),
        col_offset.reshape(tile),
        transfer_map,
        history,
        x_kernel,
    )
    arrived = lax.all_to_all(packed, "hist", 0, 0, tiled=True)
    gathered = gather_records(record)

    part = jax.ShapeDtypeStruct((spread_rows, slab_rows), f32)
    parts = call(
        functools.partial(join_kernel, slabs),
        (part, part) if slabs == 2 else jax.ShapeDtypeStruct((slabs,) + part.shape, f32),
        [VMEM, VMEM],
        (VMEM, VMEM) if slabs == 2 else VMEM,
        flops=1 << 27,
        moved=1 << 20,
    )(z_kernel, arrived)
    if slabs == 2:
        kept, sent = parts
        parts = [kept, lax.ppermute(sent, "dom", [(0, 1), (1, 0)])]
    else:
        parts = [lax.all_to_all(parts, "dom", 0, 0, tiled=True)]

    records, chosen = call(
        functools.partial(unpack_kernel, blocks),
        (
            jax.ShapeDtypeStruct((strips + 1, 4 * blocks, LANES), f32),
            jax.ShapeDtypeStruct((strips * blocks + 16,), jnp.int32),
        ),
        [VMEM] * len(gathered),
        (VMEM, SMEM),
        flops=1 << 20,
        moved=1 << 20,
    )(*gathered)

    field, samples = call(
        functools.partial(sample_kernel, blocks),
        (
            jax.ShapeDtypeStruct((comps, strip, slab_rows), f32),
            jax.ShapeDtypeStruct((strips, comps * blocks, LANES), bf16),
        ),
        [SMEM, VMEM] + [VMEM] * len(parts),
        (VMEM, VMEM),
        [pltpu.VMEM((strips + 1, comps * blocks, LANES), f32)],
        flops=1 << 29,
        moved=1 << 20,
    )(chosen, records, *parts)
    samples_here = lax.all_to_all(samples, "hist", 0, 0, tiled=True)

    deposit = call(
        functools.partial(deposit_kernel, blocks),
        jax.ShapeDtypeStruct((comps, strip, slab_rows), f32),
        [SMEM, VMEM, HBM],
        VMEM,
        [pltpu.VMEM((slab_rows, comps * strip), f32)],
        flops=1 << 29,
        moved=1 << 20,
    )(chosen, records, samples)

    kicked = call(
        kick_kernel,
        jax.ShapeDtypeStruct((6, particles), f32),
        [VMEM, VMEM],
        VMEM,
        flops=1 << 16,
        moved=1 << 18,
    )(pushed, samples_here)
    return kicked, jnp.transpose(field, (0, 2, 1)), jnp.transpose(deposit, (0, 2, 1))


def solution(mesh):
    return jax.shard_map(
        local,
        mesh=mesh,
        in_specs=(
            P(None, ("dom", "hist")),
            P(("dom", "hist")),
            P(("dom", "hist")),
            P(("dom", "hist")),
            P(("dom", "hist")),
            P(),
            P("hist", None, "dom", None),
            P("hist"),
            P("hist"),
            P("hist"),
            P(None, "dom"),
            P(),
        ),
        out_specs=(P(None, ("dom", "hist")), P(None, "dom", "hist"), P(None, "dom", "hist")),
        check_vma=False,
    )
```

```python
import functools

import jax
import jax.numpy as jnp
from jax import lax
from jax.experimental import pallas as pl
from jax.experimental.pallas import tpu as pltpu
from jax.sharding import PartitionSpec as P

LANES = 128
GROUP = 8
FIELDS = 4
NT_DIMS = (((1,), (1,)), ((), ()))
VMEM = pl.BlockSpec(memory_space=pltpu.VMEM)
SMEM = pl.BlockSpec(memory_space=pltpu.SMEM)
HBM = pl.BlockSpec(memory_space=pltpu.HBM)
LIMIT = 59 * 1024 * 1024
SMALL = 16 * 1024 * 1024


def call(kernel, out_shape, in_specs, out_specs, scratch=(), flops=0, moved=0, limit=SMALL):
    return pl.pallas_call(
        kernel,
        out_shape=out_shape,
        in_specs=in_specs,
        out_specs=out_specs,
        scratch_shapes=scratch,
        compiler_params=pltpu.CompilerParams(vmem_limit_bytes=limit),
        cost_estimate=pl.CostEstimate(flops=flops, bytes_accessed=moved, transcendentals=0),
    )


def split(value):
    high = value.astype(jnp.bfloat16)
    return high, (value - high.astype(jnp.float32)).astype(jnp.bfloat16)


def record_place(spread_rows, blocks, row_lanes, index):
    across = row_lanes // LANES
    top = spread_rows + index // across * blocks
    left = index % across * LANES
    return slice(top, top + blocks), slice(left, left + LANES)


def lag_band(lag, near, far):
    row = lax.broadcasted_iota(jnp.int32, (2 * LANES, LANES), 0)
    column = lax.broadcasted_iota(jnp.int32, (2 * LANES, LANES), 1)
    behind = column + LANES - row
    weight = jnp.where(behind == lag, near, jnp.where(behind == lag + 1, far, 0.0))
    return jnp.concatenate(split(weight), axis=1)


def push(coords, charge, rows, offsets, block_col, transfer, pushed, slab_rows):
    blocks = charge.shape[0]
    u = [
        jnp.concatenate(
            [coords[i : i + 1, LANES * b : LANES * (b + 1)] for b in range(blocks)], axis=0
        )
        for i in range(6)
    ]
    total = [jnp.full((blocks, LANES), transfer[i, 0], jnp.float32) for i in range(6)]
    pairs = {}
    terms = list(u)
    for first in range(6):
        for second in range(first, 6):
            pairs[first, second] = u[first] * u[second]
            terms.append(pairs[first, second])
    for first in range(6):
        for second in range(first, 6):
            for third in range(second, 6):
                terms.append(pairs[first, second] * u[third])
    for column, term in enumerate(terms):
        total = [total[i] + transfer[i, 1 + column] * term for i in range(6)]
    for i in range(6):
        pushed[i] = total[i]
    weight0 = charge[...]
    weight1 = weight0 * total[1]
    row_of = lax.broadcasted_iota(jnp.int32, (blocks, LANES), 0)
    column = offsets[...]
    for b in range(blocks):
        column = column + jnp.where(row_of == b, block_col[0, b], 0)
    return lax.rem(rows[...], slab_rows), column, weight0, weight1


def source_kernel(
    strips,
    block_col_from,
    lags_from,
    fracs_from,
    weights_from,
    coords_from,
    charge_from,
    rows_from,
    offsets_from,
    transfer_from,
    history,
    x_kernel,
    pushed_to,
    packed_to,
    block_col,
    lags,
    fracs,
    weights,
    coords,
    charge,
    rows,
    offsets,
    transfer,
    frames,
    x_here,
    x_parts,
    s_parts,
    spread_all,
    bands,
    first_bands,
    pushed,
    packed,
    sems,
):
    count_steps, comps, slab_rows, width = history.shape
    blocks = charge.shape[0]
    strip = width // strips
    spread_rows = packed.shape[1] - FIELDS * blocks * LANES // packed.shape[2]
    pairs = [
        (lags_from, lags),
        (fracs_from, fracs),
        (weights_from, weights),
        (block_col_from, block_col),
        (coords_from, coords),
        (charge_from, charge),
        (rows_from, rows),
        (offsets_from, offsets),
        (transfer_from, transfer),
        (x_kernel, x_here),
    ]
    pairs += [(history.at[:, comp], frames.at[:, comp]) for comp in range(comps)]
    fetch = [
        pltpu.make_async_copy(source, target, sems.at[index])
        for index, (source, target) in enumerate(pairs)
    ]
    for copy in fetch:
        copy.start()
    stored = []

    def store(source, target):
        copy = pltpu.make_async_copy(source, target, sems.at[len(fetch) + len(stored)])
        copy.start()
        stored.append(copy)

    for copy in fetch[:3]:
        copy.wait()
    for t in range(count_steps):
        far = weights[0, t] * fracs[0, t]
        near = weights[0, t] * (1.0 - fracs[0, t])
        bands[2 * LANES * t : 2 * LANES * (t + 1)] = lag_band(lags[0, t], near, far)
        first_bands[LANES * t : LANES * (t + 1)] = bands[
            2 * LANES * t + LANES : 2 * LANES * (t + 1)
        ]

    for copy in fetch[3:9]:
        copy.wait()
    row, column, weight0, weight1 = push(
        coords, charge, rows, offsets, block_col, transfer, pushed, slab_rows
    )
    store(pushed, pushed_to)
    same = [row.astype(jnp.bfloat16), None, weight0.astype(jnp.bfloat16), weight1.astype(jnp.bfloat16)]
    for partner in range(strips):
        here = column - partner * strip
        here = jnp.where((here >= 0) & (here < strip), here, -1)
        for index in range(FIELDS):
            value = here.astype(jnp.float32).astype(jnp.bfloat16) if index == 1 else same[index]
            place = record_place(spread_rows, blocks, packed.shape[2], index)
            packed[(partner,) + place] = value
    store(packed.at[:, spread_rows:], packed_to.at[:, spread_rows:])
    fetch[9].wait()
    high, low = split(x_here[...])
    x_parts[:width] = high
    x_parts[width : 2 * width] = high
    x_parts[2 * width :] = low

    def put(comp, q, both):
        high, low = split(both[:, :LANES] + both[:, LANES:])
        here = slice(comp * slab_rows, (comp + 1) * slab_rows)
        s_parts[here, LANES * q : LANES * (q + 1)] = high
        s_parts[here, width + LANES * q : width + LANES * (q + 1)] = low
        s_parts[here, 2 * width + LANES * q : 2 * width + LANES * (q + 1)] = high

    for comp in range(comps):
        fetch[10 + comp].wait()
        steps = [
            jnp.concatenate(
                [
                    frames[t, comp, :, LANES * (q - 1) : LANES * (q + 1)]
                    for q in range(1, width // LANES)
                ],
                axis=0,
            )
            for t in range(count_steps)
        ]
        rest = jnp.dot(
            jnp.concatenate(steps, axis=1), bands[...], preferred_element_type=jnp.float32
        )
        for q in range(1, width // LANES):
            put(comp, q, rest[(q - 1) * slab_rows : q * slab_rows])
        steps = [frames[t, comp, :, :LANES] for t in range(count_steps)]
        put(
            comp,
            0,
            jnp.dot(
                jnp.concatenate(steps, axis=1),
                first_bands[...],
                preferred_element_type=jnp.float32,
            ),
        )
    spread = jnp.dot(s_parts[...], x_parts[...], preferred_element_type=jnp.float32)
    for comp in range(comps):
        own = spread[comp * slab_rows : (comp + 1) * slab_rows]
        if strip % 16 == 0:
            turned = own.astype(packed.dtype).T
            part = slice(comp * strip, (comp + 1) * strip)
            for partner in range(strips):
                packed[partner, part, :slab_rows] = turned[
                    partner * strip : (partner + 1) * strip
                ]
            store(packed.at[:, part], packed_to.at[:, part])
        else:
            spread_all[comp] = own.T
    if strip % 16:
        for partner in range(strips):
            part = slice(partner * strip, (partner + 1) * strip)
            both = jnp.concatenate([spread_all[comp, part] for comp in range(comps)], axis=0)
            packed[partner, :spread_rows, :slab_rows] = both.astype(packed.dtype)
        store(packed.at[:, :spread_rows], packed_to.at[:, :spread_rows])
    for copy in stored:
        copy.wait()


def join_kernel(slabs, spread_rows, z_kernel, arrived, kept, *sent):
    slab_rows = z_kernel.shape[0] // slabs
    total = arrived[0, :spread_rows, :slab_rows].astype(jnp.float32)
    for sender in range(1, arrived.shape[0]):
        total = total + arrived[sender, :spread_rows, :slab_rows].astype(jnp.float32)
    high, low = split(total)
    left = jnp.concatenate([high, low, high], axis=1)

    def part(slab):
        start = pl.multiple_of(slab * slab_rows, slab_rows)
        z_high, z_low = split(z_kernel[pl.ds(start, slab_rows), :])
        right = jnp.concatenate([z_high, z_high, z_low], axis=1)
        return lax.dot_general(left, right, NT_DIMS, preferred_element_type=jnp.float32)

    if sent:
        me = lax.axis_index("dom")
        sent[0][...] = part(1 - me)
        kept[...] = part(me)
    else:
        for slab in range(slabs):
            kept[slab] = part(slab)


def unpack_kernel(spread_rows, blocks, arrived, records, chosen):
    senders = arrived.shape[0]
    own = lax.broadcasted_iota(jnp.int32, (blocks, 1), 0)
    bit = jnp.left_shift(jnp.ones_like(own), own).astype(jnp.float32)
    masks = []
    for sender in range(senders):
        for index in range(FIELDS):
            place = record_place(spread_rows, blocks, arrived.shape[2], index)
            value = arrived[(sender,) + place].astype(jnp.float32)
            records[sender, index * blocks : (index + 1) * blocks] = value
            if index == 1:
                meets = jnp.max(value, axis=1, keepdims=True) >= 0.0
                masks.append(jnp.sum(jnp.where(meets, bit, 0.0)).astype(jnp.int32))
    records[senders] = jnp.full(records.shape[1:], -1.0, jnp.float32)
    count = jnp.int32(0)
    for sender in range(senders):
        for block in range(blocks):
            chosen[1 + count] = sender * blocks + block
            count = count + ((masks[sender] >> block) & 1)
    chosen[0] = (count + (GROUP - 1)) // GROUP
    for member in range(GROUP):
        chosen[1 + count + member] = senders * blocks


def read_group(blocks, chosen, records, group):
    where = []
    for member in range(GROUP):
        block = chosen[1 + group * GROUP + member]
        where.append((block // blocks, lax.rem(block, blocks)))

    def field(index):
        return jnp.concatenate(
            [records[sender, pl.ds(index * blocks + own, 1), :] for sender, own in where], axis=1
        )

    return where, field


def one_hot(index, size):
    iota = lax.broadcasted_iota(jnp.int32, (size, index.shape[1]), 0).astype(jnp.float32)
    return iota == index


def one_hot_rows(row, size):
    iota = lax.broadcasted_iota(jnp.int32, (size, row.shape[1]), 0)
    if size <= 256:
        hit = iota.astype(jnp.bfloat16) == row.astype(jnp.bfloat16)
        return jnp.where(hit, jnp.bfloat16(1.0), jnp.bfloat16(0.0))
    return jnp.where(iota.astype(jnp.float32) == row, 1.0, 0.0).astype(jnp.bfloat16)


def deposit_kernel(blocks, chosen, records, after, deposit, total):
    del after
    strip, slab_rows = deposit.shape[1:]
    total[...] = jnp.zeros_like(total)

    def one_group(group, carry):
        _, field = read_group(blocks, chosen, records, group)
        hit = one_hot(field(1), strip)
        weighted = [jnp.where(hit, field(2 + comp), 0.0) for comp in range(2)]
        total[...] += lax.dot_general(
            one_hot_rows(field(0), slab_rows),
            jnp.concatenate(weighted, axis=0).astype(jnp.bfloat16),
            NT_DIMS,
            preferred_element_type=jnp.float32,
        )
        return carry

    lax.fori_loop(0, chosen[0], one_group, 0)
    turned = total[...].T
    deposit[0] = turned[:strip]
    deposit[1] = turned[strip:]


def sample_kernel(blocks, chosen, records, *refs):
    parts, (field_out, samples, found_all) = refs[:-3], refs[-3:]
    strip, slab_rows = field_out.shape[1:]
    if len(parts) == 1:
        total = parts[0][0]
        for slab in range(1, parts[0].shape[0]):
            total = total + parts[0][slab]
    else:
        total = parts[0][...] + parts[1][...]
    field_out[0] = total[:strip]
    field_out[1] = total[strip:]
    rounded = total.astype(jnp.bfloat16)
    found_all[...] = jnp.zeros_like(found_all)

    def one_group(group, carry):
        where, field = read_group(blocks, chosen, records, group)
        row_hot = one_hot_rows(field(0), slab_rows)
        found = jnp.dot(rounded, row_hot, preferred_element_type=jnp.float32)
        hit = one_hot(field(1), strip)
        for comp in range(2):
            picked = jnp.where(hit, found[comp * strip : (comp + 1) * strip], 0.0)
            values = jnp.sum(picked, axis=0, keepdims=True)
            for member, (sender, own) in enumerate(where):
                found_all[sender, pl.ds(comp * blocks + own, 1), :] = values[
                    :, LANES * member : LANES * (member + 1)
                ]
        return carry

    lax.fori_loop(0, chosen[0], one_group, 0)
    samples[...] = found_all[: samples.shape[0]].astype(samples.dtype)


def kick_kernel(pushed, received, kicked):
    blocks = pushed.shape[1]
    total = received[0].astype(jnp.float32)
    for sender in range(1, received.shape[0]):
        total = total + received[sender].astype(jnp.float32)
    values = [pushed[i] for i in range(6)]
    values[5] = values[5] + 0.5 * total[:blocks]
    values[1] = values[1] + 0.5 * total[blocks:]
    for b in range(blocks):
        kicked[:, LANES * b : LANES * (b + 1)] = jnp.concatenate(
            [value[b : b + 1] for value in values], axis=0
        )


def local(
    coords,
    charge,
    row_index,
    block_col,
    col_offset,
    transfer_map,
    history,
    retard_index,
    retard_frac,
    retard_weight,
    z_kernel,
    x_kernel,
):
    strips = lax.axis_size("hist")
    slabs = lax.axis_size("dom")
    count_steps, comps, slab_rows, width = history.shape
    strip = width // strips
    particles = coords.shape[1]
    blocks = block_col.shape[0]
    tile = (blocks, LANES)
    spread_rows = comps * strip
    row_lanes = max(slab_rows, LANES)
    packed_rows = spread_rows + FIELDS * blocks * LANES // row_lanes

    f32, bf16 = jnp.float32, jnp.bfloat16
    pushed, packed = call(
        functools.partial(source_kernel, strips),
        (
            jax.ShapeDtypeStruct((6,) + tile, f32),
            jax.ShapeDtypeStruct((strips, packed_rows, row_lanes), bf16),
        ),
        [HBM] * 11,
        (HBM, HBM),
        [
            pltpu.SMEM((1, blocks), jnp.int32),
            pltpu.SMEM((1, count_steps), jnp.int32),
            pltpu.SMEM((1, count_steps), f32),
            pltpu.SMEM((1, count_steps), f32),
            pltpu.VMEM(coords.shape, f32),
            pltpu.VMEM(tile, f32),
            pltpu.VMEM(tile, jnp.int32),
            pltpu.VMEM(tile, jnp.int32),
            pltpu.SMEM(transfer_map.shape, f32),
            pltpu.VMEM(history.shape, bf16),
            pltpu.VMEM((width, width), f32),
            pltpu.VMEM((3 * width, width), bf16),
            pltpu.VMEM((comps * slab_rows, 3 * width), bf16),
            pltpu.VMEM((comps, width, slab_rows), f32),
            pltpu.VMEM((2 * LANES * count_steps, 2 * LANES), bf16),
            pltpu.VMEM((LANES * count_steps, 2 * LANES), bf16),
            pltpu.VMEM((6,) + tile, f32),
            pltpu.VMEM((strips, packed_rows, row_lanes), bf16),
            pltpu.SemaphoreType.DMA((16,)),
        ],
        flops=6 * comps * slab_rows * width * width,
        moved=history.size * 2 + x_kernel.size * 4,
        limit=LIMIT,
    )(
        block_col.reshape(1, blocks),
        retard_index.reshape(1, count_steps),
        retard_frac.reshape(1, count_steps),
        retard_weight.reshape(1, count_steps),
        coords,
        charge.reshape(tile),
        row_index.reshape(tile),
        col_offset.reshape(tile),
        transfer_map,
        history,
        x_kernel,
    )
    arrived = lax.all_to_all(packed, "hist", 0, 0, tiled=True)

    part = jax.ShapeDtypeStruct((spread_rows, slab_rows), f32)
    parts = call(
        functools.partial(join_kernel, slabs, spread_rows),
        (part, part) if slabs == 2 else jax.ShapeDtypeStruct((slabs,) + part.shape, f32),
        [VMEM, VMEM],
        (VMEM, VMEM) if slabs == 2 else VMEM,
        flops=1 << 27,
        moved=1 << 20,
    )(z_kernel, arrived)
    if slabs == 2:
        kept, sent = parts
        parts = [kept, lax.ppermute(sent, "dom", [(0, 1), (1, 0)])]
    else:
        parts = [lax.all_to_all(parts, "dom", 0, 0, tiled=True)]

    records, chosen = call(
        functools.partial(unpack_kernel, spread_rows, blocks),
        (
            jax.ShapeDtypeStruct((strips + 1, FIELDS * blocks, LANES), f32),
            jax.ShapeDtypeStruct((strips * blocks + 16,), jnp.int32),
        ),
        [VMEM],
        (VMEM, SMEM),
        flops=1 << 20,
        moved=1 << 20,
    )(arrived)

    field, samples = call(
        functools.partial(sample_kernel, blocks),
        (
            jax.ShapeDtypeStruct((comps, strip, slab_rows), f32),
            jax.ShapeDtypeStruct((strips, comps * blocks, LANES), bf16),
        ),
        [SMEM, VMEM] + [VMEM] * len(parts),
        (VMEM, VMEM),
        [pltpu.VMEM((strips + 1, comps * blocks, LANES), f32)],
        flops=1 << 29,
        moved=1 << 20,
    )(chosen, records, *parts)
    samples_here = lax.all_to_all(samples, "hist", 0, 0, tiled=True)

    deposit = call(
        functools.partial(deposit_kernel, blocks),
        jax.ShapeDtypeStruct((comps, strip, slab_rows), f32),
        [SMEM, VMEM, HBM],
        VMEM,
        [pltpu.VMEM((slab_rows, comps * strip), f32)],
        flops=1 << 29,
        moved=1 << 20,
    )(chosen, records, samples)

    kicked = call(
        kick_kernel,
        jax.ShapeDtypeStruct((6, particles), f32),
        [VMEM, VMEM],
        VMEM,
        flops=1 << 16,
        moved=1 << 18,
    )(pushed, samples_here)
    return kicked, jnp.transpose(field, (0, 2, 1)), jnp.transpose(deposit, (0, 2, 1))


def solution(mesh):
    return jax.shard_map(
        local,
        mesh=mesh,
        in_specs=(
            P(None, ("dom", "hist")),
            P(("dom", "hist")),
            P(("dom", "hist")),
            P(("dom", "hist")),
            P(("dom", "hist")),
            P(),
            P("hist", None, "dom", None),
            P("hist"),
            P("hist"),
            P("hist"),
            P(None, "dom"),
            P(),
        ),
        out_specs=(P(None, ("dom", "hist")), P(None, "dom", "hist"), P(None, "dom", "hist")),
        check_vma=False,
    )
```

```python
import functools

import jax
import jax.numpy as jnp
from jax import lax
from jax.experimental import pallas as pl
from jax.experimental.pallas import tpu as pltpu
from jax.sharding import PartitionSpec as P

LANES = 128
GROUP = 8
FIELDS = 4
NT_DIMS = (((1,), (1,)), ((), ()))
VMEM = pl.BlockSpec(memory_space=pltpu.VMEM)
SMEM = pl.BlockSpec(memory_space=pltpu.SMEM)
HBM = pl.BlockSpec(memory_space=pltpu.HBM)
LIMIT = 59 * 1024 * 1024
SMALL = 16 * 1024 * 1024


def call(kernel, out_shape, in_specs, out_specs, scratch=(), flops=0, moved=0, limit=SMALL):
    return pl.pallas_call(
        kernel,
        out_shape=out_shape,
        in_specs=in_specs,
        out_specs=out_specs,
        scratch_shapes=scratch,
        compiler_params=pltpu.CompilerParams(vmem_limit_bytes=limit),
        cost_estimate=pl.CostEstimate(flops=flops, bytes_accessed=moved, transcendentals=0),
    )


def split(value):
    high = value.astype(jnp.bfloat16)
    return high, (value - high.astype(jnp.float32)).astype(jnp.bfloat16)


def record_place(spread_rows, blocks, row_lanes, index):
    across = row_lanes // LANES
    top = spread_rows + index // across * blocks
    left = index % across * LANES
    return slice(top, top + blocks), slice(left, left + LANES)


def lag_band(lag, near, far):
    row = lax.broadcasted_iota(jnp.int32, (2 * LANES, LANES), 0)
    column = lax.broadcasted_iota(jnp.int32, (2 * LANES, LANES), 1)
    behind = column + LANES - row
    weight = jnp.where(behind == lag, near, jnp.where(behind == lag + 1, far, 0.0))
    return jnp.concatenate(split(weight), axis=1)


def push(coords, charge, rows, offsets, block_col, transfer, pushed, slab_rows):
    blocks = charge.shape[0]
    u = [
        jnp.concatenate(
            [coords[i : i + 1, LANES * b : LANES * (b + 1)] for b in range(blocks)], axis=0
        )
        for i in range(6)
    ]
    total = [jnp.full((blocks, LANES), transfer[i, 0], jnp.float32) for i in range(6)]
    pairs = {}
    terms = list(u)
    for first in range(6):
        for second in range(first, 6):
            pairs[first, second] = u[first] * u[second]
            terms.append(pairs[first, second])
    for first in range(6):
        for second in range(first, 6):
            for third in range(second, 6):
                terms.append(pairs[first, second] * u[third])
    for column, term in enumerate(terms):
        total = [total[i] + transfer[i, 1 + column] * term for i in range(6)]
    for i in range(6):
        pushed[i] = total[i]
    weight0 = charge[...]
    weight1 = weight0 * total[1]
    row_of = lax.broadcasted_iota(jnp.int32, (blocks, LANES), 0)
    column = offsets[...]
    for b in range(blocks):
        column = column + jnp.where(row_of == b, block_col[0, b], 0)
    return lax.rem(rows[...], slab_rows), column, weight0, weight1


def source_kernel(
    strips,
    block_col_from,
    lags_from,
    fracs_from,
    weights_from,
    coords_from,
    charge_from,
    rows_from,
    offsets_from,
    transfer_from,
    history,
    x_kernel,
    pushed_to,
    packed_to,
    block_col,
    lags,
    fracs,
    weights,
    coords,
    charge,
    rows,
    offsets,
    transfer,
    frames,
    x_here,
    x_parts,
    s_parts,
    spread_all,
    bands,
    first_bands,
    pushed,
    packed,
    sems,
):
    count_steps, comps, slab_rows, width = history.shape
    blocks = charge.shape[0]
    strip = width // strips
    spread_rows = packed.shape[1] - FIELDS * blocks * LANES // packed.shape[2]
    pairs = [
        (lags_from, lags),
        (fracs_from, fracs),
        (weights_from, weights),
        (block_col_from, block_col),
        (coords_from, coords),
        (charge_from, charge),
        (rows_from, rows),
        (offsets_from, offsets),
        (transfer_from, transfer),
    ]
    for comp in range(comps):
        pairs += [(history.at[t, comp], frames.at[t, comp]) for t in range(count_steps)]
        if comp == 0:
            pairs += [(x_kernel, x_here)]
    fetch = [
        pltpu.make_async_copy(source, target, sems.at[index])
        for index, (source, target) in enumerate(pairs)
    ]
    for copy in fetch:
        copy.start()
    stored = []

    def store(source, target):
        copy = pltpu.make_async_copy(source, target, sems.at[len(fetch) + len(stored)])
        copy.start()
        stored.append(copy)

    for copy in fetch[:3]:
        copy.wait()
    for t in range(count_steps):
        far = weights[0, t] * fracs[0, t]
        near = weights[0, t] * (1.0 - fracs[0, t])
        bands[2 * LANES * t : 2 * LANES * (t + 1)] = lag_band(lags[0, t], near, far)
        first_bands[LANES * t : LANES * (t + 1)] = bands[
            2 * LANES * t + LANES : 2 * LANES * (t + 1)
        ]

    for copy in fetch[3:9]:
        copy.wait()
    row, column, weight0, weight1 = push(
        coords, charge, rows, offsets, block_col, transfer, pushed, slab_rows
    )
    store(pushed, pushed_to)
    same = [row.astype(jnp.bfloat16), None, weight0.astype(jnp.bfloat16), weight1.astype(jnp.bfloat16)]
    for partner in range(strips):
        here = column - partner * strip
        here = jnp.where((here >= 0) & (here < strip), here, -1)
        for index in range(FIELDS):
            value = here.astype(jnp.float32).astype(jnp.bfloat16) if index == 1 else same[index]
            place = record_place(spread_rows, blocks, packed.shape[2], index)
            packed[(partner,) + place] = value
    store(packed.at[:, spread_rows:], packed_to.at[:, spread_rows:])
    for comp in range(comps):
        first = 9 + comp * (count_steps + 1)
        for copy in fetch[first : first + count_steps]:
            copy.wait()
        here = slice(comp * slab_rows, (comp + 1) * slab_rows)
        for q in range(width // LANES):
            before = slice(LANES * max(q - 1, 0), LANES * (q + 1))
            steps = [frames[t, comp, :, before] for t in range(count_steps)]
            both = jnp.dot(
                jnp.concatenate(steps, axis=1),
                bands[...] if q else first_bands[...],
                preferred_element_type=jnp.float32,
            )
            high, low = split(both[:, :LANES] + both[:, LANES:])
            s_parts[here, LANES * q : LANES * (q + 1)] = high
            s_parts[here, width + LANES * q : width + LANES * (q + 1)] = low
            s_parts[here, 2 * width + LANES * q : 2 * width + LANES * (q + 1)] = high
        if comp == 0:
            fetch[9 + count_steps].wait()
            high, low = split(x_here[...])
            x_parts[:width] = high
            x_parts[width : 2 * width] = high
            x_parts[2 * width :] = low
        spread = jnp.dot(s_parts[here], x_parts[...], preferred_element_type=jnp.float32)
        if strip % 16 == 0:
            turned = spread.astype(packed.dtype).T
            part = slice(comp * strip, (comp + 1) * strip)
            for partner in range(strips):
                packed[partner, part, :slab_rows] = turned[
                    partner * strip : (partner + 1) * strip
                ]
            store(packed.at[:, part], packed_to.at[:, part])
        else:
            spread_all[comp] = spread.T
    if strip % 16:
        for partner in range(strips):
            part = slice(partner * strip, (partner + 1) * strip)
            both = jnp.concatenate([spread_all[comp, part] for comp in range(comps)], axis=0)
            packed[partner, :spread_rows, :slab_rows] = both.astype(packed.dtype)
        store(packed.at[:, :spread_rows], packed_to.at[:, :spread_rows])
    for copy in stored:
        copy.wait()


def join_kernel(slabs, spread_rows, z_kernel, arrived, kept, *sent):
    slab_rows = z_kernel.shape[0] // slabs
    total = arrived[0, :spread_rows, :slab_rows].astype(jnp.float32)
    for sender in range(1, arrived.shape[0]):
        total = total + arrived[sender, :spread_rows, :slab_rows].astype(jnp.float32)
    high, low = split(total)
    left = jnp.concatenate([high, low, high], axis=1)

    def part(slab):
        start = pl.multiple_of(slab * slab_rows, slab_rows)
        z_high, z_low = split(z_kernel[pl.ds(start, slab_rows), :])
        right = jnp.concatenate([z_high, z_high, z_low], axis=1)
        return lax.dot_general(left, right, NT_DIMS, preferred_element_type=jnp.float32)

    if sent:
        me = lax.axis_index("dom")
        sent[0][...] = part(1 - me)
        kept[...] = part(me)
    else:
        for slab in range(slabs):
            kept[slab] = part(slab)


def unpack_kernel(spread_rows, blocks, arrived, records, chosen):
    senders = arrived.shape[0]
    own = lax.broadcasted_iota(jnp.int32, (blocks, 1), 0)
    bit = jnp.left_shift(jnp.ones_like(own), own).astype(jnp.float32)
    masks = []
    for sender in range(senders):
        for index in range(FIELDS):
            place = record_place(spread_rows, blocks, arrived.shape[2], index)
            value = arrived[(sender,) + place].astype(jnp.float32)
            records[sender, index * blocks : (index + 1) * blocks] = value
            if index == 1:
                meets = jnp.max(value, axis=1, keepdims=True) >= 0.0
                masks.append(jnp.sum(jnp.where(meets, bit, 0.0)).astype(jnp.int32))
    records[senders] = jnp.full(records.shape[1:], -1.0, jnp.float32)
    count = jnp.int32(0)
    for sender in range(senders):
        for block in range(blocks):
            chosen[1 + count] = sender * blocks + block
            count = count + ((masks[sender] >> block) & 1)
    chosen[0] = (count + (GROUP - 1)) // GROUP
    for member in range(GROUP):
        chosen[1 + count + member] = senders * blocks


def read_group(blocks, chosen, records, group):
    where = []
    for member in range(GROUP):
        block = chosen[1 + group * GROUP + member]
        where.append((block // blocks, lax.rem(block, blocks)))

    def field(index):
        return jnp.concatenate(
            [records[sender, pl.ds(index * blocks + own, 1), :] for sender, own in where], axis=1
        )

    return where, field


def one_hot(index, size):
    iota = lax.broadcasted_iota(jnp.int32, (size, index.shape[1]), 0).astype(jnp.float32)
    return iota == index


def one_hot_rows(row, size):
    iota = lax.broadcasted_iota(jnp.int32, (size, row.shape[1]), 0)
    if size <= 256:
        hit = iota.astype(jnp.bfloat16) == row.astype(jnp.bfloat16)
        return jnp.where(hit, jnp.bfloat16(1.0), jnp.bfloat16(0.0))
    return jnp.where(iota.astype(jnp.float32) == row, 1.0, 0.0).astype(jnp.bfloat16)


def deposit_kernel(blocks, chosen, records, after, deposit, total):
    del after
    strip, slab_rows = deposit.shape[1:]
    total[...] = jnp.zeros_like(total)

    def one_group(group, carry):
        _, field = read_group(blocks, chosen, records, group)
        hit = one_hot(field(1), strip)
        weighted = [jnp.where(hit, field(2 + comp), 0.0) for comp in range(2)]
        total[...] += lax.dot_general(
            one_hot_rows(field(0), slab_rows),
            jnp.concatenate(weighted, axis=0).astype(jnp.bfloat16),
            NT_DIMS,
            preferred_element_type=jnp.float32,
        )
        return carry

    lax.fori_loop(0, chosen[0], one_group, 0)
    turned = total[...].T
    deposit[0] = turned[:strip]
    deposit[1] = turned[strip:]


def sample_kernel(blocks, chosen, records, *refs):
    parts, (field_out, samples, found_all) = refs[:-3], refs[-3:]
    strip, slab_rows = field_out.shape[1:]
    if len(parts) == 1:
        total = parts[0][0]
        for slab in range(1, parts[0].shape[0]):
            total = total + parts[0][slab]
    else:
        total = parts[0][...] + parts[1][...]
    field_out[0] = total[:strip]
    field_out[1] = total[strip:]
    rounded = total.astype(jnp.bfloat16)
    found_all[...] = jnp.zeros_like(found_all)

    def one_group(group, carry):
        where, field = read_group(blocks, chosen, records, group)
        row_hot = one_hot_rows(field(0), slab_rows)
        found = jnp.dot(rounded, row_hot, preferred_element_type=jnp.float32)
        hit = one_hot(field(1), strip)
        for comp in range(2):
            picked = jnp.where(hit, found[comp * strip : (comp + 1) * strip], 0.0)
            values = jnp.sum(picked, axis=0, keepdims=True)
            for member, (sender, own) in enumerate(where):
                found_all[sender, pl.ds(comp * blocks + own, 1), :] = values[
                    :, LANES * member : LANES * (member + 1)
                ]
        return carry

    lax.fori_loop(0, chosen[0], one_group, 0)
    samples[...] = found_all[: samples.shape[0]].astype(samples.dtype)


def kick_kernel(pushed, received, kicked):
    blocks = pushed.shape[1]
    total = received[0].astype(jnp.float32)
    for sender in range(1, received.shape[0]):
        total = total + received[sender].astype(jnp.float32)
    values = [pushed[i] for i in range(6)]
    values[5] = values[5] + 0.5 * total[:blocks]
    values[1] = values[1] + 0.5 * total[blocks:]
    for b in range(blocks):
        kicked[:, LANES * b : LANES * (b + 1)] = jnp.concatenate(
            [value[b : b + 1] for value in values], axis=0
        )


def local(
    coords,
    charge,
    row_index,
    block_col,
    col_offset,
    transfer_map,
    history,
    retard_index,
    retard_frac,
    retard_weight,
    z_kernel,
    x_kernel,
):
    strips = lax.axis_size("hist")
    slabs = lax.axis_size("dom")
    count_steps, comps, slab_rows, width = history.shape
    strip = width // strips
    particles = coords.shape[1]
    blocks = block_col.shape[0]
    tile = (blocks, LANES)
    spread_rows = comps * strip
    row_lanes = max(slab_rows, LANES)
    packed_rows = spread_rows + FIELDS * blocks * LANES // row_lanes

    f32, bf16 = jnp.float32, jnp.bfloat16
    pushed, packed = call(
        functools.partial(source_kernel, strips),
        (
            jax.ShapeDtypeStruct((6,) + tile, f32),
            jax.ShapeDtypeStruct((strips, packed_rows, row_lanes), bf16),
        ),
        [HBM] * 11,
        (HBM, HBM),
        [
            pltpu.SMEM((1, blocks), jnp.int32),
            pltpu.SMEM((1, count_steps), jnp.int32),
            pltpu.SMEM((1, count_steps), f32),
            pltpu.SMEM((1, count_steps), f32),
            pltpu.VMEM(coords.shape, f32),
            pltpu.VMEM(tile, f32),
            pltpu.VMEM(tile, jnp.int32),
            pltpu.VMEM(tile, jnp.int32),
            pltpu.SMEM(transfer_map.shape, f32),
            pltpu.VMEM(history.shape, bf16),
            pltpu.VMEM((width, width), f32),
            pltpu.VMEM((3 * width, width), bf16),
            pltpu.VMEM((comps * slab_rows, 3 * width), bf16),
            pltpu.VMEM((comps, width, slab_rows), f32),
            pltpu.VMEM((2 * LANES * count_steps, 2 * LANES), bf16),
            pltpu.VMEM((LANES * count_steps, 2 * LANES), bf16),
            pltpu.VMEM((6,) + tile, f32),
            pltpu.VMEM((strips, packed_rows, row_lanes), bf16),
            pltpu.SemaphoreType.DMA((14 + comps * count_steps,)),
        ],
        flops=6 * comps * slab_rows * width * width,
        moved=history.size * 2 + x_kernel.size * 4,
        limit=LIMIT,
    )(
        block_col.reshape(1, blocks),
        retard_index.reshape(1, count_steps),
        retard_frac.reshape(1, count_steps),
        retard_weight.reshape(1, count_steps),
        coords,
        charge.reshape(tile),
        row_index.reshape(tile),
        col_offset.reshape(tile),
        transfer_map,
        history,
        x_kernel,
    )
    arrived = lax.all_to_all(packed, "hist", 0, 0, tiled=True)

    part = jax.ShapeDtypeStruct((spread_rows, slab_rows), f32)
    parts = call(
        functools.partial(join_kernel, slabs, spread_rows),
        (part, part) if slabs == 2 else jax.ShapeDtypeStruct((slabs,) + part.shape, f32),
        [VMEM, VMEM],
        (VMEM, VMEM) if slabs == 2 else VMEM,
        flops=1 << 27,
        moved=1 << 20,
    )(z_kernel, arrived)
    if slabs == 2:
        kept, sent = parts
        parts = [kept, lax.ppermute(sent, "dom", [(0, 1), (1, 0)])]
    else:
        parts = [lax.all_to_all(parts, "dom", 0, 0, tiled=True)]

    records, chosen = call(
        functools.partial(unpack_kernel, spread_rows, blocks),
        (
            jax.ShapeDtypeStruct((strips + 1, FIELDS * blocks, LANES), f32),
            jax.ShapeDtypeStruct((strips * blocks + 16,), jnp.int32),
        ),
        [VMEM],
        (VMEM, SMEM),
        flops=1 << 20,
        moved=1 << 20,
    )(arrived)

    field, samples = call(
        functools.partial(sample_kernel, blocks),
        (
            jax.ShapeDtypeStruct((comps, strip, slab_rows), f32),
            jax.ShapeDtypeStruct((strips, comps * blocks, LANES), bf16),
        ),
        [SMEM, VMEM] + [VMEM] * len(parts),
        (VMEM, VMEM),
        [pltpu.VMEM((strips + 1, comps * blocks, LANES), f32)],
        flops=1 << 29,
        moved=1 << 20,
    )(chosen, records, *parts)
    samples_here = lax.all_to_all(samples, "hist", 0, 0, tiled=True)

    deposit = call(
        functools.partial(deposit_kernel, blocks),
        jax.ShapeDtypeStruct((comps, strip, slab_rows), f32),
        [SMEM, VMEM, HBM],
        VMEM,
        [pltpu.VMEM((slab_rows, comps * strip), f32)],
        flops=1 << 29,
        moved=1 << 20,
    )(chosen, records, samples)

    kicked = call(
        kick_kernel,
        jax.ShapeDtypeStruct((6, particles), f32),
        [VMEM, VMEM],
        VMEM,
        flops=1 << 16,
        moved=1 << 18,
    )(pushed, samples_here)
    return kicked, jnp.transpose(field, (0, 2, 1)), jnp.transpose(deposit, (0, 2, 1))


def solution(mesh):
    return jax.shard_map(
        local,
        mesh=mesh,
        in_specs=(
            P(None, ("dom", "hist")),
            P(("dom", "hist")),
            P(("dom", "hist")),
            P(("dom", "hist")),
            P(("dom", "hist")),
            P(),
            P("hist", None, "dom", None),
            P("hist"),
            P("hist"),
            P("hist"),
            P(None, "dom"),
            P(),
        ),
        out_specs=(P(None, ("dom", "hist")), P(None, "dom", "hist"), P(None, "dom", "hist")),
        check_vma=False,
    )
```

```python
import functools

import jax
import jax.numpy as jnp
from jax import lax
from jax.experimental import pallas as pl
from jax.experimental.pallas import tpu as pltpu
from jax.sharding import PartitionSpec as P

LANES = 128
GROUP = 8
SPAN = 16
SEATS = 8
FIELDS = 4
MORE = 64.0
NT_DIMS = (((1,), (1,)), ((), ()))
VMEM = pl.BlockSpec(memory_space=pltpu.VMEM)
SMEM = pl.BlockSpec(memory_space=pltpu.SMEM)
HBM = pl.BlockSpec(memory_space=pltpu.HBM)
LIMIT = 59 * 1024 * 1024
SMALL = 16 * 1024 * 1024


def call(kernel, out_shape, in_specs, out_specs, scratch=(), flops=0, moved=0, limit=SMALL):
    return pl.pallas_call(
        kernel,
        out_shape=out_shape,
        in_specs=in_specs,
        out_specs=out_specs,
        scratch_shapes=scratch,
        compiler_params=pltpu.CompilerParams(vmem_limit_bytes=limit),
        cost_estimate=pl.CostEstimate(flops=flops, bytes_accessed=moved, transcendentals=0),
    )


def split(value):
    high = value.astype(jnp.bfloat16)
    return high, (value - high.astype(jnp.float32)).astype(jnp.bfloat16)


def seats_of(strips, slabs, blocks):
    if strips == 16 and slabs == 2 and blocks == 2 * SEATS:
        return SEATS, True
    return blocks, False


def strips_met(strip):
    return (SPAN + strip - 2) // strip + 1


def lag_band(lag, near, far):
    row = lax.broadcasted_iota(jnp.int32, (2 * LANES, LANES), 0)
    column = lax.broadcasted_iota(jnp.int32, (2 * LANES, LANES), 1)
    behind = column + LANES - row
    weight = jnp.where(behind == lag, near, jnp.where(behind == lag + 1, far, 0.0))
    return jnp.concatenate(split(weight), axis=1)


def push(coords, charge, rows, offsets, block_col, transfer, pushed, slab_rows):
    blocks = charge.shape[0]
    u = [
        jnp.concatenate(
            [coords[i : i + 1, LANES * b : LANES * (b + 1)] for b in range(blocks)], axis=0
        )
        for i in range(6)
    ]
    total = [jnp.full((blocks, LANES), transfer[i, 0], jnp.float32) for i in range(6)]
    pairs = {}
    terms = list(u)
    for first in range(6):
        for second in range(first, 6):
            pairs[first, second] = u[first] * u[second]
            terms.append(pairs[first, second])
    for first in range(6):
        for second in range(first, 6):
            for third in range(second, 6):
                terms.append(pairs[first, second] * u[third])
    for column, term in enumerate(terms):
        total = [total[i] + transfer[i, 1 + column] * term for i in range(6)]
    for i in range(6):
        pushed[i] = total[i]
    weight0 = charge[...]
    weight1 = weight0 * total[1]
    row_of = lax.broadcasted_iota(jnp.int32, (blocks, LANES), 0)
    column = offsets[...]
    for b in range(blocks):
        column = column + jnp.where(row_of == b, block_col[0, b], 0)
    return lax.rem(rows[...], slab_rows), column, weight0, weight1


def seat_blocks(strips, strip, seats, rounds, block_col, fields, counts, seat, stage):
    row, column, weight0, weight1 = fields
    blocks = row.shape[0]
    nobody = rounds * strips * seats
    meets = strips_met(strip)
    stage[...] = jnp.full(stage.shape, -1.0, jnp.float32)
    for place in range(strips):
        counts[0, place] = 0
    left_out = jnp.int32(0)
    for block in range(blocks):
        start = block_col[0, block]
        first = start // strip
        for step in range(meets):
            place = jnp.minimum(first + step, strips - 1)
            met = (first + step) * strip <= start + (SPAN - 1)
            taken = counts[0, place]
            counts[0, place] = taken + jnp.where(met, 1, 0)
            later = taken // seats
            number = (later * strips + place) * seats + lax.rem(taken, seats)
            number = jnp.where(met, number, nobody)
            left_out = jnp.maximum(left_out, jnp.where(met, later, 0))
            seat[0, block * meets + step] = number
            own = column[block : block + 1] - place * strip
            own = jnp.where((own >= 0) & (own < strip), own, -1)
            pieces = [row[block : block + 1], own, weight0[block : block + 1], weight1[block : block + 1]]
            stage[pl.ds(number * FIELDS, FIELDS), :] = jnp.concatenate(
                [piece.astype(jnp.float32) for piece in pieces], axis=0
            )
    return left_out


def source_kernel(
    strips,
    block_col_from,
    lags_from,
    fracs_from,
    weights_from,
    coords_from,
    charge_from,
    rows_from,
    offsets_from,
    transfer_from,
    history,
    x_kernel,
    pushed_to,
    packed_to,
    later_to,
    seat_to,
    block_col,
    lags,
    fracs,
    weights,
    coords,
    charge,
    rows,
    offsets,
    transfer,
    frames,
    x_here,
    x_parts,
    s_parts,
    spread_all,
    bands,
    first_bands,
    pushed,
    packed,
    later,
    counts,
    seat,
    stage,
    sems,
):
    count_steps, comps, slab_rows, width = history.shape
    blocks = charge.shape[0]
    strip = width // strips
    spread_rows = comps * strip
    record_rows = packed.shape[1] - spread_rows
    across = packed.shape[2] // LANES
    seats = record_rows * across // FIELDS
    rounds = stage.shape[0] // (FIELDS * strips * seats)
    pairs = [
        (lags_from, lags),
        (fracs_from, fracs),
        (weights_from, weights),
        (block_col_from, block_col),
        (coords_from, coords),
        (charge_from, charge),
        (rows_from, rows),
        (offsets_from, offsets),
        (transfer_from, transfer),
    ]
    for comp in range(comps):
        pairs += [(history.at[t, comp], frames.at[t, comp]) for t in range(count_steps)]
        if comp == 0:
            pairs += [(x_kernel, x_here)]
    fetch = [
        pltpu.make_async_copy(source, target, sems.at[index])
        for index, (source, target) in enumerate(pairs)
    ]
    for copy in fetch:
        copy.start()
    stored = []

    def store(source, target):
        copy = pltpu.make_async_copy(source, target, sems.at[len(fetch) + len(stored)])
        copy.start()
        stored.append(copy)

    for copy in fetch[:3]:
        copy.wait()
    for t in range(count_steps):
        far = weights[0, t] * fracs[0, t]
        near = weights[0, t] * (1.0 - fracs[0, t])
        bands[2 * LANES * t : 2 * LANES * (t + 1)] = lag_band(lags[0, t], near, far)
        first_bands[LANES * t : LANES * (t + 1)] = bands[
            2 * LANES * t + LANES : 2 * LANES * (t + 1)
        ]

    for copy in fetch[3:9]:
        copy.wait()
    row, column, weight0, weight1 = push(
        coords, charge, rows, offsets, block_col, transfer, pushed, slab_rows
    )
    store(pushed, pushed_to)
    left_out = seat_blocks(
        strips,
        strip,
        seats,
        rounds,
        block_col,
        (row, column, weight0, weight1),
        counts,
        seat,
        stage,
    )
    store(seat, seat_to)
    is_column = lax.rem(lax.broadcasted_iota(jnp.int32, (record_rows, LANES), 0), FIELDS) == 1
    mark = jnp.where(is_column, MORE * left_out.astype(jnp.float32), 0.0)
    for turn in range(rounds):
        for partner in range(strips):
            for side in range(across):
                start = ((turn * strips + partner) * across + side) * record_rows
                value = stage[start : start + record_rows]
                lanes = slice(side * LANES, (side + 1) * LANES)
                if turn == 0:
                    packed[partner, spread_rows:, lanes] = (value + mark).astype(packed.dtype)
                else:
                    later[partner, :, lanes] = value.astype(later.dtype)
    if rounds == 2:
        store(later, later_to)
    store(packed.at[:, spread_rows:], packed_to.at[:, spread_rows:])
    for comp in range(comps):
        first = 9 + comp * (count_steps + 1)
        for copy in fetch[first : first + count_steps]:
            copy.wait()
        here = slice(comp * slab_rows, (comp + 1) * slab_rows)
        for q in range(width // LANES):
            before = slice(LANES * max(q - 1, 0), LANES * (q + 1))
            steps = [frames[t, comp, :, before] for t in range(count_steps)]
            both = jnp.dot(
                jnp.concatenate(steps, axis=1),
                bands[...] if q else first_bands[...],
                preferred_element_type=jnp.float32,
            )
            high, low = split(both[:, :LANES] + both[:, LANES:])
            s_parts[here, LANES * q : LANES * (q + 1)] = high
            s_parts[here, width + LANES * q : width + LANES * (q + 1)] = low
            s_parts[here, 2 * width + LANES * q : 2 * width + LANES * (q + 1)] = high
        if comp == 0:
            fetch[9 + count_steps].wait()
            high, low = split(x_here[...])
            x_parts[:width] = high
            x_parts[width : 2 * width] = high
            x_parts[2 * width :] = low
        spread = jnp.dot(s_parts[here], x_parts[...], preferred_element_type=jnp.float32)
        if strip % 16 == 0:
            turned = spread.astype(packed.dtype).T
            part = slice(comp * strip, (comp + 1) * strip)
            for partner in range(strips):
                packed[partner, part, :slab_rows] = turned[
                    partner * strip : (partner + 1) * strip
                ]
            store(packed.at[:, part], packed_to.at[:, part])
        else:
            spread_all[comp] = spread.T
    if strip % 16:
        for partner in range(strips):
            part = slice(partner * strip, (partner + 1) * strip)
            both = jnp.concatenate([spread_all[comp, part] for comp in range(comps)], axis=0)
            packed[partner, :spread_rows, :slab_rows] = both.astype(packed.dtype)
        store(packed.at[:, :spread_rows], packed_to.at[:, :spread_rows])
    for copy in stored:
        copy.wait()


def join_kernel(slabs, spread_rows, z_kernel, arrived, kept, *sent):
    slab_rows = z_kernel.shape[0] // slabs
    extra_rows = kept.shape[0] - spread_rows if sent else 0
    total = arrived[0, :spread_rows, :slab_rows].astype(jnp.float32)
    for sender in range(1, arrived.shape[0]):
        total = total + arrived[sender, :spread_rows, :slab_rows].astype(jnp.float32)
    high, low = split(total)
    left = jnp.concatenate([high, low, high], axis=1)

    def part(slab):
        start = pl.multiple_of(slab * slab_rows, slab_rows)
        z_high, z_low = split(z_kernel[pl.ds(start, slab_rows), :])
        right = jnp.concatenate([z_high, z_high, z_low], axis=1)
        return lax.dot_general(left, right, NT_DIMS, preferred_element_type=jnp.float32)

    if sent:
        me = lax.axis_index("dom")
        sent[0][:spread_rows] = part(1 - me)
        kept[:spread_rows] = part(me)
        if extra_rows:
            records = jnp.max(arrived[:, spread_rows:].astype(jnp.float32), axis=0)
            is_column = lax.rem(lax.broadcasted_iota(jnp.int32, records.shape, 0), FIELDS) == 1
            most = jnp.max(jnp.where(is_column, records, -1.0))
            flag = jnp.full((extra_rows, slab_rows), jnp.where(most >= MORE - 1.0, 1.0, 0.0))
            sent[0][spread_rows:] = flag
            kept[spread_rows:] = flag
    else:
        for slab in range(slabs):
            kept[slab] = part(slab)


def unpack_kernel(spread_rows, arrived, records, chosen):
    senders = arrived.shape[0]
    record_rows = arrived.shape[1] - spread_rows
    across = arrived.shape[2] // LANES
    blocks = record_rows * across // FIELDS
    line = lax.broadcasted_iota(jnp.int32, (record_rows, LANES), 0)
    is_column = lax.rem(line, FIELDS) == 1
    first_line = lax.broadcasted_iota(jnp.int32, (record_rows, 1), 0)
    first_column = lax.rem(first_line, FIELDS) == 1
    masks = []
    for sender in range(senders):
        mask = jnp.float32(0.0)
        for side in range(across):
            lanes = slice(side * LANES, (side + 1) * LANES)
            value = arrived[sender, spread_rows:, lanes].astype(jnp.float32)
            value = jnp.where(is_column & (value >= MORE - 1.0), value - MORE, value)
            records[sender, side * record_rows : (side + 1) * record_rows] = value
            taken = first_column & (jnp.max(value, axis=1, keepdims=True) >= 0.0)
            seat = first_line // FIELDS + side * (record_rows // FIELDS)
            bit = jnp.left_shift(jnp.ones_like(seat), seat).astype(jnp.float32)
            mask = mask + jnp.sum(jnp.where(taken, bit, 0.0))
        masks.append(mask.astype(jnp.int32))
    records[senders] = jnp.full(records.shape[1:], -1.0, jnp.float32)
    count = jnp.int32(0)
    for sender in range(senders):
        for block in range(blocks):
            chosen[1 + count] = sender * blocks + block
            count = count + ((masks[sender] >> block) & 1)
    chosen[0] = (count + (GROUP - 1)) // GROUP
    for member in range(GROUP):
        chosen[1 + count + member] = senders * blocks


def read_group(blocks, chosen, records, group):
    where = []
    for member in range(GROUP):
        block = chosen[1 + group * GROUP + member]
        where.append((block // blocks, lax.rem(block, blocks)))

    lines = jnp.concatenate(
        [records[sender, pl.ds(own * FIELDS, FIELDS), :] for sender, own in where], axis=1
    )

    def field(index):
        return lines[index : index + 1]

    return where, field


def one_hot(index, size):
    iota = lax.broadcasted_iota(jnp.int32, (size, index.shape[1]), 0).astype(jnp.float32)
    return iota == index


def one_hot_rows(row, size):
    iota = lax.broadcasted_iota(jnp.int32, (size, row.shape[1]), 0)
    if size <= 256:
        hit = iota.astype(jnp.bfloat16) == row.astype(jnp.bfloat16)
        return jnp.where(hit, jnp.bfloat16(1.0), jnp.bfloat16(0.0))
    return jnp.where(iota.astype(jnp.float32) == row, 1.0, 0.0).astype(jnp.bfloat16)


def deposit_kernel(blocks, chosen, records, after, deposit, total):
    del after
    strip, slab_rows = deposit.shape[1:]
    total[...] = jnp.zeros_like(total)

    def one_group(group, carry):
        _, field = read_group(blocks, chosen, records, group)
        hit = one_hot(field(1), strip)
        weighted = [jnp.where(hit, field(2 + comp), 0.0) for comp in range(2)]
        total[...] += lax.dot_general(
            one_hot_rows(field(0), slab_rows),
            jnp.concatenate(weighted, axis=0).astype(jnp.bfloat16),
            NT_DIMS,
            preferred_element_type=jnp.float32,
        )
        return carry

    lax.fori_loop(0, chosen[0], one_group, 0)
    turned = total[...].T
    deposit[0] = turned[:strip]
    deposit[1] = turned[strip:]


def sample_kernel(blocks, chosen, records, *refs):
    parts, (field_out, samples, flag, found_all) = refs[:-4], refs[-4:]
    strip, slab_rows = field_out.shape[1:]
    if len(parts) == 1:
        total = parts[0][0]
        for slab in range(1, parts[0].shape[0]):
            total = total + parts[0][slab]
    else:
        total = parts[0][: 2 * strip] + parts[1][: 2 * strip]
    if len(parts) == 2 and parts[0].shape[0] > 2 * strip:
        most = jnp.max(jnp.maximum(parts[0][2 * strip :], parts[1][2 * strip :]))
        flag[0] = jnp.where(most > 0.5, 1, 0)
    else:
        flag[0] = 0
    field_out[0] = total[:strip]
    field_out[1] = total[strip:]
    rounded = total.astype(jnp.bfloat16)
    found_all[...] = jnp.zeros_like(found_all)

    def one_group(group, carry):
        where, field = read_group(blocks, chosen, records, group)
        row_hot = one_hot_rows(field(0), slab_rows)
        found = jnp.dot(rounded, row_hot, preferred_element_type=jnp.float32)
        hit = one_hot(field(1), strip)
        values = []
        for comp in range(2):
            picked = jnp.where(hit, found[comp * strip : (comp + 1) * strip], 0.0)
            values.append(jnp.sum(picked, axis=0, keepdims=True))
        values = jnp.concatenate(values, axis=0)
        for member, (sender, own) in enumerate(where):
            found_all[sender, pl.ds(2 * own, 2), :] = values[
                :, LANES * member : LANES * (member + 1)
            ]
        return carry

    lax.fori_loop(0, chosen[0], one_group, 0)
    samples[...] = found_all[: samples.shape[0]].astype(samples.dtype)


def kick_kernel(seat, pushed, *refs):
    rounds = 1 if len(refs) == 3 else 2
    if rounds == 1:
        received, (kicked, back) = refs[:1], refs[1:]
    else:
        received, (first, second, kicked, deposit, back) = refs[:2], refs[2:]
        deposit[...] = first[...] + second[...]
    blocks = pushed.shape[1]
    meets = seat.shape[1] // blocks
    lines = received[0].shape[0] * received[0].shape[1]
    for turn, found in enumerate(received):
        for sender in range(found.shape[0]):
            start = turn * lines + sender * found.shape[1]
            back[start : start + found.shape[1]] = found[sender].astype(jnp.float32)
    back[rounds * lines :] = jnp.zeros((back.shape[0] - rounds * lines, LANES), jnp.float32)
    values = [pushed[i] for i in range(6)]
    for block in range(blocks):
        total = back[pl.ds(2 * seat[0, block * meets], 2), :]
        for step in range(1, meets):
            total = total + back[pl.ds(2 * seat[0, block * meets + step], 2), :]
        lines_here = [value[block : block + 1] for value in values]
        lines_here[5] = lines_here[5] + 0.5 * total[0:1]
        lines_here[1] = lines_here[1] + 0.5 * total[1:2]
        kicked[:, LANES * block : LANES * (block + 1)] = jnp.concatenate(lines_here, axis=0)


def local(
    coords,
    charge,
    row_index,
    block_col,
    col_offset,
    transfer_map,
    history,
    retard_index,
    retard_frac,
    retard_weight,
    z_kernel,
    x_kernel,
):
    strips = lax.axis_size("hist")
    slabs = lax.axis_size("dom")
    count_steps, comps, slab_rows, width = history.shape
    strip = width // strips
    particles = coords.shape[1]
    blocks = block_col.shape[0]
    tile = (blocks, LANES)
    spread_rows = comps * strip
    row_lanes = max(slab_rows, LANES)
    seats, second_round = seats_of(strips, slabs, blocks)
    rounds = 2 if second_round else 1
    record_rows = FIELDS * seats * LANES // row_lanes
    packed_rows = spread_rows + record_rows
    meets = strips_met(strip)

    f32, bf16 = jnp.float32, jnp.bfloat16
    pushed, packed, later, seat = call(
        functools.partial(source_kernel, strips),
        (
            jax.ShapeDtypeStruct((6,) + tile, f32),
            jax.ShapeDtypeStruct((strips, packed_rows, row_lanes), bf16),
            jax.ShapeDtypeStruct((strips, record_rows, row_lanes), bf16),
            jax.ShapeDtypeStruct((1, blocks * meets), jnp.int32),
        ),
        [HBM] * 11,
        (HBM, HBM, HBM, HBM),
        [
            pltpu.SMEM((1, blocks), jnp.int32),
            pltpu.SMEM((1, count_steps), jnp.int32),
            pltpu.SMEM((1, count_steps), f32),
            pltpu.SMEM((1, count_steps), f32),
            pltpu.VMEM(coords.shape, f32),
            pltpu.VMEM(tile, f32),
            pltpu.VMEM(tile, jnp.int32),
            pltpu.VMEM(tile, jnp.int32),
            pltpu.SMEM(transfer_map.shape, f32),
            pltpu.VMEM(history.shape, bf16),
            pltpu.VMEM((width, width), f32),
            pltpu.VMEM((3 * width, width), bf16),
            pltpu.VMEM((comps * slab_rows, 3 * width), bf16),
            pltpu.VMEM((comps, width, slab_rows), f32),
            pltpu.VMEM((2 * LANES * count_steps, 2 * LANES), bf16),
            pltpu.VMEM((LANES * count_steps, 2 * LANES), bf16),
            pltpu.VMEM((6,) + tile, f32),
            pltpu.VMEM((strips, packed_rows, row_lanes), bf16),
            pltpu.VMEM((strips, record_rows, row_lanes), bf16),
            pltpu.SMEM((1, strips), jnp.int32),
            pltpu.SMEM((1, blocks * meets), jnp.int32),
            pltpu.VMEM((FIELDS * (rounds * strips * seats + 2), LANES), f32),
            pltpu.SemaphoreType.DMA((16 + comps * count_steps,)),
        ],
        flops=6 * comps * slab_rows * width * width,
        moved=history.size * 2 + x_kernel.size * 4,
        limit=LIMIT,
    )(
        block_col.reshape(1, blocks),
        retard_index.reshape(1, count_steps),
        retard_frac.reshape(1, count_steps),
        retard_weight.reshape(1, count_steps),
        coords,
        charge.reshape(tile),
        row_index.reshape(tile),
        col_offset.reshape(tile),
        transfer_map,
        history,
        x_kernel,
    )
    arrived = lax.all_to_all(packed, "hist", 0, 0, tiled=True)

    part = jax.ShapeDtypeStruct((spread_rows + (8 if second_round else 0), slab_rows), f32)
    parts = call(
        functools.partial(join_kernel, slabs, spread_rows),
        (part, part) if slabs == 2 else jax.ShapeDtypeStruct((slabs,) + part.shape, f32),
        [VMEM, VMEM],
        (VMEM, VMEM) if slabs == 2 else VMEM,
        flops=1 << 27,
        moved=1 << 20,
    )(z_kernel, arrived)
    if slabs == 2:
        kept, sent = parts
        parts = [kept, lax.ppermute(sent, "dom", [(0, 1), (1, 0)])]
    else:
        parts = [lax.all_to_all(parts, "dom", 0, 0, tiled=True)]

    def unpack(arrived, spread_rows):
        return call(
            functools.partial(unpack_kernel, spread_rows),
            (
                jax.ShapeDtypeStruct((strips + 1, FIELDS * seats, LANES), f32),
                jax.ShapeDtypeStruct((strips * seats + 16,), jnp.int32),
            ),
            [VMEM],
            (VMEM, SMEM),
            flops=1 << 20,
            moved=1 << 20,
        )(arrived)

    def sample(chosen, records, parts):
        return call(
            functools.partial(sample_kernel, seats),
            (
                jax.ShapeDtypeStruct((comps, strip, slab_rows), f32),
                jax.ShapeDtypeStruct((strips, comps * seats, LANES), bf16),
                jax.ShapeDtypeStruct((8,), jnp.int32),
            ),
            [SMEM, VMEM] + [VMEM] * len(parts),
            (VMEM, VMEM, SMEM),
            [pltpu.VMEM((strips + 1, comps * seats, LANES), f32)],
            flops=1 << 29,
            moved=1 << 20,
        )(chosen, records, *parts)

    def deposits(chosen, records, after):
        return call(
            functools.partial(deposit_kernel, seats),
            jax.ShapeDtypeStruct((comps, strip, slab_rows), f32),
            [SMEM, VMEM, HBM],
            VMEM,
            [pltpu.VMEM((slab_rows, comps * strip), f32)],
            flops=1 << 29,
            moved=1 << 20,
        )(chosen, records, after)

    def exchange(value):
        return lax.all_to_all(value, "hist", 0, 0, tiled=True)

    records, chosen = unpack(arrived, spread_rows)
    field, samples, flag = sample(chosen, records, parts)
    received = [exchange(samples)]
    deposit = deposits(chosen, records, samples)
    deposit_shape = jax.ShapeDtypeStruct(deposit.shape, f32)
    kicked_shape = jax.ShapeDtypeStruct((6, particles), f32)
    back = pltpu.VMEM((comps * rounds * strips * seats + 8, LANES), f32)
    if second_round:

        def another(later, field):
            records, chosen = unpack(exchange(later), 0)
            whole = field.reshape(1, spread_rows, slab_rows)
            _, samples, _ = sample(chosen, records, [whole])
            return exchange(samples), deposits(chosen, records, samples)

        def nothing(later, field):
            return jnp.zeros(samples.shape, bf16), jnp.zeros(deposit.shape, f32)

        more, extra = lax.cond(flag[0] > 0, another, nothing, later, field)
        kicked, deposit = call(
            kick_kernel,
            (deposit_shape, kicked_shape)[::-1],
            [SMEM] + [VMEM] * 5,
            (VMEM, VMEM),
            [back],
            flops=1 << 16,
            moved=1 << 18,
        )(seat, pushed, received[0], more, deposit, extra)
    else:
        kicked = call(
            kick_kernel,
            kicked_shape,
            [SMEM] + [VMEM] * 2,
            VMEM,
            [back],
            flops=1 << 16,
            moved=1 << 18,
        )(seat, pushed, received[0])
    return kicked, jnp.transpose(field, (0, 2, 1)), jnp.transpose(deposit, (0, 2, 1))


def solution(mesh):
    return jax.shard_map(
        local,
        mesh=mesh,
        in_specs=(
            P(None, ("dom", "hist")),
            P(("dom", "hist")),
            P(("dom", "hist")),
            P(("dom", "hist")),
            P(("dom", "hist")),
            P(),
            P("hist", None, "dom", None),
            P("hist"),
            P("hist"),
            P("hist"),
            P(None, "dom"),
            P(),
        ),
        out_specs=(P(None, ("dom", "hist")), P(None, "dom", "hist"), P(None, "dom", "hist")),
        check_vma=False,
    )
```

```python
import functools

import jax
import jax.numpy as jnp
from jax import lax
from jax.experimental import pallas as pl
from jax.experimental.pallas import tpu as pltpu
from jax.sharding import PartitionSpec as P

LANES = 128
GROUP = 8
SPAN = 16
SEATS = 8
FIELDS = 4
MORE = 64.0
NT_DIMS = (((1,), (1,)), ((), ()))
VMEM = pl.BlockSpec(memory_space=pltpu.VMEM)
SMEM = pl.BlockSpec(memory_space=pltpu.SMEM)
HBM = pl.BlockSpec(memory_space=pltpu.HBM)
LIMIT = 59 * 1024 * 1024
SMALL = 16 * 1024 * 1024


def call(kernel, out_shape, in_specs, out_specs, scratch=(), flops=0, moved=0, limit=SMALL):
    return pl.pallas_call(
        kernel,
        out_shape=out_shape,
        in_specs=in_specs,
        out_specs=out_specs,
        scratch_shapes=scratch,
        compiler_params=pltpu.CompilerParams(vmem_limit_bytes=limit),
        cost_estimate=pl.CostEstimate(flops=flops, bytes_accessed=moved, transcendentals=0),
    )


def split(value):
    high = value.astype(jnp.bfloat16)
    return high, (value - high.astype(jnp.float32)).astype(jnp.bfloat16)


def seats_of(strips, slabs, blocks):
    if strips == 16 and slabs == 2 and blocks == 2 * SEATS:
        return SEATS, True
    return blocks, False


def strips_met(strip):
    return (SPAN + strip - 2) // strip + 1


def lag_band(lag, near, far):
    row = lax.broadcasted_iota(jnp.int32, (2 * LANES, LANES), 0)
    column = lax.broadcasted_iota(jnp.int32, (2 * LANES, LANES), 1)
    behind = column + LANES - row
    weight = jnp.where(behind == lag, near, jnp.where(behind == lag + 1, far, 0.0))
    return jnp.concatenate(split(weight), axis=1)


def push(coords, charge, rows, offsets, block_col, transfer, pushed, slab_rows):
    blocks = charge.shape[0]
    u = [
        jnp.concatenate(
            [coords[i : i + 1, LANES * b : LANES * (b + 1)] for b in range(blocks)], axis=0
        )
        for i in range(6)
    ]
    total = [jnp.full((blocks, LANES), transfer[i, 0], jnp.float32) for i in range(6)]
    pairs = {}
    terms = list(u)
    for first in range(6):
        for second in range(first, 6):
            pairs[first, second] = u[first] * u[second]
            terms.append(pairs[first, second])
    for first in range(6):
        for second in range(first, 6):
            for third in range(second, 6):
                terms.append(pairs[first, second] * u[third])
    for column, term in enumerate(terms):
        total = [total[i] + transfer[i, 1 + column] * term for i in range(6)]
    for i in range(6):
        pushed[i] = total[i]
    weight0 = charge[...]
    weight1 = weight0 * total[1]
    row_of = lax.broadcasted_iota(jnp.int32, (blocks, LANES), 0)
    column = offsets[...]
    for b in range(blocks):
        column = column + jnp.where(row_of == b, block_col[0, b], 0)
    return lax.rem(rows[...], slab_rows), column, weight0, weight1


def seat_blocks(strips, strip, seats, rounds, block_col, fields, counts, seat, stage):
    row, column, weight0, weight1 = fields
    blocks = row.shape[0]
    nobody = rounds * strips * seats
    meets = strips_met(strip)
    stage[...] = jnp.full(stage.shape, -1.0, jnp.float32)
    for place in range(strips):
        counts[0, place] = 0
    left_out = jnp.int32(0)
    for block in range(blocks):
        start = block_col[0, block]
        first = start // strip
        for step in range(meets):
            place = jnp.minimum(first + step, strips - 1)
            met = (first + step) * strip <= start + (SPAN - 1)
            taken = counts[0, place]
            counts[0, place] = taken + jnp.where(met, 1, 0)
            later = taken // seats
            number = (later * strips + place) * seats + lax.rem(taken, seats)
            number = jnp.where(met, number, nobody)
            left_out = jnp.maximum(left_out, jnp.where(met, later, 0))
            seat[0, block * meets + step] = number
            own = column[block : block + 1] - place * strip
            own = jnp.where((own >= 0) & (own < strip), own, -1)
            pieces = [row[block : block + 1], own, weight0[block : block + 1], weight1[block : block + 1]]
            stage[pl.ds(number * FIELDS, FIELDS), :] = jnp.concatenate(
                [piece.astype(jnp.float32) for piece in pieces], axis=0
            )
    return left_out


def source_kernel(
    strips,
    block_col_from,
    lags_from,
    fracs_from,
    weights_from,
    coords_from,
    charge_from,
    rows_from,
    offsets_from,
    transfer_from,
    history,
    x_kernel,
    pushed_to,
    packed_to,
    later_to,
    seat_to,
    block_col,
    lags,
    fracs,
    weights,
    coords,
    charge,
    rows,
    offsets,
    transfer,
    frames,
    x_here,
    x_parts,
    s_parts,
    spread_all,
    bands,
    first_bands,
    pushed,
    packed,
    later,
    counts,
    seat,
    stage,
    sems,
):
    count_steps, comps, slab_rows, width = history.shape
    blocks = charge.shape[0]
    strip = width // strips
    spread_rows = comps * strip
    record_rows = packed.shape[1] - spread_rows
    across = packed.shape[2] // LANES
    seats = record_rows * across // FIELDS
    rounds = stage.shape[0] // (FIELDS * strips * seats)
    pairs = [
        (lags_from, lags),
        (fracs_from, fracs),
        (weights_from, weights),
        (block_col_from, block_col),
        (coords_from, coords),
        (charge_from, charge),
        (rows_from, rows),
        (offsets_from, offsets),
        (transfer_from, transfer),
    ]
    for comp in range(comps):
        pairs += [(history.at[t, comp], frames.at[t, comp]) for t in range(count_steps)]
        if comp == 0:
            pairs += [(x_kernel, x_here)]
    fetch = [
        pltpu.make_async_copy(source, target, sems.at[index])
        for index, (source, target) in enumerate(pairs)
    ]
    for copy in fetch:
        copy.start()
    stored = []

    def store(source, target):
        copy = pltpu.make_async_copy(source, target, sems.at[len(fetch) + len(stored)])
        copy.start()
        stored.append(copy)

    for copy in fetch[:3]:
        copy.wait()
    for t in range(count_steps):
        far = weights[0, t] * fracs[0, t]
        near = weights[0, t] * (1.0 - fracs[0, t])
        bands[2 * LANES * t : 2 * LANES * (t + 1)] = lag_band(lags[0, t], near, far)
        first_bands[LANES * t : LANES * (t + 1)] = bands[
            2 * LANES * t + LANES : 2 * LANES * (t + 1)
        ]

    for comp in range(comps):
        first = 9 + comp * (count_steps + 1)
        for copy in fetch[first : first + count_steps] + (fetch[3:9] if comp == 0 else []):
            copy.wait()
        here = slice(comp * slab_rows, (comp + 1) * slab_rows)
        for q in range(width // LANES):
            before = slice(LANES * max(q - 1, 0), LANES * (q + 1))
            steps = [frames[t, comp, :, before] for t in range(count_steps)]
            both = jnp.dot(
                jnp.concatenate(steps, axis=1),
                bands[...] if q else first_bands[...],
                preferred_element_type=jnp.float32,
            )
            high, low = split(both[:, :LANES] + both[:, LANES:])
            s_parts[here, LANES * q : LANES * (q + 1)] = high
            s_parts[here, width + LANES * q : width + LANES * (q + 1)] = low
            s_parts[here, 2 * width + LANES * q : 2 * width + LANES * (q + 1)] = high
        if comp == 0:
            row, column, weight0, weight1 = push(
                coords, charge, rows, offsets, block_col, transfer, pushed, slab_rows
            )
            store(pushed, pushed_to)
            left_out = seat_blocks(
                strips,
                strip,
                seats,
                rounds,
                block_col,
                (row, column, weight0, weight1),
                counts,
                seat,
                stage,
            )
            store(seat, seat_to)
            is_column = lax.rem(lax.broadcasted_iota(jnp.int32, (record_rows, LANES), 0), FIELDS) == 1
            mark = jnp.where(is_column, MORE * left_out.astype(jnp.float32), 0.0)
            for turn in range(rounds):
                for partner in range(strips):
                    for side in range(across):
                        start = ((turn * strips + partner) * across + side) * record_rows
                        value = stage[start : start + record_rows]
                        lanes = slice(side * LANES, (side + 1) * LANES)
                        if turn == 0:
                            packed[partner, spread_rows:, lanes] = (value + mark).astype(packed.dtype)
                        else:
                            later[partner, :, lanes] = value.astype(later.dtype)
            if rounds == 2:
                store(later, later_to)
            store(packed.at[:, spread_rows:], packed_to.at[:, spread_rows:])
            fetch[9 + count_steps].wait()
            high, low = split(x_here[...])
            x_parts[:width] = high
            x_parts[width : 2 * width] = high
            x_parts[2 * width :] = low
        spread = jnp.dot(s_parts[here], x_parts[...], preferred_element_type=jnp.float32)
        if strip % 16 == 0:
            turned = spread.astype(packed.dtype).T
            part = slice(comp * strip, (comp + 1) * strip)
            for partner in range(strips):
                packed[partner, part, :slab_rows] = turned[
                    partner * strip : (partner + 1) * strip
                ]
            store(packed.at[:, part], packed_to.at[:, part])
        else:
            spread_all[comp] = spread.T
    if strip % 16:
        for partner in range(strips):
            part = slice(partner * strip, (partner + 1) * strip)
            both = jnp.concatenate([spread_all[comp, part] for comp in range(comps)], axis=0)
            packed[partner, :spread_rows, :slab_rows] = both.astype(packed.dtype)
        store(packed.at[:, :spread_rows], packed_to.at[:, :spread_rows])
    for copy in stored:
        copy.wait()


def join_kernel(slabs, spread_rows, z_kernel, arrived, kept, *sent):
    slab_rows = z_kernel.shape[0] // slabs
    extra_rows = kept.shape[0] - spread_rows if sent else 0
    total = arrived[0, :spread_rows, :slab_rows].astype(jnp.float32)
    for sender in range(1, arrived.shape[0]):
        total = total + arrived[sender, :spread_rows, :slab_rows].astype(jnp.float32)
    high, low = split(total)
    left = jnp.concatenate([high, low, high], axis=1)

    def part(slab):
        start = pl.multiple_of(slab * slab_rows, slab_rows)
        z_high, z_low = split(z_kernel[pl.ds(start, slab_rows), :])
        right = jnp.concatenate([z_high, z_high, z_low], axis=1)
        return lax.dot_general(left, right, NT_DIMS, preferred_element_type=jnp.float32)

    if sent:
        me = lax.axis_index("dom")
        sent[0][:spread_rows] = part(1 - me)
        kept[:spread_rows] = part(me)
        if extra_rows:
            records = jnp.max(arrived[:, spread_rows:].astype(jnp.float32), axis=0)
            is_column = lax.rem(lax.broadcasted_iota(jnp.int32, records.shape, 0), FIELDS) == 1
            most = jnp.max(jnp.where(is_column, records, -1.0))
            flag = jnp.full((extra_rows, slab_rows), jnp.where(most >= MORE - 1.0, 1.0, 0.0))
            sent[0][spread_rows:] = flag
            kept[spread_rows:] = flag
    else:
        for slab in range(slabs):
            kept[slab] = part(slab)


def unpack_kernel(spread_rows, arrived, records, chosen):
    senders = arrived.shape[0]
    record_rows = arrived.shape[1] - spread_rows
    across = arrived.shape[2] // LANES
    blocks = record_rows * across // FIELDS
    line = lax.broadcasted_iota(jnp.int32, (record_rows, LANES), 0)
    is_column = lax.rem(line, FIELDS) == 1
    first_line = lax.broadcasted_iota(jnp.int32, (record_rows, 1), 0)
    first_column = lax.rem(first_line, FIELDS) == 1
    masks = []
    for sender in range(senders):
        mask = jnp.float32(0.0)
        for side in range(across):
            lanes = slice(side * LANES, (side + 1) * LANES)
            value = arrived[sender, spread_rows:, lanes].astype(jnp.float32)
            value = jnp.where(is_column & (value >= MORE - 1.0), value - MORE, value)
            records[sender, side * record_rows : (side + 1) * record_rows] = value
            taken = first_column & (jnp.max(value, axis=1, keepdims=True) >= 0.0)
            seat = first_line // FIELDS + side * (record_rows // FIELDS)
            bit = jnp.left_shift(jnp.ones_like(seat), seat).astype(jnp.float32)
            mask = mask + jnp.sum(jnp.where(taken, bit, 0.0))
        masks.append(mask.astype(jnp.int32))
    records[senders] = jnp.full(records.shape[1:], -1.0, jnp.float32)
    count = jnp.int32(0)
    for sender in range(senders):
        for block in range(blocks):
            chosen[1 + count] = sender * blocks + block
            count = count + ((masks[sender] >> block) & 1)
    chosen[0] = (count + (GROUP - 1)) // GROUP
    for member in range(GROUP):
        chosen[1 + count + member] = senders * blocks


def read_group(blocks, chosen, records, group):
    where = []
    for member in range(GROUP):
        block = chosen[1 + group * GROUP + member]
        where.append((block // blocks, lax.rem(block, blocks)))

    lines = jnp.concatenate(
        [records[sender, pl.ds(own * FIELDS, FIELDS), :] for sender, own in where], axis=1
    )

    def field(index):
        return lines[index : index + 1]

    return where, field


def one_hot(index, size):
    iota = lax.broadcasted_iota(jnp.int32, (size, index.shape[1]), 0).astype(jnp.float32)
    return iota == index


def one_hot_rows(row, size):
    iota = lax.broadcasted_iota(jnp.int32, (size, row.shape[1]), 0)
    if size <= 256:
        hit = iota.astype(jnp.bfloat16) == row.astype(jnp.bfloat16)
        return jnp.where(hit, jnp.bfloat16(1.0), jnp.bfloat16(0.0))
    return jnp.where(iota.astype(jnp.float32) == row, 1.0, 0.0).astype(jnp.bfloat16)


def deposit_kernel(blocks, chosen, records, after, *refs):
    del after
    extra, (deposit, total) = refs[:-2], refs[-2:]
    strip, slab_rows = deposit.shape[1:]
    total[...] = jnp.zeros_like(total)

    def one_group(group, carry):
        _, field = read_group(blocks, chosen, records, group)
        hit = one_hot(field(1), strip)
        weighted = [jnp.where(hit, field(2 + comp), 0.0) for comp in range(2)]
        total[...] += lax.dot_general(
            one_hot_rows(field(0), slab_rows),
            jnp.concatenate(weighted, axis=0).astype(jnp.bfloat16),
            NT_DIMS,
            preferred_element_type=jnp.float32,
        )
        return carry

    lax.fori_loop(0, chosen[0], one_group, 0)
    turned = total[...].T
    for comp in range(2):
        own = turned[comp * strip : (comp + 1) * strip]
        deposit[comp] = own + extra[0][comp] if extra else own


def sample_kernel(blocks, chosen, records, *refs):
    parts, (field_out, samples, flag, found_all) = refs[:-4], refs[-4:]
    strip, slab_rows = field_out.shape[1:]
    if len(parts) == 1:
        total = parts[0][0]
        for slab in range(1, parts[0].shape[0]):
            total = total + parts[0][slab]
    else:
        total = parts[0][: 2 * strip] + parts[1][: 2 * strip]
    if len(parts) == 2 and parts[0].shape[0] > 2 * strip:
        most = jnp.max(jnp.maximum(parts[0][2 * strip :], parts[1][2 * strip :]))
        flag[0] = jnp.where(most > 0.5, 1, 0)
    else:
        flag[0] = 0
    field_out[0] = total[:strip]
    field_out[1] = total[strip:]
    rounded = total.astype(jnp.bfloat16)
    found_all[...] = jnp.zeros_like(found_all)

    def one_group(group, carry):
        where, field = read_group(blocks, chosen, records, group)
        row_hot = one_hot_rows(field(0), slab_rows)
        found = jnp.dot(rounded, row_hot, preferred_element_type=jnp.float32)
        hit = one_hot(field(1), strip)
        values = []
        for comp in range(2):
            picked = jnp.where(hit, found[comp * strip : (comp + 1) * strip], 0.0)
            values.append(jnp.sum(picked, axis=0, keepdims=True))
        values = jnp.concatenate(values, axis=0)
        for member, (sender, own) in enumerate(where):
            found_all[sender, pl.ds(2 * own, 2), :] = values[
                :, LANES * member : LANES * (member + 1)
            ]
        return carry

    lax.fori_loop(0, chosen[0], one_group, 0)
    samples[...] = found_all[: samples.shape[0]].astype(samples.dtype)


def found_for_blocks(seat, blocks, turn, received, back):
    lines = received.shape[0] * received.shape[1]
    for sender in range(received.shape[0]):
        start = sender * received.shape[1]
        back[start : start + received.shape[1]] = received[sender].astype(jnp.float32)
    back[lines:] = jnp.zeros((back.shape[0] - lines, LANES), jnp.float32)
    meets = seat.shape[1] // blocks
    totals = []
    for block in range(blocks):
        total = None
        for step in range(meets):
            line = 2 * seat[0, block * meets + step] - turn * lines
            line = jnp.where((line >= 0) & (line < lines), line, lines)
            found = back[pl.ds(line, 2), :]
            total = found if total is None else total + found
        totals.append(total)
    return totals


def more_kernel(seat, received, more, back):
    blocks = more.shape[0] // 2
    for block, total in enumerate(found_for_blocks(seat, blocks, 1, received, back)):
        more[2 * block : 2 * block + 2] = total


def kick_kernel(seat, pushed, received, *refs):
    more, (kicked, back) = refs[:-2], refs[-2:]
    blocks = pushed.shape[1]
    values = [pushed[i] for i in range(6)]
    for block, total in enumerate(found_for_blocks(seat, blocks, 0, received, back)):
        if more:
            total = total + more[0][2 * block : 2 * block + 2]
        lines = [value[block : block + 1] for value in values]
        lines[5] = lines[5] + 0.5 * total[0:1]
        lines[1] = lines[1] + 0.5 * total[1:2]
        kicked[:, LANES * block : LANES * (block + 1)] = jnp.concatenate(lines, axis=0)


def local(
    coords,
    charge,
    row_index,
    block_col,
    col_offset,
    transfer_map,
    history,
    retard_index,
    retard_frac,
    retard_weight,
    z_kernel,
    x_kernel,
):
    strips = lax.axis_size("hist")
    slabs = lax.axis_size("dom")
    count_steps, comps, slab_rows, width = history.shape
    strip = width // strips
    particles = coords.shape[1]
    blocks = block_col.shape[0]
    tile = (blocks, LANES)
    spread_rows = comps * strip
    row_lanes = max(slab_rows, LANES)
    seats, second_round = seats_of(strips, slabs, blocks)
    rounds = 2 if second_round else 1
    record_rows = FIELDS * seats * LANES // row_lanes
    packed_rows = spread_rows + record_rows
    meets = strips_met(strip)

    f32, bf16 = jnp.float32, jnp.bfloat16
    pushed, packed, later, seat = call(
        functools.partial(source_kernel, strips),
        (
            jax.ShapeDtypeStruct((6,) + tile, f32),
            jax.ShapeDtypeStruct((strips, packed_rows, row_lanes), bf16),
            jax.ShapeDtypeStruct((strips, record_rows, row_lanes), bf16),
            jax.ShapeDtypeStruct((1, blocks * meets), jnp.int32),
        ),
        [HBM] * 11,
        (HBM, HBM, HBM, HBM),
        [
            pltpu.SMEM((1, blocks), jnp.int32),
            pltpu.SMEM((1, count_steps), jnp.int32),
            pltpu.SMEM((1, count_steps), f32),
            pltpu.SMEM((1, count_steps), f32),
            pltpu.VMEM(coords.shape, f32),
            pltpu.VMEM(tile, f32),
            pltpu.VMEM(tile, jnp.int32),
            pltpu.VMEM(tile, jnp.int32),
            pltpu.SMEM(transfer_map.shape, f32),
            pltpu.VMEM(history.shape, bf16),
            pltpu.VMEM((width, width), f32),
            pltpu.VMEM((3 * width, width), bf16),
            pltpu.VMEM((comps * slab_rows, 3 * width), bf16),
            pltpu.VMEM((comps, width, slab_rows), f32),
            pltpu.VMEM((2 * LANES * count_steps, 2 * LANES), bf16),
            pltpu.VMEM((LANES * count_steps, 2 * LANES), bf16),
            pltpu.VMEM((6,) + tile, f32),
            pltpu.VMEM((strips, packed_rows, row_lanes), bf16),
            pltpu.VMEM((strips, record_rows, row_lanes), bf16),
            pltpu.SMEM((1, strips), jnp.int32),
            pltpu.SMEM((1, blocks * meets), jnp.int32),
            pltpu.VMEM((FIELDS * (rounds * strips * seats + 2), LANES), f32),
            pltpu.SemaphoreType.DMA((16 + comps * count_steps,)),
        ],
        flops=6 * comps * slab_rows * width * width,
        moved=history.size * 2 + x_kernel.size * 4,
        limit=LIMIT,
    )(
        block_col.reshape(1, blocks),
        retard_index.reshape(1, count_steps),
        retard_frac.reshape(1, count_steps),
        retard_weight.reshape(1, count_steps),
        coords,
        charge.reshape(tile),
        row_index.reshape(tile),
        col_offset.reshape(tile),
        transfer_map,
        history,
        x_kernel,
    )
    arrived = lax.all_to_all(packed, "hist", 0, 0, tiled=True)

    part = jax.ShapeDtypeStruct((spread_rows + (8 if second_round else 0), slab_rows), f32)
    parts = call(
        functools.partial(join_kernel, slabs, spread_rows),
        (part, part) if slabs == 2 else jax.ShapeDtypeStruct((slabs,) + part.shape, f32),
        [VMEM, VMEM],
        (VMEM, VMEM) if slabs == 2 else VMEM,
        flops=1 << 27,
        moved=1 << 20,
    )(z_kernel, arrived)
    if slabs == 2:
        kept, sent = parts
        parts = [kept, lax.ppermute(sent, "dom", [(0, 1), (1, 0)])]
    else:
        parts = [lax.all_to_all(parts, "dom", 0, 0, tiled=True)]

    def unpack(arrived, spread_rows):
        return call(
            functools.partial(unpack_kernel, spread_rows),
            (
                jax.ShapeDtypeStruct((strips + 1, FIELDS * seats, LANES), f32),
                jax.ShapeDtypeStruct((strips * seats + 16,), jnp.int32),
            ),
            [VMEM],
            (VMEM, SMEM),
            flops=1 << 20,
            moved=1 << 20,
        )(arrived)

    def sample(chosen, records, parts):
        return call(
            functools.partial(sample_kernel, seats),
            (
                jax.ShapeDtypeStruct((comps, strip, slab_rows), f32),
                jax.ShapeDtypeStruct((strips, comps * seats, LANES), bf16),
                jax.ShapeDtypeStruct((8,), jnp.int32),
            ),
            [SMEM, VMEM] + [VMEM] * len(parts),
            (VMEM, VMEM, SMEM),
            [pltpu.VMEM((strips + 1, comps * seats, LANES), f32)],
            flops=1 << 29,
            moved=1 << 20,
        )(chosen, records, *parts)

    def deposits(chosen, records, after, *extra):
        return call(
            functools.partial(deposit_kernel, seats),
            jax.ShapeDtypeStruct((comps, strip, slab_rows), f32),
            [SMEM, VMEM, HBM] + [VMEM] * len(extra),
            VMEM,
            [pltpu.VMEM((slab_rows, comps * strip), f32)],
            flops=1 << 29,
            moved=1 << 20,
        )(chosen, records, after, *extra)

    def exchange(value):
        return lax.all_to_all(value, "hist", 0, 0, tiled=True)

    records, chosen = unpack(arrived, spread_rows)
    field, samples, flag = sample(chosen, records, parts)
    back = pltpu.VMEM((comps * strips * seats + 8, LANES), f32)
    more, extra = [], []
    if second_round:

        def another(later, field, seat):
            records, chosen = unpack(exchange(later), 0)
            whole = field.reshape(1, spread_rows, slab_rows)
            _, samples, _ = sample(chosen, records, [whole])
            more = call(
                more_kernel,
                jax.ShapeDtypeStruct((comps * blocks, LANES), f32),
                [SMEM, VMEM],
                VMEM,
                [back],
            )(seat, exchange(samples))
            return more, deposits(chosen, records, samples)

        def nothing(later, field, seat):
            return jnp.zeros((comps * blocks, LANES), f32), jnp.zeros(field.shape, f32)

        found, left = lax.cond(flag[0] > 0, another, nothing, later, field, seat)
        more, extra = [found], [left]
    received = exchange(samples)
    deposit = deposits(chosen, records, samples, *extra)
    kicked = call(
        kick_kernel,
        jax.ShapeDtypeStruct((6, particles), f32),
        [SMEM] + [VMEM] * (2 + len(more)),
        VMEM,
        [back],
        flops=1 << 16,
        moved=1 << 18,
    )(seat, pushed, received, *more)
    return kicked, jnp.transpose(field, (0, 2, 1)), jnp.transpose(deposit, (0, 2, 1))


def solution(mesh):
    return jax.shard_map(
        local,
        mesh=mesh,
        in_specs=(
            P(None, ("dom", "hist")),
            P(("dom", "hist")),
            P(("dom", "hist")),
            P(("dom", "hist")),
            P(("dom", "hist")),
            P(),
            P("hist", None, "dom", None),
            P("hist"),
            P("hist"),
            P("hist"),
            P(None, "dom"),
            P(),
        ),
        out_specs=(P(None, ("dom", "hist")), P(None, "dom", "hist"), P(None, "dom", "hist")),
        check_vma=False,
    )
```

```python
import functools

import jax
import jax.numpy as jnp
from jax import lax
from jax.experimental import pallas as pl
from jax.experimental.pallas import tpu as pltpu
from jax.sharding import PartitionSpec as P

LANES = 128
GROUP = 8
SPAN = 16
SEATS = 8
FIELDS = 4
MORE = 64.0
NT_DIMS = (((1,), (1,)), ((), ()))
VMEM = pl.BlockSpec(memory_space=pltpu.VMEM)
SMEM = pl.BlockSpec(memory_space=pltpu.SMEM)
HBM = pl.BlockSpec(memory_space=pltpu.HBM)
LIMIT = 59 * 1024 * 1024
SMALL = 16 * 1024 * 1024


def call(kernel, out_shape, in_specs, out_specs, scratch=(), flops=0, moved=0, limit=SMALL):
    return pl.pallas_call(
        kernel,
        out_shape=out_shape,
        in_specs=in_specs,
        out_specs=out_specs,
        scratch_shapes=scratch,
        compiler_params=pltpu.CompilerParams(vmem_limit_bytes=limit),
        cost_estimate=pl.CostEstimate(flops=flops, bytes_accessed=moved, transcendentals=0),
    )


def split(value):
    high = value.astype(jnp.bfloat16)
    return high, (value - high.astype(jnp.float32)).astype(jnp.bfloat16)


def seats_of(strips, slabs, blocks):
    if strips == 16 and slabs == 2 and blocks == 2 * SEATS:
        return SEATS, True
    return blocks, False


def strips_met(strip):
    return (SPAN + strip - 2) // strip + 1


def lag_band(lag, near, far):
    row = lax.broadcasted_iota(jnp.int32, (2 * LANES, LANES), 0)
    column = lax.broadcasted_iota(jnp.int32, (2 * LANES, LANES), 1)
    behind = column + LANES - row
    weight = jnp.where(behind == lag, near, jnp.where(behind == lag + 1, far, 0.0))
    return jnp.concatenate(split(weight), axis=1)


def push(coords, charge, rows, offsets, block_col, transfer, pushed, slab_rows):
    blocks = charge.shape[0]
    u = [
        jnp.concatenate(
            [coords[i : i + 1, LANES * b : LANES * (b + 1)] for b in range(blocks)], axis=0
        )
        for i in range(6)
    ]
    total = [jnp.full((blocks, LANES), transfer[i, 0], jnp.float32) for i in range(6)]
    pairs = {}
    terms = list(u)
    for first in range(6):
        for second in range(first, 6):
            pairs[first, second] = u[first] * u[second]
            terms.append(pairs[first, second])
    for first in range(6):
        for second in range(first, 6):
            for third in range(second, 6):
                terms.append(pairs[first, second] * u[third])
    for column, term in enumerate(terms):
        total = [total[i] + transfer[i, 1 + column] * term for i in range(6)]
    for i in range(6):
        pushed[i] = total[i]
    weight0 = charge[...]
    weight1 = weight0 * total[1]
    row_of = lax.broadcasted_iota(jnp.int32, (blocks, LANES), 0)
    column = offsets[...]
    for b in range(blocks):
        column = column + jnp.where(row_of == b, block_col[0, b], 0)
    return lax.rem(rows[...], slab_rows), column, weight0, weight1


def seat_blocks(strips, strip, seats, rounds, block_col, fields, counts, pick, stage):
    row, column, weight0, weight1 = fields
    blocks = row.shape[0]
    nobody = rounds * strips * seats
    meets = strips_met(strip)
    stage[...] = jnp.full(stage.shape, -1.0, jnp.float32)
    for place in range(strips):
        counts[0, place] = 0
    left_out = jnp.int32(0)
    pick_row = lax.broadcasted_iota(jnp.int32, (2 * blocks, LANES), 0)
    lane = lax.broadcasted_iota(jnp.int32, (2 * blocks, LANES), 1)
    wanted = [jnp.zeros((2 * blocks, LANES), jnp.int32)] * meets
    for block in range(blocks):
        start = block_col[0, block]
        first = start // strip
        for step in range(meets):
            place = jnp.minimum(first + step, strips - 1)
            met = (first + step) * strip <= start + (SPAN - 1)
            taken = counts[0, place]
            counts[0, place] = taken + jnp.where(met, 1, 0)
            later = taken // seats
            number = (later * strips + place) * seats + lax.rem(taken, seats)
            number = jnp.where(met, number, nobody)
            left_out = jnp.maximum(left_out, jnp.where(met, later, 0))
            wanted[step] = jnp.where(pick_row >> 1 == block, 2 * number, wanted[step])
            own = column[block : block + 1] - place * strip
            own = jnp.where((own >= 0) & (own < strip), own, -1)
            pieces = [row[block : block + 1], own, weight0[block : block + 1], weight1[block : block + 1]]
            stage[pl.ds(number * FIELDS, FIELDS), :] = jnp.concatenate(
                [piece.astype(jnp.float32) for piece in pieces], axis=0
            )
    lines = 2 * strips * seats
    for turn in range(rounds):
        for left in range(0, lines, LANES):
            line = lane + (turn * lines + left)
            hit = wanted[0] + (pick_row & 1) == line
            for step in range(1, meets):
                hit = hit | (wanted[step] + (pick_row & 1) == line)
            pick[turn, :, left : left + LANES] = jnp.where(hit, 1.0, 0.0).astype(pick.dtype)
    return left_out


def source_kernel(
    strips,
    block_col_from,
    lags_from,
    fracs_from,
    weights_from,
    coords_from,
    charge_from,
    rows_from,
    offsets_from,
    transfer_from,
    history,
    x_kernel,
    pushed_to,
    packed_to,
    later_to,
    pick_to,
    block_col,
    lags,
    fracs,
    weights,
    coords,
    charge,
    rows,
    offsets,
    transfer,
    frames,
    x_here,
    x_parts,
    s_parts,
    spread_all,
    bands,
    first_bands,
    pushed,
    packed,
    later,
    counts,
    pick,
    stage,
    sems,
):
    count_steps, comps, slab_rows, width = history.shape
    blocks = charge.shape[0]
    strip = width // strips
    spread_rows = comps * strip
    record_rows = packed.shape[1] - spread_rows
    across = packed.shape[2] // LANES
    seats = record_rows * across // FIELDS
    rounds = stage.shape[0] // (FIELDS * strips * seats)
    pairs = [
        (lags_from, lags),
        (fracs_from, fracs),
        (weights_from, weights),
        (block_col_from, block_col),
        (coords_from, coords),
        (charge_from, charge),
        (rows_from, rows),
        (offsets_from, offsets),
        (transfer_from, transfer),
    ]
    for comp in range(comps):
        pairs += [(history.at[t, comp], frames.at[t, comp]) for t in range(count_steps)]
        if comp == 0:
            pairs += [(x_kernel, x_here)]
    fetch = [
        pltpu.make_async_copy(source, target, sems.at[index])
        for index, (source, target) in enumerate(pairs)
    ]
    for copy in fetch:
        copy.start()
    stored = []

    def store(source, target):
        copy = pltpu.make_async_copy(source, target, sems.at[len(fetch) + len(stored)])
        copy.start()
        stored.append(copy)

    for copy in fetch[:3]:
        copy.wait()
    for t in range(count_steps):
        far = weights[0, t] * fracs[0, t]
        near = weights[0, t] * (1.0 - fracs[0, t])
        bands[2 * LANES * t : 2 * LANES * (t + 1)] = lag_band(lags[0, t], near, far)
        first_bands[LANES * t : LANES * (t + 1)] = bands[
            2 * LANES * t + LANES : 2 * LANES * (t + 1)
        ]

    for copy in fetch[3:9]:
        copy.wait()
    row, column, weight0, weight1 = push(
        coords, charge, rows, offsets, block_col, transfer, pushed, slab_rows
    )
    store(pushed, pushed_to)
    left_out = seat_blocks(
        strips,
        strip,
        seats,
        rounds,
        block_col,
        (row, column, weight0, weight1),
        counts,
        pick,
        stage,
    )
    store(pick, pick_to)
    is_column = lax.rem(lax.broadcasted_iota(jnp.int32, (record_rows, LANES), 0), FIELDS) == 1
    mark = jnp.where(is_column, MORE * left_out.astype(jnp.float32), 0.0)
    for turn in range(rounds):
        for partner in range(strips):
            for side in range(across):
                start = ((turn * strips + partner) * across + side) * record_rows
                value = stage[start : start + record_rows]
                lanes = slice(side * LANES, (side + 1) * LANES)
                if turn == 0:
                    packed[partner, spread_rows:, lanes] = (value + mark).astype(packed.dtype)
                else:
                    later[partner, :, lanes] = value.astype(later.dtype)
    if rounds == 2:
        store(later, later_to)
    store(packed.at[:, spread_rows:], packed_to.at[:, spread_rows:])

    for comp in range(comps):
        first = 9 + comp * (count_steps + 1)
        for copy in fetch[first : first + count_steps]:
            copy.wait()
        here = slice(comp * slab_rows, (comp + 1) * slab_rows)
        part_rows = min(128, slab_rows)
        for top in range(0, slab_rows, part_rows):
            for q in range(width // LANES):
                before = slice(LANES * max(q - 1, 0), LANES * (q + 1))
                steps = [
                    frames[t, comp, top : top + part_rows, before] for t in range(count_steps)
                ]
                both = jnp.dot(
                    jnp.concatenate(steps, axis=1),
                    bands[...] if q else first_bands[...],
                    preferred_element_type=jnp.float32,
                )
                high, low = split(both[:, :LANES] + both[:, LANES:])
                part = slice(comp * slab_rows + top, comp * slab_rows + top + part_rows)
                s_parts[part, LANES * q : LANES * (q + 1)] = high
                s_parts[part, width + LANES * q : width + LANES * (q + 1)] = low
                s_parts[part, 2 * width + LANES * q : 2 * width + LANES * (q + 1)] = high
        if comp == 0:
            fetch[9 + count_steps].wait()
            high, low = split(x_here[...])
            x_parts[:width] = high
            x_parts[width : 2 * width] = high
            x_parts[2 * width :] = low
        spread = jnp.dot(s_parts[here], x_parts[...], preferred_element_type=jnp.float32)
        if strip % 16 == 0:
            turned = spread.astype(packed.dtype).T
            part = slice(comp * strip, (comp + 1) * strip)
            for partner in range(strips):
                packed[partner, part, :slab_rows] = turned[
                    partner * strip : (partner + 1) * strip
                ]
            store(packed.at[:, part], packed_to.at[:, part])
        else:
            spread_all[comp] = spread.T
    if strip % 16:
        for partner in range(strips):
            part = slice(partner * strip, (partner + 1) * strip)
            both = jnp.concatenate([spread_all[comp, part] for comp in range(comps)], axis=0)
            packed[partner, :spread_rows, :slab_rows] = both.astype(packed.dtype)
        store(packed.at[:, :spread_rows], packed_to.at[:, :spread_rows])
    for copy in stored:
        copy.wait()


def join_kernel(slabs, spread_rows, z_kernel, arrived, kept, *sent):
    slab_rows = z_kernel.shape[0] // slabs
    extra_rows = kept.shape[0] - spread_rows if sent else 0
    total = arrived[0, :spread_rows, :slab_rows].astype(jnp.float32)
    for sender in range(1, arrived.shape[0]):
        total = total + arrived[sender, :spread_rows, :slab_rows].astype(jnp.float32)
    high, low = split(total)
    left = jnp.concatenate([high, low, high], axis=1)

    def part(slab):
        start = pl.multiple_of(slab * slab_rows, slab_rows)
        z_high, z_low = split(z_kernel[pl.ds(start, slab_rows), :])
        right = jnp.concatenate([z_high, z_high, z_low], axis=1)
        return lax.dot_general(left, right, NT_DIMS, preferred_element_type=jnp.float32)

    if sent:
        me = lax.axis_index("dom")
        sent[0][:spread_rows] = part(1 - me)
        kept[:spread_rows] = part(me)
        if extra_rows:
            records = jnp.max(arrived[:, spread_rows:].astype(jnp.float32), axis=0)
            is_column = lax.rem(lax.broadcasted_iota(jnp.int32, records.shape, 0), FIELDS) == 1
            most = jnp.max(jnp.where(is_column, records, -1.0))
            flag = jnp.full((extra_rows, slab_rows), jnp.where(most >= MORE - 1.0, 1.0, 0.0))
            sent[0][spread_rows:] = flag
            kept[spread_rows:] = flag
    else:
        for slab in range(slabs):
            kept[slab] = part(slab)


def unpack_kernel(spread_rows, arrived, records, chosen):
    senders = arrived.shape[0]
    record_rows = arrived.shape[1] - spread_rows
    across = arrived.shape[2] // LANES
    blocks = record_rows * across // FIELDS
    line = lax.broadcasted_iota(jnp.int32, (record_rows, LANES), 0)
    is_column = lax.rem(line, FIELDS) == 1
    first_line = lax.broadcasted_iota(jnp.int32, (record_rows, 1), 0)
    first_column = lax.rem(first_line, FIELDS) == 1
    masks = []
    for sender in range(senders):
        mask = jnp.float32(0.0)
        for side in range(across):
            lanes = slice(side * LANES, (side + 1) * LANES)
            value = arrived[sender, spread_rows:, lanes].astype(jnp.float32)
            value = jnp.where(is_column & (value >= MORE - 1.0), value - MORE, value)
            records[sender, side * record_rows : (side + 1) * record_rows] = value
            taken = first_column & (jnp.max(value, axis=1, keepdims=True) >= 0.0)
            seat = first_line // FIELDS + side * (record_rows // FIELDS)
            bit = jnp.left_shift(jnp.ones_like(seat), seat).astype(jnp.float32)
            mask = mask + jnp.sum(jnp.where(taken, bit, 0.0))
        masks.append(mask.astype(jnp.int32))
    records[senders] = jnp.full(records.shape[1:], -1.0, jnp.float32)
    count = jnp.int32(0)
    for sender in range(senders):
        for block in range(blocks):
            chosen[1 + count] = sender * blocks + block
            count = count + ((masks[sender] >> block) & 1)
    chosen[0] = (count + (GROUP - 1)) // GROUP
    for member in range(GROUP):
        chosen[1 + count + member] = senders * blocks


def read_group(blocks, chosen, records, group):
    where = []
    for member in range(GROUP):
        block = chosen[1 + group * GROUP + member]
        where.append((block // blocks, lax.rem(block, blocks)))

    lines = jnp.concatenate(
        [records[sender, pl.ds(own * FIELDS, FIELDS), :] for sender, own in where], axis=1
    )

    def field(index):
        return lines[index : index + 1]

    return where, field


def one_hot(index, size):
    iota = lax.broadcasted_iota(jnp.int32, (size, index.shape[1]), 0).astype(jnp.float32)
    return iota == index


def one_hot_rows(row, size):
    iota = lax.broadcasted_iota(jnp.int32, (size, row.shape[1]), 0)
    if size <= 256:
        hit = iota.astype(jnp.bfloat16) == row.astype(jnp.bfloat16)
        return jnp.where(hit, jnp.bfloat16(1.0), jnp.bfloat16(0.0))
    return jnp.where(iota.astype(jnp.float32) == row, 1.0, 0.0).astype(jnp.bfloat16)


def deposit_kernel(blocks, chosen, records, after, *refs):
    del after
    extra, (deposit, total) = refs[:-2], refs[-2:]
    strip, slab_rows = deposit.shape[1:]
    total[...] = jnp.zeros_like(total)

    def one_group(group, carry):
        _, field = read_group(blocks, chosen, records, group)
        hit = one_hot(field(1), strip)
        weighted = [jnp.where(hit, field(2 + comp), 0.0) for comp in range(2)]
        total[...] += lax.dot_general(
            one_hot_rows(field(0), slab_rows),
            jnp.concatenate(weighted, axis=0).astype(jnp.bfloat16),
            NT_DIMS,
            preferred_element_type=jnp.float32,
        )
        return carry

    lax.fori_loop(0, chosen[0], one_group, 0)
    turned = total[...].T
    for comp in range(2):
        own = turned[comp * strip : (comp + 1) * strip]
        deposit[comp] = own + extra[0][comp] if extra else own


def sample_kernel(blocks, chosen, records, *refs):
    parts, (field_out, samples, flag, found_all) = refs[:-4], refs[-4:]
    strip, slab_rows = field_out.shape[1:]
    if len(parts) == 1:
        total = parts[0][0]
        for slab in range(1, parts[0].shape[0]):
            total = total + parts[0][slab]
    else:
        total = parts[0][: 2 * strip] + parts[1][: 2 * strip]
    if len(parts) == 2 and parts[0].shape[0] > 2 * strip:
        most = jnp.max(jnp.maximum(parts[0][2 * strip :], parts[1][2 * strip :]))
        flag[0] = jnp.where(most > 0.5, 1, 0)
    else:
        flag[0] = 0
    field_out[0] = total[:strip]
    field_out[1] = total[strip:]
    rounded = total.astype(jnp.bfloat16)
    found_all[...] = jnp.zeros_like(found_all)

    def one_group(group, carry):
        where, field = read_group(blocks, chosen, records, group)
        row_hot = one_hot_rows(field(0), slab_rows)
        found = jnp.dot(rounded, row_hot, preferred_element_type=jnp.float32)
        hit = one_hot(field(1), strip)
        values = []
        for comp in range(2):
            picked = jnp.where(hit, found[comp * strip : (comp + 1) * strip], 0.0)
            values.append(jnp.sum(picked, axis=0, keepdims=True))
        values = jnp.concatenate(values, axis=0)
        for member, (sender, own) in enumerate(where):
            found_all[sender, pl.ds(2 * own, 2), :] = values[
                :, LANES * member : LANES * (member + 1)
            ]
        return carry

    lax.fori_loop(0, chosen[0], one_group, 0)
    samples[...] = found_all[: samples.shape[0]].astype(samples.dtype)


def found_for_blocks(pick, received):
    flat = received[...].reshape(received.shape[0] * received.shape[1], LANES)
    return jnp.dot(pick, flat, preferred_element_type=jnp.float32)


def more_kernel(pick, received, more):
    more[...] = found_for_blocks(pick[1], received)


def kick_kernel(pick, pushed, received, *refs):
    more, kicked = refs[:-1], refs[-1]
    blocks = pushed.shape[1]
    values = [pushed[i] for i in range(6)]
    total = found_for_blocks(pick[0], received)
    if more:
        total = total + more[0][...]
    for block in range(blocks):
        lines = [value[block : block + 1] for value in values]
        lines[5] = lines[5] + 0.5 * total[2 * block : 2 * block + 1]
        lines[1] = lines[1] + 0.5 * total[2 * block + 1 : 2 * block + 2]
        kicked[:, LANES * block : LANES * (block + 1)] = jnp.concatenate(lines, axis=0)


def local(
    coords,
    charge,
    row_index,
    block_col,
    col_offset,
    transfer_map,
    history,
    retard_index,
    retard_frac,
    retard_weight,
    z_kernel,
    x_kernel,
):
    strips = lax.axis_size("hist")
    slabs = lax.axis_size("dom")
    count_steps, comps, slab_rows, width = history.shape
    strip = width // strips
    particles = coords.shape[1]
    blocks = block_col.shape[0]
    tile = (blocks, LANES)
    spread_rows = comps * strip
    row_lanes = max(slab_rows, LANES)
    seats, second_round = seats_of(strips, slabs, blocks)
    rounds = 2 if second_round else 1
    record_rows = FIELDS * seats * LANES // row_lanes
    packed_rows = spread_rows + record_rows

    f32, bf16 = jnp.float32, jnp.bfloat16
    pushed, packed, later, pick = call(
        functools.partial(source_kernel, strips),
        (
            jax.ShapeDtypeStruct((6,) + tile, f32),
            jax.ShapeDtypeStruct((strips, packed_rows, row_lanes), bf16),
            jax.ShapeDtypeStruct((strips, record_rows, row_lanes), bf16),
            jax.ShapeDtypeStruct((rounds, comps * blocks, comps * strips * seats), bf16),
        ),
        [HBM] * 11,
        (HBM, HBM, HBM, HBM),
        [
            pltpu.SMEM((1, blocks), jnp.int32),
            pltpu.SMEM((1, count_steps), jnp.int32),
            pltpu.SMEM((1, count_steps), f32),
            pltpu.SMEM((1, count_steps), f32),
            pltpu.VMEM(coords.shape, f32),
            pltpu.VMEM(tile, f32),
            pltpu.VMEM(tile, jnp.int32),
            pltpu.VMEM(tile, jnp.int32),
            pltpu.SMEM(transfer_map.shape, f32),
            pltpu.VMEM(history.shape, bf16),
            pltpu.VMEM((width, width), f32),
            pltpu.VMEM((3 * width, width), bf16),
            pltpu.VMEM((comps * slab_rows, 3 * width), bf16),
            pltpu.VMEM((comps, width, slab_rows), f32),
            pltpu.VMEM((2 * LANES * count_steps, 2 * LANES), bf16),
            pltpu.VMEM((LANES * count_steps, 2 * LANES), bf16),
            pltpu.VMEM((6,) + tile, f32),
            pltpu.VMEM((strips, packed_rows, row_lanes), bf16),
            pltpu.VMEM((strips, record_rows, row_lanes), bf16),
            pltpu.SMEM((1, strips), jnp.int32),
            pltpu.VMEM((rounds, comps * blocks, comps * strips * seats), bf16),
            pltpu.VMEM((FIELDS * (rounds * strips * seats + 2), LANES), f32),
            pltpu.SemaphoreType.DMA((16 + comps * count_steps,)),
        ],
        flops=6 * comps * slab_rows * width * width,
        moved=history.size * 2 + x_kernel.size * 4,
        limit=LIMIT,
    )(
        block_col.reshape(1, blocks),
        retard_index.reshape(1, count_steps),
        retard_frac.reshape(1, count_steps),
        retard_weight.reshape(1, count_steps),
        coords,
        charge.reshape(tile),
        row_index.reshape(tile),
        col_offset.reshape(tile),
        transfer_map,
        history,
        x_kernel,
    )
    arrived = lax.all_to_all(packed, "hist", 0, 0, tiled=True)

    part = jax.ShapeDtypeStruct((spread_rows + (8 if second_round else 0), slab_rows), f32)
    parts = call(
        functools.partial(join_kernel, slabs, spread_rows),
        (part, part) if slabs == 2 else jax.ShapeDtypeStruct((slabs,) + part.shape, f32),
        [VMEM, VMEM],
        (VMEM, VMEM) if slabs == 2 else VMEM,
        flops=1 << 27,
        moved=1 << 20,
    )(z_kernel, arrived)
    if slabs == 2:
        kept, sent = parts
        parts = [kept, lax.ppermute(sent, "dom", [(0, 1), (1, 0)])]
    else:
        parts = [lax.all_to_all(parts, "dom", 0, 0, tiled=True)]

    def unpack(arrived, spread_rows):
        return call(
            functools.partial(unpack_kernel, spread_rows),
            (
                jax.ShapeDtypeStruct((strips + 1, FIELDS * seats, LANES), f32),
                jax.ShapeDtypeStruct((strips * seats + 16,), jnp.int32),
            ),
            [VMEM],
            (VMEM, SMEM),
            flops=1 << 20,
            moved=1 << 20,
        )(arrived)

    def sample(chosen, records, parts):
        return call(
            functools.partial(sample_kernel, seats),
            (
                jax.ShapeDtypeStruct((comps, strip, slab_rows), f32),
                jax.ShapeDtypeStruct((strips, comps * seats, LANES), bf16),
                jax.ShapeDtypeStruct((8,), jnp.int32),
            ),
            [SMEM, VMEM] + [VMEM] * len(parts),
            (VMEM, VMEM, SMEM),
            [pltpu.VMEM((strips + 1, comps * seats, LANES), f32)],
            flops=1 << 29,
            moved=1 << 20,
        )(chosen, records, *parts)

    def deposits(chosen, records, after, *extra):
        return call(
            functools.partial(deposit_kernel, seats),
            jax.ShapeDtypeStruct((comps, strip, slab_rows), f32),
            [SMEM, VMEM, HBM] + [VMEM] * len(extra),
            VMEM,
            [pltpu.VMEM((slab_rows, comps * strip), f32)],
            flops=1 << 29,
            moved=1 << 20,
        )(chosen, records, after, *extra)

    def exchange(value):
        return lax.all_to_all(value, "hist", 0, 0, tiled=True)

    records, chosen = unpack(arrived, spread_rows)
    field, samples, flag = sample(chosen, records, parts)
    more, extra = [], []
    if second_round:

        def another(later, field, pick):
            records, chosen = unpack(exchange(later), 0)
            whole = field.reshape(1, spread_rows, slab_rows)
            _, samples, _ = sample(chosen, records, [whole])
            more = call(
                more_kernel,
                jax.ShapeDtypeStruct((comps * blocks, LANES), f32),
                [VMEM, VMEM],
                VMEM,
            )(pick, exchange(samples))
            return more, deposits(chosen, records, samples)

        def nothing(later, field, pick):
            return jnp.zeros((comps * blocks, LANES), f32), jnp.zeros(field.shape, f32)

        found, left = lax.cond(flag[0] > 0, another, nothing, later, field, pick)
        more, extra = [found], [left]
    received = exchange(samples)
    deposit = deposits(chosen, records, samples, *extra)
    kicked = call(
        kick_kernel,
        jax.ShapeDtypeStruct((6, particles), f32),
        [VMEM] * (3 + len(more)),
        VMEM,
        flops=1 << 16,
        moved=1 << 18,
    )(pick, pushed, received, *more)
    return kicked, jnp.transpose(field, (0, 2, 1)), jnp.transpose(deposit, (0, 2, 1))


def solution(mesh):
    return jax.shard_map(
        local,
        mesh=mesh,
        in_specs=(
            P(None, ("dom", "hist")),
            P(("dom", "hist")),
            P(("dom", "hist")),
            P(("dom", "hist")),
            P(("dom", "hist")),
            P(),
            P("hist", None, "dom", None),
            P("hist"),
            P("hist"),
            P("hist"),
            P(None, "dom"),
            P(),
        ),
        out_specs=(P(None, ("dom", "hist")), P(None, "dom", "hist"), P(None, "dom", "hist")),
        check_vma=False,
    )
```

```python
import functools

import jax
import jax.numpy as jnp
from jax import lax
from jax.experimental import pallas as pl
from jax.experimental.pallas import tpu as pltpu
from jax.sharding import PartitionSpec as P

LANES = 128
GROUP = 8
SPAN = 16
SEATS = 8
FIELDS = 4
MORE = 64.0
NT_DIMS = (((1,), (1,)), ((), ()))
VMEM = pl.BlockSpec(memory_space=pltpu.VMEM)
SMEM = pl.BlockSpec(memory_space=pltpu.SMEM)
HBM = pl.BlockSpec(memory_space=pltpu.HBM)
LIMIT = 59 * 1024 * 1024
SMALL = 16 * 1024 * 1024


def call(kernel, out_shape, in_specs, out_specs, scratch=(), flops=0, moved=0, limit=SMALL):
    return pl.pallas_call(
        kernel,
        out_shape=out_shape,
        in_specs=in_specs,
        out_specs=out_specs,
        scratch_shapes=scratch,
        compiler_params=pltpu.CompilerParams(vmem_limit_bytes=limit),
        cost_estimate=pl.CostEstimate(flops=flops, bytes_accessed=moved, transcendentals=0),
    )


def split(value):
    high = value.astype(jnp.bfloat16)
    return high, (value - high.astype(jnp.float32)).astype(jnp.bfloat16)


def seats_of(strips, slabs, blocks):
    if strips == 16 and slabs == 2 and blocks == 2 * SEATS:
        return SEATS, True
    return blocks, False


def strips_met(strip):
    return (SPAN + strip - 2) // strip + 1


def lag_band(lag, near, far):
    row = lax.broadcasted_iota(jnp.int32, (2 * LANES, LANES), 0)
    column = lax.broadcasted_iota(jnp.int32, (2 * LANES, LANES), 1)
    behind = column + LANES - row
    weight = jnp.where(behind == lag, near, jnp.where(behind == lag + 1, far, 0.0))
    return jnp.concatenate(split(weight), axis=1)


def push(coords, charge, rows, offsets, block_col, transfer, pushed, slab_rows):
    blocks = charge.shape[0]
    u = [
        jnp.concatenate(
            [coords[i : i + 1, LANES * b : LANES * (b + 1)] for b in range(blocks)], axis=0
        )
        for i in range(6)
    ]
    total = [jnp.full((blocks, LANES), transfer[i, 0], jnp.float32) for i in range(6)]
    pairs = {}
    terms = list(u)
    for first in range(6):
        for second in range(first, 6):
            pairs[first, second] = u[first] * u[second]
            terms.append(pairs[first, second])
    for first in range(6):
        for second in range(first, 6):
            for third in range(second, 6):
                terms.append(pairs[first, second] * u[third])
    for column, term in enumerate(terms):
        total = [total[i] + transfer[i, 1 + column] * term for i in range(6)]
    for i in range(6):
        pushed[i] = total[i]
    weight0 = charge[...]
    weight1 = weight0 * total[1]
    row_of = lax.broadcasted_iota(jnp.int32, (blocks, LANES), 0)
    column = offsets[...]
    for b in range(blocks):
        column = column + jnp.where(row_of == b, block_col[0, b], 0)
    return lax.rem(rows[...], slab_rows), column, weight0, weight1


def seat_blocks(strips, strip, seats, rounds, block_col, fields, counts, pick, stage):
    row, column, weight0, weight1 = fields
    blocks = row.shape[0]
    nobody = rounds * strips * seats
    meets = strips_met(strip)
    stage[...] = jnp.full(stage.shape, -1.0, jnp.float32)
    for place in range(strips):
        counts[0, place] = 0
    left_out = jnp.int32(0)
    pick_row = lax.broadcasted_iota(jnp.int32, (2 * blocks, LANES), 0)
    lane = lax.broadcasted_iota(jnp.int32, (2 * blocks, LANES), 1)
    wanted = [jnp.zeros((2 * blocks, LANES), jnp.int32)] * meets
    for block in range(blocks):
        start = block_col[0, block]
        first = start // strip
        for step in range(meets):
            place = jnp.minimum(first + step, strips - 1)
            met = (first + step) * strip <= start + (SPAN - 1)
            taken = counts[0, place]
            counts[0, place] = taken + jnp.where(met, 1, 0)
            later = taken // seats
            number = (later * strips + place) * seats + lax.rem(taken, seats)
            number = jnp.where(met, number, nobody)
            left_out = jnp.maximum(left_out, jnp.where(met, later, 0))
            wanted[step] = jnp.where(pick_row >> 1 == block, 2 * number, wanted[step])
            own = column[block : block + 1] - place * strip
            own = jnp.where((own >= 0) & (own < strip), own, -1)
            pieces = [row[block : block + 1], own, weight0[block : block + 1], weight1[block : block + 1]]
            stage[pl.ds(number * FIELDS, FIELDS), :] = jnp.concatenate(
                [piece.astype(jnp.float32) for piece in pieces], axis=0
            )
    lines = 2 * strips * seats
    for turn in range(rounds):
        for left in range(0, lines, LANES):
            line = lane + (turn * lines + left)
            hit = wanted[0] + (pick_row & 1) == line
            for step in range(1, meets):
                hit = hit | (wanted[step] + (pick_row & 1) == line)
            pick[turn, :, left : left + LANES] = jnp.where(hit, 1.0, 0.0).astype(pick.dtype)
    return left_out


def source_kernel(
    strips,
    block_col_from,
    lags_from,
    fracs_from,
    weights_from,
    coords_from,
    charge_from,
    rows_from,
    offsets_from,
    transfer_from,
    history,
    x_kernel,
    pushed_to,
    packed_to,
    later_to,
    pick_to,
    block_col,
    lags,
    fracs,
    weights,
    coords,
    charge,
    rows,
    offsets,
    transfer,
    frames,
    x_here,
    x_parts,
    s_parts,
    spread_all,
    bands,
    first_bands,
    pushed,
    packed,
    later,
    counts,
    pick,
    stage,
    sems,
):
    count_steps, comps, slab_rows, width = history.shape
    blocks = charge.shape[0]
    strip = width // strips
    spread_rows = comps * strip
    record_rows = packed.shape[1] - spread_rows
    across = packed.shape[2] // LANES
    seats = record_rows * across // FIELDS
    rounds = stage.shape[0] // (FIELDS * strips * seats)
    pairs = [
        (lags_from, lags),
        (fracs_from, fracs),
        (weights_from, weights),
        (block_col_from, block_col),
        (coords_from, coords),
        (charge_from, charge),
        (rows_from, rows),
        (offsets_from, offsets),
        (transfer_from, transfer),
    ]
    for comp in range(comps):
        pairs += [(history.at[t, comp], frames.at[t, comp]) for t in range(count_steps)]
        if comp == 0:
            pairs += [(x_kernel, x_here)]
    fetch = [
        pltpu.make_async_copy(source, target, sems.at[index])
        for index, (source, target) in enumerate(pairs)
    ]
    for copy in fetch:
        copy.start()
    stored = []

    def store(source, target):
        copy = pltpu.make_async_copy(source, target, sems.at[len(fetch) + len(stored)])
        copy.start()
        stored.append(copy)

    for copy in fetch[:3]:
        copy.wait()
    for t in range(count_steps):
        far = weights[0, t] * fracs[0, t]
        near = weights[0, t] * (1.0 - fracs[0, t])
        bands[2 * LANES * t : 2 * LANES * (t + 1)] = lag_band(lags[0, t], near, far)
        first_bands[LANES * t : LANES * (t + 1)] = bands[
            2 * LANES * t + LANES : 2 * LANES * (t + 1)
        ]

    for copy in fetch[3:9]:
        copy.wait()
    row, column, weight0, weight1 = push(
        coords, charge, rows, offsets, block_col, transfer, pushed, slab_rows
    )
    store(pushed, pushed_to)
    left_out = seat_blocks(
        strips,
        strip,
        seats,
        rounds,
        block_col,
        (row, column, weight0, weight1),
        counts,
        pick,
        stage,
    )
    store(pick, pick_to)
    is_column = lax.rem(lax.broadcasted_iota(jnp.int32, (record_rows, LANES), 0), FIELDS) == 1
    mark = jnp.where(is_column, MORE * left_out.astype(jnp.float32), 0.0)
    for turn in range(rounds):
        for partner in range(strips):
            for side in range(across):
                start = ((turn * strips + partner) * across + side) * record_rows
                value = stage[start : start + record_rows]
                lanes = slice(side * LANES, (side + 1) * LANES)
                if turn == 0:
                    packed[partner, spread_rows:, lanes] = (value + mark).astype(packed.dtype)
                else:
                    later[partner, :, lanes] = value.astype(later.dtype)
    if rounds == 2:
        store(later, later_to)
    store(packed.at[:, spread_rows:], packed_to.at[:, spread_rows:])

    for comp in range(comps):
        first = 9 + comp * (count_steps + 1)
        for copy in fetch[first : first + count_steps]:
            copy.wait()
        part_rows = min(128, slab_rows)
        for top in range(0, slab_rows, part_rows):
            for q in range(width // LANES):
                before = slice(LANES * max(q - 1, 0), LANES * (q + 1))
                steps = [
                    frames[t, comp, top : top + part_rows, before] for t in range(count_steps)
                ]
                both = jnp.dot(
                    jnp.concatenate(steps, axis=1),
                    bands[...] if q else first_bands[...],
                    preferred_element_type=jnp.float32,
                )
                high, low = split(both[:, :LANES] + both[:, LANES:])
                part = slice(comp * slab_rows + top, comp * slab_rows + top + part_rows)
                s_parts[part, LANES * q : LANES * (q + 1)] = high
                s_parts[part, width + LANES * q : width + LANES * (q + 1)] = low
                s_parts[part, 2 * width + LANES * q : 2 * width + LANES * (q + 1)] = high
        if comp == 0:
            fetch[9 + count_steps].wait()
            high, low = split(x_here[...])
            x_parts[:width] = high
            x_parts[width : 2 * width] = high
            x_parts[2 * width :] = low
        piece = 256
        for left in range(0, width, piece):
            for top in range(0, slab_rows, part_rows):
                spread = jnp.dot(
                    s_parts[comp * slab_rows + top : comp * slab_rows + top + part_rows],
                    x_parts[:, left : left + piece],
                    preferred_element_type=jnp.float32,
                )
                if strip % 16:
                    spread_all[comp, left : left + piece, top : top + part_rows] = spread.T
                    continue
                turned = spread.astype(packed.dtype).T
                for place in range(0, piece, strip):
                    packed[
                        (left + place) // strip,
                        comp * strip : (comp + 1) * strip,
                        top : top + part_rows,
                    ] = turned[place : place + strip]
        if strip % 16 == 0:
            part = slice(comp * strip, (comp + 1) * strip)
            store(packed.at[:, part], packed_to.at[:, part])
    if strip % 16:
        for partner in range(strips):
            part = slice(partner * strip, (partner + 1) * strip)
            both = jnp.concatenate([spread_all[comp, part] for comp in range(comps)], axis=0)
            packed[partner, :spread_rows, :slab_rows] = both.astype(packed.dtype)
        store(packed.at[:, :spread_rows], packed_to.at[:, :spread_rows])
    for copy in stored:
        copy.wait()


def join_kernel(slabs, spread_rows, z_kernel, arrived, kept, *sent):
    slab_rows = z_kernel.shape[0] // slabs
    extra_rows = kept.shape[0] - spread_rows if sent else 0
    total = arrived[0, :spread_rows, :slab_rows].astype(jnp.float32)
    for sender in range(1, arrived.shape[0]):
        total = total + arrived[sender, :spread_rows, :slab_rows].astype(jnp.float32)
    high, low = split(total)
    left = jnp.concatenate([high, low, high], axis=1)

    def part(slab):
        start = pl.multiple_of(slab * slab_rows, slab_rows)
        z_high, z_low = split(z_kernel[pl.ds(start, slab_rows), :])
        right = jnp.concatenate([z_high, z_high, z_low], axis=1)
        return lax.dot_general(left, right, NT_DIMS, preferred_element_type=jnp.float32)

    if sent:
        me = lax.axis_index("dom")
        sent[0][:spread_rows] = part(1 - me)
        kept[:spread_rows] = part(me)
        if extra_rows:
            records = jnp.max(arrived[:, spread_rows:].astype(jnp.float32), axis=0)
            is_column = lax.rem(lax.broadcasted_iota(jnp.int32, records.shape, 0), FIELDS) == 1
            most = jnp.max(jnp.where(is_column, records, -1.0))
            flag = jnp.full((extra_rows, slab_rows), jnp.where(most >= MORE - 1.0, 1.0, 0.0))
            sent[0][spread_rows:] = flag
            kept[spread_rows:] = flag
    else:
        for slab in range(slabs):
            kept[slab] = part(slab)


def unpack_kernel(spread_rows, arrived, records, chosen):
    senders = arrived.shape[0]
    record_rows = arrived.shape[1] - spread_rows
    across = arrived.shape[2] // LANES
    blocks = record_rows * across // FIELDS
    line = lax.broadcasted_iota(jnp.int32, (record_rows, LANES), 0)
    is_column = lax.rem(line, FIELDS) == 1
    first_line = lax.broadcasted_iota(jnp.int32, (record_rows, 1), 0)
    first_column = lax.rem(first_line, FIELDS) == 1
    masks = []
    for sender in range(senders):
        mask = jnp.float32(0.0)
        for side in range(across):
            lanes = slice(side * LANES, (side + 1) * LANES)
            value = arrived[sender, spread_rows:, lanes].astype(jnp.float32)
            value = jnp.where(is_column & (value >= MORE - 1.0), value - MORE, value)
            records[sender, side * record_rows : (side + 1) * record_rows] = value
            taken = first_column & (jnp.max(value, axis=1, keepdims=True) >= 0.0)
            seat = first_line // FIELDS + side * (record_rows // FIELDS)
            bit = jnp.left_shift(jnp.ones_like(seat), seat).astype(jnp.float32)
            mask = mask + jnp.sum(jnp.where(taken, bit, 0.0))
        masks.append(mask.astype(jnp.int32))
    records[senders] = jnp.full(records.shape[1:], -1.0, jnp.float32)
    count = jnp.int32(0)
    for sender in range(senders):
        for block in range(blocks):
            chosen[1 + count] = sender * blocks + block
            count = count + ((masks[sender] >> block) & 1)
    chosen[0] = (count + (GROUP - 1)) // GROUP
    for member in range(GROUP):
        chosen[1 + count + member] = senders * blocks


def read_group(blocks, chosen, records, group):
    where = []
    for member in range(GROUP):
        block = chosen[1 + group * GROUP + member]
        where.append((block // blocks, lax.rem(block, blocks)))

    lines = jnp.concatenate(
        [records[sender, pl.ds(own * FIELDS, FIELDS), :] for sender, own in where], axis=1
    )

    def field(index):
        return lines[index : index + 1]

    return where, field


def one_hot(index, size):
    iota = lax.broadcasted_iota(jnp.int32, (size, index.shape[1]), 0).astype(jnp.float32)
    return iota == index


def one_hot_rows(row, size):
    iota = lax.broadcasted_iota(jnp.int32, (size, row.shape[1]), 0)
    if size <= 256:
        hit = iota.astype(jnp.bfloat16) == row.astype(jnp.bfloat16)
        return jnp.where(hit, jnp.bfloat16(1.0), jnp.bfloat16(0.0))
    return jnp.where(iota.astype(jnp.float32) == row, 1.0, 0.0).astype(jnp.bfloat16)


def deposit_kernel(blocks, chosen, records, after, *refs):
    del after
    extra, (deposit, total) = refs[:-2], refs[-2:]
    strip, slab_rows = deposit.shape[1:]
    total[...] = jnp.zeros_like(total)

    def one_group(group, carry):
        _, field = read_group(blocks, chosen, records, group)
        hit = one_hot(field(1), strip)
        weighted = [jnp.where(hit, field(2 + comp), 0.0) for comp in range(2)]
        total[...] += lax.dot_general(
            one_hot_rows(field(0), slab_rows),
            jnp.concatenate(weighted, axis=0).astype(jnp.bfloat16),
            NT_DIMS,
            preferred_element_type=jnp.float32,
        )
        return carry

    lax.fori_loop(0, chosen[0], one_group, 0)
    turned = total[...].T
    for comp in range(2):
        own = turned[comp * strip : (comp + 1) * strip]
        deposit[comp] = own + extra[0][comp] if extra else own


def sample_kernel(blocks, chosen, records, *refs):
    parts, (field_out, samples, flag, found_all) = refs[:-4], refs[-4:]
    strip, slab_rows = field_out.shape[1:]
    if len(parts) == 1:
        total = parts[0][0]
        for slab in range(1, parts[0].shape[0]):
            total = total + parts[0][slab]
    else:
        total = parts[0][: 2 * strip] + parts[1][: 2 * strip]
    if len(parts) == 2 and parts[0].shape[0] > 2 * strip:
        most = jnp.max(jnp.maximum(parts[0][2 * strip :], parts[1][2 * strip :]))
        flag[0] = jnp.where(most > 0.5, 1, 0)
    else:
        flag[0] = 0
    field_out[0] = total[:strip]
    field_out[1] = total[strip:]
    rounded = total.astype(jnp.bfloat16)
    found_all[...] = jnp.zeros_like(found_all)

    def one_group(group, carry):
        where, field = read_group(blocks, chosen, records, group)
        row_hot = one_hot_rows(field(0), slab_rows)
        found = jnp.dot(rounded, row_hot, preferred_element_type=jnp.float32)
        hit = one_hot(field(1), strip)
        values = []
        for comp in range(2):
            picked = jnp.where(hit, found[comp * strip : (comp + 1) * strip], 0.0)
            values.append(jnp.sum(picked, axis=0, keepdims=True))
        values = jnp.concatenate(values, axis=0)
        for member, (sender, own) in enumerate(where):
            found_all[sender, pl.ds(2 * own, 2), :] = values[
                :, LANES * member : LANES * (member + 1)
            ]
        return carry

    lax.fori_loop(0, chosen[0], one_group, 0)
    samples[...] = found_all[: samples.shape[0]].astype(samples.dtype)


def found_for_blocks(pick, received):
    flat = received[...].reshape(received.shape[0] * received.shape[1], LANES)
    return jnp.dot(pick, flat, preferred_element_type=jnp.float32)


def more_kernel(pick, received, more):
    more[...] = found_for_blocks(pick[1], received)


def kick_kernel(pick, pushed, received, *refs):
    more, kicked = refs[:-1], refs[-1]
    blocks = pushed.shape[1]
    values = [pushed[i] for i in range(6)]
    total = found_for_blocks(pick[0], received)
    if more:
        total = total + more[0][...]
    for block in range(blocks):
        lines = [value[block : block + 1] for value in values]
        lines[5] = lines[5] + 0.5 * total[2 * block : 2 * block + 1]
        lines[1] = lines[1] + 0.5 * total[2 * block + 1 : 2 * block + 2]
        kicked[:, LANES * block : LANES * (block + 1)] = jnp.concatenate(lines, axis=0)


def local(
    coords,
    charge,
    row_index,
    block_col,
    col_offset,
    transfer_map,
    history,
    retard_index,
    retard_frac,
    retard_weight,
    z_kernel,
    x_kernel,
):
    strips = lax.axis_size("hist")
    slabs = lax.axis_size("dom")
    count_steps, comps, slab_rows, width = history.shape
    strip = width // strips
    particles = coords.shape[1]
    blocks = block_col.shape[0]
    tile = (blocks, LANES)
    spread_rows = comps * strip
    row_lanes = max(slab_rows, LANES)
    seats, second_round = seats_of(strips, slabs, blocks)
    rounds = 2 if second_round else 1
    record_rows = FIELDS * seats * LANES // row_lanes
    packed_rows = spread_rows + record_rows

    f32, bf16 = jnp.float32, jnp.bfloat16
    pushed, packed, later, pick = call(
        functools.partial(source_kernel, strips),
        (
            jax.ShapeDtypeStruct((6,) + tile, f32),
            jax.ShapeDtypeStruct((strips, packed_rows, row_lanes), bf16),
            jax.ShapeDtypeStruct((strips, record_rows, row_lanes), bf16),
            jax.ShapeDtypeStruct((rounds, comps * blocks, comps * strips * seats), bf16),
        ),
        [HBM] * 11,
        (HBM, HBM, HBM, HBM),
        [
            pltpu.SMEM((1, blocks), jnp.int32),
            pltpu.SMEM((1, count_steps), jnp.int32),
            pltpu.SMEM((1, count_steps), f32),
            pltpu.SMEM((1, count_steps), f32),
            pltpu.VMEM(coords.shape, f32),
            pltpu.VMEM(tile, f32),
            pltpu.VMEM(tile, jnp.int32),
            pltpu.VMEM(tile, jnp.int32),
            pltpu.SMEM(transfer_map.shape, f32),
            pltpu.VMEM(history.shape, bf16),
            pltpu.VMEM((width, width), f32),
            pltpu.VMEM((3 * width, width), bf16),
            pltpu.VMEM((comps * slab_rows, 3 * width), bf16),
            pltpu.VMEM((comps, width, slab_rows), f32),
            pltpu.VMEM((2 * LANES * count_steps, 2 * LANES), bf16),
            pltpu.VMEM((LANES * count_steps, 2 * LANES), bf16),
            pltpu.VMEM((6,) + tile, f32),
            pltpu.VMEM((strips, packed_rows, row_lanes), bf16),
            pltpu.VMEM((strips, record_rows, row_lanes), bf16),
            pltpu.SMEM((1, strips), jnp.int32),
            pltpu.VMEM((rounds, comps * blocks, comps * strips * seats), bf16),
            pltpu.VMEM((FIELDS * (rounds * strips * seats + 2), LANES), f32),
            pltpu.SemaphoreType.DMA((16 + comps * count_steps,)),
        ],
        flops=6 * comps * slab_rows * width * width,
        moved=history.size * 2 + x_kernel.size * 4,
        limit=LIMIT,
    )(
        block_col.reshape(1, blocks),
        retard_index.reshape(1, count_steps),
        retard_frac.reshape(1, count_steps),
        retard_weight.reshape(1, count_steps),
        coords,
        charge.reshape(tile),
        row_index.reshape(tile),
        col_offset.reshape(tile),
        transfer_map,
        history,
        x_kernel,
    )
    arrived = lax.all_to_all(packed, "hist", 0, 0, tiled=True)

    part = jax.ShapeDtypeStruct((spread_rows + (8 if second_round else 0), slab_rows), f32)
    parts = call(
        functools.partial(join_kernel, slabs, spread_rows),
        (part, part) if slabs == 2 else jax.ShapeDtypeStruct((slabs,) + part.shape, f32),
        [VMEM, VMEM],
        (VMEM, VMEM) if slabs == 2 else VMEM,
        flops=1 << 27,
        moved=1 << 20,
    )(z_kernel, arrived)
    if slabs == 2:
        kept, sent = parts
        parts = [kept, lax.ppermute(sent, "dom", [(0, 1), (1, 0)])]
    else:
        parts = [lax.all_to_all(parts, "dom", 0, 0, tiled=True)]

    def unpack(arrived, spread_rows):
        return call(
            functools.partial(unpack_kernel, spread_rows),
            (
                jax.ShapeDtypeStruct((strips + 1, FIELDS * seats, LANES), f32),
                jax.ShapeDtypeStruct((strips * seats + 16,), jnp.int32),
            ),
            [VMEM],
            (VMEM, SMEM),
            flops=1 << 20,
            moved=1 << 20,
        )(arrived)

    def sample(chosen, records, parts):
        return call(
            functools.partial(sample_kernel, seats),
            (
                jax.ShapeDtypeStruct((comps, strip, slab_rows), f32),
                jax.ShapeDtypeStruct((strips, comps * seats, LANES), bf16),
                jax.ShapeDtypeStruct((8,), jnp.int32),
            ),
            [SMEM, VMEM] + [VMEM] * len(parts),
            (VMEM, VMEM, SMEM),
            [pltpu.VMEM((strips + 1, comps * seats, LANES), f32)],
            flops=1 << 29,
            moved=1 << 20,
        )(chosen, records, *parts)

    def deposits(chosen, records, after, *extra):
        return call(
            functools.partial(deposit_kernel, seats),
            jax.ShapeDtypeStruct((comps, strip, slab_rows), f32),
            [SMEM, VMEM, HBM] + [VMEM] * len(extra),
            VMEM,
            [pltpu.VMEM((slab_rows, comps * strip), f32)],
            flops=1 << 29,
            moved=1 << 20,
        )(chosen, records, after, *extra)

    def exchange(value):
        return lax.all_to_all(value, "hist", 0, 0, tiled=True)

    records, chosen = unpack(arrived, spread_rows)
    field, samples, flag = sample(chosen, records, parts)
    more, extra = [], []
    if second_round:

        def another(later, field, pick):
            records, chosen = unpack(exchange(later), 0)
            whole = field.reshape(1, spread_rows, slab_rows)
            _, samples, _ = sample(chosen, records, [whole])
            more = call(
                more_kernel,
                jax.ShapeDtypeStruct((comps * blocks, LANES), f32),
                [VMEM, VMEM],
                VMEM,
            )(pick, exchange(samples))
            return more, deposits(chosen, records, samples)

        def nothing(later, field, pick):
            return jnp.zeros((comps * blocks, LANES), f32), jnp.zeros(field.shape, f32)

        found, left = lax.cond(flag[0] > 0, another, nothing, later, field, pick)
        more, extra = [found], [left]
    received = exchange(samples)
    deposit = deposits(chosen, records, samples, *extra)
    kicked = call(
        kick_kernel,
        jax.ShapeDtypeStruct((6, particles), f32),
        [VMEM] * (3 + len(more)),
        VMEM,
        flops=1 << 16,
        moved=1 << 18,
    )(pick, pushed, received, *more)
    return kicked, jnp.transpose(field, (0, 2, 1)), jnp.transpose(deposit, (0, 2, 1))


def solution(mesh):
    return jax.shard_map(
        local,
        mesh=mesh,
        in_specs=(
            P(None, ("dom", "hist")),
            P(("dom", "hist")),
            P(("dom", "hist")),
            P(("dom", "hist")),
            P(("dom", "hist")),
            P(),
            P("hist", None, "dom", None),
            P("hist"),
            P("hist"),
            P("hist"),
            P(None, "dom"),
            P(),
        ),
        out_specs=(P(None, ("dom", "hist")), P(None, "dom", "hist"), P(None, "dom", "hist")),
        check_vma=False,
    )
```

```python
import functools

import jax
import jax.numpy as jnp
from jax import lax
from jax.experimental import pallas as pl
from jax.experimental.pallas import tpu as pltpu
from jax.sharding import PartitionSpec as P

LANES = 128
GROUP = 16
SPAN = 16
SEATS = 8
FIELDS = 4
MORE = 64.0
NT_DIMS = (((1,), (1,)), ((), ()))
VMEM = pl.BlockSpec(memory_space=pltpu.VMEM)
SMEM = pl.BlockSpec(memory_space=pltpu.SMEM)
HBM = pl.BlockSpec(memory_space=pltpu.HBM)
LIMIT = 59 * 1024 * 1024
SMALL = 16 * 1024 * 1024


def call(kernel, out_shape, in_specs, out_specs, scratch=(), flops=0, moved=0, limit=SMALL):
    return pl.pallas_call(
        kernel,
        out_shape=out_shape,
        in_specs=in_specs,
        out_specs=out_specs,
        scratch_shapes=scratch,
        compiler_params=pltpu.CompilerParams(vmem_limit_bytes=limit),
        cost_estimate=pl.CostEstimate(flops=flops, bytes_accessed=moved, transcendentals=0),
    )


def split(value):
    high = value.astype(jnp.bfloat16)
    return high, (value - high.astype(jnp.float32)).astype(jnp.bfloat16)


def seats_of(strips, slabs, blocks):
    if strips == 16 and slabs == 2 and blocks == 2 * SEATS:
        return SEATS, True
    return blocks, False


def strips_met(strip):
    return (SPAN + strip - 2) // strip + 1


def lag_band(lag, near, far):
    row = lax.broadcasted_iota(jnp.int32, (2 * LANES, LANES), 0)
    column = lax.broadcasted_iota(jnp.int32, (2 * LANES, LANES), 1)
    behind = column + LANES - row
    weight = jnp.where(behind == lag, near, jnp.where(behind == lag + 1, far, 0.0))
    return jnp.concatenate(split(weight), axis=1)


def push(coords, transfer, wanted):
    blocks = coords.shape[1] // LANES
    u = [
        jnp.concatenate(
            [coords[i : i + 1, LANES * b : LANES * (b + 1)] for b in range(blocks)], axis=0
        )
        for i in range(6)
    ]
    total = [jnp.full((blocks, LANES), transfer[i, 0], jnp.float32) for i in wanted]
    pairs = {}
    terms = list(u)
    for first in range(6):
        for second in range(first, 6):
            pairs[first, second] = u[first] * u[second]
            terms.append(pairs[first, second])
    for first in range(6):
        for second in range(first, 6):
            for third in range(second, 6):
                terms.append(pairs[first, second] * u[third])
    for column, term in enumerate(terms):
        total = [value + transfer[i, 1 + column] * term for i, value in zip(wanted, total)]
    return total


def push_kernel(transfer, coords, after, pushed):
    del after
    for i, value in enumerate(push(coords, transfer, range(6))):
        pushed[i] = value


def particle_fields(coords, charge, rows, offsets, block_col, transfer, slab_rows):
    blocks = charge.shape[0]
    weight0 = charge[...]
    weight1 = weight0 * push(coords, transfer, [1])[0]
    row_of = lax.broadcasted_iota(jnp.int32, (blocks, LANES), 0)
    column = offsets[...]
    for b in range(blocks):
        column = column + jnp.where(row_of == b, block_col[0, b], 0)
    return lax.rem(rows[...], slab_rows), column, weight0, weight1


def seat_blocks(strips, strip, seats, rounds, block_col, fields, counts, pick, stage):
    row, column, weight0, weight1 = fields
    blocks = row.shape[0]
    nobody = rounds * strips * seats
    meets = strips_met(strip)
    stage[...] = jnp.full(stage.shape, -1.0, jnp.float32)
    for place in range(strips):
        counts[0, place] = 0
    left_out = jnp.int32(0)
    pick_row = lax.broadcasted_iota(jnp.int32, (2 * blocks, LANES), 0)
    lane = lax.broadcasted_iota(jnp.int32, (2 * blocks, LANES), 1)
    wanted = [jnp.zeros((2 * blocks, LANES), jnp.int32)] * meets
    for block in range(blocks):
        start = block_col[0, block]
        first = start // strip
        for step in range(meets):
            place = jnp.minimum(first + step, strips - 1)
            met = (first + step) * strip <= start + (SPAN - 1)
            taken = counts[0, place]
            counts[0, place] = taken + jnp.where(met, 1, 0)
            later = taken // seats
            number = (later * strips + place) * seats + lax.rem(taken, seats)
            number = jnp.where(met, number, nobody)
            left_out = jnp.maximum(left_out, jnp.where(met, later, 0))
            wanted[step] = jnp.where(pick_row >> 1 == block, 2 * number, wanted[step])
            own = column[block : block + 1] - place * strip
            own = jnp.where((own >= 0) & (own < strip), own, -1)
            pieces = [row[block : block + 1], own, weight0[block : block + 1], weight1[block : block + 1]]
            stage[pl.ds(number * FIELDS, FIELDS), :] = jnp.concatenate(
                [piece.astype(jnp.float32) for piece in pieces], axis=0
            )
    lines = 2 * strips * seats
    for turn in range(rounds):
        for left in range(0, lines, LANES):
            line = lane + (turn * lines + left)
            hit = wanted[0] + (pick_row & 1) == line
            for step in range(1, meets):
                hit = hit | (wanted[step] + (pick_row & 1) == line)
            pick[turn, :, left : left + LANES] = jnp.where(hit, 1.0, 0.0).astype(pick.dtype)
    return left_out


def source_kernel(
    strips,
    block_col_from,
    lags_from,
    fracs_from,
    weights_from,
    coords_from,
    charge_from,
    rows_from,
    offsets_from,
    transfer_from,
    history,
    x_kernel,
    packed_to,
    later_to,
    pick_to,
    block_col,
    lags,
    fracs,
    weights,
    coords,
    charge,
    rows,
    offsets,
    transfer,
    frames,
    x_here,
    x_parts,
    s_parts,
    spread_all,
    bands,
    first_bands,
    packed,
    later,
    counts,
    pick,
    stage,
    sems,
):
    count_steps, comps, slab_rows, width = history.shape
    blocks = charge.shape[0]
    strip = width // strips
    spread_rows = comps * strip
    record_rows = packed.shape[1] - spread_rows
    across = packed.shape[2] // LANES
    seats = record_rows * across // FIELDS
    rounds = stage.shape[0] // (FIELDS * strips * seats)
    pairs = [
        (lags_from, lags),
        (fracs_from, fracs),
        (weights_from, weights),
        (block_col_from, block_col),
        (coords_from, coords),
        (charge_from, charge),
        (rows_from, rows),
        (offsets_from, offsets),
        (transfer_from, transfer),
    ]
    for comp in range(comps):
        pairs += [(history.at[t, comp], frames.at[t, comp]) for t in range(count_steps)]
        if comp == 0:
            pairs += [(x_kernel, x_here)]
    fetch = [
        pltpu.make_async_copy(source, target, sems.at[index])
        for index, (source, target) in enumerate(pairs)
    ]
    for copy in fetch:
        copy.start()
    stored = []

    def store(source, target):
        copy = pltpu.make_async_copy(source, target, sems.at[len(fetch) + len(stored)])
        copy.start()
        stored.append(copy)

    for copy in fetch[:3]:
        copy.wait()
    for t in range(count_steps):
        far = weights[0, t] * fracs[0, t]
        near = weights[0, t] * (1.0 - fracs[0, t])
        bands[2 * LANES * t : 2 * LANES * (t + 1)] = lag_band(lags[0, t], near, far)
        first_bands[LANES * t : LANES * (t + 1)] = bands[
            2 * LANES * t + LANES : 2 * LANES * (t + 1)
        ]

    for copy in fetch[3:9]:
        copy.wait()
    row, column, weight0, weight1 = particle_fields(
        coords, charge, rows, offsets, block_col, transfer, slab_rows
    )
    left_out = seat_blocks(
        strips,
        strip,
        seats,
        rounds,
        block_col,
        (row, column, weight0, weight1),
        counts,
        pick,
        stage,
    )
    store(pick, pick_to)
    is_column = lax.rem(lax.broadcasted_iota(jnp.int32, (record_rows, LANES), 0), FIELDS) == 1
    mark = jnp.where(is_column, MORE * left_out.astype(jnp.float32), 0.0)
    for turn in range(rounds):
        for partner in range(strips):
            for side in range(across):
                start = ((turn * strips + partner) * across + side) * record_rows
                value = stage[start : start + record_rows]
                lanes = slice(side * LANES, (side + 1) * LANES)
                if turn == 0:
                    packed[partner, spread_rows:, lanes] = (value + mark).astype(packed.dtype)
                else:
                    later[partner, :, lanes] = value.astype(later.dtype)
    if rounds == 2:
        store(later, later_to)
    store(packed.at[:, spread_rows:], packed_to.at[:, spread_rows:])

    for comp in range(comps):
        first = 9 + comp * (count_steps + 1)
        for copy in fetch[first : first + count_steps]:
            copy.wait()
        here = slice(comp * slab_rows, (comp + 1) * slab_rows)
        part_rows = min(128, slab_rows)
        for top in range(0, slab_rows, part_rows):
            for q in range(width // LANES):
                before = slice(LANES * max(q - 1, 0), LANES * (q + 1))
                steps = [
                    frames[t, comp, top : top + part_rows, before] for t in range(count_steps)
                ]
                both = jnp.dot(
                    jnp.concatenate(steps, axis=1),
                    bands[...] if q else first_bands[...],
                    preferred_element_type=jnp.float32,
                )
                high, low = split(both[:, :LANES] + both[:, LANES:])
                part = slice(comp * slab_rows + top, comp * slab_rows + top + part_rows)
                s_parts[part, LANES * q : LANES * (q + 1)] = high
                s_parts[part, width + LANES * q : width + LANES * (q + 1)] = low
                s_parts[part, 2 * width + LANES * q : 2 * width + LANES * (q + 1)] = high
        if comp == 0:
            fetch[9 + count_steps].wait()
            high, low = split(x_here[...])
            x_parts[:width] = high
            x_parts[width : 2 * width] = high
            x_parts[2 * width :] = low
        spread = jnp.dot(s_parts[here], x_parts[...], preferred_element_type=jnp.float32)
        if strip % 16 == 0:
            turned = spread.astype(packed.dtype).T
            part = slice(comp * strip, (comp + 1) * strip)
            for partner in range(strips):
                packed[partner, part, :slab_rows] = turned[
                    partner * strip : (partner + 1) * strip
                ]
            store(packed.at[:, part], packed_to.at[:, part])
        else:
            spread_all[comp] = spread.T
    if strip % 16:
        for partner in range(strips):
            part = slice(partner * strip, (partner + 1) * strip)
            both = jnp.concatenate([spread_all[comp, part] for comp in range(comps)], axis=0)
            packed[partner, :spread_rows, :slab_rows] = both.astype(packed.dtype)
        store(packed.at[:, :spread_rows], packed_to.at[:, :spread_rows])
    for copy in stored:
        copy.wait()


def join_kernel(slabs, spread_rows, z_kernel, arrived, kept, *sent):
    slab_rows = z_kernel.shape[0] // slabs
    extra_rows = kept.shape[0] - spread_rows if sent else 0
    total = arrived[0, :spread_rows, :slab_rows].astype(jnp.float32)
    for sender in range(1, arrived.shape[0]):
        total = total + arrived[sender, :spread_rows, :slab_rows].astype(jnp.float32)
    high, low = split(total)
    left = jnp.concatenate([high, low, high], axis=1)

    def part(slab):
        start = pl.multiple_of(slab * slab_rows, slab_rows)
        z_high, z_low = split(z_kernel[pl.ds(start, slab_rows), :])
        right = jnp.concatenate([z_high, z_high, z_low], axis=1)
        return lax.dot_general(left, right, NT_DIMS, preferred_element_type=jnp.float32)

    if sent:
        me = lax.axis_index("dom")
        sent[0][:spread_rows] = part(1 - me)
        kept[:spread_rows] = part(me)
        if extra_rows:
            records = jnp.max(arrived[:, spread_rows:].astype(jnp.float32), axis=0)
            is_column = lax.rem(lax.broadcasted_iota(jnp.int32, records.shape, 0), FIELDS) == 1
            most = jnp.max(jnp.where(is_column, records, -1.0))
            flag = jnp.full((extra_rows, slab_rows), jnp.where(most >= MORE - 1.0, 1.0, 0.0))
            sent[0][spread_rows:] = flag
            kept[spread_rows:] = flag
    else:
        for slab in range(slabs):
            kept[slab] = part(slab)


def unpack_kernel(spread_rows, arrived, records, chosen):
    senders = arrived.shape[0]
    record_rows = arrived.shape[1] - spread_rows
    across = arrived.shape[2] // LANES
    blocks = record_rows * across // FIELDS
    line = lax.broadcasted_iota(jnp.int32, (record_rows, LANES), 0)
    is_column = lax.rem(line, FIELDS) == 1
    first_line = lax.broadcasted_iota(jnp.int32, (record_rows, 1), 0)
    first_column = lax.rem(first_line, FIELDS) == 1
    masks = []
    for sender in range(senders):
        mask = jnp.float32(0.0)
        for side in range(across):
            lanes = slice(side * LANES, (side + 1) * LANES)
            value = arrived[sender, spread_rows:, lanes].astype(jnp.float32)
            value = jnp.where(is_column & (value >= MORE - 1.0), value - MORE, value)
            records[sender, side * record_rows : (side + 1) * record_rows] = value
            taken = first_column & (jnp.max(value, axis=1, keepdims=True) >= 0.0)
            seat = first_line // FIELDS + side * (record_rows // FIELDS)
            bit = jnp.left_shift(jnp.ones_like(seat), seat).astype(jnp.float32)
            mask = mask + jnp.sum(jnp.where(taken, bit, 0.0))
        masks.append(mask.astype(jnp.int32))
    records[senders] = jnp.full(records.shape[1:], -1.0, jnp.float32)
    count = jnp.int32(0)
    for sender in range(senders):
        for block in range(blocks):
            chosen[1 + count] = sender * blocks + block
            count = count + ((masks[sender] >> block) & 1)
    chosen[0] = (count + (GROUP - 1)) // GROUP
    for member in range(GROUP):
        chosen[1 + count + member] = senders * blocks


def read_group(blocks, chosen, records, group):
    where = []
    for member in range(GROUP):
        block = chosen[1 + group * GROUP + member]
        where.append((block // blocks, lax.rem(block, blocks)))

    lines = jnp.concatenate(
        [records[sender, pl.ds(own * FIELDS, FIELDS), :] for sender, own in where], axis=1
    )

    def field(index):
        return lines[index : index + 1]

    return where, field


def one_hot(index, size):
    iota = lax.broadcasted_iota(jnp.int32, (size, index.shape[1]), 0).astype(jnp.float32)
    return iota == index


def one_hot_rows(row, size):
    iota = lax.broadcasted_iota(jnp.int32, (size, row.shape[1]), 0)
    if size <= 256:
        hit = iota.astype(jnp.bfloat16) == row.astype(jnp.bfloat16)
        return jnp.where(hit, jnp.bfloat16(1.0), jnp.bfloat16(0.0))
    return jnp.where(iota.astype(jnp.float32) == row, 1.0, 0.0).astype(jnp.bfloat16)


def deposit_kernel(blocks, chosen, records, after, *refs):
    del after
    extra, (deposit, total) = refs[:-2], refs[-2:]
    strip, slab_rows = deposit.shape[1:]
    total[...] = jnp.zeros_like(total)

    def one_group(group, carry):
        _, field = read_group(blocks, chosen, records, group)
        hit = one_hot(field(1), strip)
        weighted = [jnp.where(hit, field(2 + comp), 0.0) for comp in range(2)]
        total[...] += lax.dot_general(
            one_hot_rows(field(0), slab_rows),
            jnp.concatenate(weighted, axis=0).astype(jnp.bfloat16),
            NT_DIMS,
            preferred_element_type=jnp.float32,
        )
        return carry

    lax.fori_loop(0, chosen[0], one_group, 0)
    turned = total[...].T
    for comp in range(2):
        own = turned[comp * strip : (comp + 1) * strip]
        deposit[comp] = own + extra[0][comp] if extra else own


def sample_kernel(blocks, chosen, records, *refs):
    parts, (field_out, samples, flag, found_all) = refs[:-4], refs[-4:]
    strip, slab_rows = field_out.shape[1:]
    if len(parts) == 1:
        total = parts[0][0]
        for slab in range(1, parts[0].shape[0]):
            total = total + parts[0][slab]
    else:
        total = parts[0][: 2 * strip] + parts[1][: 2 * strip]
    if len(parts) == 2 and parts[0].shape[0] > 2 * strip:
        most = jnp.max(jnp.maximum(parts[0][2 * strip :], parts[1][2 * strip :]))
        flag[0] = jnp.where(most > 0.5, 1, 0)
    else:
        flag[0] = 0
    field_out[0] = total[:strip]
    field_out[1] = total[strip:]
    rounded = total.astype(jnp.bfloat16)
    found_all[...] = jnp.zeros_like(found_all)

    def one_group(group, carry):
        where, field = read_group(blocks, chosen, records, group)
        row_hot = one_hot_rows(field(0), slab_rows)
        found = jnp.dot(rounded, row_hot, preferred_element_type=jnp.float32)
        hit = one_hot(field(1), strip)
        values = []
        for comp in range(2):
            picked = jnp.where(hit, found[comp * strip : (comp + 1) * strip], 0.0)
            values.append(jnp.sum(picked, axis=0, keepdims=True))
        values = jnp.concatenate(values, axis=0)
        for member, (sender, own) in enumerate(where):
            found_all[sender, pl.ds(2 * own, 2), :] = values[
                :, LANES * member : LANES * (member + 1)
            ]
        return carry

    lax.fori_loop(0, chosen[0], one_group, 0)
    samples[...] = found_all[: samples.shape[0]].astype(samples.dtype)


def found_for_blocks(pick, received):
    flat = received[...].reshape(received.shape[0] * received.shape[1], LANES)
    return jnp.dot(pick, flat, preferred_element_type=jnp.float32)


def more_kernel(pick, received, more):
    more[...] = found_for_blocks(pick[1], received)


def kick_kernel(pick, pushed, received, *refs):
    more, kicked = refs[:-1], refs[-1]
    blocks = pushed.shape[1]
    values = [pushed[i] for i in range(6)]
    total = found_for_blocks(pick[0], received)
    if more:
        total = total + more[0][...]
    for block in range(blocks):
        lines = [value[block : block + 1] for value in values]
        lines[5] = lines[5] + 0.5 * total[2 * block : 2 * block + 1]
        lines[1] = lines[1] + 0.5 * total[2 * block + 1 : 2 * block + 2]
        kicked[:, LANES * block : LANES * (block + 1)] = jnp.concatenate(lines, axis=0)


def local(
    coords,
    charge,
    row_index,
    block_col,
    col_offset,
    transfer_map,
    history,
    retard_index,
    retard_frac,
    retard_weight,
    z_kernel,
    x_kernel,
):
    strips = lax.axis_size("hist")
    slabs = lax.axis_size("dom")
    count_steps, comps, slab_rows, width = history.shape
    strip = width // strips
    particles = coords.shape[1]
    blocks = block_col.shape[0]
    tile = (blocks, LANES)
    spread_rows = comps * strip
    row_lanes = max(slab_rows, LANES)
    seats, second_round = seats_of(strips, slabs, blocks)
    rounds = 2 if second_round else 1
    record_rows = FIELDS * seats * LANES // row_lanes
    packed_rows = spread_rows + record_rows

    f32, bf16 = jnp.float32, jnp.bfloat16
    packed, later, pick = call(
        functools.partial(source_kernel, strips),
        (
            jax.ShapeDtypeStruct((strips, packed_rows, row_lanes), bf16),
            jax.ShapeDtypeStruct((strips, record_rows, row_lanes), bf16),
            jax.ShapeDtypeStruct((rounds, comps * blocks, comps * strips * seats), bf16),
        ),
        [HBM] * 11,
        (HBM, HBM, HBM),
        [
            pltpu.SMEM((1, blocks), jnp.int32),
            pltpu.SMEM((1, count_steps), jnp.int32),
            pltpu.SMEM((1, count_steps), f32),
            pltpu.SMEM((1, count_steps), f32),
            pltpu.VMEM(coords.shape, f32),
            pltpu.VMEM(tile, f32),
            pltpu.VMEM(tile, jnp.int32),
            pltpu.VMEM(tile, jnp.int32),
            pltpu.SMEM(transfer_map.shape, f32),
            pltpu.VMEM(history.shape, bf16),
            pltpu.VMEM((width, width), f32),
            pltpu.VMEM((3 * width, width), bf16),
            pltpu.VMEM((comps * slab_rows, 3 * width), bf16),
            pltpu.VMEM((comps, width, slab_rows), f32),
            pltpu.VMEM((2 * LANES * count_steps, 2 * LANES), bf16),
            pltpu.VMEM((LANES * count_steps, 2 * LANES), bf16),
            pltpu.VMEM((strips, packed_rows, row_lanes), bf16),
            pltpu.VMEM((strips, record_rows, row_lanes), bf16),
            pltpu.SMEM((1, strips), jnp.int32),
            pltpu.VMEM((rounds, comps * blocks, comps * strips * seats), bf16),
            pltpu.VMEM((FIELDS * (rounds * strips * seats + 2), LANES), f32),
            pltpu.SemaphoreType.DMA((16 + comps * count_steps,)),
        ],
        flops=6 * comps * slab_rows * width * width,
        moved=history.size * 2 + x_kernel.size * 4,
        limit=LIMIT,
    )(
        block_col.reshape(1, blocks),
        retard_index.reshape(1, count_steps),
        retard_frac.reshape(1, count_steps),
        retard_weight.reshape(1, count_steps),
        coords,
        charge.reshape(tile),
        row_index.reshape(tile),
        col_offset.reshape(tile),
        transfer_map,
        history,
        x_kernel,
    )
    arrived = lax.all_to_all(packed, "hist", 0, 0, tiled=True)

    part = jax.ShapeDtypeStruct((spread_rows + (8 if second_round else 0), slab_rows), f32)
    parts = call(
        functools.partial(join_kernel, slabs, spread_rows),
        (part, part) if slabs == 2 else jax.ShapeDtypeStruct((slabs,) + part.shape, f32),
        [VMEM, VMEM],
        (VMEM, VMEM) if slabs == 2 else VMEM,
        flops=1 << 27,
        moved=1 << 20,
    )(z_kernel, arrived)
    if slabs == 2:
        kept, sent = parts
        parts = [kept, lax.ppermute(sent, "dom", [(0, 1), (1, 0)])]
    else:
        parts = [lax.all_to_all(parts, "dom", 0, 0, tiled=True)]

    def unpack(arrived, spread_rows):
        return call(
            functools.partial(unpack_kernel, spread_rows),
            (
                jax.ShapeDtypeStruct((strips + 1, FIELDS * seats, LANES), f32),
                jax.ShapeDtypeStruct((strips * seats + 32,), jnp.int32),
            ),
            [VMEM],
            (VMEM, SMEM),
            flops=1 << 20,
            moved=1 << 20,
        )(arrived)

    def sample(chosen, records, parts):
        return call(
            functools.partial(sample_kernel, seats),
            (
                jax.ShapeDtypeStruct((comps, strip, slab_rows), f32),
                jax.ShapeDtypeStruct((strips, comps * seats, LANES), bf16),
                jax.ShapeDtypeStruct((8,), jnp.int32),
            ),
            [SMEM, VMEM] + [VMEM] * len(parts),
            (VMEM, VMEM, SMEM),
            [pltpu.VMEM((strips + 1, comps * seats, LANES), f32)],
            flops=1 << 29,
            moved=1 << 20,
        )(chosen, records, *parts)

    def deposits(chosen, records, after, *extra):
        return call(
            functools.partial(deposit_kernel, seats),
            jax.ShapeDtypeStruct((comps, strip, slab_rows), f32),
            [SMEM, VMEM, HBM] + [VMEM] * len(extra),
            VMEM,
            [pltpu.VMEM((slab_rows, comps * strip), f32)],
            flops=1 << 29,
            moved=1 << 20,
        )(chosen, records, after, *extra)

    def exchange(value):
        return lax.all_to_all(value, "hist", 0, 0, tiled=True)

    records, chosen = unpack(arrived, spread_rows)
    field, samples, flag = sample(chosen, records, parts)
    more, extra = [], []
    if second_round:

        def another(later, field, pick):
            records, chosen = unpack(exchange(later), 0)
            whole = field.reshape(1, spread_rows, slab_rows)
            _, samples, _ = sample(chosen, records, [whole])
            more = call(
                more_kernel,
                jax.ShapeDtypeStruct((comps * blocks, LANES), f32),
                [VMEM, VMEM],
                VMEM,
            )(pick, exchange(samples))
            return more, deposits(chosen, records, samples)

        def nothing(later, field, pick):
            return jnp.zeros((comps * blocks, LANES), f32), jnp.zeros(field.shape, f32)

        found, left = lax.cond(flag[0] > 0, another, nothing, later, field, pick)
        more, extra = [found], [left]
    received = exchange(samples)
    deposit = deposits(chosen, records, samples, *extra)
    pushed = call(
        push_kernel,
        jax.ShapeDtypeStruct((6,) + tile, f32),
        [SMEM, VMEM, HBM],
        VMEM,
        flops=1200 * particles,
        moved=1 << 18,
    )(transfer_map, coords, samples)
    kicked = call(
        kick_kernel,
        jax.ShapeDtypeStruct((6, particles), f32),
        [VMEM] * (3 + len(more)),
        VMEM,
        flops=1 << 16,
        moved=1 << 18,
    )(pick, pushed, received, *more)
    return kicked, jnp.transpose(field, (0, 2, 1)), jnp.transpose(deposit, (0, 2, 1))


def solution(mesh):
    return jax.shard_map(
        local,
        mesh=mesh,
        in_specs=(
            P(None, ("dom", "hist")),
            P(("dom", "hist")),
            P(("dom", "hist")),
            P(("dom", "hist")),
            P(("dom", "hist")),
            P(),
            P("hist", None, "dom", None),
            P("hist"),
            P("hist"),
            P("hist"),
            P(None, "dom"),
            P(),
        ),
        out_specs=(P(None, ("dom", "hist")), P(None, "dom", "hist"), P(None, "dom", "hist")),
        check_vma=False,
    )
```

```python
import functools

import jax
import jax.numpy as jnp
from jax import lax
from jax.experimental import pallas as pl
from jax.experimental.pallas import tpu as pltpu
from jax.sharding import PartitionSpec as P

LANES = 128
GROUP = 16
SPAN = 16
SEATS = 8
FIELDS = 4
MORE = 64.0
NT_DIMS = (((1,), (1,)), ((), ()))
VMEM = pl.BlockSpec(memory_space=pltpu.VMEM)
SMEM = pl.BlockSpec(memory_space=pltpu.SMEM)
HBM = pl.BlockSpec(memory_space=pltpu.HBM)
LIMIT = 59 * 1024 * 1024
SMALL = 16 * 1024 * 1024


def call(kernel, out_shape, in_specs, out_specs, scratch=(), flops=0, moved=0, limit=SMALL):
    return pl.pallas_call(
        kernel,
        out_shape=out_shape,
        in_specs=in_specs,
        out_specs=out_specs,
        scratch_shapes=scratch,
        compiler_params=pltpu.CompilerParams(vmem_limit_bytes=limit),
        cost_estimate=pl.CostEstimate(flops=flops, bytes_accessed=moved, transcendentals=0),
    )


def split(value):
    high = value.astype(jnp.bfloat16)
    return high, (value - high.astype(jnp.float32)).astype(jnp.bfloat16)


def seats_of(strips, slabs, blocks):
    if strips == 16 and slabs == 2 and blocks == 2 * SEATS:
        return SEATS, True
    return blocks, False


def strips_met(strip):
    return (SPAN + strip - 2) // strip + 1


def lag_band(lag, near, far):
    row = lax.broadcasted_iota(jnp.int32, (2 * LANES, LANES), 0)
    column = lax.broadcasted_iota(jnp.int32, (2 * LANES, LANES), 1)
    behind = column + LANES - row
    weight = jnp.where(behind == lag, near, jnp.where(behind == lag + 1, far, 0.0))
    return jnp.concatenate(split(weight), axis=1)


def push(coords, transfer, wanted):
    blocks = coords.shape[1] // LANES
    u = [
        jnp.concatenate(
            [coords[i : i + 1, LANES * b : LANES * (b + 1)] for b in range(blocks)], axis=0
        )
        for i in range(6)
    ]
    total = [jnp.full((blocks, LANES), transfer[i, 0], jnp.float32) for i in wanted]
    pairs = {}
    terms = list(u)
    for first in range(6):
        for second in range(first, 6):
            pairs[first, second] = u[first] * u[second]
            terms.append(pairs[first, second])
    for first in range(6):
        for second in range(first, 6):
            for third in range(second, 6):
                terms.append(pairs[first, second] * u[third])
    for column, term in enumerate(terms):
        total = [value + transfer[i, 1 + column] * term for i, value in zip(wanted, total)]
    return total


def push_kernel(transfer, coords, after, pushed):
    del after
    for i, value in enumerate(push(coords, transfer, range(6))):
        pushed[i] = value


def particle_fields(coords, charge, rows, offsets, block_col, transfer, slab_rows):
    blocks = charge.shape[0]
    weight0 = charge[...]
    weight1 = weight0 * push(coords, transfer, [1])[0]
    row_of = lax.broadcasted_iota(jnp.int32, (blocks, LANES), 0)
    column = offsets[...]
    for b in range(blocks):
        column = column + jnp.where(row_of == b, block_col[0, b], 0)
    return lax.rem(rows[...], slab_rows), column, weight0, weight1


def seat_blocks(strips, strip, seats, rounds, block_col, fields, counts, pick, stage):
    row, column, weight0, weight1 = fields
    blocks = row.shape[0]
    nobody = rounds * strips * seats
    meets = strips_met(strip)
    stage[...] = jnp.full(stage.shape, -1.0, jnp.float32)
    for place in range(strips):
        counts[0, place] = 0
    left_out = jnp.int32(0)
    pick_row = lax.broadcasted_iota(jnp.int32, (2 * blocks, LANES), 0)
    lane = lax.broadcasted_iota(jnp.int32, (2 * blocks, LANES), 1)
    wanted = [jnp.zeros((2 * blocks, LANES), jnp.int32)] * meets
    is_column = lax.broadcasted_iota(jnp.int32, (FIELDS, LANES), 0) == 1
    fields = [field.astype(jnp.float32) for field in (row, column, weight0, weight1)]
    for block in range(blocks):
        tile = jnp.concatenate([field[block : block + 1] for field in fields], axis=0)
        start = block_col[0, block]
        first = start // strip
        for step in range(meets):
            place = jnp.minimum(first + step, strips - 1)
            met = (first + step) * strip <= start + (SPAN - 1)
            taken = counts[0, place]
            counts[0, place] = taken + jnp.where(met, 1, 0)
            later = taken // seats
            number = (later * strips + place) * seats + lax.rem(taken, seats)
            number = jnp.where(met, number, nobody)
            left_out = jnp.maximum(left_out, jnp.where(met, later, 0))
            wanted[step] = jnp.where(pick_row >> 1 == block, 2 * number, wanted[step])
            own = tile - (place * strip).astype(jnp.float32)
            own = jnp.where((own >= 0.0) & (own < strip), own, -1.0)
            stage[pl.ds(number * FIELDS, FIELDS), :] = jnp.where(is_column, own, tile)
    lines = 2 * strips * seats
    for turn in range(rounds):
        for left in range(0, lines, LANES):
            line = lane + (turn * lines + left)
            hit = wanted[0] + (pick_row & 1) == line
            for step in range(1, meets):
                hit = hit | (wanted[step] + (pick_row & 1) == line)
            pick[turn, :, left : left + LANES] = jnp.where(hit, 1.0, 0.0).astype(pick.dtype)
    return left_out


def source_kernel(
    strips,
    block_col_from,
    lags_from,
    fracs_from,
    weights_from,
    coords_from,
    charge_from,
    rows_from,
    offsets_from,
    transfer_from,
    history,
    x_kernel,
    packed_to,
    later_to,
    pick_to,
    block_col,
    lags,
    fracs,
    weights,
    coords,
    charge,
    rows,
    offsets,
    transfer,
    frames,
    x_here,
    x_parts,
    s_parts,
    spread_all,
    bands,
    first_bands,
    packed,
    later,
    counts,
    pick,
    stage,
    sems,
):
    count_steps, comps, slab_rows, width = history.shape
    blocks = charge.shape[0]
    strip = width // strips
    spread_rows = comps * strip
    record_rows = packed.shape[1] - spread_rows
    across = packed.shape[2] // LANES
    seats = record_rows * across // FIELDS
    rounds = stage.shape[0] // (FIELDS * strips * seats)
    pairs = [
        (lags_from, lags),
        (fracs_from, fracs),
        (weights_from, weights),
        (block_col_from, block_col),
        (coords_from, coords),
        (charge_from, charge),
        (rows_from, rows),
        (offsets_from, offsets),
        (transfer_from, transfer),
    ]
    for comp in range(comps):
        pairs += [(history.at[t, comp], frames.at[t, comp]) for t in range(count_steps)]
        if comp == 0:
            pairs += [(x_kernel, x_here)]
    fetch = [
        pltpu.make_async_copy(source, target, sems.at[index])
        for index, (source, target) in enumerate(pairs)
    ]
    for copy in fetch:
        copy.start()
    stored = []

    def store(source, target):
        copy = pltpu.make_async_copy(source, target, sems.at[len(fetch) + len(stored)])
        copy.start()
        stored.append(copy)

    for copy in fetch[:9]:
        copy.wait()
    for t in range(count_steps):
        far = weights[0, t] * fracs[0, t]
        near = weights[0, t] * (1.0 - fracs[0, t])
        bands[2 * LANES * t : 2 * LANES * (t + 1)] = lag_band(lags[0, t], near, far)
        first_bands[LANES * t : LANES * (t + 1)] = bands[
            2 * LANES * t + LANES : 2 * LANES * (t + 1)
        ]

    row, column, weight0, weight1 = particle_fields(
        coords, charge, rows, offsets, block_col, transfer, slab_rows
    )
    left_out = seat_blocks(
        strips,
        strip,
        seats,
        rounds,
        block_col,
        (row, column, weight0, weight1),
        counts,
        pick,
        stage,
    )
    is_column = lax.rem(lax.broadcasted_iota(jnp.int32, (record_rows, LANES), 0), FIELDS) == 1
    mark = jnp.where(is_column, MORE * left_out.astype(jnp.float32), 0.0)
    for turn in range(rounds):
        for partner in range(strips):
            for side in range(across):
                start = ((turn * strips + partner) * across + side) * record_rows
                value = stage[start : start + record_rows]
                lanes = slice(side * LANES, (side + 1) * LANES)
                if turn == 0:
                    packed[partner, spread_rows:, lanes] = (value + mark).astype(packed.dtype)
                else:
                    later[partner, :, lanes] = value.astype(later.dtype)

    for comp in range(comps):
        first = 9 + comp * (count_steps + 1)
        for copy in fetch[first : first + count_steps]:
            copy.wait()
        here = slice(comp * slab_rows, (comp + 1) * slab_rows)
        part_rows = min(128, slab_rows)
        for top in range(0, slab_rows, part_rows):
            for q in range(width // LANES):
                before = slice(LANES * max(q - 1, 0), LANES * (q + 1))
                steps = [
                    frames[t, comp, top : top + part_rows, before] for t in range(count_steps)
                ]
                both = jnp.dot(
                    jnp.concatenate(steps, axis=1),
                    bands[...] if q else first_bands[...],
                    preferred_element_type=jnp.float32,
                )
                high, low = split(both[:, :LANES] + both[:, LANES:])
                part = slice(comp * slab_rows + top, comp * slab_rows + top + part_rows)
                s_parts[part, LANES * q : LANES * (q + 1)] = high
                s_parts[part, width + LANES * q : width + LANES * (q + 1)] = low
                s_parts[part, 2 * width + LANES * q : 2 * width + LANES * (q + 1)] = high
        if comp == 0:
            store(pick, pick_to)
            if rounds == 2:
                store(later, later_to)
            store(packed.at[:, spread_rows:], packed_to.at[:, spread_rows:])
            fetch[9 + count_steps].wait()
            high, low = split(x_here[...])
            x_parts[:width] = high
            x_parts[width : 2 * width] = high
            x_parts[2 * width :] = low
        spread = jnp.dot(s_parts[here], x_parts[...], preferred_element_type=jnp.float32)
        if strip % 16 == 0:
            turned = spread.astype(packed.dtype).T
            part = slice(comp * strip, (comp + 1) * strip)
            for partner in range(strips):
                packed[partner, part, :slab_rows] = turned[
                    partner * strip : (partner + 1) * strip
                ]
            store(packed.at[:, part], packed_to.at[:, part])
        else:
            spread_all[comp] = spread.T
    if strip % 16:
        for partner in range(strips):
            part = slice(partner * strip, (partner + 1) * strip)
            both = jnp.concatenate([spread_all[comp, part] for comp in range(comps)], axis=0)
            packed[partner, :spread_rows, :slab_rows] = both.astype(packed.dtype)
        store(packed.at[:, :spread_rows], packed_to.at[:, :spread_rows])
    for copy in stored:
        copy.wait()


def join_kernel(slabs, spread_rows, z_kernel, arrived, kept, *sent):
    slab_rows = z_kernel.shape[0] // slabs
    extra_rows = kept.shape[0] - spread_rows if sent else 0
    total = arrived[0, :spread_rows, :slab_rows].astype(jnp.float32)
    for sender in range(1, arrived.shape[0]):
        total = total + arrived[sender, :spread_rows, :slab_rows].astype(jnp.float32)
    high, low = split(total)
    left = jnp.concatenate([high, low, high], axis=1)

    def part(slab):
        start = pl.multiple_of(slab * slab_rows, slab_rows)
        z_high, z_low = split(z_kernel[pl.ds(start, slab_rows), :])
        right = jnp.concatenate([z_high, z_high, z_low], axis=1)
        return lax.dot_general(left, right, NT_DIMS, preferred_element_type=jnp.float32)

    if sent:
        me = lax.axis_index("dom")
        sent[0][:spread_rows] = part(1 - me)
        kept[:spread_rows] = part(me)
        if extra_rows:
            records = jnp.max(arrived[:, spread_rows:].astype(jnp.float32), axis=0)
            is_column = lax.rem(lax.broadcasted_iota(jnp.int32, records.shape, 0), FIELDS) == 1
            most = jnp.max(jnp.where(is_column, records, -1.0))
            flag = jnp.full((extra_rows, slab_rows), jnp.where(most >= MORE - 1.0, 1.0, 0.0))
            sent[0][spread_rows:] = flag
            kept[spread_rows:] = flag
    else:
        for slab in range(slabs):
            kept[slab] = part(slab)


def unpack_kernel(spread_rows, arrived, records, chosen):
    senders = arrived.shape[0]
    record_rows = arrived.shape[1] - spread_rows
    across = arrived.shape[2] // LANES
    blocks = record_rows * across // FIELDS
    line = lax.broadcasted_iota(jnp.int32, (record_rows, LANES), 0)
    is_column = lax.rem(line, FIELDS) == 1
    first_line = lax.broadcasted_iota(jnp.int32, (record_rows, 1), 0)
    first_column = lax.rem(first_line, FIELDS) == 1
    masks = []
    for sender in range(senders):
        mask = jnp.float32(0.0)
        for side in range(across):
            lanes = slice(side * LANES, (side + 1) * LANES)
            value = arrived[sender, spread_rows:, lanes].astype(jnp.float32)
            value = jnp.where(is_column & (value >= MORE - 1.0), value - MORE, value)
            records[sender, side * record_rows : (side + 1) * record_rows] = value
            taken = first_column & (jnp.max(value, axis=1, keepdims=True) >= 0.0)
            seat = first_line // FIELDS + side * (record_rows // FIELDS)
            bit = jnp.left_shift(jnp.ones_like(seat), seat).astype(jnp.float32)
            mask = mask + jnp.sum(jnp.where(taken, bit, 0.0))
        masks.append(mask.astype(jnp.int32))
    records[senders] = jnp.full(records.shape[1:], -1.0, jnp.float32)
    count = jnp.int32(0)
    for sender in range(senders):
        for block in range(blocks):
            chosen[1 + count] = sender * blocks + block
            count = count + ((masks[sender] >> block) & 1)
    chosen[0] = (count + (GROUP - 1)) // GROUP
    for member in range(GROUP):
        chosen[1 + count + member] = senders * blocks


def read_group(blocks, chosen, records, group):
    where = []
    for member in range(GROUP):
        block = chosen[1 + group * GROUP + member]
        where.append((block // blocks, lax.rem(block, blocks)))

    lines = jnp.concatenate(
        [records[sender, pl.ds(own * FIELDS, FIELDS), :] for sender, own in where], axis=1
    )

    def field(index):
        return lines[index : index + 1]

    return where, field


def one_hot(index, size):
    iota = lax.broadcasted_iota(jnp.int32, (size, index.shape[1]), 0).astype(jnp.float32)
    return iota == index


def one_hot_rows(row, size):
    iota = lax.broadcasted_iota(jnp.int32, (size, row.shape[1]), 0)
    if size <= 256:
        hit = iota.astype(jnp.bfloat16) == row.astype(jnp.bfloat16)
        return jnp.where(hit, jnp.bfloat16(1.0), jnp.bfloat16(0.0))
    return jnp.where(iota.astype(jnp.float32) == row, 1.0, 0.0).astype(jnp.bfloat16)


def deposit_kernel(blocks, chosen, records, after, *refs):
    del after
    extra, (deposit, total) = refs[:-2], refs[-2:]
    strip, slab_rows = deposit.shape[1:]
    total[...] = jnp.zeros_like(total)

    def one_group(group, carry):
        _, field = read_group(blocks, chosen, records, group)
        hit = one_hot(field(1), strip)
        weighted = [jnp.where(hit, field(2 + comp), 0.0) for comp in range(2)]
        total[...] += lax.dot_general(
            one_hot_rows(field(0), slab_rows),
            jnp.concatenate(weighted, axis=0).astype(jnp.bfloat16),
            NT_DIMS,
            preferred_element_type=jnp.float32,
        )
        return carry

    lax.fori_loop(0, chosen[0], one_group, 0)
    turned = total[...].T
    for comp in range(2):
        own = turned[comp * strip : (comp + 1) * strip]
        deposit[comp] = own + extra[0][comp] if extra else own


def sample_kernel(blocks, chosen, records, *refs):
    parts, (field_out, samples, flag, found_all) = refs[:-4], refs[-4:]
    strip, slab_rows = field_out.shape[1:]
    if len(parts) == 1:
        total = parts[0][0]
        for slab in range(1, parts[0].shape[0]):
            total = total + parts[0][slab]
    else:
        total = parts[0][: 2 * strip] + parts[1][: 2 * strip]
    if len(parts) == 2 and parts[0].shape[0] > 2 * strip:
        most = jnp.max(jnp.maximum(parts[0][2 * strip :], parts[1][2 * strip :]))
        flag[0] = jnp.where(most > 0.5, 1, 0)
    else:
        flag[0] = 0
    field_out[0] = total[:strip]
    field_out[1] = total[strip:]
    rounded = total.astype(jnp.bfloat16)
    found_all[...] = jnp.zeros_like(found_all)

    def one_group(group, carry):
        where, field = read_group(blocks, chosen, records, group)
        row_hot = one_hot_rows(field(0), slab_rows)
        found = jnp.dot(rounded, row_hot, preferred_element_type=jnp.float32)
        hit = one_hot(field(1), strip)
        values = []
        for comp in range(2):
            picked = jnp.where(hit, found[comp * strip : (comp + 1) * strip], 0.0)
            values.append(jnp.sum(picked, axis=0, keepdims=True))
        values = jnp.concatenate(values, axis=0)
        for member, (sender, own) in enumerate(where):
            found_all[sender, pl.ds(2 * own, 2), :] = values[
                :, LANES * member : LANES * (member + 1)
            ]
        return carry

    lax.fori_loop(0, chosen[0], one_group, 0)
    samples[...] = found_all[: samples.shape[0]].astype(samples.dtype)


def found_for_blocks(pick, received):
    flat = received[...].reshape(received.shape[0] * received.shape[1], LANES)
    return jnp.dot(pick, flat, preferred_element_type=jnp.float32)


def more_kernel(pick, received, more):
    more[...] = found_for_blocks(pick[1], received)


def kick_kernel(pick, pushed, received, *refs):
    more, kicked = refs[:-1], refs[-1]
    blocks = pushed.shape[1]
    values = [pushed[i] for i in range(6)]
    total = found_for_blocks(pick[0], received)
    if more:
        total = total + more[0][...]
    for block in range(blocks):
        lines = [value[block : block + 1] for value in values]
        lines[5] = lines[5] + 0.5 * total[2 * block : 2 * block + 1]
        lines[1] = lines[1] + 0.5 * total[2 * block + 1 : 2 * block + 2]
        kicked[:, LANES * block : LANES * (block + 1)] = jnp.concatenate(lines, axis=0)


def local(
    coords,
    charge,
    row_index,
    block_col,
    col_offset,
    transfer_map,
    history,
    retard_index,
    retard_frac,
    retard_weight,
    z_kernel,
    x_kernel,
):
    strips = lax.axis_size("hist")
    slabs = lax.axis_size("dom")
    count_steps, comps, slab_rows, width = history.shape
    strip = width // strips
    particles = coords.shape[1]
    blocks = block_col.shape[0]
    tile = (blocks, LANES)
    spread_rows = comps * strip
    row_lanes = max(slab_rows, LANES)
    seats, second_round = seats_of(strips, slabs, blocks)
    rounds = 2 if second_round else 1
    record_rows = FIELDS * seats * LANES // row_lanes
    packed_rows = spread_rows + record_rows

    f32, bf16 = jnp.float32, jnp.bfloat16
    packed, later, pick = call(
        functools.partial(source_kernel, strips),
        (
            jax.ShapeDtypeStruct((strips, packed_rows, row_lanes), bf16),
            jax.ShapeDtypeStruct((strips, record_rows, row_lanes), bf16),
            jax.ShapeDtypeStruct((rounds, comps * blocks, comps * strips * seats), bf16),
        ),
        [HBM] * 11,
        (HBM, HBM, HBM),
        [
            pltpu.SMEM((1, blocks), jnp.int32),
            pltpu.SMEM((1, count_steps), jnp.int32),
            pltpu.SMEM((1, count_steps), f32),
            pltpu.SMEM((1, count_steps), f32),
            pltpu.VMEM(coords.shape, f32),
            pltpu.VMEM(tile, f32),
            pltpu.VMEM(tile, jnp.int32),
            pltpu.VMEM(tile, jnp.int32),
            pltpu.SMEM(transfer_map.shape, f32),
            pltpu.VMEM(history.shape, bf16),
            pltpu.VMEM((width, width), f32),
            pltpu.VMEM((3 * width, width), bf16),
            pltpu.VMEM((comps * slab_rows, 3 * width), bf16),
            pltpu.VMEM((comps, width, slab_rows), f32),
            pltpu.VMEM((2 * LANES * count_steps, 2 * LANES), bf16),
            pltpu.VMEM((LANES * count_steps, 2 * LANES), bf16),
            pltpu.VMEM((strips, packed_rows, row_lanes), bf16),
            pltpu.VMEM((strips, record_rows, row_lanes), bf16),
            pltpu.SMEM((1, strips), jnp.int32),
            pltpu.VMEM((rounds, comps * blocks, comps * strips * seats), bf16),
            pltpu.VMEM((FIELDS * (rounds * strips * seats + 2), LANES), f32),
            pltpu.SemaphoreType.DMA((16 + comps * count_steps,)),
        ],
        flops=6 * comps * slab_rows * width * width,
        moved=history.size * 2 + x_kernel.size * 4,
        limit=LIMIT,
    )(
        block_col.reshape(1, blocks),
        retard_index.reshape(1, count_steps),
        retard_frac.reshape(1, count_steps),
        retard_weight.reshape(1, count_steps),
        coords,
        charge.reshape(tile),
        row_index.reshape(tile),
        col_offset.reshape(tile),
        transfer_map,
        history,
        x_kernel,
    )
    arrived = lax.all_to_all(packed, "hist", 0, 0, tiled=True)

    part = jax.ShapeDtypeStruct((spread_rows + (8 if second_round else 0), slab_rows), f32)
    parts = call(
        functools.partial(join_kernel, slabs, spread_rows),
        (part, part) if slabs == 2 else jax.ShapeDtypeStruct((slabs,) + part.shape, f32),
        [VMEM, VMEM],
        (VMEM, VMEM) if slabs == 2 else VMEM,
        flops=1 << 27,
        moved=1 << 20,
    )(z_kernel, arrived)
    if slabs == 2:
        kept, sent = parts
        parts = [kept, lax.ppermute(sent, "dom", [(0, 1), (1, 0)])]
    else:
        parts = [lax.all_to_all(parts, "dom", 0, 0, tiled=True)]

    def unpack(arrived, spread_rows):
        return call(
            functools.partial(unpack_kernel, spread_rows),
            (
                jax.ShapeDtypeStruct((strips + 1, FIELDS * seats, LANES), f32),
                jax.ShapeDtypeStruct((strips * seats + 32,), jnp.int32),
            ),
            [VMEM],
            (VMEM, SMEM),
            flops=1 << 20,
            moved=1 << 20,
        )(arrived)

    def sample(chosen, records, parts):
        return call(
            functools.partial(sample_kernel, seats),
            (
                jax.ShapeDtypeStruct((comps, strip, slab_rows), f32),
                jax.ShapeDtypeStruct((strips, comps * seats, LANES), bf16),
                jax.ShapeDtypeStruct((8,), jnp.int32),
            ),
            [SMEM, VMEM] + [VMEM] * len(parts),
            (VMEM, VMEM, SMEM),
            [pltpu.VMEM((strips + 1, comps * seats, LANES), f32)],
            flops=1 << 29,
            moved=1 << 20,
        )(chosen, records, *parts)

    def deposits(chosen, records, after, *extra):
        return call(
            functools.partial(deposit_kernel, seats),
            jax.ShapeDtypeStruct((comps, strip, slab_rows), f32),
            [SMEM, VMEM, HBM] + [VMEM] * len(extra),
            VMEM,
            [pltpu.VMEM((slab_rows, comps * strip), f32)],
            flops=1 << 29,
            moved=1 << 20,
        )(chosen, records, after, *extra)

    def exchange(value):
        return lax.all_to_all(value, "hist", 0, 0, tiled=True)

    records, chosen = unpack(arrived, spread_rows)
    field, samples, flag = sample(chosen, records, parts)
    more, extra = [], []
    if second_round:

        def another(later, field, pick):
            records, chosen = unpack(exchange(later), 0)
            whole = field.reshape(1, spread_rows, slab_rows)
            _, samples, _ = sample(chosen, records, [whole])
            more = call(
                more_kernel,
                jax.ShapeDtypeStruct((comps * blocks, LANES), f32),
                [VMEM, VMEM],
                VMEM,
            )(pick, exchange(samples))
            return more, deposits(chosen, records, samples)

        def nothing(later, field, pick):
            return jnp.zeros((comps * blocks, LANES), f32), jnp.zeros(field.shape, f32)

        found, left = lax.cond(flag[0] > 0, another, nothing, later, field, pick)
        more, extra = [found], [left]
    received = exchange(samples)
    deposit = deposits(chosen, records, samples, *extra)
    pushed = call(
        push_kernel,
        jax.ShapeDtypeStruct((6,) + tile, f32),
        [SMEM, VMEM, HBM],
        VMEM,
        flops=1200 * particles,
        moved=1 << 18,
    )(transfer_map, coords, samples)
    kicked = call(
        kick_kernel,
        jax.ShapeDtypeStruct((6, particles), f32),
        [VMEM] * (3 + len(more)),
        VMEM,
        flops=1 << 16,
        moved=1 << 18,
    )(pick, pushed, received, *more)
    return kicked, jnp.transpose(field, (0, 2, 1)), jnp.transpose(deposit, (0, 2, 1))


def solution(mesh):
    return jax.shard_map(
        local,
        mesh=mesh,
        in_specs=(
            P(None, ("dom", "hist")),
            P(("dom", "hist")),
            P(("dom", "hist")),
            P(("dom", "hist")),
            P(("dom", "hist")),
            P(),
            P("hist", None, "dom", None),
            P("hist"),
            P("hist"),
            P("hist"),
            P(None, "dom"),
            P(),
        ),
        out_specs=(P(None, ("dom", "hist")), P(None, "dom", "hist"), P(None, "dom", "hist")),
        check_vma=False,
    )
```

```python
import functools

import jax
import jax.numpy as jnp
from jax import lax
from jax.experimental import pallas as pl
from jax.experimental.pallas import tpu as pltpu
from jax.sharding import PartitionSpec as P

LANES = 128
GROUP = 16
SPAN = 16
SEATS = 8
FIELDS = 4
MORE = 64.0
NT_DIMS = (((1,), (1,)), ((), ()))
VMEM = pl.BlockSpec(memory_space=pltpu.VMEM)
SMEM = pl.BlockSpec(memory_space=pltpu.SMEM)
HBM = pl.BlockSpec(memory_space=pltpu.HBM)
LIMIT = 59 * 1024 * 1024
SMALL = 16 * 1024 * 1024


def call(kernel, out_shape, in_specs, out_specs, scratch=(), flops=0, moved=0, limit=SMALL):
    return pl.pallas_call(
        kernel,
        out_shape=out_shape,
        in_specs=in_specs,
        out_specs=out_specs,
        scratch_shapes=scratch,
        compiler_params=pltpu.CompilerParams(vmem_limit_bytes=limit),
        cost_estimate=pl.CostEstimate(flops=flops, bytes_accessed=moved, transcendentals=0),
    )


def split(value):
    high = value.astype(jnp.bfloat16)
    return high, (value - high.astype(jnp.float32)).astype(jnp.bfloat16)


def seats_of(strips, slabs, blocks):
    if strips == 16 and slabs == 2 and blocks == 2 * SEATS:
        return SEATS, True
    return blocks, False


def strips_met(strip):
    return (SPAN + strip - 2) // strip + 1


def lag_band(lag, near, far):
    row = lax.broadcasted_iota(jnp.int32, (2 * LANES, LANES), 0)
    column = lax.broadcasted_iota(jnp.int32, (2 * LANES, LANES), 1)
    behind = column + LANES - row
    weight = jnp.where(behind == lag, near, jnp.where(behind == lag + 1, far, 0.0))
    return jnp.concatenate(split(weight), axis=1)


def push(coords, transfer, wanted):
    blocks = coords.shape[1] // LANES
    u = [
        jnp.concatenate(
            [coords[i : i + 1, LANES * b : LANES * (b + 1)] for b in range(blocks)], axis=0
        )
        for i in range(6)
    ]
    total = [jnp.full((blocks, LANES), transfer[i, 0], jnp.float32) for i in wanted]
    pairs = {}
    terms = list(u)
    for first in range(6):
        for second in range(first, 6):
            pairs[first, second] = u[first] * u[second]
            terms.append(pairs[first, second])
    for first in range(6):
        for second in range(first, 6):
            for third in range(second, 6):
                terms.append(pairs[first, second] * u[third])
    for column, term in enumerate(terms):
        total = [value + transfer[i, 1 + column] * term for i, value in zip(wanted, total)]
    return total


def push_kernel(transfer, coords, after, pushed):
    del after
    for i, value in enumerate(push(coords, transfer, range(6))):
        pushed[i] = value


def particle_fields(coords, charge, rows, offsets, block_col, transfer, slab_rows):
    blocks = charge.shape[0]
    weight0 = charge[...]
    weight1 = weight0 * push(coords, transfer, [1])[0]
    row_of = lax.broadcasted_iota(jnp.int32, (blocks, LANES), 0)
    column = offsets[...]
    for b in range(blocks):
        column = column + jnp.where(row_of == b, block_col[0, b], 0)
    return lax.rem(rows[...], slab_rows), column, weight0, weight1


def seat_blocks(strips, strip, seats, rounds, block_col, fields, counts, pick, stage):
    row, column, weight0, weight1 = fields
    blocks = row.shape[0]
    nobody = rounds * strips * seats
    meets = strips_met(strip)
    stage[...] = jnp.full(stage.shape, -1.0, jnp.float32)
    for place in range(strips):
        counts[0, place] = 0
    left_out = jnp.int32(0)
    pick_row = lax.broadcasted_iota(jnp.int32, (2 * blocks, LANES), 0)
    lane = lax.broadcasted_iota(jnp.int32, (2 * blocks, LANES), 1)
    wanted = [jnp.zeros((2 * blocks, LANES), jnp.int32)] * meets
    is_column = lax.broadcasted_iota(jnp.int32, (FIELDS, LANES), 0) == 1
    fields = [field.astype(jnp.float32) for field in (row, column, weight0, weight1)]
    for block in range(blocks):
        tile = jnp.concatenate([field[block : block + 1] for field in fields], axis=0)
        start = block_col[0, block]
        first = start // strip
        for step in range(meets):
            place = jnp.minimum(first + step, strips - 1)
            met = (first + step) * strip <= start + (SPAN - 1)
            taken = counts[0, place]
            counts[0, place] = taken + jnp.where(met, 1, 0)
            later = taken // seats
            number = (later * strips + place) * seats + lax.rem(taken, seats)
            number = jnp.where(met, number, nobody)
            left_out = jnp.maximum(left_out, jnp.where(met, later, 0))
            wanted[step] = jnp.where(pick_row >> 1 == block, 2 * number, wanted[step])
            own = tile - (place * strip).astype(jnp.float32)
            own = jnp.where((own >= 0.0) & (own < strip), own, -1.0)
            stage[pl.ds(number * FIELDS, FIELDS), :] = jnp.where(is_column, own, tile)
    lines = 2 * strips * seats
    for turn in range(rounds):
        for left in range(0, lines, LANES):
            line = lane + (turn * lines + left)
            hit = wanted[0] + (pick_row & 1) == line
            for step in range(1, meets):
                hit = hit | (wanted[step] + (pick_row & 1) == line)
            pick[turn, :, left : left + LANES] = jnp.where(hit, 1.0, 0.0).astype(pick.dtype)
    return left_out


def source_kernel(
    strips,
    block_col_from,
    lags_from,
    fracs_from,
    weights_from,
    coords_from,
    charge_from,
    rows_from,
    offsets_from,
    transfer_from,
    history,
    x_kernel,
    packed_to,
    later_to,
    pick_to,
    block_col,
    lags,
    fracs,
    weights,
    coords,
    charge,
    rows,
    offsets,
    transfer,
    frames,
    x_here,
    x_parts,
    s_parts,
    spread_all,
    bands,
    first_bands,
    packed,
    later,
    counts,
    pick,
    stage,
    sems,
):
    count_steps, comps, slab_rows, width = history.shape
    blocks = charge.shape[0]
    strip = width // strips
    spread_rows = comps * strip
    record_rows = packed.shape[1] - spread_rows
    across = packed.shape[2] // LANES
    seats = record_rows * across // FIELDS
    rounds = stage.shape[0] // (FIELDS * strips * seats)
    pairs = [
        (lags_from, lags),
        (fracs_from, fracs),
        (weights_from, weights),
        (block_col_from, block_col),
        (coords_from, coords),
        (charge_from, charge),
        (rows_from, rows),
        (offsets_from, offsets),
        (transfer_from, transfer),
    ]
    part_rows = min(128, slab_rows)
    tops = range(0, slab_rows, part_rows)
    arrival = {}
    for comp in range(comps):
        for top in tops:
            part = pl.ds(top, part_rows)
            arrival[comp, top] = len(pairs)
            pairs += [
                (history.at[t, comp, part], frames.at[t, comp, part]) for t in range(count_steps)
            ]
        if comp == 0:
            x_arrival = len(pairs)
            pairs += [(x_kernel, x_here)]
    fetch = [
        pltpu.make_async_copy(source, target, sems.at[index])
        for index, (source, target) in enumerate(pairs)
    ]
    for copy in fetch:
        copy.start()
    stored = []

    def store(source, target):
        copy = pltpu.make_async_copy(source, target, sems.at[len(fetch) + len(stored)])
        copy.start()
        stored.append(copy)

    for copy in fetch[:9]:
        copy.wait()
    for t in range(count_steps):
        far = weights[0, t] * fracs[0, t]
        near = weights[0, t] * (1.0 - fracs[0, t])
        bands[2 * LANES * t : 2 * LANES * (t + 1)] = lag_band(lags[0, t], near, far)
        first_bands[LANES * t : LANES * (t + 1)] = bands[
            2 * LANES * t + LANES : 2 * LANES * (t + 1)
        ]

    row, column, weight0, weight1 = particle_fields(
        coords, charge, rows, offsets, block_col, transfer, slab_rows
    )
    left_out = seat_blocks(
        strips,
        strip,
        seats,
        rounds,
        block_col,
        (row, column, weight0, weight1),
        counts,
        pick,
        stage,
    )
    is_column = lax.rem(lax.broadcasted_iota(jnp.int32, (record_rows, LANES), 0), FIELDS) == 1
    mark = jnp.where(is_column, MORE * left_out.astype(jnp.float32), 0.0)
    for turn in range(rounds):
        for partner in range(strips):
            for side in range(across):
                start = ((turn * strips + partner) * across + side) * record_rows
                value = stage[start : start + record_rows]
                lanes = slice(side * LANES, (side + 1) * LANES)
                if turn == 0:
                    packed[partner, spread_rows:, lanes] = (value + mark).astype(packed.dtype)
                else:
                    later[partner, :, lanes] = value.astype(later.dtype)

    for comp in range(comps):
        here = slice(comp * slab_rows, (comp + 1) * slab_rows)
        for top in tops:
            for t in range(count_steps):
                fetch[arrival[comp, top] + t].wait()
            for q in range(width // LANES):
                before = slice(LANES * max(q - 1, 0), LANES * (q + 1))
                steps = [
                    frames[t, comp, top : top + part_rows, before] for t in range(count_steps)
                ]
                both = jnp.dot(
                    jnp.concatenate(steps, axis=1),
                    bands[...] if q else first_bands[...],
                    preferred_element_type=jnp.float32,
                )
                high, low = split(both[:, :LANES] + both[:, LANES:])
                part = slice(comp * slab_rows + top, comp * slab_rows + top + part_rows)
                s_parts[part, LANES * q : LANES * (q + 1)] = high
                s_parts[part, width + LANES * q : width + LANES * (q + 1)] = low
                s_parts[part, 2 * width + LANES * q : 2 * width + LANES * (q + 1)] = high
        if comp == 0:
            store(pick, pick_to)
            if rounds == 2:
                store(later, later_to)
            store(packed.at[:, spread_rows:], packed_to.at[:, spread_rows:])
            fetch[x_arrival].wait()
            high, low = split(x_here[...])
            x_parts[:width] = high
            x_parts[width : 2 * width] = high
            x_parts[2 * width :] = low
        spread = jnp.dot(s_parts[here], x_parts[...], preferred_element_type=jnp.float32)
        if strip % 16 == 0:
            turned = spread.astype(packed.dtype).T
            part = slice(comp * strip, (comp + 1) * strip)
            for partner in range(strips):
                packed[partner, part, :slab_rows] = turned[
                    partner * strip : (partner + 1) * strip
                ]
            store(packed.at[:, part], packed_to.at[:, part])
        else:
            spread_all[comp] = spread.T
    if strip % 16:
        for partner in range(strips):
            part = slice(partner * strip, (partner + 1) * strip)
            both = jnp.concatenate([spread_all[comp, part] for comp in range(comps)], axis=0)
            packed[partner, :spread_rows, :slab_rows] = both.astype(packed.dtype)
        store(packed.at[:, :spread_rows], packed_to.at[:, :spread_rows])
    for copy in stored:
        copy.wait()


def join_kernel(slabs, spread_rows, z_kernel, arrived, kept, *sent):
    slab_rows = z_kernel.shape[0] // slabs
    extra_rows = kept.shape[0] - spread_rows if sent else 0
    total = arrived[0, :spread_rows, :slab_rows].astype(jnp.float32)
    for sender in range(1, arrived.shape[0]):
        total = total + arrived[sender, :spread_rows, :slab_rows].astype(jnp.float32)
    high, low = split(total)
    left = jnp.concatenate([high, low, high], axis=1)

    def part(slab):
        start = pl.multiple_of(slab * slab_rows, slab_rows)
        z_high, z_low = split(z_kernel[pl.ds(start, slab_rows), :])
        right = jnp.concatenate([z_high, z_high, z_low], axis=1)
        return lax.dot_general(left, right, NT_DIMS, preferred_element_type=jnp.float32)

    if sent:
        me = lax.axis_index("dom")
        sent[0][:spread_rows] = part(1 - me)
        kept[:spread_rows] = part(me)
        if extra_rows:
            records = jnp.max(arrived[:, spread_rows:].astype(jnp.float32), axis=0)
            is_column = lax.rem(lax.broadcasted_iota(jnp.int32, records.shape, 0), FIELDS) == 1
            most = jnp.max(jnp.where(is_column, records, -1.0))
            flag = jnp.full((extra_rows, slab_rows), jnp.where(most >= MORE - 1.0, 1.0, 0.0))
            sent[0][spread_rows:] = flag
            kept[spread_rows:] = flag
    else:
        for slab in range(slabs):
            kept[slab] = part(slab)


def unpack_kernel(spread_rows, arrived, records, chosen):
    senders = arrived.shape[0]
    record_rows = arrived.shape[1] - spread_rows
    across = arrived.shape[2] // LANES
    blocks = record_rows * across // FIELDS
    line = lax.broadcasted_iota(jnp.int32, (record_rows, LANES), 0)
    is_column = lax.rem(line, FIELDS) == 1
    first_line = lax.broadcasted_iota(jnp.int32, (record_rows, 1), 0)
    first_column = lax.rem(first_line, FIELDS) == 1
    masks = []
    for sender in range(senders):
        mask = jnp.float32(0.0)
        for side in range(across):
            lanes = slice(side * LANES, (side + 1) * LANES)
            value = arrived[sender, spread_rows:, lanes].astype(jnp.float32)
            value = jnp.where(is_column & (value >= MORE - 1.0), value - MORE, value)
            records[sender, side * record_rows : (side + 1) * record_rows] = value
            taken = first_column & (jnp.max(value, axis=1, keepdims=True) >= 0.0)
            seat = first_line // FIELDS + side * (record_rows // FIELDS)
            bit = jnp.left_shift(jnp.ones_like(seat), seat).astype(jnp.float32)
            mask = mask + jnp.sum(jnp.where(taken, bit, 0.0))
        masks.append(mask.astype(jnp.int32))
    records[senders] = jnp.full(records.shape[1:], -1.0, jnp.float32)
    count = jnp.int32(0)
    for sender in range(senders):
        for block in range(blocks):
            chosen[1 + count] = sender * blocks + block
            count = count + ((masks[sender] >> block) & 1)
    chosen[0] = (count + (GROUP - 1)) // GROUP
    for member in range(GROUP):
        chosen[1 + count + member] = senders * blocks


def read_group(blocks, chosen, records, group):
    where = []
    for member in range(GROUP):
        block = chosen[1 + group * GROUP + member]
        where.append((block // blocks, lax.rem(block, blocks)))

    lines = jnp.concatenate(
        [records[sender, pl.ds(own * FIELDS, FIELDS), :] for sender, own in where], axis=1
    )

    def field(index):
        return lines[index : index + 1]

    return where, field


def one_hot(index, size):
    iota = lax.broadcasted_iota(jnp.int32, (size, index.shape[1]), 0).astype(jnp.float32)
    return iota == index


def one_hot_rows(row, size):
    iota = lax.broadcasted_iota(jnp.int32, (size, row.shape[1]), 0)
    if size <= 256:
        hit = iota.astype(jnp.bfloat16) == row.astype(jnp.bfloat16)
        return jnp.where(hit, jnp.bfloat16(1.0), jnp.bfloat16(0.0))
    return jnp.where(iota.astype(jnp.float32) == row, 1.0, 0.0).astype(jnp.bfloat16)


def deposit_kernel(blocks, chosen, records, after, *refs):
    del after
    extra, (deposit, total) = refs[:-2], refs[-2:]
    strip, slab_rows = deposit.shape[1:]
    total[...] = jnp.zeros_like(total)

    def one_group(group, carry):
        _, field = read_group(blocks, chosen, records, group)
        hit = one_hot(field(1), strip)
        weighted = [jnp.where(hit, field(2 + comp), 0.0) for comp in range(2)]
        total[...] += lax.dot_general(
            one_hot_rows(field(0), slab_rows),
            jnp.concatenate(weighted, axis=0).astype(jnp.bfloat16),
            NT_DIMS,
            preferred_element_type=jnp.float32,
        )
        return carry

    lax.fori_loop(0, chosen[0], one_group, 0)
    turned = total[...].T
    for comp in range(2):
        own = turned[comp * strip : (comp + 1) * strip]
        deposit[comp] = own + extra[0][comp] if extra else own


def sample_kernel(blocks, chosen, records, *refs):
    parts, (field_out, samples, flag, found_all) = refs[:-4], refs[-4:]
    strip, slab_rows = field_out.shape[1:]
    if len(parts) == 1:
        total = parts[0][0]
        for slab in range(1, parts[0].shape[0]):
            total = total + parts[0][slab]
    else:
        total = parts[0][: 2 * strip] + parts[1][: 2 * strip]
    if len(parts) == 2 and parts[0].shape[0] > 2 * strip:
        most = jnp.max(jnp.maximum(parts[0][2 * strip :], parts[1][2 * strip :]))
        flag[0] = jnp.where(most > 0.5, 1, 0)
    else:
        flag[0] = 0
    field_out[0] = total[:strip]
    field_out[1] = total[strip:]
    rounded = total.astype(jnp.bfloat16)
    found_all[...] = jnp.zeros_like(found_all)

    def one_group(group, carry):
        where, field = read_group(blocks, chosen, records, group)
        row_hot = one_hot_rows(field(0), slab_rows)
        found = jnp.dot(rounded, row_hot, preferred_element_type=jnp.float32)
        hit = one_hot(field(1), strip)
        values = []
        for comp in range(2):
            picked = jnp.where(hit, found[comp * strip : (comp + 1) * strip], 0.0)
            values.append(jnp.sum(picked, axis=0, keepdims=True))
        values = jnp.concatenate(values, axis=0)
        for member, (sender, own) in enumerate(where):
            found_all[sender, pl.ds(2 * own, 2), :] = values[
                :, LANES * member : LANES * (member + 1)
            ]
        return carry

    lax.fori_loop(0, chosen[0], one_group, 0)
    samples[...] = found_all[: samples.shape[0]].astype(samples.dtype)


def found_for_blocks(pick, received):
    flat = received[...].reshape(received.shape[0] * received.shape[1], LANES)
    return jnp.dot(pick, flat, preferred_element_type=jnp.float32)


def more_kernel(pick, received, more):
    more[...] = found_for_blocks(pick[1], received)


def kick_kernel(pick, pushed, received, *refs):
    more, kicked = refs[:-1], refs[-1]
    blocks = pushed.shape[1]
    values = [pushed[i] for i in range(6)]
    total = found_for_blocks(pick[0], received)
    if more:
        total = total + more[0][...]
    for block in range(blocks):
        lines = [value[block : block + 1] for value in values]
        lines[5] = lines[5] + 0.5 * total[2 * block : 2 * block + 1]
        lines[1] = lines[1] + 0.5 * total[2 * block + 1 : 2 * block + 2]
        kicked[:, LANES * block : LANES * (block + 1)] = jnp.concatenate(lines, axis=0)


def local(
    coords,
    charge,
    row_index,
    block_col,
    col_offset,
    transfer_map,
    history,
    retard_index,
    retard_frac,
    retard_weight,
    z_kernel,
    x_kernel,
):
    strips = lax.axis_size("hist")
    slabs = lax.axis_size("dom")
    count_steps, comps, slab_rows, width = history.shape
    strip = width // strips
    particles = coords.shape[1]
    blocks = block_col.shape[0]
    tile = (blocks, LANES)
    spread_rows = comps * strip
    row_lanes = max(slab_rows, LANES)
    seats, second_round = seats_of(strips, slabs, blocks)
    rounds = 2 if second_round else 1
    record_rows = FIELDS * seats * LANES // row_lanes
    packed_rows = spread_rows + record_rows

    f32, bf16 = jnp.float32, jnp.bfloat16
    packed, later, pick = call(
        functools.partial(source_kernel, strips),
        (
            jax.ShapeDtypeStruct((strips, packed_rows, row_lanes), bf16),
            jax.ShapeDtypeStruct((strips, record_rows, row_lanes), bf16),
            jax.ShapeDtypeStruct((rounds, comps * blocks, comps * strips * seats), bf16),
        ),
        [HBM] * 11,
        (HBM, HBM, HBM),
        [
            pltpu.SMEM((1, blocks), jnp.int32),
            pltpu.SMEM((1, count_steps), jnp.int32),
            pltpu.SMEM((1, count_steps), f32),
            pltpu.SMEM((1, count_steps), f32),
            pltpu.VMEM(coords.shape, f32),
            pltpu.VMEM(tile, f32),
            pltpu.VMEM(tile, jnp.int32),
            pltpu.VMEM(tile, jnp.int32),
            pltpu.SMEM(transfer_map.shape, f32),
            pltpu.VMEM(history.shape, bf16),
            pltpu.VMEM((width, width), f32),
            pltpu.VMEM((3 * width, width), bf16),
            pltpu.VMEM((comps * slab_rows, 3 * width), bf16),
            pltpu.VMEM((comps, width, slab_rows), f32),
            pltpu.VMEM((2 * LANES * count_steps, 2 * LANES), bf16),
            pltpu.VMEM((LANES * count_steps, 2 * LANES), bf16),
            pltpu.VMEM((strips, packed_rows, row_lanes), bf16),
            pltpu.VMEM((strips, record_rows, row_lanes), bf16),
            pltpu.SMEM((1, strips), jnp.int32),
            pltpu.VMEM((rounds, comps * blocks, comps * strips * seats), bf16),
            pltpu.VMEM((FIELDS * (rounds * strips * seats + 2), LANES), f32),
            pltpu.SemaphoreType.DMA((16 + 2 * comps * count_steps,)),
        ],
        flops=6 * comps * slab_rows * width * width,
        moved=history.size * 2 + x_kernel.size * 4,
        limit=LIMIT,
    )(
        block_col.reshape(1, blocks),
        retard_index.reshape(1, count_steps),
        retard_frac.reshape(1, count_steps),
        retard_weight.reshape(1, count_steps),
        coords,
        charge.reshape(tile),
        row_index.reshape(tile),
        col_offset.reshape(tile),
        transfer_map,
        history,
        x_kernel,
    )
    arrived = lax.all_to_all(packed, "hist", 0, 0, tiled=True)

    part = jax.ShapeDtypeStruct((spread_rows + (8 if second_round else 0), slab_rows), f32)
    parts = call(
        functools.partial(join_kernel, slabs, spread_rows),
        (part, part) if slabs == 2 else jax.ShapeDtypeStruct((slabs,) + part.shape, f32),
        [VMEM, VMEM],
        (VMEM, VMEM) if slabs == 2 else VMEM,
        flops=1 << 27,
        moved=1 << 20,
    )(z_kernel, arrived)
    if slabs == 2:
        kept, sent = parts
        parts = [kept, lax.ppermute(sent, "dom", [(0, 1), (1, 0)])]
    else:
        parts = [lax.all_to_all(parts, "dom", 0, 0, tiled=True)]

    def unpack(arrived, spread_rows):
        return call(
            functools.partial(unpack_kernel, spread_rows),
            (
                jax.ShapeDtypeStruct((strips + 1, FIELDS * seats, LANES), f32),
                jax.ShapeDtypeStruct((strips * seats + 32,), jnp.int32),
            ),
            [VMEM],
            (VMEM, SMEM),
            flops=1 << 20,
            moved=1 << 20,
        )(arrived)

    def sample(chosen, records, parts):
        return call(
            functools.partial(sample_kernel, seats),
            (
                jax.ShapeDtypeStruct((comps, strip, slab_rows), f32),
                jax.ShapeDtypeStruct((strips, comps * seats, LANES), bf16),
                jax.ShapeDtypeStruct((8,), jnp.int32),
            ),
            [SMEM, VMEM] + [VMEM] * len(parts),
            (VMEM, VMEM, SMEM),
            [pltpu.VMEM((strips + 1, comps * seats, LANES), f32)],
            flops=1 << 29,
            moved=1 << 20,
        )(chosen, records, *parts)

    def deposits(chosen, records, after, *extra):
        return call(
            functools.partial(deposit_kernel, seats),
            jax.ShapeDtypeStruct((comps, strip, slab_rows), f32),
            [SMEM, VMEM, HBM] + [VMEM] * len(extra),
            VMEM,
            [pltpu.VMEM((slab_rows, comps * strip), f32)],
            flops=1 << 29,
            moved=1 << 20,
        )(chosen, records, after, *extra)

    def exchange(value):
        return lax.all_to_all(value, "hist", 0, 0, tiled=True)

    records, chosen = unpack(arrived, spread_rows)
    field, samples, flag = sample(chosen, records, parts)
    more, extra = [], []
    if second_round:

        def another(later, field, pick):
            records, chosen = unpack(exchange(later), 0)
            whole = field.reshape(1, spread_rows, slab_rows)
            _, samples, _ = sample(chosen, records, [whole])
            more = call(
                more_kernel,
                jax.ShapeDtypeStruct((comps * blocks, LANES), f32),
                [VMEM, VMEM],
                VMEM,
            )(pick, exchange(samples))
            return more, deposits(chosen, records, samples)

        def nothing(later, field, pick):
            return jnp.zeros((comps * blocks, LANES), f32), jnp.zeros(field.shape, f32)

        found, left = lax.cond(flag[0] > 0, another, nothing, later, field, pick)
        more, extra = [found], [left]
    received = exchange(samples)
    deposit = deposits(chosen, records, samples, *extra)
    pushed = call(
        push_kernel,
        jax.ShapeDtypeStruct((6,) + tile, f32),
        [SMEM, VMEM, HBM],
        VMEM,
        flops=1200 * particles,
        moved=1 << 18,
    )(transfer_map, coords, samples)
    kicked = call(
        kick_kernel,
        jax.ShapeDtypeStruct((6, particles), f32),
        [VMEM] * (3 + len(more)),
        VMEM,
        flops=1 << 16,
        moved=1 << 18,
    )(pick, pushed, received, *more)
    return kicked, jnp.transpose(field, (0, 2, 1)), jnp.transpose(deposit, (0, 2, 1))


def solution(mesh):
    return jax.shard_map(
        local,
        mesh=mesh,
        in_specs=(
            P(None, ("dom", "hist")),
            P(("dom", "hist")),
            P(("dom", "hist")),
            P(("dom", "hist")),
            P(("dom", "hist")),
            P(),
            P("hist", None, "dom", None),
            P("hist"),
            P("hist"),
            P("hist"),
            P(None, "dom"),
            P(),
        ),
        out_specs=(P(None, ("dom", "hist")), P(None, "dom", "hist"), P(None, "dom", "hist")),
        check_vma=False,
    )
```

```python
import functools

import jax
import jax.numpy as jnp
from jax import lax
from jax.experimental import pallas as pl
from jax.experimental.pallas import tpu as pltpu
from jax.sharding import PartitionSpec as P

LANES = 128
GROUP = 16
SPAN = 16
SEATS = 8
FIELDS = 4
MORE = 64.0
NT_DIMS = (((1,), (1,)), ((), ()))
VMEM = pl.BlockSpec(memory_space=pltpu.VMEM)
SMEM = pl.BlockSpec(memory_space=pltpu.SMEM)
HBM = pl.BlockSpec(memory_space=pltpu.HBM)
LIMIT = 59 * 1024 * 1024
SMALL = 16 * 1024 * 1024


def call(kernel, out_shape, in_specs, out_specs, scratch=(), flops=0, moved=0, limit=SMALL):
    return pl.pallas_call(
        kernel,
        out_shape=out_shape,
        in_specs=in_specs,
        out_specs=out_specs,
        scratch_shapes=scratch,
        compiler_params=pltpu.CompilerParams(vmem_limit_bytes=limit),
        cost_estimate=pl.CostEstimate(flops=flops, bytes_accessed=moved, transcendentals=0),
    )


def split(value):
    high = value.astype(jnp.bfloat16)
    return high, (value - high.astype(jnp.float32)).astype(jnp.bfloat16)


def seats_of(strips, slabs, blocks):
    if strips == 16 and slabs == 2 and blocks == 2 * SEATS:
        return SEATS, True
    return blocks, False


def strips_met(strip):
    return (SPAN + strip - 2) // strip + 1


def lag_band(lag, near, far):
    row = lax.broadcasted_iota(jnp.int32, (2 * LANES, LANES), 0)
    column = lax.broadcasted_iota(jnp.int32, (2 * LANES, LANES), 1)
    behind = column + LANES - row
    weight = jnp.where(behind == lag, near, jnp.where(behind == lag + 1, far, 0.0))
    return jnp.concatenate(split(weight), axis=1)


def push(coords, transfer, wanted):
    blocks = coords.shape[1] // LANES
    u = [
        jnp.concatenate(
            [coords[i : i + 1, LANES * b : LANES * (b + 1)] for b in range(blocks)], axis=0
        )
        for i in range(6)
    ]
    total = [jnp.full((blocks, LANES), transfer[i, 0], jnp.float32) for i in wanted]
    pairs = {}
    terms = list(u)
    for first in range(6):
        for second in range(first, 6):
            pairs[first, second] = u[first] * u[second]
            terms.append(pairs[first, second])
    for first in range(6):
        for second in range(first, 6):
            for third in range(second, 6):
                terms.append(pairs[first, second] * u[third])
    for column, term in enumerate(terms):
        total = [value + transfer[i, 1 + column] * term for i, value in zip(wanted, total)]
    return total


def push_kernel(transfer, coords, after, pushed):
    del after
    for i, value in enumerate(push(coords, transfer, range(6))):
        pushed[i] = value


def particle_fields(coords, charge, rows, offsets, block_col, transfer, slab_rows):
    blocks = charge.shape[0]
    weight0 = charge[...]
    weight1 = weight0 * push(coords, transfer, [1])[0]
    row_of = lax.broadcasted_iota(jnp.int32, (blocks, LANES), 0)
    column = offsets[...]
    for b in range(blocks):
        column = column + jnp.where(row_of == b, block_col[0, b], 0)
    return lax.rem(rows[...], slab_rows), column, weight0, weight1


def seat_blocks(strips, strip, seats, rounds, block_col, fields, counts, pick, stage):
    row, column, weight0, weight1 = fields
    blocks = row.shape[0]
    nobody = rounds * strips * seats
    meets = strips_met(strip)
    stage[...] = jnp.full(stage.shape, -1.0, jnp.float32)
    for place in range(strips):
        counts[0, place] = 0
    left_out = jnp.int32(0)
    pick_row = lax.broadcasted_iota(jnp.int32, (2 * blocks, LANES), 0)
    lane = lax.broadcasted_iota(jnp.int32, (2 * blocks, LANES), 1)
    wanted = [jnp.zeros((2 * blocks, LANES), jnp.int32)] * meets
    is_column = lax.broadcasted_iota(jnp.int32, (FIELDS, LANES), 0) == 1
    fields = [field.astype(jnp.float32) for field in (row, column, weight0, weight1)]
    for block in range(blocks):
        tile = jnp.concatenate([field[block : block + 1] for field in fields], axis=0)
        start = block_col[0, block]
        first = start // strip
        for step in range(meets):
            place = jnp.minimum(first + step, strips - 1)
            met = (first + step) * strip <= start + (SPAN - 1)
            taken = counts[0, place]
            counts[0, place] = taken + jnp.where(met, 1, 0)
            later = taken // seats
            number = (later * strips + place) * seats + lax.rem(taken, seats)
            number = jnp.where(met, number, nobody)
            left_out = jnp.maximum(left_out, jnp.where(met, later, 0))
            wanted[step] = jnp.where(pick_row >> 1 == block, 2 * number, wanted[step])
            own = tile - (place * strip).astype(jnp.float32)
            own = jnp.where((own >= 0.0) & (own < strip), own, -1.0)
            stage[pl.ds(number * FIELDS, FIELDS), :] = jnp.where(is_column, own, tile)
    lines = 2 * strips * seats
    for turn in range(rounds):
        for left in range(0, lines, LANES):
            line = lane + (turn * lines + left)
            hit = wanted[0] + (pick_row & 1) == line
            for step in range(1, meets):
                hit = hit | (wanted[step] + (pick_row & 1) == line)
            pick[turn, :, left : left + LANES] = jnp.where(hit, 1.0, 0.0).astype(pick.dtype)
    return left_out


def source_kernel(
    strips,
    block_col_from,
    lags_from,
    fracs_from,
    weights_from,
    coords_from,
    charge_from,
    rows_from,
    offsets_from,
    transfer_from,
    history,
    x_kernel,
    packed_to,
    later_to,
    pick_to,
    block_col,
    lags,
    fracs,
    weights,
    coords,
    charge,
    rows,
    offsets,
    transfer,
    frames,
    x_here,
    x_parts,
    s_parts,
    spread_all,
    bands,
    first_bands,
    packed,
    later,
    counts,
    pick,
    stage,
    sems,
):
    count_steps, comps, slab_rows, width = history.shape
    blocks = charge.shape[0]
    strip = width // strips
    spread_rows = comps * strip
    record_rows = packed.shape[1] - spread_rows
    across = packed.shape[2] // LANES
    seats = record_rows * across // FIELDS
    rounds = stage.shape[0] // (FIELDS * strips * seats)
    pairs = [
        (lags_from, lags),
        (fracs_from, fracs),
        (weights_from, weights),
        (block_col_from, block_col),
        (coords_from, coords),
        (charge_from, charge),
        (rows_from, rows),
        (offsets_from, offsets),
        (transfer_from, transfer),
    ]
    for comp in range(comps):
        pairs += [(history.at[:, comp], frames.at[:, comp])]
        if comp == 0:
            pairs += [(x_kernel, x_here)]
    fetch = [
        pltpu.make_async_copy(source, target, sems.at[index])
        for index, (source, target) in enumerate(pairs)
    ]
    for copy in fetch:
        copy.start()
    stored = []

    def store(source, target):
        copy = pltpu.make_async_copy(source, target, sems.at[len(fetch) + len(stored)])
        copy.start()
        stored.append(copy)

    for copy in fetch[:9]:
        copy.wait()
    for t in range(count_steps):
        far = weights[0, t] * fracs[0, t]
        near = weights[0, t] * (1.0 - fracs[0, t])
        bands[2 * LANES * t : 2 * LANES * (t + 1)] = lag_band(lags[0, t], near, far)
        first_bands[LANES * t : LANES * (t + 1)] = bands[
            2 * LANES * t + LANES : 2 * LANES * (t + 1)
        ]

    row, column, weight0, weight1 = particle_fields(
        coords, charge, rows, offsets, block_col, transfer, slab_rows
    )
    left_out = seat_blocks(
        strips,
        strip,
        seats,
        rounds,
        block_col,
        (row, column, weight0, weight1),
        counts,
        pick,
        stage,
    )
    is_column = lax.rem(lax.broadcasted_iota(jnp.int32, (record_rows, LANES), 0), FIELDS) == 1
    mark = jnp.where(is_column, MORE * left_out.astype(jnp.float32), 0.0)
    for turn in range(rounds):
        for partner in range(strips):
            for side in range(across):
                start = ((turn * strips + partner) * across + side) * record_rows
                value = stage[start : start + record_rows]
                lanes = slice(side * LANES, (side + 1) * LANES)
                if turn == 0:
                    packed[partner, spread_rows:, lanes] = (value + mark).astype(packed.dtype)
                else:
                    later[partner, :, lanes] = value.astype(later.dtype)

    for comp in range(comps):
        fetch[9 + (comp + 1 if comp else 0)].wait()
        here = slice(comp * slab_rows, (comp + 1) * slab_rows)
        part_rows = min(128, slab_rows)
        for top in range(0, slab_rows, part_rows):
            for q in range(width // LANES):
                before = slice(LANES * max(q - 1, 0), LANES * (q + 1))
                steps = [
                    frames[t, comp, top : top + part_rows, before] for t in range(count_steps)
                ]
                both = jnp.dot(
                    jnp.concatenate(steps, axis=1),
                    bands[...] if q else first_bands[...],
                    preferred_element_type=jnp.float32,
                )
                high, low = split(both[:, :LANES] + both[:, LANES:])
                part = slice(comp * slab_rows + top, comp * slab_rows + top + part_rows)
                s_parts[part, LANES * q : LANES * (q + 1)] = high
                s_parts[part, width + LANES * q : width + LANES * (q + 1)] = low
                s_parts[part, 2 * width + LANES * q : 2 * width + LANES * (q + 1)] = high
        if comp == 0:
            store(pick, pick_to)
            if rounds == 2:
                store(later, later_to)
            store(packed.at[:, spread_rows:], packed_to.at[:, spread_rows:])
            fetch[10].wait()
            high, low = split(x_here[...])
            x_parts[:width] = high
            x_parts[width : 2 * width] = high
            x_parts[2 * width :] = low
        spread = jnp.dot(s_parts[here], x_parts[...], preferred_element_type=jnp.float32)
        if strip % 16 == 0:
            turned = spread.astype(packed.dtype).T
            part = slice(comp * strip, (comp + 1) * strip)
            for partner in range(strips):
                packed[partner, part, :slab_rows] = turned[
                    partner * strip : (partner + 1) * strip
                ]
            store(packed.at[:, part], packed_to.at[:, part])
        else:
            spread_all[comp] = spread.T
    if strip % 16:
        for partner in range(strips):
            part = slice(partner * strip, (partner + 1) * strip)
            both = jnp.concatenate([spread_all[comp, part] for comp in range(comps)], axis=0)
            packed[partner, :spread_rows, :slab_rows] = both.astype(packed.dtype)
        store(packed.at[:, :spread_rows], packed_to.at[:, :spread_rows])
    for copy in stored:
        copy.wait()


def join_kernel(slabs, spread_rows, z_kernel, arrived, kept, *sent):
    slab_rows = z_kernel.shape[0] // slabs
    extra_rows = kept.shape[0] - spread_rows if sent else 0
    total = arrived[0, :spread_rows, :slab_rows].astype(jnp.float32)
    for sender in range(1, arrived.shape[0]):
        total = total + arrived[sender, :spread_rows, :slab_rows].astype(jnp.float32)
    high, low = split(total)
    left = jnp.concatenate([high, low, high], axis=1)

    def part(slab):
        start = pl.multiple_of(slab * slab_rows, slab_rows)
        z_high, z_low = split(z_kernel[pl.ds(start, slab_rows), :])
        right = jnp.concatenate([z_high, z_high, z_low], axis=1)
        return lax.dot_general(left, right, NT_DIMS, preferred_element_type=jnp.float32)

    if sent:
        me = lax.axis_index("dom")
        sent[0][:spread_rows] = part(1 - me)
        kept[:spread_rows] = part(me)
        if extra_rows:
            records = jnp.max(arrived[:, spread_rows:].astype(jnp.float32), axis=0)
            is_column = lax.rem(lax.broadcasted_iota(jnp.int32, records.shape, 0), FIELDS) == 1
            most = jnp.max(jnp.where(is_column, records, -1.0))
            flag = jnp.full((extra_rows, slab_rows), jnp.where(most >= MORE - 1.0, 1.0, 0.0))
            sent[0][spread_rows:] = flag
            kept[spread_rows:] = flag
    else:
        for slab in range(slabs):
            kept[slab] = part(slab)


def unpack_kernel(spread_rows, arrived, records, chosen):
    senders = arrived.shape[0]
    record_rows = arrived.shape[1] - spread_rows
    across = arrived.shape[2] // LANES
    blocks = record_rows * across // FIELDS
    line = lax.broadcasted_iota(jnp.int32, (record_rows, LANES), 0)
    is_column = lax.rem(line, FIELDS) == 1
    first_line = lax.broadcasted_iota(jnp.int32, (record_rows, 1), 0)
    first_column = lax.rem(first_line, FIELDS) == 1
    masks = []
    for sender in range(senders):
        mask = jnp.float32(0.0)
        for side in range(across):
            lanes = slice(side * LANES, (side + 1) * LANES)
            value = arrived[sender, spread_rows:, lanes].astype(jnp.float32)
            value = jnp.where(is_column & (value >= MORE - 1.0), value - MORE, value)
            records[sender, side * record_rows : (side + 1) * record_rows] = value
            taken = first_column & (jnp.max(value, axis=1, keepdims=True) >= 0.0)
            seat = first_line // FIELDS + side * (record_rows // FIELDS)
            bit = jnp.left_shift(jnp.ones_like(seat), seat).astype(jnp.float32)
            mask = mask + jnp.sum(jnp.where(taken, bit, 0.0))
        masks.append(mask.astype(jnp.int32))
    records[senders] = jnp.full(records.shape[1:], -1.0, jnp.float32)
    count = jnp.int32(0)
    for sender in range(senders):
        for block in range(blocks):
            chosen[1 + count] = sender * blocks + block
            count = count + ((masks[sender] >> block) & 1)
    chosen[0] = (count + (GROUP - 1)) // GROUP
    for member in range(GROUP):
        chosen[1 + count + member] = senders * blocks


def read_group(blocks, chosen, records, group):
    where = []
    for member in range(GROUP):
        block = chosen[1 + group * GROUP + member]
        where.append((block // blocks, lax.rem(block, blocks)))

    lines = jnp.concatenate(
        [records[sender, pl.ds(own * FIELDS, FIELDS), :] for sender, own in where], axis=1
    )

    def field(index):
        return lines[index : index + 1]

    return where, field


def one_hot(index, size):
    iota = lax.broadcasted_iota(jnp.int32, (size, index.shape[1]), 0).astype(jnp.float32)
    return iota == index


def one_hot_rows(row, size):
    iota = lax.broadcasted_iota(jnp.int32, (size, row.shape[1]), 0)
    if size <= 256:
        hit = iota.astype(jnp.bfloat16) == row.astype(jnp.bfloat16)
        return jnp.where(hit, jnp.bfloat16(1.0), jnp.bfloat16(0.0))
    return jnp.where(iota.astype(jnp.float32) == row, 1.0, 0.0).astype(jnp.bfloat16)


def deposit_kernel(blocks, chosen, records, after, *refs):
    del after
    extra, (deposit, total) = refs[:-2], refs[-2:]
    strip, slab_rows = deposit.shape[1:]
    total[...] = jnp.zeros_like(total)

    def one_group(group, carry):
        _, field = read_group(blocks, chosen, records, group)
        hit = one_hot(field(1), strip)
        weighted = [jnp.where(hit, field(2 + comp), 0.0) for comp in range(2)]
        total[...] += lax.dot_general(
            one_hot_rows(field(0), slab_rows),
            jnp.concatenate(weighted, axis=0).astype(jnp.bfloat16),
            NT_DIMS,
            preferred_element_type=jnp.float32,
        )
        return carry

    lax.fori_loop(0, chosen[0], one_group, 0)
    turned = total[...].T
    for comp in range(2):
        own = turned[comp * strip : (comp + 1) * strip]
        deposit[comp] = own + extra[0][comp] if extra else own


def sample_kernel(blocks, chosen, records, *refs):
    parts, (field_out, samples, flag, found_all) = refs[:-4], refs[-4:]
    strip, slab_rows = field_out.shape[1:]
    if len(parts) == 1:
        total = parts[0][0]
        for slab in range(1, parts[0].shape[0]):
            total = total + parts[0][slab]
    else:
        total = parts[0][: 2 * strip] + parts[1][: 2 * strip]
    if len(parts) == 2 and parts[0].shape[0] > 2 * strip:
        most = jnp.max(jnp.maximum(parts[0][2 * strip :], parts[1][2 * strip :]))
        flag[0] = jnp.where(most > 0.5, 1, 0)
    else:
        flag[0] = 0
    field_out[0] = total[:strip]
    field_out[1] = total[strip:]
    rounded = total.astype(jnp.bfloat16)
    found_all[...] = jnp.zeros_like(found_all)

    def one_group(group, carry):
        where, field = read_group(blocks, chosen, records, group)
        row_hot = one_hot_rows(field(0), slab_rows)
        found = jnp.dot(rounded, row_hot, preferred_element_type=jnp.float32)
        hit = one_hot(field(1), strip)
        values = []
        for comp in range(2):
            picked = jnp.where(hit, found[comp * strip : (comp + 1) * strip], 0.0)
            values.append(jnp.sum(picked, axis=0, keepdims=True))
        values = jnp.concatenate(values, axis=0)
        for member, (sender, own) in enumerate(where):
            found_all[sender, pl.ds(2 * own, 2), :] = values[
                :, LANES * member : LANES * (member + 1)
            ]
        return carry

    lax.fori_loop(0, chosen[0], one_group, 0)
    samples[...] = found_all[: samples.shape[0]].astype(samples.dtype)


def found_for_blocks(pick, received):
    flat = received[...].reshape(received.shape[0] * received.shape[1], LANES)
    return jnp.dot(pick, flat, preferred_element_type=jnp.float32)


def more_kernel(pick, received, more):
    more[...] = found_for_blocks(pick[1], received)


def kick_kernel(pick, pushed, received, *refs):
    more, kicked = refs[:-1], refs[-1]
    blocks = pushed.shape[1]
    values = [pushed[i] for i in range(6)]
    total = found_for_blocks(pick[0], received)
    if more:
        total = total + more[0][...]
    for block in range(blocks):
        lines = [value[block : block + 1] for value in values]
        lines[5] = lines[5] + 0.5 * total[2 * block : 2 * block + 1]
        lines[1] = lines[1] + 0.5 * total[2 * block + 1 : 2 * block + 2]
        kicked[:, LANES * block : LANES * (block + 1)] = jnp.concatenate(lines, axis=0)


def local(
    coords,
    charge,
    row_index,
    block_col,
    col_offset,
    transfer_map,
    history,
    retard_index,
    retard_frac,
    retard_weight,
    z_kernel,
    x_kernel,
):
    strips = lax.axis_size("hist")
    slabs = lax.axis_size("dom")
    count_steps, comps, slab_rows, width = history.shape
    strip = width // strips
    particles = coords.shape[1]
    blocks = block_col.shape[0]
    tile = (blocks, LANES)
    spread_rows = comps * strip
    row_lanes = max(slab_rows, LANES)
    seats, second_round = seats_of(strips, slabs, blocks)
    rounds = 2 if second_round else 1
    record_rows = FIELDS * seats * LANES // row_lanes
    packed_rows = spread_rows + record_rows

    f32, bf16 = jnp.float32, jnp.bfloat16
    packed, later, pick = call(
        functools.partial(source_kernel, strips),
        (
            jax.ShapeDtypeStruct((strips, packed_rows, row_lanes), bf16),
            jax.ShapeDtypeStruct((strips, record_rows, row_lanes), bf16),
            jax.ShapeDtypeStruct((rounds, comps * blocks, comps * strips * seats), bf16),
        ),
        [HBM] * 11,
        (HBM, HBM, HBM),
        [
            pltpu.SMEM((1, blocks), jnp.int32),
            pltpu.SMEM((1, count_steps), jnp.int32),
            pltpu.SMEM((1, count_steps), f32),
            pltpu.SMEM((1, count_steps), f32),
            pltpu.VMEM(coords.shape, f32),
            pltpu.VMEM(tile, f32),
            pltpu.VMEM(tile, jnp.int32),
            pltpu.VMEM(tile, jnp.int32),
            pltpu.SMEM(transfer_map.shape, f32),
            pltpu.VMEM(history.shape, bf16),
            pltpu.VMEM((width, width), f32),
            pltpu.VMEM((3 * width, width), bf16),
            pltpu.VMEM((comps * slab_rows, 3 * width), bf16),
            pltpu.VMEM((comps, width, slab_rows), f32),
            pltpu.VMEM((2 * LANES * count_steps, 2 * LANES), bf16),
            pltpu.VMEM((LANES * count_steps, 2 * LANES), bf16),
            pltpu.VMEM((strips, packed_rows, row_lanes), bf16),
            pltpu.VMEM((strips, record_rows, row_lanes), bf16),
            pltpu.SMEM((1, strips), jnp.int32),
            pltpu.VMEM((rounds, comps * blocks, comps * strips * seats), bf16),
            pltpu.VMEM((FIELDS * (rounds * strips * seats + 2), LANES), f32),
            pltpu.SemaphoreType.DMA((20,)),
        ],
        flops=6 * comps * slab_rows * width * width,
        moved=history.size * 2 + x_kernel.size * 4,
        limit=LIMIT,
    )(
        block_col.reshape(1, blocks),
        retard_index.reshape(1, count_steps),
        retard_frac.reshape(1, count_steps),
        retard_weight.reshape(1, count_steps),
        coords,
        charge.reshape(tile),
        row_index.reshape(tile),
        col_offset.reshape(tile),
        transfer_map,
        history,
        x_kernel,
    )
    arrived = lax.all_to_all(packed, "hist", 0, 0, tiled=True)

    part = jax.ShapeDtypeStruct((spread_rows + (8 if second_round else 0), slab_rows), f32)
    parts = call(
        functools.partial(join_kernel, slabs, spread_rows),
        (part, part) if slabs == 2 else jax.ShapeDtypeStruct((slabs,) + part.shape, f32),
        [VMEM, VMEM],
        (VMEM, VMEM) if slabs == 2 else VMEM,
        flops=1 << 27,
        moved=1 << 20,
    )(z_kernel, arrived)
    if slabs == 2:
        kept, sent = parts
        parts = [kept, lax.ppermute(sent, "dom", [(0, 1), (1, 0)])]
    else:
        parts = [lax.all_to_all(parts, "dom", 0, 0, tiled=True)]

    def unpack(arrived, spread_rows):
        return call(
            functools.partial(unpack_kernel, spread_rows),
            (
                jax.ShapeDtypeStruct((strips + 1, FIELDS * seats, LANES), f32),
                jax.ShapeDtypeStruct((strips * seats + 32,), jnp.int32),
            ),
            [VMEM],
            (VMEM, SMEM),
            flops=1 << 20,
            moved=1 << 20,
        )(arrived)

    def sample(chosen, records, parts):
        return call(
            functools.partial(sample_kernel, seats),
            (
                jax.ShapeDtypeStruct((comps, strip, slab_rows), f32),
                jax.ShapeDtypeStruct((strips, comps * seats, LANES), bf16),
                jax.ShapeDtypeStruct((8,), jnp.int32),
            ),
            [SMEM, VMEM] + [VMEM] * len(parts),
            (VMEM, VMEM, SMEM),
            [pltpu.VMEM((strips + 1, comps * seats, LANES), f32)],
            flops=1 << 29,
            moved=1 << 20,
        )(chosen, records, *parts)

    def deposits(chosen, records, after, *extra):
        return call(
            functools.partial(deposit_kernel, seats),
            jax.ShapeDtypeStruct((comps, strip, slab_rows), f32),
            [SMEM, VMEM, HBM] + [VMEM] * len(extra),
            VMEM,
            [pltpu.VMEM((slab_rows, comps * strip), f32)],
            flops=1 << 29,
            moved=1 << 20,
        )(chosen, records, after, *extra)

    def exchange(value):
        return lax.all_to_all(value, "hist", 0, 0, tiled=True)

    records, chosen = unpack(arrived, spread_rows)
    field, samples, flag = sample(chosen, records, parts)
    more, extra = [], []
    if second_round:

        def another(later, field, pick):
            records, chosen = unpack(exchange(later), 0)
            whole = field.reshape(1, spread_rows, slab_rows)
            _, samples, _ = sample(chosen, records, [whole])
            more = call(
                more_kernel,
                jax.ShapeDtypeStruct((comps * blocks, LANES), f32),
                [VMEM, VMEM],
                VMEM,
            )(pick, exchange(samples))
            return more, deposits(chosen, records, samples)

        def nothing(later, field, pick):
            return jnp.zeros((comps * blocks, LANES), f32), jnp.zeros(field.shape, f32)

        found, left = lax.cond(flag[0] > 0, another, nothing, later, field, pick)
        more, extra = [found], [left]
    received = exchange(samples)
    deposit = deposits(chosen, records, samples, *extra)
    pushed = call(
        push_kernel,
        jax.ShapeDtypeStruct((6,) + tile, f32),
        [SMEM, VMEM, HBM],
        VMEM,
        flops=1200 * particles,
        moved=1 << 18,
    )(transfer_map, coords, samples)
    kicked = call(
        kick_kernel,
        jax.ShapeDtypeStruct((6, particles), f32),
        [VMEM] * (3 + len(more)),
        VMEM,
        flops=1 << 16,
        moved=1 << 18,
    )(pick, pushed, received, *more)
    return kicked, jnp.transpose(field, (0, 2, 1)), jnp.transpose(deposit, (0, 2, 1))


def solution(mesh):
    return jax.shard_map(
        local,
        mesh=mesh,
        in_specs=(
            P(None, ("dom", "hist")),
            P(("dom", "hist")),
            P(("dom", "hist")),
            P(("dom", "hist")),
            P(("dom", "hist")),
            P(),
            P("hist", None, "dom", None),
            P("hist"),
            P("hist"),
            P("hist"),
            P(None, "dom"),
            P(),
        ),
        out_specs=(P(None, ("dom", "hist")), P(None, "dom", "hist"), P(None, "dom", "hist")),
        check_vma=False,
    )
```

```python
import functools

import jax
import jax.numpy as jnp
from jax import lax
from jax.experimental import pallas as pl
from jax.experimental.pallas import tpu as pltpu
from jax.sharding import PartitionSpec as P

LANES = 128
GROUP = 16
SPAN = 16
SEATS = 8
FIELDS = 4
MORE = 64.0
NT_DIMS = (((1,), (1,)), ((), ()))
VMEM = pl.BlockSpec(memory_space=pltpu.VMEM)
SMEM = pl.BlockSpec(memory_space=pltpu.SMEM)
HBM = pl.BlockSpec(memory_space=pltpu.HBM)
LIMIT = 59 * 1024 * 1024
SMALL = 16 * 1024 * 1024


def call(kernel, out_shape, in_specs, out_specs, scratch=(), flops=0, moved=0, limit=SMALL):
    return pl.pallas_call(
        kernel,
        out_shape=out_shape,
        in_specs=in_specs,
        out_specs=out_specs,
        scratch_shapes=scratch,
        compiler_params=pltpu.CompilerParams(vmem_limit_bytes=limit),
        cost_estimate=pl.CostEstimate(flops=flops, bytes_accessed=moved, transcendentals=0),
    )


def split(value):
    high = value.astype(jnp.bfloat16)
    return high, (value - high.astype(jnp.float32)).astype(jnp.bfloat16)


def seats_of(strips, slabs, blocks):
    if strips == 16 and slabs == 2 and blocks == 2 * SEATS:
        return SEATS, True
    return blocks, False


def strips_met(strip):
    return (SPAN + strip - 2) // strip + 1


def lag_band(lag, near, far):
    row = lax.broadcasted_iota(jnp.int32, (2 * LANES, LANES), 0)
    column = lax.broadcasted_iota(jnp.int32, (2 * LANES, LANES), 1)
    behind = column + LANES - row
    weight = jnp.where(behind == lag, near, jnp.where(behind == lag + 1, far, 0.0))
    return jnp.concatenate(split(weight), axis=1)


def push(coords, transfer, wanted):
    blocks = coords.shape[1] // LANES
    u = [
        jnp.concatenate(
            [coords[i : i + 1, LANES * b : LANES * (b + 1)] for b in range(blocks)], axis=0
        )
        for i in range(6)
    ]
    total = [jnp.full((blocks, LANES), transfer[i, 0], jnp.float32) for i in wanted]
    pairs = {}
    terms = list(u)
    for first in range(6):
        for second in range(first, 6):
            pairs[first, second] = u[first] * u[second]
            terms.append(pairs[first, second])
    for first in range(6):
        for second in range(first, 6):
            for third in range(second, 6):
                terms.append(pairs[first, second] * u[third])
    for column, term in enumerate(terms):
        total = [value + transfer[i, 1 + column] * term for i, value in zip(wanted, total)]
    return total


def push_kernel(transfer, coords, after, pushed):
    del after
    for i, value in enumerate(push(coords, transfer, range(6))):
        pushed[i] = value


def particle_fields(coords, charge, rows, offsets, block_col, transfer, slab_rows):
    blocks = charge.shape[0]
    weight0 = charge[...]
    weight1 = weight0 * push(coords, transfer, [1])[0]
    row_of = lax.broadcasted_iota(jnp.int32, (blocks, LANES), 0)
    column = offsets[...]
    for b in range(blocks):
        column = column + jnp.where(row_of == b, block_col[0, b], 0)
    return lax.rem(rows[...], slab_rows), column, weight0, weight1


def seat_blocks(strips, strip, seats, rounds, block_col, fields, counts, pick, stage):
    row, column, weight0, weight1 = fields
    blocks = row.shape[0]
    nobody = rounds * strips * seats
    meets = strips_met(strip)
    stage[...] = jnp.full(stage.shape, -1.0, jnp.float32)
    for place in range(strips):
        counts[0, place] = 0
    left_out = jnp.int32(0)
    pick_row = lax.broadcasted_iota(jnp.int32, (2 * blocks, LANES), 0)
    lane = lax.broadcasted_iota(jnp.int32, (2 * blocks, LANES), 1)
    wanted = [jnp.zeros((2 * blocks, LANES), jnp.int32)] * meets
    is_column = lax.broadcasted_iota(jnp.int32, (FIELDS, LANES), 0) == 1
    fields = [field.astype(jnp.float32) for field in (row, column, weight0, weight1)]
    for block in range(blocks):
        tile = jnp.concatenate([field[block : block + 1] for field in fields], axis=0)
        start = block_col[0, block]
        first = start // strip
        for step in range(meets):
            place = jnp.minimum(first + step, strips - 1)
            met = (first + step) * strip <= start + (SPAN - 1)
            taken = counts[0, place]
            counts[0, place] = taken + jnp.where(met, 1, 0)
            later = taken // seats
            number = (later * strips + place) * seats + lax.rem(taken, seats)
            number = jnp.where(met, number, nobody)
            left_out = jnp.maximum(left_out, jnp.where(met, later, 0))
            wanted[step] = jnp.where(pick_row >> 1 == block, 2 * number, wanted[step])
            own = tile - (place * strip).astype(jnp.float32)
            own = jnp.where((own >= 0.0) & (own < strip), own, -1.0)
            stage[pl.ds(number * FIELDS, FIELDS), :] = jnp.where(is_column, own, tile)
    lines = 2 * strips * seats
    for turn in range(rounds):
        for left in range(0, lines, LANES):
            line = lane + (turn * lines + left)
            hit = wanted[0] + (pick_row & 1) == line
            for step in range(1, meets):
                hit = hit | (wanted[step] + (pick_row & 1) == line)
            pick[turn, :, left : left + LANES] = jnp.where(hit, 1.0, 0.0).astype(pick.dtype)
    return left_out


def source_kernel(
    strips,
    block_col_from,
    lags_from,
    fracs_from,
    weights_from,
    coords_from,
    charge_from,
    rows_from,
    offsets_from,
    transfer_from,
    history,
    x_kernel,
    packed_to,
    later_to,
    pick_to,
    block_col,
    lags,
    fracs,
    weights,
    coords,
    charge,
    rows,
    offsets,
    transfer,
    frames,
    x_here,
    x_parts,
    s_parts,
    spread_all,
    bands,
    first_bands,
    packed,
    later,
    counts,
    pick,
    stage,
    sems,
):
    count_steps, comps, slab_rows, width = history.shape
    blocks = charge.shape[0]
    strip = width // strips
    spread_rows = comps * strip
    record_rows = packed.shape[1] - spread_rows
    across = packed.shape[2] // LANES
    seats = record_rows * across // FIELDS
    rounds = stage.shape[0] // (FIELDS * strips * seats)
    pairs = [
        (lags_from, lags),
        (fracs_from, fracs),
        (weights_from, weights),
        (block_col_from, block_col),
        (coords_from, coords),
        (charge_from, charge),
        (rows_from, rows),
        (offsets_from, offsets),
        (transfer_from, transfer),
    ]
    for comp in range(comps):
        pairs += [(history.at[:, comp], frames.at[:, comp])]
        if comp == 0:
            pairs += [(x_kernel, x_here)]
    fetch = [
        pltpu.make_async_copy(source, target, sems.at[index])
        for index, (source, target) in enumerate(pairs)
    ]
    fetch[9].start()
    for copy in fetch[:9] + fetch[10:]:
        copy.start()
    stored = []

    def store(source, target):
        copy = pltpu.make_async_copy(source, target, sems.at[len(fetch) + len(stored)])
        copy.start()
        stored.append(copy)

    for copy in fetch[:9]:
        copy.wait()
    for t in range(count_steps):
        far = weights[0, t] * fracs[0, t]
        near = weights[0, t] * (1.0 - fracs[0, t])
        bands[2 * LANES * t : 2 * LANES * (t + 1)] = lag_band(lags[0, t], near, far)
        first_bands[LANES * t : LANES * (t + 1)] = bands[
            2 * LANES * t + LANES : 2 * LANES * (t + 1)
        ]

    row, column, weight0, weight1 = particle_fields(
        coords, charge, rows, offsets, block_col, transfer, slab_rows
    )
    left_out = seat_blocks(
        strips,
        strip,
        seats,
        rounds,
        block_col,
        (row, column, weight0, weight1),
        counts,
        pick,
        stage,
    )
    is_column = lax.rem(lax.broadcasted_iota(jnp.int32, (record_rows, LANES), 0), FIELDS) == 1
    mark = jnp.where(is_column, MORE * left_out.astype(jnp.float32), 0.0)
    for turn in range(rounds):
        for partner in range(strips):
            for side in range(across):
                start = ((turn * strips + partner) * across + side) * record_rows
                value = stage[start : start + record_rows]
                lanes = slice(side * LANES, (side + 1) * LANES)
                if turn == 0:
                    packed[partner, spread_rows:, lanes] = (value + mark).astype(packed.dtype)
                else:
                    later[partner, :, lanes] = value.astype(later.dtype)

    for comp in range(comps):
        fetch[9 + (comp + 1 if comp else 0)].wait()
        here = slice(comp * slab_rows, (comp + 1) * slab_rows)
        part_rows = min(128, slab_rows)
        for top in range(0, slab_rows, part_rows):
            for q in range(width // LANES):
                before = slice(LANES * max(q - 1, 0), LANES * (q + 1))
                steps = [
                    frames[t, comp, top : top + part_rows, before] for t in range(count_steps)
                ]
                both = jnp.dot(
                    jnp.concatenate(steps, axis=1),
                    bands[...] if q else first_bands[...],
                    preferred_element_type=jnp.float32,
                )
                high, low = split(both[:, :LANES] + both[:, LANES:])
                part = slice(comp * slab_rows + top, comp * slab_rows + top + part_rows)
                s_parts[part, LANES * q : LANES * (q + 1)] = high
                s_parts[part, width + LANES * q : width + LANES * (q + 1)] = low
                s_parts[part, 2 * width + LANES * q : 2 * width + LANES * (q + 1)] = high
        if comp == 0:
            store(pick, pick_to)
            if rounds == 2:
                store(later, later_to)
            store(packed.at[:, spread_rows:], packed_to.at[:, spread_rows:])
            fetch[10].wait()
            high, low = split(x_here[...])
            x_parts[:width] = high
            x_parts[width : 2 * width] = high
            x_parts[2 * width :] = low
        spread = jnp.dot(s_parts[here], x_parts[...], preferred_element_type=jnp.float32)
        if strip % 16 == 0:
            turned = spread.astype(packed.dtype).T
            part = slice(comp * strip, (comp + 1) * strip)
            for partner in range(strips):
                packed[partner, part, :slab_rows] = turned[
                    partner * strip : (partner + 1) * strip
                ]
            store(packed.at[:, part], packed_to.at[:, part])
        else:
            spread_all[comp] = spread.T
    if strip % 16:
        for partner in range(strips):
            part = slice(partner * strip, (partner + 1) * strip)
            both = jnp.concatenate([spread_all[comp, part] for comp in range(comps)], axis=0)
            packed[partner, :spread_rows, :slab_rows] = both.astype(packed.dtype)
        store(packed.at[:, :spread_rows], packed_to.at[:, :spread_rows])
    for copy in stored:
        copy.wait()


def join_kernel(slabs, spread_rows, z_kernel, arrived, kept, *sent):
    slab_rows = z_kernel.shape[0] // slabs
    extra_rows = kept.shape[0] - spread_rows if sent else 0
    total = arrived[0, :spread_rows, :slab_rows].astype(jnp.float32)
    for sender in range(1, arrived.shape[0]):
        total = total + arrived[sender, :spread_rows, :slab_rows].astype(jnp.float32)
    high, low = split(total)
    left = jnp.concatenate([high, low, high], axis=1)

    def part(slab):
        start = pl.multiple_of(slab * slab_rows, slab_rows)
        z_high, z_low = split(z_kernel[pl.ds(start, slab_rows), :])
        right = jnp.concatenate([z_high, z_high, z_low], axis=1)
        return lax.dot_general(left, right, NT_DIMS, preferred_element_type=jnp.float32)

    if sent:
        me = lax.axis_index("dom")
        sent[0][:spread_rows] = part(1 - me)
        kept[:spread_rows] = part(me)
        if extra_rows:
            records = jnp.max(arrived[:, spread_rows:].astype(jnp.float32), axis=0)
            is_column = lax.rem(lax.broadcasted_iota(jnp.int32, records.shape, 0), FIELDS) == 1
            most = jnp.max(jnp.where(is_column, records, -1.0))
            flag = jnp.full((extra_rows, slab_rows), jnp.where(most >= MORE - 1.0, 1.0, 0.0))
            sent[0][spread_rows:] = flag
            kept[spread_rows:] = flag
    else:
        for slab in range(slabs):
            kept[slab] = part(slab)


def unpack_kernel(spread_rows, arrived, records, chosen):
    senders = arrived.shape[0]
    record_rows = arrived.shape[1] - spread_rows
    across = arrived.shape[2] // LANES
    blocks = record_rows * across // FIELDS
    line = lax.broadcasted_iota(jnp.int32, (record_rows, LANES), 0)
    is_column = lax.rem(line, FIELDS) == 1
    first_line = lax.broadcasted_iota(jnp.int32, (record_rows, 1), 0)
    first_column = lax.rem(first_line, FIELDS) == 1
    masks = []
    for sender in range(senders):
        mask = jnp.float32(0.0)
        for side in range(across):
            lanes = slice(side * LANES, (side + 1) * LANES)
            value = arrived[sender, spread_rows:, lanes].astype(jnp.float32)
            value = jnp.where(is_column & (value >= MORE - 1.0), value - MORE, value)
            records[sender, side * record_rows : (side + 1) * record_rows] = value
            taken = first_column & (jnp.max(value, axis=1, keepdims=True) >= 0.0)
            seat = first_line // FIELDS + side * (record_rows // FIELDS)
            bit = jnp.left_shift(jnp.ones_like(seat), seat).astype(jnp.float32)
            mask = mask + jnp.sum(jnp.where(taken, bit, 0.0))
        masks.append(mask.astype(jnp.int32))
    records[senders] = jnp.full(records.shape[1:], -1.0, jnp.float32)
    count = jnp.int32(0)
    for sender in range(senders):
        for block in range(blocks):
            chosen[1 + count] = sender * blocks + block
            count = count + ((masks[sender] >> block) & 1)
    chosen[0] = (count + (GROUP - 1)) // GROUP
    for member in range(GROUP):
        chosen[1 + count + member] = senders * blocks


def read_group(blocks, chosen, records, group):
    where = []
    for member in range(GROUP):
        block = chosen[1 + group * GROUP + member]
        where.append((block // blocks, lax.rem(block, blocks)))

    lines = jnp.concatenate(
        [records[sender, pl.ds(own * FIELDS, FIELDS), :] for sender, own in where], axis=1
    )

    def field(index):
        return lines[index : index + 1]

    return where, field


def one_hot(index, size):
    iota = lax.broadcasted_iota(jnp.int32, (size, index.shape[1]), 0).astype(jnp.float32)
    return iota == index


def one_hot_rows(row, size):
    iota = lax.broadcasted_iota(jnp.int32, (size, row.shape[1]), 0)
    if size <= 256:
        hit = iota.astype(jnp.bfloat16) == row.astype(jnp.bfloat16)
        return jnp.where(hit, jnp.bfloat16(1.0), jnp.bfloat16(0.0))
    return jnp.where(iota.astype(jnp.float32) == row, 1.0, 0.0).astype(jnp.bfloat16)


def deposit_kernel(blocks, chosen, records, after, *refs):
    del after
    extra, (deposit, total) = refs[:-2], refs[-2:]
    strip, slab_rows = deposit.shape[1:]
    total[...] = jnp.zeros_like(total)

    def one_group(group, carry):
        _, field = read_group(blocks, chosen, records, group)
        hit = one_hot(field(1), strip)
        weighted = [jnp.where(hit, field(2 + comp), 0.0) for comp in range(2)]
        total[...] += lax.dot_general(
            one_hot_rows(field(0), slab_rows),
            jnp.concatenate(weighted, axis=0).astype(jnp.bfloat16),
            NT_DIMS,
            preferred_element_type=jnp.float32,
        )
        return carry

    lax.fori_loop(0, chosen[0], one_group, 0)
    turned = total[...].T
    for comp in range(2):
        own = turned[comp * strip : (comp + 1) * strip]
        deposit[comp] = own + extra[0][comp] if extra else own


def sample_kernel(blocks, chosen, records, *refs):
    parts, (field_out, samples, flag, found_all) = refs[:-4], refs[-4:]
    strip, slab_rows = field_out.shape[1:]
    if len(parts) == 1:
        total = parts[0][0]
        for slab in range(1, parts[0].shape[0]):
            total = total + parts[0][slab]
    else:
        total = parts[0][: 2 * strip] + parts[1][: 2 * strip]
    if len(parts) == 2 and parts[0].shape[0] > 2 * strip:
        most = jnp.max(jnp.maximum(parts[0][2 * strip :], parts[1][2 * strip :]))
        flag[0] = jnp.where(most > 0.5, 1, 0)
    else:
        flag[0] = 0
    field_out[0] = total[:strip]
    field_out[1] = total[strip:]
    rounded = total.astype(jnp.bfloat16)
    found_all[...] = jnp.zeros_like(found_all)

    def one_group(group, carry):
        where, field = read_group(blocks, chosen, records, group)
        row_hot = one_hot_rows(field(0), slab_rows)
        found = jnp.dot(rounded, row_hot, preferred_element_type=jnp.float32)
        hit = one_hot(field(1), strip)
        values = []
        for comp in range(2):
            picked = jnp.where(hit, found[comp * strip : (comp + 1) * strip], 0.0)
            values.append(jnp.sum(picked, axis=0, keepdims=True))
        values = jnp.concatenate(values, axis=0)
        for member, (sender, own) in enumerate(where):
            found_all[sender, pl.ds(2 * own, 2), :] = values[
                :, LANES * member : LANES * (member + 1)
            ]
        return carry

    lax.fori_loop(0, chosen[0], one_group, 0)
    samples[...] = found_all[: samples.shape[0]].astype(samples.dtype)


def found_for_blocks(pick, received):
    flat = received[...].reshape(received.shape[0] * received.shape[1], LANES)
    return jnp.dot(pick, flat, preferred_element_type=jnp.float32)


def more_kernel(pick, received, more):
    more[...] = found_for_blocks(pick[1], received)


def kick_kernel(pick, pushed, received, *refs):
    more, kicked = refs[:-1], refs[-1]
    blocks = pushed.shape[1]
    values = [pushed[i] for i in range(6)]
    total = found_for_blocks(pick[0], received)
    if more:
        total = total + more[0][...]
    for block in range(blocks):
        lines = [value[block : block + 1] for value in values]
        lines[5] = lines[5] + 0.5 * total[2 * block : 2 * block + 1]
        lines[1] = lines[1] + 0.5 * total[2 * block + 1 : 2 * block + 2]
        kicked[:, LANES * block : LANES * (block + 1)] = jnp.concatenate(lines, axis=0)


def local(
    coords,
    charge,
    row_index,
    block_col,
    col_offset,
    transfer_map,
    history,
    retard_index,
    retard_frac,
    retard_weight,
    z_kernel,
    x_kernel,
):
    strips = lax.axis_size("hist")
    slabs = lax.axis_size("dom")
    count_steps, comps, slab_rows, width = history.shape
    strip = width // strips
    particles = coords.shape[1]
    blocks = block_col.shape[0]
    tile = (blocks, LANES)
    spread_rows = comps * strip
    row_lanes = max(slab_rows, LANES)
    seats, second_round = seats_of(strips, slabs, blocks)
    rounds = 2 if second_round else 1
    record_rows = FIELDS * seats * LANES // row_lanes
    packed_rows = spread_rows + record_rows

    f32, bf16 = jnp.float32, jnp.bfloat16
    packed, later, pick = call(
        functools.partial(source_kernel, strips),
        (
            jax.ShapeDtypeStruct((strips, packed_rows, row_lanes), bf16),
            jax.ShapeDtypeStruct((strips, record_rows, row_lanes), bf16),
            jax.ShapeDtypeStruct((rounds, comps * blocks, comps * strips * seats), bf16),
        ),
        [HBM] * 11,
        (HBM, HBM, HBM),
        [
            pltpu.SMEM((1, blocks), jnp.int32),
            pltpu.SMEM((1, count_steps), jnp.int32),
            pltpu.SMEM((1, count_steps), f32),
            pltpu.SMEM((1, count_steps), f32),
            pltpu.VMEM(coords.shape, f32),
            pltpu.VMEM(tile, f32),
            pltpu.VMEM(tile, jnp.int32),
            pltpu.VMEM(tile, jnp.int32),
            pltpu.SMEM(transfer_map.shape, f32),
            pltpu.VMEM(history.shape, bf16),
            pltpu.VMEM((width, width), f32),
            pltpu.VMEM((3 * width, width), bf16),
            pltpu.VMEM((comps * slab_rows, 3 * width), bf16),
            pltpu.VMEM((comps, width, slab_rows), f32),
            pltpu.VMEM((2 * LANES * count_steps, 2 * LANES), bf16),
            pltpu.VMEM((LANES * count_steps, 2 * LANES), bf16),
            pltpu.VMEM((strips, packed_rows, row_lanes), bf16),
            pltpu.VMEM((strips, record_rows, row_lanes), bf16),
            pltpu.SMEM((1, strips), jnp.int32),
            pltpu.VMEM((rounds, comps * blocks, comps * strips * seats), bf16),
            pltpu.VMEM((FIELDS * (rounds * strips * seats + 2), LANES), f32),
            pltpu.SemaphoreType.DMA((20,)),
        ],
        flops=6 * comps * slab_rows * width * width,
        moved=history.size * 2 + x_kernel.size * 4,
        limit=LIMIT,
    )(
        block_col.reshape(1, blocks),
        retard_index.reshape(1, count_steps),
        retard_frac.reshape(1, count_steps),
        retard_weight.reshape(1, count_steps),
        coords,
        charge.reshape(tile),
        row_index.reshape(tile),
        col_offset.reshape(tile),
        transfer_map,
        history,
        x_kernel,
    )
    arrived = lax.all_to_all(packed, "hist", 0, 0, tiled=True)

    part = jax.ShapeDtypeStruct((spread_rows + (8 if second_round else 0), slab_rows), f32)
    parts = call(
        functools.partial(join_kernel, slabs, spread_rows),
        (part, part) if slabs == 2 else jax.ShapeDtypeStruct((slabs,) + part.shape, f32),
        [VMEM, VMEM],
        (VMEM, VMEM) if slabs == 2 else VMEM,
        flops=1 << 27,
        moved=1 << 20,
    )(z_kernel, arrived)
    if slabs == 2:
        kept, sent = parts
        parts = [kept, lax.ppermute(sent, "dom", [(0, 1), (1, 0)])]
    else:
        parts = [lax.all_to_all(parts, "dom", 0, 0, tiled=True)]

    def unpack(arrived, spread_rows):
        return call(
            functools.partial(unpack_kernel, spread_rows),
            (
                jax.ShapeDtypeStruct((strips + 1, FIELDS * seats, LANES), f32),
                jax.ShapeDtypeStruct((strips * seats + 32,), jnp.int32),
            ),
            [VMEM],
            (VMEM, SMEM),
            flops=1 << 20,
            moved=1 << 20,
        )(arrived)

    def sample(chosen, records, parts):
        return call(
            functools.partial(sample_kernel, seats),
            (
                jax.ShapeDtypeStruct((comps, strip, slab_rows), f32),
                jax.ShapeDtypeStruct((strips, comps * seats, LANES), bf16),
                jax.ShapeDtypeStruct((8,), jnp.int32),
            ),
            [SMEM, VMEM] + [VMEM] * len(parts),
            (VMEM, VMEM, SMEM),
            [pltpu.VMEM((strips + 1, comps * seats, LANES), f32)],
            flops=1 << 29,
            moved=1 << 20,
        )(chosen, records, *parts)

    def deposits(chosen, records, after, *extra):
        return call(
            functools.partial(deposit_kernel, seats),
            jax.ShapeDtypeStruct((comps, strip, slab_rows), f32),
            [SMEM, VMEM, HBM] + [VMEM] * len(extra),
            VMEM,
            [pltpu.VMEM((slab_rows, comps * strip), f32)],
            flops=1 << 29,
            moved=1 << 20,
        )(chosen, records, after, *extra)

    def exchange(value):
        return lax.all_to_all(value, "hist", 0, 0, tiled=True)

    records, chosen = unpack(arrived, spread_rows)
    field, samples, flag = sample(chosen, records, parts)
    more, extra = [], []
    if second_round:

        def another(later, field, pick):
            records, chosen = unpack(exchange(later), 0)
            whole = field.reshape(1, spread_rows, slab_rows)
            _, samples, _ = sample(chosen, records, [whole])
            more = call(
                more_kernel,
                jax.ShapeDtypeStruct((comps * blocks, LANES), f32),
                [VMEM, VMEM],
                VMEM,
            )(pick, exchange(samples))
            return more, deposits(chosen, records, samples)

        def nothing(later, field, pick):
            return jnp.zeros((comps * blocks, LANES), f32), jnp.zeros(field.shape, f32)

        found, left = lax.cond(flag[0] > 0, another, nothing, later, field, pick)
        more, extra = [found], [left]
    received = exchange(samples)
    deposit = deposits(chosen, records, samples, *extra)
    pushed = call(
        push_kernel,
        jax.ShapeDtypeStruct((6,) + tile, f32),
        [SMEM, VMEM, HBM],
        VMEM,
        flops=1200 * particles,
        moved=1 << 18,
    )(transfer_map, coords, samples)
    kicked = call(
        kick_kernel,
        jax.ShapeDtypeStruct((6, particles), f32),
        [VMEM] * (3 + len(more)),
        VMEM,
        flops=1 << 16,
        moved=1 << 18,
    )(pick, pushed, received, *more)
    return kicked, jnp.transpose(field, (0, 2, 1)), jnp.transpose(deposit, (0, 2, 1))


def solution(mesh):
    return jax.shard_map(
        local,
        mesh=mesh,
        in_specs=(
            P(None, ("dom", "hist")),
            P(("dom", "hist")),
            P(("dom", "hist")),
            P(("dom", "hist")),
            P(("dom", "hist")),
            P(),
            P("hist", None, "dom", None),
            P("hist"),
            P("hist"),
            P("hist"),
            P(None, "dom"),
            P(),
        ),
        out_specs=(P(None, ("dom", "hist")), P(None, "dom", "hist"), P(None, "dom", "hist")),
        check_vma=False,
    )
```
